32 devices in a mesh: dp: 8 (over z, core), tensor: 4 (over y, x).
Axes of the slice: x: 2, y: 2, z: 4, core: 2. Of those that a mesh axis runs over, the one named last changes fastest.
Arguments:
- hidden_in: bfloat16 [8192, 2048], P(('dp', 'tensor')), may hold values from -6 to 6
- doc_lengths: int32 [8, 8], P('dp'), may hold values from 1 to 512, 1024 in all within a row
- gain_attn: bfloat16 [2048], P('dp'), may hold values from 0.099609375 to 1.8984375
- w_query: bfloat16 [2048, 2048], P('dp', 'tensor'), may hold values from -0.125 to 0.125
- w_key: bfloat16 [2048, 2048], P('dp', 'tensor'), may hold values from -0.125 to 0.125
- w_value: bfloat16 [2048, 2048], P('dp', 'tensor'), may hold values from -0.125 to 0.125
- w_out: bfloat16 [2048, 2048], P('tensor', 'dp'), may hold values from -1 to 1
- gain_mlp: bfloat16 [2048], P('dp'), may hold values from 0.099609375 to 1.8984375
- w_gate: bfloat16 [2048, 8192], P('dp', 'tensor'), may hold values from -0.125 to 0.125
- w_up: bfloat16 [2048, 8192], P('dp', 'tensor'), may hold values from -0.125 to 0.125
- w_down: bfloat16 [8192, 2048], P('tensor', 'dp'), may hold values from -0.125 to 0.125
- cotangent: bfloat16 [8192, 2048], P(('dp', 'tensor')), may hold values from -16 to 16
Outputs:
- output: bfloat16 [8192, 2048], P(('dp', 'tensor'))
- input_grad: float32 [8192, 2048], P(('dp', 'tensor'))
- grad_gain_attn: float32 [2048], P(('dp', 'tensor'))
- grad_query: float32 [2048, 2048], P('dp', 'tensor')
- grad_key: float32 [2048, 2048], P('dp', 'tensor')
- grad_value: float32 [2048, 2048], P('dp', 'tensor')
- grad_out: float32 [2048, 2048], P('tensor', 'dp')
- grad_gain_mlp: float32 [2048], P(('dp', 'tensor'))
- grad_gate: float32 [2048, 8192], P('dp', 'tensor')
- grad_up: float32 [2048, 8192], P('dp', 'tensor')
- grad_down: float32 [8192, 2048], P('tensor', 'dp')
The draws below stay inside these ranges and needn't reach their ends.
Inputs may be any that keep to these rules, and one draw needn't show every extreme that they name: `doc_lengths`: each row holds the lengths of the 8 documents of one packed sequence in order; a row sums to 1024 and its largest length is exactly 512.
All inputs are finite; a program needn't handle non-finite values.
Results may differ from the reference program's by a relative error of at most 0.02.
Values may be sent and summed in bfloat16 or wider, within the bound.
A program may use at most 256 MiB of HBM per device.

```python
import math
import jax
import jax.numpy as jnp
import numpy as np
from jax import lax

D = 2048
HEADS = 32
HEAD_DIM = 64
FF = 8192
LEN = 1024
DOCS = 8
MOST = 512
NSEQ = 8
TOKENS = 8192


def draw_cotangent(key, part):
    key = jax.random.fold_in(key, 11)
    first_key = jax.random.fold_in(key, 0)
    rising = jnp.arange(TOKENS, dtype=jnp.float32) / max(TOKENS - 1, 1)
    values = jnp.clip(jax.random.normal(first_key, (TOKENS, D), jnp.float32), -4.0, 4.0)
    factor = 1.0 + 2.0 * rising
    return (values * factor[:, None]).astype(jnp.bfloat16)


def block_scale(own_key, dims, cuts, least, high):
    level, own = 1.0, jax.random.fold_in(own_key, 6)
    for dim, blocks in cuts:
        draws = jnp.exp(jax.random.uniform(jax.random.fold_in(own, dim), (blocks,), jnp.float32, least / len(cuts), high / len(cuts)))
        level = level * jnp.repeat(draws, dims[dim] // blocks).reshape([-1 if axis == dim else 1 for axis in range(len(dims))])
    return level


def length_profile(count, total, most, lean):
    weights = [(1 << 20) // math.isqrt(grade ** lean) + 1 for grade in range(2, count + 1)]
    spare, holding = total - most - (count - 1), [1] * (count - 1)
    while spare > 0:
        free = [i for i in range(count - 1) if holding[i] < most]
        pool, budget = sum([weights[i] for i in free]), spare
        for i in free:
            more = min(most - holding[i], max(1, budget * weights[i] // pool), spare)
            holding[i] = holding[i] + more
            spare = spare - more
    return np.array([most] + holding)


def uneven_parts(rng, number_of, total, bound, slope):
    if number_of == 2:
        one = jax.random.randint(rng, (), max(1, total - bound), min(bound, total - 1) + 1)
        return jnp.stack([one, total - one])
    lengths = jnp.asarray(length_profile(number_of, total, bound, slope), jnp.int32)
    couples = (number_of - 1) // 2
    source_of, sink = lengths[1:1 + 2 * couples:2], lengths[2:2 + 2 * couples:2]
    slack = jnp.minimum(source_of - 1, bound - sink)
    moved = jax.random.randint(jax.random.fold_in(rng, 1), (couples,), 0, 1 << 20) % (slack + 1)
    lengths = lengths.at[1:1 + 2 * couples:2].set(source_of - moved).at[2:2 + 2 * couples:2].set(sink + moved)
    return lengths[jax.random.permutation(jax.random.fold_in(rng, 2), number_of)]


def normal_values(stream_key, extent, width, limit, shards=(), kind=jnp.bfloat16):
    level = block_scale(stream_key, extent, shards, -0.22, 0.18) if shards else 1.0
    drawn = jax.random.normal(stream_key, extent, jnp.float32) * width * level
    return jnp.minimum(jnp.maximum(drawn, -limit), limit).astype(kind)


def setup_inputs(seed: int = 0) -> dict:
    splits = jax.random.split(jax.random.key(seed), 13)
    return {
        "hidden_in": normal_values(splits[0], (TOKENS, D), 1.0, 6.0, ((0, 32),)),
        "doc_lengths": jax.vmap(lambda own: uneven_parts(own, DOCS, LEN, MOST, 2))(jax.random.split(splits[1], NSEQ)).reshape((NSEQ, DOCS)).astype(jnp.int32),
        "gain_attn": jnp.clip(1.0 + 0.18 * jax.random.normal(splits[2], (D,), jnp.float32), 0.099609375, 1.8984375).astype(jnp.bfloat16),
        "w_query": normal_values(splits[3], (D, D), D ** -0.5, 0.125, ((0, 8), (1, 4))),
        "w_key": normal_values(splits[4], (D, D), D ** -0.5, 0.125, ((0, 8), (1, 4))),
        "w_value": normal_values(splits[5], (D, D), D ** -0.5, 0.125, ((0, 8), (1, 4))),
        "w_out": normal_values(splits[6], (D, D), (D // 64) ** -0.5, 1.0, ((0, 4), (1, 8))),
        "gain_mlp": jnp.clip(1.0 + 0.18 * jax.random.normal(splits[7], (D,), jnp.float32), 0.099609375, 1.8984375).astype(jnp.bfloat16),
        "w_gate": normal_values(splits[8], (D, FF), D ** -0.5, 0.125, ((0, 8), (1, 4))),
        "w_up": normal_values(splits[9], (D, FF), D ** -0.5, 0.125, ((0, 8), (1, 4))),
        "w_down": normal_values(splits[10], (FF, D), (FF // 4) ** -0.5, 0.125, ((0, 4), (1, 8))),
        "cotangent": draw_cotangent(jax.random.fold_in(splits[12], 71), 0),
    }


EPSILON = 1e-05
ROPE_BASE = 130000.0

@jax.custom_vjp
def low(v):
    return lax.optimization_barrier(v.astype(jnp.bfloat16)).astype(jnp.float32)

@jax.custom_vjp
def low_back(v):
    return v

def low_keep(v):
    return (low(v), None)

def low_pass(kept, grad):
    return (grad,)

def back_keep(v):
    return (v, None)

def back_low(kept, grad):
    return (low(grad),)
low.defvjp(low_keep, low_pass)
low_back.defvjp(back_keep, back_low)

def matmul(left, right):
    return jnp.dot(left, right, precision=lax.Precision.HIGHEST, preferred_element_type=jnp.float32)

def doc_tables(doc_lengths):
    steps_axis = jnp.arange(LEN, dtype=jnp.int32)
    doc_ends = jnp.cumsum(doc_lengths, axis=1).astype(jnp.int32)
    passed_end = steps_axis[None, :, None] >= doc_ends[:, None, :]
    segment = lax.optimization_barrier(jnp.sum(passed_end.astype(jnp.int32), axis=2)).astype(jnp.int32)
    doc_start = lax.optimization_barrier(jnp.sum(jnp.where(passed_end, doc_lengths[:, None, :], 0), axis=2)).astype(jnp.int32)
    return (segment, (steps_axis[None, :] - doc_start).astype(jnp.int32))

def rotary_tables(position):
    half_dim = HEAD_DIM // 2
    inverse = jnp.power(ROPE_BASE, -jnp.arange(half_dim, dtype=jnp.float32) * 2.0 / HEAD_DIM)
    angles = position.astype(jnp.float32)[..., None] * inverse
    return (jnp.cos(angles), jnp.sin(angles))

def rotate(values, cosine_table, sine_table):
    half_dim = values.shape[-1] // 2
    front_half = values[..., :half_dim]
    back_half = values[..., half_dim:]
    cosine_part = cosine_table[..., None, :]
    sine_part = sine_table[..., None, :]
    return jnp.concatenate([front_half * cosine_part - back_half * sine_part, back_half * cosine_part + front_half * sine_part], axis=-1)

def rms_norm(values, gain):
    factor = lax.rsqrt(lax.optimization_barrier(jnp.mean(values * values, axis=-1, keepdims=True)) + EPSILON)
    return values * factor * gain

def one_sequence(packed):
    query, keys, values, segment = packed
    scores = low_back(jnp.einsum('qhc,khc->hqk', query, keys, precision=lax.Precision.HIGHEST)) * HEAD_DIM ** (-0.5)
    token_rows = jnp.arange(LEN, dtype=jnp.int32)
    allowed = (segment[:, None] == segment[None, :]) & (token_rows[None, :] <= token_rows[:, None])
    masked = jnp.where(allowed[None], scores, -1e+30)
    row_max = lax.optimization_barrier(jnp.max(masked, axis=-1, keepdims=True))
    exponent = jnp.exp(masked - row_max)
    weights = exponent / lax.optimization_barrier(jnp.sum(exponent, axis=-1, keepdims=True))
    return jnp.einsum('hqk,khc->qhc', low(weights), values, precision=lax.Precision.HIGHEST)

def layer(params, hidden_group, segment, position):
    gain_attn, w_query, w_key, w_value, w_out, gain_mlp, w_gate, w_up, w_down = params
    seq_count = hidden_group.shape[0]
    flat_rows = hidden_group.reshape(seq_count * LEN, D)
    normed = low(rms_norm(flat_rows, gain_attn))
    cosine_table, sine_table = rotary_tables(position)
    head_shape = (seq_count, LEN, HEADS, HEAD_DIM)
    query = low(rotate(low_back(matmul(normed, w_query)).reshape(head_shape), cosine_table, sine_table))
    keys = low(rotate(low_back(matmul(normed, w_key)).reshape(head_shape), cosine_table, sine_table))
    values = low(low_back(matmul(normed, w_value))).reshape(head_shape)
    mixed = lax.map(jax.checkpoint(one_sequence), (query, keys, values, segment))
    mixed = low(low_back(mixed.reshape(seq_count * LEN, D)))
    middle = flat_rows + low_back(matmul(mixed, w_out))
    normed_mlp = low(rms_norm(middle, gain_mlp))
    gate_pre = low_back(matmul(normed_mlp, w_gate))
    upward = low_back(matmul(normed_mlp, w_up))
    hidden = low(jax.nn.silu(gate_pre) * upward)
    result = middle + low_back(matmul(hidden, w_down))
    return result.reshape(seq_count, LEN, D)

def reference(hidden_in, doc_lengths, gain_attn, w_query, w_key, w_value, w_out, gain_mlp, w_gate, w_up, w_down, cotangent):
    segment, position = doc_tables(doc_lengths)
    per_step = max(1, min(NSEQ, 4096 // LEN))
    while NSEQ % per_step != 0:
        per_step = per_step - 1
    group_count = NSEQ // per_step
    inputs = hidden_in.astype(jnp.float32).reshape(group_count, per_step, LEN, D)
    seg_groups = segment.reshape(group_count, per_step, LEN)
    pos_groups = position.reshape(group_count, per_step, LEN)
    params = tuple((weight.astype(jnp.float32) for weight in (gain_attn, w_query, w_key, w_value, w_out, gain_mlp, w_gate, w_up, w_down)))
    step_layer = jax.checkpoint(layer)

    def forward(inputs_all, params_all):

        def scan_body(running, slices):
            return (running, step_layer(params_all, slices[0], slices[1], slices[2]))
        unused, outputs = lax.scan(scan_body, jnp.zeros((), jnp.float32), (inputs_all, seg_groups, pos_groups))
        return outputs
    outputs, pullback = jax.vjp(forward, inputs, params)
    grad_inputs, grad_params = pullback(cotangent.astype(jnp.float32).reshape(outputs.shape))
    return (outputs.reshape(TOKENS, D).astype(jnp.bfloat16), grad_inputs.reshape(TOKENS, D), grad_params[0], grad_params[1], grad_params[2], grad_params[3], grad_params[4], grad_params[5], grad_params[6], grad_params[7], grad_params[8])
```

```python
import functools

import jax
import jax.numpy as jnp
from jax import lax
from jax.experimental import pallas as pl
from jax.experimental.pallas import tpu as pltpu
from jax.sharding import PartitionSpec as P

HEAD_DIM = 64
LEN = 1024
MOST = 512
EPSILON = 1e-05
ROPE_BASE = 130000.0
NEG = -1e30
GROUP = 256
FF_BLOCKS = 4
F32 = jnp.float32
BF16 = jnp.bfloat16
VMEM_BYTES = 56 * 1024 * 1024


def dot_nn(a, b):
    return jnp.dot(a, b, preferred_element_type=F32)


def dot_tn(a, b):
    return lax.dot_general(a, b, (((0,), (0,)), ((), ())), preferred_element_type=F32)


def dot_nt(a, b):
    return lax.dot_general(a, b, (((1,), (1,)), ((), ())), preferred_element_type=F32)


def norm_factor(values):
    return lax.rsqrt(jnp.mean(values * values, axis=-1, keepdims=True) + EPSILON)


def norm_back(values, factor, gain, grads):
    scaled = grads * gain
    grad_in = factor * scaled - values * factor * factor * factor * jnp.mean(
        scaled * values, axis=-1, keepdims=True
    )
    return grad_in, jnp.sum(grads * values * factor, axis=0)


def doc_tables(doc_lengths, tokens):
    ends = jnp.cumsum(doc_lengths, axis=1)[0]
    passed = tokens[:, None] >= ends[None, :]
    segment = jnp.sum(passed.astype(jnp.int32), axis=1)
    start = jnp.sum(jnp.where(passed, doc_lengths, 0), axis=1)
    return segment, tokens - start


def rotary_tables(position):
    half = HEAD_DIM // 2
    inverse = jnp.power(ROPE_BASE, -jnp.arange(half, dtype=F32) * 2.0 / HEAD_DIM)
    angles = position.astype(F32)[:, None] * inverse
    cosine, sine = jnp.cos(angles), jnp.sin(angles)
    heads = GROUP // HEAD_DIM
    return (
        jnp.tile(jnp.concatenate([cosine, cosine], axis=1), (1, heads)),
        jnp.tile(jnp.concatenate([-sine, sine], axis=1), (1, heads)),
    )


def swap_halves(v):
    half, width = HEAD_DIM // 2, v.shape[1]
    lane = lax.broadcasted_iota(jnp.int32, v.shape, 1)
    ahead = pltpu.roll(v, width - half, 1)
    behind = pltpu.roll(v, half, 1)
    return jnp.where(lane % HEAD_DIM < half, ahead, behind)


def key_blocks(i, rows):
    reach = -(-(MOST - 1) // rows)
    return list(range(max(0, i - reach), i + 1))


def fill_bias(bias_ref, seg_col, seg_ref, i, places):
    rows = seg_col.shape[0]
    for n, (j, place) in enumerate(places):
        same = seg_col == seg_ref[place][0:1, :]
        if j == i:
            row = lax.broadcasted_iota(jnp.int32, (rows, rows), 0)
            col = lax.broadcasted_iota(jnp.int32, (rows, rows), 1)
            same = same & (col <= row)
        bias_ref[n] = jnp.where(same, 0.0, NEG)


def attn_forward_kernel(
    blocks, key_ref, x_ref, qo, qs, ko, ks, vo, vs, cos_ref, sin_ref, segc_ref, segr_ref,
    q_ref, k_ref, v_ref, mixed_ref, lse_ref, bias_ref,
):
    rows = LEN // blocks
    half = x_ref.shape[1] // 2
    key = key_ref[0]

    @pl.loop(0, blocks)
    def _(b):
        at = pl.ds(pl.multiple_of(b * rows, rows), rows)
        left, right = x_ref[at, :half], x_ref[at, half:]
        cosine, sine = cos_ref[at, :], sin_ref[at, :]
        query = dot_nn(left, qo[...]) + dot_nn(right, qs[...])
        q_ref[at, :] = (query * cosine + swap_halves(query) * sine).astype(BF16)
        keys = dot_nn(left, ko[...]) + dot_nn(right, ks[...])
        k_ref[at, :] = (keys * cosine + swap_halves(keys) * sine).astype(BF16)
        v_ref[at, :] = (dot_nn(left, vo[...]) + dot_nn(right, vs[...])).astype(BF16)

    head_lane = lax.broadcasted_iota(jnp.int32, (rows, 128), 1)
    for i in range(blocks):
        places = [(j, j ^ key) for j in key_blocks(i, rows)]
        at = pl.ds(pl.multiple_of((i ^ key) * rows, rows), rows)
        fill_bias(bias_ref, segc_ref[at, 0:1], segr_ref, i, places)
        spots = [pl.ds(pl.multiple_of(p * rows, rows), rows) for _, p in places]

        @pl.loop(0, GROUP // 128)
        def _(pair, at=at, spots=spots):
            lanes = pl.ds(pl.multiple_of(pair * 128, 128), 128)
            query = q_ref[at, lanes]
            outs, stats = [], []
            for h in range(2):
                mine = (head_lane < HEAD_DIM) if h == 0 else (head_lane >= HEAD_DIM)
                qm = jnp.where(mine, query, 0) * jnp.asarray(HEAD_DIM**-0.5, BF16)
                scores = [
                    dot_nt(qm, k_ref[s, lanes]) + bias_ref[n] for n, s in enumerate(spots)
                ]
                top = functools.reduce(
                    jnp.maximum, [jnp.max(s, axis=1, keepdims=True) for s in scores]
                )
                weights = [jnp.exp(s - top) for s in scores]
                total = sum(jnp.sum(w, axis=1, keepdims=True) for w in weights)
                out = sum(
                    dot_nn(w.astype(BF16), v_ref[s, lanes]) for w, s in zip(weights, spots)
                )
                outs.append(out / total)
                stats.append(top + jnp.log(total))
            mixed_ref[at, lanes] = jnp.where(head_lane < HEAD_DIM, outs[0], outs[1]).astype(BF16)
            kept = jnp.where(pair == 0, 0.0, lse_ref[at, :])
            for h in range(2):
                kept = jnp.where(head_lane == pair * 2 + h, stats[h], kept)
            lse_ref[at, :] = kept


def attn_forward(blocks, key, x, own, sib, cosine, sine, segc, segr):
    d = x.shape[1]
    cols = own.shape[1] // 4
    steps = cols // GROUP
    rows = LEN // blocks

    def weight(part):
        return pl.BlockSpec((d // 2, GROUP), lambda i, part=part: (0, part * steps + i))

    def whole(shape):
        return pl.BlockSpec(shape, lambda i: (0,) * len(shape))

    col_block = pl.BlockSpec((LEN, GROUP), lambda i: (0, i))
    slab = jax.ShapeDtypeStruct((LEN, cols), BF16)
    return pl.pallas_call(
        functools.partial(attn_forward_kernel, blocks),
        grid=(steps,),
        in_specs=[pl.BlockSpec(memory_space=pltpu.SMEM), whole((LEN, d))]
        + [weight(p) for p in (0, 0, 1, 1, 2, 2)]
        + [whole((LEN, GROUP))] * 2
        + [whole((LEN, 128)), whole(segr.shape)],
        out_specs=[col_block] * 4 + [pl.BlockSpec((LEN, 128), lambda i: (0, i))],
        out_shape=[slab] * 4 + [jax.ShapeDtypeStruct((LEN, 128 * steps), F32)],
        scratch_shapes=[pltpu.VMEM((blocks, rows, rows), F32)],
        compiler_params=pltpu.CompilerParams(vmem_limit_bytes=VMEM_BYTES),
        name="attn_forward",
    )(key, x, own, sib, own, sib, own, sib, cosine, sine, segc, segr)


def attn_backward_kernel(
    blocks, key_ref, g_ref, wo, ws, q_ref, k_ref, v_ref, lse_ref, cos_ref, sin_ref, segc_ref,
    segr_ref, dq_ref, dk_ref, dv_ref, dm_ref, dqa_ref, dka_ref, dva_ref, bias_ref,
):
    rows = LEN // blocks
    half = g_ref.shape[1] // 2
    key = key_ref[0]

    @pl.loop(0, blocks)
    def _(b):
        at = pl.ds(pl.multiple_of(b * rows, rows), rows)
        dm_ref[at, :] = (dot_nn(g_ref[at, :half], wo[...]) + dot_nn(g_ref[at, half:], ws[...])).astype(BF16)
        dka_ref[at, :] = jnp.zeros((rows, GROUP), F32)
        dva_ref[at, :] = jnp.zeros((rows, GROUP), F32)

    head_lane = lax.broadcasted_iota(jnp.int32, (rows, 128), 1)
    scale = HEAD_DIM**-0.5
    for i in range(blocks):
        places = [(j, j ^ key) for j in key_blocks(i, rows)]
        at = pl.ds(pl.multiple_of((i ^ key) * rows, rows), rows)
        fill_bias(bias_ref, segc_ref[at, 0:1], segr_ref, i, places)
        spots = [pl.ds(pl.multiple_of(p * rows, rows), rows) for _, p in places]

        @pl.loop(0, GROUP // 128)
        def _(pair, at=at, spots=spots):
            lanes = pl.ds(pl.multiple_of(pair * 128, 128), 128)
            query, grad = q_ref[at, lanes], dm_ref[at, lanes]
            logs = lse_ref[at, :]
            outs = []
            for h in range(2):
                mine = (head_lane < HEAD_DIM) if h == 0 else (head_lane >= HEAD_DIM)
                qm = jnp.where(mine, query, 0) * jnp.asarray(scale, BF16)
                gm = jnp.where(mine, grad, 0)
                log = jnp.sum(
                    jnp.where(head_lane == pair * 2 + h, logs, 0.0), axis=1, keepdims=True
                )
                weights = [
                    jnp.exp(dot_nt(qm, k_ref[s, lanes]) + bias_ref[n] - log)
                    for n, s in enumerate(spots)
                ]
                grads = [dot_nt(gm, v_ref[s, lanes]) for s in spots]
                inner = sum(
                    jnp.sum(w * g, axis=1, keepdims=True) for w, g in zip(weights, grads)
                )
                dq = jnp.zeros((rows, 128), F32)
                for w, g, s in zip(weights, grads, spots):
                    ds = (w * (g - inner)).astype(BF16)
                    dva_ref[s, lanes] += dot_tn(w.astype(BF16), gm)
                    dka_ref[s, lanes] += dot_tn(ds, qm)
                    dq = dq + dot_nn(ds, k_ref[s, lanes])
                outs.append(dq)
            dqa_ref[at, lanes] = jnp.where(head_lane < HEAD_DIM, outs[0], outs[1]) * scale

    @pl.loop(0, blocks)
    def _(b):
        at = pl.ds(pl.multiple_of(b * rows, rows), rows)
        cosine, sine = cos_ref[at, :], sin_ref[at, :]
        dq = dqa_ref[at, :]
        dq_ref[at, :] = (dq * cosine - swap_halves(dq) * sine).astype(BF16)
        dk = dka_ref[at, :]
        dk_ref[at, :] = (dk * cosine - swap_halves(dk) * sine).astype(BF16)
        dv_ref[at, :] = dva_ref[at, :].astype(BF16)


def attn_backward(blocks, key, g, own, sib, q, k, v, lse, cosine, sine, segc, segr):
    d = g.shape[1]
    cols = q.shape[1]
    steps = cols // GROUP
    rows = LEN // blocks

    def whole(shape):
        return pl.BlockSpec(shape, lambda i: (0,) * len(shape))

    col_block = pl.BlockSpec((LEN, GROUP), lambda i: (0, i))
    weight = pl.BlockSpec((d // 2, GROUP), lambda i: (0, 3 * steps + i))
    slab = jax.ShapeDtypeStruct((LEN, cols), BF16)
    return pl.pallas_call(
        functools.partial(attn_backward_kernel, blocks),
        grid=(steps,),
        in_specs=[pl.BlockSpec(memory_space=pltpu.SMEM), whole((LEN, d)), weight, weight]
        + [col_block] * 3
        + [pl.BlockSpec((LEN, 128), lambda i: (0, i))]
        + [whole((LEN, GROUP))] * 2
        + [whole((LEN, 128)), whole(segr.shape)],
        out_specs=[col_block] * 3,
        out_shape=[slab] * 3,
        scratch_shapes=[
            pltpu.VMEM((LEN, GROUP), BF16),
            pltpu.VMEM((LEN, GROUP), F32),
            pltpu.VMEM((LEN, GROUP), F32),
            pltpu.VMEM((LEN, GROUP), F32),
            pltpu.VMEM((blocks, rows, rows), F32),
        ],
        compiler_params=pltpu.CompilerParams(vmem_limit_bytes=VMEM_BYTES),
        name="attn_backward",
    )(key, g, own, sib, q, k, v, lse, cosine, sine, segc, segr)


def on_device(
    dp, tensor, hidden_in, doc_lengths, gain_attn, w_query, w_key, w_value, w_out, gain_mlp,
    w_gate, w_up, w_down, cotangent,
):
    line = dp // 2
    core = lax.axis_index("dp") % 2
    place = lax.axis_index("tensor")
    square = tensor == 4
    same_core = [[c + 2 * z for z in range(line)] for c in range(2)]
    sibling = [(i, i ^ 1) for i in range(dp)]
    d = hidden_in.shape[1]
    local = hidden_in.shape[0]

    def own_first(a):
        s = a.reshape(a.shape[:-1] + (line, 2, d // dp))
        even, odd = s[..., 0, :], s[..., 1, :]
        out = jnp.concatenate(
            [jnp.where(core == 0, even, odd), jnp.where(core == 0, odd, even)], axis=-2
        )
        return out.reshape(a.shape)

    def true_order(a):
        s = a.reshape(a.shape[:-1] + (2, line, d // dp))
        first, second = s[..., 0, :, :], s[..., 1, :, :]
        out = jnp.stack(
            [jnp.where(core == 0, first, second), jnp.where(core == 0, second, first)], axis=-2
        )
        return out.reshape(a.shape)

    def hop(a, step):
        return lax.ppermute(a, "tensor", [(i, i ^ step) for i in range(tensor)])

    def gather_rows(a):
        if not square:
            return lax.all_gather(a, "tensor", axis=0, tiled=True)
        half = a.shape[0] // 2
        from_x, from_y = hop(a, 1), hop(a, 2)
        top, bottom = hop(from_x[:half], 2), hop(from_y[half:], 1)
        return jnp.concatenate([a, from_x, from_y, top, bottom], axis=0)

    def scatter_rows(a):
        if not square:
            return lax.psum_scatter(a, "tensor", scatter_dimension=0, tiled=True).astype(F32)
        n = a.shape[0] // 4
        half = n // 2
        top = hop(a[3 * n : 3 * n + half], 2)
        bottom = hop(a[3 * n + half :], 1)
        for_x = jnp.concatenate([a[n : n + half] + top, a[n + half : 2 * n]], axis=0)
        for_y = jnp.concatenate([a[2 * n : 2 * n + half], a[2 * n + half : 3 * n] + bottom], axis=0)
        return (a[:n].astype(F32) + hop(for_x, 1).astype(F32)) + hop(for_y, 2).astype(F32)

    def line_gather(a):
        own = lax.all_gather(a, "dp", axis=0, axis_index_groups=same_core, tiled=True)
        return own, lax.ppermute(own, "dp", sibling)

    def line_scatter(own, sib):
        mine = own + lax.ppermute(sib, "dp", sibling)
        return lax.psum_scatter(
            mine, "dp", scatter_dimension=0, axis_index_groups=same_core, tiled=True
        ).astype(F32)

    blocks = 4
    rows = LEN // blocks
    key = place if square else jnp.zeros((), jnp.int32)
    tokens = (
        (jnp.arange(blocks, dtype=jnp.int32) ^ key)[:, None] * rows
        + jnp.arange(rows, dtype=jnp.int32)[None, :]
    ).reshape(LEN)
    segment, position = doc_tables(doc_lengths, tokens)
    cosine, sine = rotary_tables(position)
    segc = jnp.broadcast_to(segment[:, None], (LEN, 128))
    segr = jnp.broadcast_to(segment.reshape(blocks, 1, rows), (blocks, 8, rows))
    key = key.reshape(1)

    gains = lax.all_gather(jnp.stack([gain_attn, gain_mlp]), "dp", axis=0)
    gains = own_first(jnp.moveaxis(gains, 0, 1).reshape(2, d)).astype(F32)
    gain_one, gain_two = gains[0], gains[1]

    ff = w_gate.shape[1]
    fb = ff // FF_BLOCKS
    attn_own, attn_sib = line_gather(
        jnp.concatenate([w_query, w_key, w_value, w_out.T], axis=1)
    )
    down_t = w_down.T
    ff_sets = []
    for b in range(FF_BLOCKS):
        cut = slice(b * fb, (b + 1) * fb)
        own, sib = line_gather(
            jnp.concatenate([w_gate[:, cut], w_up[:, cut], down_t[:, cut]], axis=1)
        )
        ff_sets.append(jnp.concatenate([own, sib], axis=0))

    inputs = own_first(hidden_in).astype(F32)
    g_local = own_first(cotangent)
    factor_one = norm_factor(inputs)
    normed = gather_rows((inputs * factor_one * gain_one).astype(BF16))
    g_all = gather_rows(g_local)

    query, keys, values, mixed, lse = attn_forward(
        blocks, key, normed, attn_own, attn_sib, cosine, sine, segc, segr
    )
    cols = query.shape[1]
    out_own, out_sib = attn_own[:, 3 * cols :], attn_sib[:, 3 * cols :]
    attended = jnp.concatenate(
        [dot_nt(mixed, out_own).astype(BF16), dot_nt(mixed, out_sib).astype(BF16)], axis=1
    )
    middle = inputs + scatter_rows(attended)
    factor_two = norm_factor(middle)
    normed_mlp = gather_rows((middle * factor_two * gain_two).astype(BF16))

    down_sum = jnp.zeros((LEN, d), F32)
    back_sum = jnp.zeros((LEN, d), F32)
    ff_grads = []
    for b in range(FF_BLOCKS):
        gate_w, up_w, down_w = jnp.split(ff_sets[b], 3, axis=1)
        gate_pre = dot_nn(normed_mlp, gate_w)
        upward = dot_nn(normed_mlp, up_w)
        grad_hidden = dot_nn(g_all, down_w)
        sig = jax.nn.sigmoid(gate_pre)
        activated = gate_pre * sig
        hidden = (activated * upward).astype(BF16)
        grad_gate_pre = (grad_hidden * upward * sig * (1.0 + gate_pre * (1.0 - sig))).astype(BF16)
        grad_upward = (grad_hidden * activated).astype(BF16)
        down_sum = down_sum + dot_nt(hidden, down_w)
        back_sum = back_sum + dot_nt(grad_gate_pre, gate_w) + dot_nt(grad_upward, up_w)
        grad = jnp.concatenate(
            [
                dot_tn(normed_mlp, grad_gate_pre).astype(BF16),
                dot_tn(normed_mlp, grad_upward).astype(BF16),
                dot_tn(g_all, hidden).astype(BF16),
            ],
            axis=1,
        )
        ff_grads.append(line_scatter(grad[: d // 2], grad[d // 2 :]))
    grad_norm_two = scatter_rows(back_sum.astype(BF16))
    output = true_order((middle + scatter_rows(down_sum.astype(BF16))).astype(BF16))
    grad_mid_norm, gain_two_part = norm_back(middle, factor_two, gain_two, grad_norm_two)
    grad_middle = g_local.astype(F32) + grad_mid_norm
    grad_mid_all = gather_rows(grad_middle.astype(BF16))

    dq, dk, dv = attn_backward(
        blocks, key, grad_mid_all, attn_own, attn_sib, query, keys, values, lse, cosine, sine,
        segc, segr,
    )
    grad = jnp.concatenate(
        [dot_tn(normed, dq), dot_tn(normed, dk), dot_tn(normed, dv), dot_tn(grad_mid_all, mixed)],
        axis=1,
    ).astype(BF16)
    attn_grads = line_scatter(grad[: d // 2], grad[d // 2 :])
    rows_grad = jnp.concatenate([dq, dk, dv], axis=1)
    back = jnp.concatenate(
        [
            dot_nt(rows_grad, attn_own[:, : 3 * cols]).astype(BF16),
            dot_nt(rows_grad, attn_sib[:, : 3 * cols]).astype(BF16),
        ],
        axis=1,
    )
    grad_in_norm, gain_one_part = norm_back(inputs, factor_one, gain_one, scatter_rows(back))
    input_grad = true_order(grad_middle + grad_in_norm)

    parts = true_order(jnp.stack([gain_one_part, gain_two_part])).reshape(2 * d)
    shares = lax.all_gather(parts, ("dp", "tensor"), axis=0)
    gain_sum = jnp.sum(shares, axis=0).reshape(2, d)
    share = d // (dp * tensor)
    first = (lax.axis_index("dp") * tensor + place) * share
    gain_sum = lax.dynamic_slice_in_dim(gain_sum, first, share, 1)

    return (
        output,
        input_grad,
        gain_sum[0],
        attn_grads[:, :cols],
        attn_grads[:, cols : 2 * cols],
        attn_grads[:, 2 * cols : 3 * cols],
        attn_grads[:, 3 * cols :].T,
        gain_sum[1],
        jnp.concatenate([g[:, :fb] for g in ff_grads], axis=1),
        jnp.concatenate([g[:, fb : 2 * fb] for g in ff_grads], axis=1),
        jnp.concatenate([g[:, 2 * fb :] for g in ff_grads], axis=1).T,
    )


def solution(mesh):
    shape = dict(mesh.shape)
    return jax.shard_map(
        functools.partial(on_device, shape["dp"], shape["tensor"]),
        mesh=mesh,
        in_specs=(
            P(("dp", "tensor"), None),
            P("dp", None),
            P("dp"),
            P("dp", "tensor"),
            P("dp", "tensor"),
            P("dp", "tensor"),
            P("tensor", "dp"),
            P("dp"),
            P("dp", "tensor"),
            P("dp", "tensor"),
            P("tensor", "dp"),
            P(("dp", "tensor"), None),
        ),
        out_specs=(
            P(("dp", "tensor"), None),
            P(("dp", "tensor"), None),
            P(("dp", "tensor")),
            P("dp", "tensor"),
            P("dp", "tensor"),
            P("dp", "tensor"),
            P("tensor", "dp"),
            P(("dp", "tensor")),
            P("dp", "tensor"),
            P("dp", "tensor"),
            P("tensor", "dp"),
        ),
        check_vma=False,
    )
```

```python
import functools

import jax
import jax.numpy as jnp
from jax import lax
from jax.experimental import pallas as pl
from jax.experimental.pallas import tpu as pltpu
from jax.sharding import PartitionSpec as P

HEAD_DIM = 64
LEN = 1024
MOST = 512
EPSILON = 1e-05
ROPE_BASE = 130000.0
NEG = -1e30
GROUP = 256
FF_BLOCKS = 4
FF_EARLY = 2
F32 = jnp.float32
BF16 = jnp.bfloat16
VMEM_BYTES = 56 * 1024 * 1024


def dot_nn(a, b):
    return jnp.dot(a, b, preferred_element_type=F32)


def dot_tn(a, b):
    return lax.dot_general(a, b, (((0,), (0,)), ((), ())), preferred_element_type=F32)


def dot_nt(a, b):
    return lax.dot_general(a, b, (((1,), (1,)), ((), ())), preferred_element_type=F32)


def norm_factor(values):
    return lax.rsqrt(jnp.mean(values * values, axis=-1, keepdims=True) + EPSILON)


def norm_back(values, factor, gain, grads):
    scaled = grads * gain
    grad_in = factor * scaled - values * factor * factor * factor * jnp.mean(
        scaled * values, axis=-1, keepdims=True
    )
    return grad_in, jnp.sum(grads * values * factor, axis=0)


def doc_tables(doc_lengths, tokens):
    ends = jnp.cumsum(doc_lengths, axis=1)[0]
    passed = tokens[:, None] >= ends[None, :]
    segment = jnp.sum(passed.astype(jnp.int32), axis=1)
    start = jnp.sum(jnp.where(passed, doc_lengths, 0), axis=1)
    return segment, tokens - start


def rotary_tables(position):
    half = HEAD_DIM // 2
    inverse = jnp.power(ROPE_BASE, -jnp.arange(half, dtype=F32) * 2.0 / HEAD_DIM)
    angles = position.astype(F32)[:, None] * inverse
    cosine, sine = jnp.cos(angles), jnp.sin(angles)
    heads = GROUP // HEAD_DIM
    return (
        jnp.tile(jnp.concatenate([cosine, cosine], axis=1), (1, heads)),
        jnp.tile(jnp.concatenate([-sine, sine], axis=1), (1, heads)),
    )


def swap_halves(v):
    half, width = HEAD_DIM // 2, v.shape[1]
    lane = lax.broadcasted_iota(jnp.int32, v.shape, 1)
    ahead = pltpu.roll(v, width - half, 1)
    behind = pltpu.roll(v, half, 1)
    return jnp.where(lane % HEAD_DIM < half, ahead, behind)


def key_blocks(i, rows):
    reach = -(-(MOST - 1) // rows)
    return list(range(max(0, i - reach), i + 1))


def fill_bias(bias_ref, seg_col, seg_ref, i, places):
    rows = seg_col.shape[0]
    for n, (j, place) in enumerate(places):
        same = seg_col == seg_ref[place][0:1, :]
        if j == i:
            row = lax.broadcasted_iota(jnp.int32, (rows, rows), 0)
            col = lax.broadcasted_iota(jnp.int32, (rows, rows), 1)
            same = same & (col <= row)
        bias_ref[n] = jnp.where(same, 0.0, NEG)


def attn_forward_kernel(
    blocks, key_ref, x_ref, qo, qs, ko, ks, vo, vs, cos_ref, sin_ref, segc_ref, segr_ref,
    q_ref, k_ref, v_ref, mixed_ref, lse_ref, bias_ref,
):
    rows = LEN // blocks
    half = x_ref.shape[1] // 2
    key = key_ref[0]

    @pl.loop(0, blocks)
    def _(b):
        at = pl.ds(pl.multiple_of(b * rows, rows), rows)
        left, right = x_ref[at, :half], x_ref[at, half:]
        cosine, sine = cos_ref[at, :], sin_ref[at, :]
        query = dot_nn(left, qo[...]) + dot_nn(right, qs[...])
        q_ref[at, :] = (query * cosine + swap_halves(query) * sine).astype(BF16)
        keys = dot_nn(left, ko[...]) + dot_nn(right, ks[...])
        k_ref[at, :] = (keys * cosine + swap_halves(keys) * sine).astype(BF16)
        v_ref[at, :] = (dot_nn(left, vo[...]) + dot_nn(right, vs[...])).astype(BF16)

    head_lane = lax.broadcasted_iota(jnp.int32, (rows, 128), 1)
    for i in range(blocks):
        places = [(j, j ^ key) for j in key_blocks(i, rows)]
        at = pl.ds(pl.multiple_of((i ^ key) * rows, rows), rows)
        fill_bias(bias_ref, segc_ref[at, 0:1], segr_ref, i, places)
        spots = [pl.ds(pl.multiple_of(p * rows, rows), rows) for _, p in places]

        @pl.loop(0, GROUP // 128)
        def _(pair, at=at, spots=spots):
            first = pl.program_id(0) * (GROUP // HEAD_DIM)
            attend(pair, first, at, spots, head_lane, q_ref, k_ref, v_ref, mixed_ref, lse_ref, bias_ref)


def attn_forward(blocks, key, x, own, sib, cosine, sine, segc, segr):
    d = x.shape[1]
    cols = own.shape[1] // 3
    steps = cols // GROUP
    rows = LEN // blocks

    def weight(part):
        return pl.BlockSpec((d // 2, GROUP), lambda i, part=part: (0, part * steps + i))

    def whole(shape):
        return pl.BlockSpec(shape, lambda i: (0,) * len(shape))

    col_block = pl.BlockSpec((LEN, GROUP), lambda i: (0, i))
    slab = jax.ShapeDtypeStruct((LEN, cols), BF16)
    return pl.pallas_call(
        functools.partial(attn_forward_kernel, blocks),
        grid=(steps,),
        in_specs=[pl.BlockSpec(memory_space=pltpu.SMEM), whole((LEN, d))]
        + [weight(p) for p in (0, 0, 1, 1, 2, 2)]
        + [whole((LEN, GROUP))] * 2
        + [whole((LEN, 128)), whole(segr.shape)],
        out_specs=[col_block] * 4 + [whole((LEN, 128))],
        out_shape=[slab] * 4 + [jax.ShapeDtypeStruct((LEN, 128), F32)],
        scratch_shapes=[pltpu.VMEM((blocks, rows, rows), F32)],
        compiler_params=pltpu.CompilerParams(vmem_limit_bytes=VMEM_BYTES),
        name="attn_forward",
    )(key, x, own, sib, own, sib, own, sib, cosine, sine, segc, segr)


def attn_backward_kernel(
    blocks, key_ref, g_ref, wo, ws, q_ref, k_ref, v_ref, lse_ref, cos_ref, sin_ref, segc_ref,
    segr_ref, dq_ref, dk_ref, dv_ref, dm_ref, dqa_ref, dka_ref, dva_ref, bias_ref,
):
    rows = LEN // blocks
    half = g_ref.shape[1] // 2
    key = key_ref[0]

    @pl.loop(0, blocks)
    def _(b):
        at = pl.ds(pl.multiple_of(b * rows, rows), rows)
        dm_ref[at, :] = (dot_nn(g_ref[at, :half], wo[...]) + dot_nn(g_ref[at, half:], ws[...])).astype(BF16)
        dka_ref[at, :] = jnp.zeros((rows, GROUP), F32)
        dva_ref[at, :] = jnp.zeros((rows, GROUP), F32)

    head_lane = lax.broadcasted_iota(jnp.int32, (rows, 128), 1)
    scale = HEAD_DIM**-0.5
    for i in range(blocks):
        places = [(j, j ^ key) for j in key_blocks(i, rows)]
        at = pl.ds(pl.multiple_of((i ^ key) * rows, rows), rows)
        fill_bias(bias_ref, segc_ref[at, 0:1], segr_ref, i, places)
        spots = [pl.ds(pl.multiple_of(p * rows, rows), rows) for _, p in places]

        @pl.loop(0, GROUP // 128)
        def _(pair, at=at, spots=spots):
            lanes = pl.ds(pl.multiple_of(pair * 128, 128), 128)
            first = pl.program_id(0) * (GROUP // HEAD_DIM)
            query, grad = q_ref[at, lanes], dm_ref[at, lanes]
            logs = lse_ref[at, :]
            outs = []
            for h in range(2):
                mine = (head_lane < HEAD_DIM) if h == 0 else (head_lane >= HEAD_DIM)
                qm = jnp.where(mine, query, 0) * jnp.asarray(scale, BF16)
                gm = jnp.where(mine, grad, 0)
                log = jnp.sum(
                    jnp.where(head_lane == first + pair * 2 + h, logs, 0.0), axis=1, keepdims=True
                )
                weights = [
                    jnp.exp(dot_nt(qm, k_ref[s, lanes]) + bias_ref[n] - log)
                    for n, s in enumerate(spots)
                ]
                grads = [dot_nt(gm, v_ref[s, lanes]) for s in spots]
                inner = sum(
                    jnp.sum(w * g, axis=1, keepdims=True) for w, g in zip(weights, grads)
                )
                dq = jnp.zeros((rows, 128), F32)
                for w, g, s in zip(weights, grads, spots):
                    ds = (w * (g - inner)).astype(BF16)
                    dva_ref[s, lanes] += dot_tn(w.astype(BF16), gm)
                    dka_ref[s, lanes] += dot_tn(ds, qm)
                    dq = dq + dot_nn(ds, k_ref[s, lanes])
                outs.append(dq)
            dqa_ref[at, lanes] = jnp.where(head_lane < HEAD_DIM, outs[0], outs[1]) * scale

    @pl.loop(0, blocks)
    def _(b):
        at = pl.ds(pl.multiple_of(b * rows, rows), rows)
        cosine, sine = cos_ref[at, :], sin_ref[at, :]
        dq = dqa_ref[at, :]
        dq_ref[at, :] = (dq * cosine - swap_halves(dq) * sine).astype(BF16)
        dk = dka_ref[at, :]
        dk_ref[at, :] = (dk * cosine - swap_halves(dk) * sine).astype(BF16)
        dv_ref[at, :] = dva_ref[at, :].astype(BF16)


def attn_backward(blocks, key, g, own, sib, q, k, v, lse, cosine, sine, segc, segr):
    d = g.shape[1]
    cols = q.shape[1]
    steps = cols // GROUP
    rows = LEN // blocks

    def whole(shape):
        return pl.BlockSpec(shape, lambda i: (0,) * len(shape))

    col_block = pl.BlockSpec((LEN, GROUP), lambda i: (0, i))
    weight = pl.BlockSpec((d // 2, GROUP), lambda i: (0, i))
    slab = jax.ShapeDtypeStruct((LEN, cols), BF16)
    return pl.pallas_call(
        functools.partial(attn_backward_kernel, blocks),
        grid=(steps,),
        in_specs=[pl.BlockSpec(memory_space=pltpu.SMEM), whole((LEN, d)), weight, weight]
        + [col_block] * 3
        + [whole((LEN, 128))]
        + [whole((LEN, GROUP))] * 2
        + [whole((LEN, 128)), whole(segr.shape)],
        out_specs=[col_block] * 3,
        out_shape=[slab] * 3,
        scratch_shapes=[
            pltpu.VMEM((LEN, GROUP), BF16),
            pltpu.VMEM((LEN, GROUP), F32),
            pltpu.VMEM((LEN, GROUP), F32),
            pltpu.VMEM((LEN, GROUP), F32),
            pltpu.VMEM((blocks, rows, rows), F32),
        ],
        compiler_params=pltpu.CompilerParams(vmem_limit_bytes=VMEM_BYTES),
        name="attn_backward",
    )(key, g, own, sib, q, k, v, lse, cosine, sine, segc, segr)


class LineGather:
    def __init__(self, me, src, full, sems):
        self.me, self.src, self.full, self.sems = me, src, full, sems
        self.rows = src.shape[0]

    def spot(self, side, s):
        return self.full.at[side, pl.ds(pl.multiple_of(s * self.rows, self.rows), self.rows)]

    def to_line(self, src, s, way):
        device = self.me.up if way == 0 else self.me.down
        return remote(src, self.spot(0, s), self.sems.at[way, s], self.sems.at[3, s], device)

    def to_core(self, src, s):
        return remote(src, self.spot(1, s), self.sems.at[2, s], self.sems.at[4, s], self.me.other)

    def keep(self):
        return pltpu.make_async_copy(self.src, self.spot(0, self.me.z), self.sems.at[5, 0])

    def start(self):
        z, line = self.me.z, self.me.line

        @pl.when(z + 1 < line)
        def _():
            self.to_line(self.src, z, 0).start()

        @pl.when(z >= 1)
        def _():
            self.to_line(self.src, z, 1).start()

        self.to_core(self.src, z).start()
        self.keep().start()

    def hop(self, h):
        z, line = self.me.z, self.me.line
        for s, arrives, goes_on, way in (
            (z - h, z >= h, z + 1 < line, 0),
            (z + h, z + h < line, z >= 1, 1),
        ):

            @pl.when(arrives)
            def _(s=s, goes_on=goes_on, way=way):
                here = self.spot(0, s)
                self.to_line(here, s, way).wait_recv()

                @pl.when(goes_on)
                def _():
                    self.to_line(here, s, way).start()

                self.to_core(here, s).start()

    def arrived(self):
        self.keep().wait()
        for s in range(self.me.line):
            self.to_core(self.spot(0, s), s).wait_recv()

    def done(self):
        z, line = self.me.z, self.me.line
        for s in range(line):
            here = self.spot(0, s)
            self.to_core(here, s).wait_send()

            @pl.when((s <= z) & (z + 1 < line))
            def _(s=s, here=here):
                self.to_line(here, s, 0).wait_send()

            @pl.when((s >= z) & (z >= 1))
            def _(s=s, here=here):
                self.to_line(here, s, 1).wait_send()


class SquareGather:
    def __init__(self, me, full, sems):
        self.me, self.full, self.sems = me, full, sems
        self.half = full.shape[1] // 2

    def copies(self):
        me, full, sems, half = self.me, self.full, self.sems, self.half
        top, bottom = pl.ds(0, half), pl.ds(half, half)
        return (
            remote(full.at[0], full.at[1], sems.at[0], sems.at[1], me.x),
            remote(full.at[0], full.at[2], sems.at[2], sems.at[3], me.y),
            remote(full.at[1, top], full.at[3, top], sems.at[4], sems.at[5], me.y),
            remote(full.at[2, bottom], full.at[3, bottom], sems.at[6], sems.at[7], me.x),
        )

    def start(self):
        x, y, _, _ = self.copies()
        x.start()
        y.start()

    def forward(self):
        x, y, top, bottom = self.copies()
        x.wait_recv()
        top.start()
        y.wait_recv()
        bottom.start()

    def arrived(self):
        _, _, top, bottom = self.copies()
        top.wait_recv()
        bottom.wait_recv()

    def done(self):
        for copy in self.copies():
            copy.wait_send()


class SquareScatter:
    def __init__(self, me, stage, landed, sems):
        self.me, self.stage, self.landed, self.sems = me, stage, landed, sems
        self.half = stage.shape[1] // 2
        self.top, self.bottom = pl.ds(0, self.half), pl.ds(self.half, self.half)

    def copies(self):
        me, stage, landed, sems = self.me, self.stage, self.landed, self.sems
        top, bottom = self.top, self.bottom
        return (
            remote(stage.at[2, top], landed.at[2, top], sems.at[0], sems.at[1], me.y),
            remote(stage.at[2, bottom], landed.at[2, bottom], sems.at[2], sems.at[3], me.x),
            remote(stage.at[0, bottom], landed.at[0, bottom], sems.at[4], sems.at[5], me.x),
            remote(stage.at[1, top], landed.at[1, top], sems.at[6], sems.at[7], me.y),
            remote(stage.at[0, top], landed.at[0, top], sems.at[8], sems.at[9], me.x),
            remote(stage.at[1, bottom], landed.at[1, bottom], sems.at[10], sems.at[11], me.y),
        )

    def diagonal_ready(self):
        copies = self.copies()
        copies[0].start()
        copies[1].start()

    def sides_ready(self):
        copies = self.copies()
        copies[2].start()
        copies[3].start()

    def combine(self):
        copies = self.copies()
        for n, slot, at in ((0, 0, self.top), (1, 1, self.bottom)):
            copies[n].wait_recv()
            add_rows(self.stage, slot, at, self.landed)
            copies[4 + n].start()

    def arrived(self):
        for copy in self.copies()[2:]:
            copy.wait_recv()

    def done(self):
        for copy in self.copies():
            copy.wait_send()


def add_rows(stage, slot, at, landed):
    step = 32

    @pl.loop(0, at.size // step)
    def _(n):
        here = pl.ds(pl.multiple_of(at.start + n * step, step), step)
        total = stage[slot, here, :].astype(F32) + landed[2, here, :].astype(F32)
        stage[slot, here, :] = total.astype(BF16)


def remote(src, dst, send_sem, recv_sem, device):
    return pltpu.make_async_remote_copy(
        src_ref=src, dst_ref=dst, send_sem=send_sem, recv_sem=recv_sem, device_id=device,
        device_id_type=pl.DeviceIdType.MESH,
    )


class Place:
    def __init__(self, dp):
        index = lax.axis_index("dp")
        self.line = dp // 2
        self.z, self.core = index // 2, index % 2
        self.t = lax.axis_index("tensor")
        tx, ty = self.t % 2, self.t // 2
        self.other = {"dp": index + 1 - 2 * self.core}
        self.up, self.down = {"dp": index + 2}, {"dp": index - 2}
        self.x = {"tensor": self.t + 1 - 2 * tx}
        self.y = {"tensor": self.t + 2 - 4 * ty}
        self.spots = [
            (tx if i % 2 == 0 else 1 - tx) + 2 * (ty if i // 2 == 0 else 1 - ty) for i in range(4)
        ]

    def greet(self):
        barrier = pltpu.get_barrier_semaphore()

        def signal(device):
            pl.semaphore_signal(
                barrier, inc=1, device_id=device, device_id_type=pl.DeviceIdType.MESH
            )

        for device in (self.other, self.x, self.y):
            signal(device)
        pl.when(self.z + 1 < self.line)(lambda: signal(self.up))
        pl.when(self.z >= 1)(lambda: signal(self.down))
        ends = (self.z == 0) | (self.z == self.line - 1)
        pl.when(ends)(lambda: pl.semaphore_wait(barrier, 4))
        pl.when(jnp.logical_not(ends))(lambda: pl.semaphore_wait(barrier, 5))


def norm_rows(count, body, step=32):
    @pl.loop(0, count // step)
    def _(n):
        body(pl.ds(pl.multiple_of(n * step, step), step))


def forward_kernel(
    dp, x_ref, wa_ref, wo_ref, wf_ref, g_ref, gain_ref, cos_ref, sin_ref, segc_ref, segr_ref,
    normed_ref, gall_ref, normed_mlp_ref, q_ref, k_ref, v_ref, mixed_ref, lse_ref, middle_ref,
    wa_full, wo_full, wf_full, gains_ref,
    bias_ref, local_ref, stage_ref, landed_ref,
    sem_gain, sem_a, sem_o, sem_f, sem_n, sem_g, sem_s, sem_m, sem_c,
):
    me = Place(dp)
    me.greet()
    nf = wf_ref.shape[0]
    gain = LineGather(me, gain_ref, gains_ref, sem_gain)
    wa = LineGather(me, wa_ref, wa_full, sem_a)
    wo = LineGather(me, wo_ref, wo_full, sem_o)
    wf = [LineGather(me, wf_ref.at[b], wf_full.at[b], sem_f.at[b]) for b in range(nf)]
    normed = SquareGather(me, normed_ref, sem_n)
    grads = SquareGather(me, gall_ref, sem_g)
    normed_mlp = SquareGather(me, normed_mlp_ref, sem_m)
    hops = range(1, me.line)

    gain.start()
    wa.start()
    keep_g = pltpu.make_async_copy(g_ref, gall_ref.at[0], sem_c.at[0])
    keep_g.start()
    for h in hops:
        gain.hop(h)
    gain.arrived()

    half = x_ref.shape[1] // 2
    shard = gain_ref.shape[1]

    def gain_row(which, width):
        return jnp.concatenate(
            [
                gains_ref[side, pl.ds(s * 16 + which, 1), :].astype(F32)
                for side in range(2)
                for s in range(me.line)
            ],
            axis=1,
        )

    gain_one, gain_two = gain_row(0, shard), gain_row(1, shard)

    def first_norm(at):
        values = x_ref[at, :].astype(F32)
        normed_ref[0, at, :] = (values * norm_factor(values) * gain_one).astype(BF16)

    norm_rows(x_ref.shape[0], first_norm)
    normed.start()
    wa.hop(1)
    normed.forward()
    wa.hop(2)
    grads_started = False
    for h in range(3, me.line):
        wa.hop(h)
    wo.start()
    keep_g.wait()
    grads.start()
    normed.arrived()
    wa.arrived()
    wf[0].start()

    rows = LEN // 4
    cols = q_ref.shape[1]
    groups = cols // GROUP

    @pl.loop(0, 4 * groups)
    def _(n):
        b, group = n // groups, n % groups
        at = pl.ds(pl.multiple_of(b * rows, rows), rows)
        lanes = pl.ds(pl.multiple_of(group * GROUP, GROUP), GROUP)
        left, right = normed_ref[b, :, :half], normed_ref[b, :, half:]
        cosine, sine = cos_ref[at, :], sin_ref[at, :]

        def product(part):
            here = pl.ds(pl.multiple_of(part * cols + group * GROUP, GROUP), GROUP)
            return dot_nn(left, wa_full[0, :, here]) + dot_nn(right, wa_full[1, :, here])

        query = product(0)
        q_ref[at, lanes] = (query * cosine + swap_halves(query) * sine).astype(BF16)
        keys = product(1)
        k_ref[at, lanes] = (keys * cosine + swap_halves(keys) * sine).astype(BF16)
        v_ref[at, lanes] = product(2).astype(BF16)

    wo.hop(1)
    head_lane = lax.broadcasted_iota(jnp.int32, (rows, 128), 1)
    for i in range(4):
        places = [(j, me.spots[j]) for j in key_blocks(i, rows)]
        at = pl.ds(pl.multiple_of(me.spots[i] * rows, rows), rows)
        fill_bias(bias_ref, segc_ref[at, 0:1], segr_ref, i, places)
        spots = [pl.ds(pl.multiple_of(p * rows, rows), rows) for _, p in places]

        @pl.loop(0, cols // 128)
        def _(pair, at=at, spots=spots):
            attend(pair, 0, at, spots, head_lane, q_ref, k_ref, v_ref, mixed_ref, lse_ref, bias_ref)

        if i == 0:
            wo.hop(2)
        if i == 1:
            for h in range(3, me.line):
                wo.hop(h)
            grads.forward()
        if i == 2:
            wf[0].hop(1)

    wo.arrived()
    scatter = SquareScatter(me, stage_ref, landed_ref, sem_s)

    def out_rows(b, slot):
        at = pl.ds(b * rows, rows)

        @pl.loop(0, 2)
        def _(side):
            @pl.loop(0, half // GROUP)
            def _(n):
                here = pl.ds(pl.multiple_of(n * GROUP, GROUP), GROUP)
                there = pl.ds(pl.multiple_of(side * half + n * GROUP, GROUP), GROUP)
                total = dot_nt(mixed_ref[at, :], wo_full[side, here, :])
                if slot is None:
                    middle_ref[:, there] = total
                else:
                    stage_ref[slot, :, there] = total.astype(BF16)

    out_rows(3, 2)
    scatter.diagonal_ready()
    out_rows(1, 0)
    out_rows(2, 1)
    scatter.sides_ready()
    out_rows(0, None)
    wf[0].hop(2)
    scatter.combine()
    for h in range(3, me.line):
        wf[0].hop(h)
    if nf > 1:
        wf[1].start()
    scatter.arrived()

    def second_norm(at):
        total = middle_ref[at, :] + landed_ref[0, at, :].astype(F32)
        total = total + landed_ref[1, at, :].astype(F32)
        middle = x_ref[at, :].astype(F32) + total
        middle_ref[at, :] = middle
        local_ref[at, :] = (middle * norm_factor(middle) * gain_two).astype(BF16)

    norm_rows(x_ref.shape[0], second_norm)
    keep_m = pltpu.make_async_copy(local_ref, normed_mlp_ref.at[0], sem_c.at[1])
    keep_m.start()
    keep_m.wait()
    normed_mlp.start()
    if nf > 1:
        wf[1].hop(1)
    normed_mlp.forward()
    if nf > 1:
        for h in range(2, me.line):
            wf[1].hop(h)
    normed_mlp.arrived()
    grads.arrived()
    for one in wf:
        one.arrived()
    for one in (gain, wa, wo, *wf, normed, grads, normed_mlp, scatter):
        one.done()


def attend(pair, first, at, spots, head_lane, q_ref, k_ref, v_ref, mixed_ref, lse_ref, bias_ref):
    lanes = pl.ds(pl.multiple_of(pair * 128, 128), 128)
    query = q_ref[at, lanes]
    outs, stats = [], []
    for h in range(2):
        mine = (head_lane < HEAD_DIM) if h == 0 else (head_lane >= HEAD_DIM)
        qm = jnp.where(mine, query, 0) * jnp.asarray(HEAD_DIM**-0.5, BF16)
        scores = [dot_nt(qm, k_ref[s, lanes]) + bias_ref[n] for n, s in enumerate(spots)]
        top = functools.reduce(jnp.maximum, [jnp.max(s, axis=1, keepdims=True) for s in scores])
        weights = [jnp.exp(s - top) for s in scores]
        total = sum(jnp.sum(w, axis=1, keepdims=True) for w in weights)
        out = sum(dot_nn(w.astype(BF16), v_ref[s, lanes]) for w, s in zip(weights, spots))
        outs.append(out / total)
        stats.append(top + jnp.log(total))
    mixed_ref[at, lanes] = jnp.where(head_lane < HEAD_DIM, outs[0], outs[1]).astype(BF16)
    kept = jnp.where(pair + first == 0, 0.0, lse_ref[at, :])
    for h in range(2):
        kept = jnp.where(head_lane == first + pair * 2 + h, stats[h], kept)
    lse_ref[at, :] = kept


def forward(dp, x, wa, wo, wf, g, gains, cosine, sine, segc, segr):
    line = dp // 2
    local, d = x.shape
    cols = wo.shape[1]
    nf, _, fcols = wf.shape
    vmem, hbm = pl.BlockSpec(memory_space=pltpu.VMEM), pl.BlockSpec(memory_space=pl.ANY)
    S = jax.ShapeDtypeStruct
    slab = S((LEN, cols), BF16)
    rows = LEN // 4
    dma = pltpu.SemaphoreType.DMA
    return pl.pallas_call(
        functools.partial(forward_kernel, dp),
        in_specs=[vmem, vmem, vmem, hbm, hbm, vmem, vmem, vmem, vmem, vmem],
        out_specs=[vmem, hbm, hbm, vmem, vmem, vmem, vmem, vmem, vmem, vmem, vmem, hbm, vmem],
        out_shape=[
            S((4, local, d), BF16), S((4, local, d), BF16), S((4, local, d), BF16),
            slab, slab, slab, slab, S((LEN, 128), F32), S((local, d), F32),
            S((2, d // 2, 3 * cols), BF16), S((2, d // 2, cols), BF16),
            S((nf, 2, d // 2, fcols), BF16), S((2, line * 16, d // dp), BF16),
        ],
        scratch_shapes=[
            pltpu.VMEM((3, rows, rows), F32),
            pltpu.VMEM((local, d), BF16),
            pltpu.VMEM((3, local, d), BF16),
            pltpu.VMEM((3, local, d), BF16),
            dma((6, line)), dma((6, line)), dma((6, line)), dma((nf, 6, line)),
            dma((8,)), dma((8,)), dma((12,)), dma((8,)), dma((2,)),
        ],
        compiler_params=pltpu.CompilerParams(
            vmem_limit_bytes=VMEM_BYTES, collective_id=0, has_side_effects=True
        ),
        name="forward",
    )(x, wa, wo, wf, g, gains, cosine, sine, segc, segr)


def on_device(
    dp, tensor, hidden_in, doc_lengths, gain_attn, w_query, w_key, w_value, w_out, gain_mlp,
    w_gate, w_up, w_down, cotangent,
):
    line = dp // 2
    core = lax.axis_index("dp") % 2
    place = lax.axis_index("tensor")
    square = tensor == 4
    same_core = [[c + 2 * z for z in range(line)] for c in range(2)]
    sibling = [(i, i ^ 1) for i in range(dp)]
    d = hidden_in.shape[1]
    local = hidden_in.shape[0]

    def own_first(a):
        s = a.reshape(a.shape[:-1] + (line, 2, d // dp))
        even, odd = s[..., 0, :], s[..., 1, :]
        out = jnp.concatenate(
            [jnp.where(core == 0, even, odd), jnp.where(core == 0, odd, even)], axis=-2
        )
        return out.reshape(a.shape)

    def true_order(a):
        s = a.reshape(a.shape[:-1] + (2, line, d // dp))
        first, second = s[..., 0, :, :], s[..., 1, :, :]
        out = jnp.stack(
            [jnp.where(core == 0, first, second), jnp.where(core == 0, second, first)], axis=-2
        )
        return out.reshape(a.shape)

    def hop(a, step):
        return lax.ppermute(a, "tensor", [(i, i ^ step) for i in range(tensor)])

    def gather_rows(a):
        if not square:
            return lax.all_gather(a, "tensor", axis=0, tiled=True)
        half = a.shape[0] // 2
        from_x, from_y = hop(a, 1), hop(a, 2)
        top, bottom = hop(from_x[:half], 2), hop(from_y[half:], 1)
        return jnp.concatenate([a, from_x, from_y, top, bottom], axis=0)

    def scatter_rows(a):
        if not square:
            return lax.psum_scatter(a, "tensor", scatter_dimension=0, tiled=True).astype(F32)
        n = a.shape[0] // 4
        half = n // 2
        top = hop(a[3 * n : 3 * n + half], 2)
        bottom = hop(a[3 * n + half :], 1)
        for_x = jnp.concatenate([a[n : n + half] + top, a[n + half : 2 * n]], axis=0)
        for_y = jnp.concatenate([a[2 * n : 2 * n + half], a[2 * n + half : 3 * n] + bottom], axis=0)
        return (a[:n].astype(F32) + hop(for_x, 1).astype(F32)) + hop(for_y, 2).astype(F32)

    def line_gather(a):
        own = lax.all_gather(a, "dp", axis=0, axis_index_groups=same_core, tiled=True)
        return own, lax.ppermute(own, "dp", sibling)

    def line_scatter(own, sib):
        mine = own + lax.ppermute(sib, "dp", sibling)
        return lax.psum_scatter(
            mine, "dp", scatter_dimension=0, axis_index_groups=same_core, tiled=True
        ).astype(F32)

    blocks = 4
    rows = LEN // blocks
    key = place if square else jnp.zeros((), jnp.int32)
    tokens = (
        (jnp.arange(blocks, dtype=jnp.int32) ^ key)[:, None] * rows
        + jnp.arange(rows, dtype=jnp.int32)[None, :]
    ).reshape(LEN)
    segment, position = doc_tables(doc_lengths, tokens)
    cosine, sine = rotary_tables(position)
    segc = jnp.broadcast_to(segment[:, None], (LEN, 128))
    segr = jnp.broadcast_to(segment.reshape(blocks, 1, rows), (blocks, 8, rows))
    key = key.reshape(1)

    ff = w_gate.shape[1]
    fb = ff // FF_BLOCKS
    down_t = w_down.T
    shards = [
        jnp.concatenate([w[:, b * fb : (b + 1) * fb] for w in (w_gate, w_up, down_t)], axis=1)
        for b in range(FF_BLOCKS)
    ]
    qkv_shard = jnp.concatenate([w_query, w_key, w_value], axis=1)
    cols = w_query.shape[1]
    hidden_mine = own_first(hidden_in)
    g_local = own_first(cotangent)
    inputs = hidden_mine.astype(F32)
    factor_one = norm_factor(inputs)
    early = FF_EARLY if square else 0
    ff_sets = [jnp.concatenate(line_gather(shard), axis=0) for shard in shards[early:]]
    if square:
        gain_rows = jnp.pad(jnp.stack([gain_attn, gain_mlp]), ((0, 14), (0, 0)))
        (
            normed, g_all, normed_mlp, query, keys, values, mixed, lse, middle, qkv_full,
            out_full, ff_full, gains,
        ) = forward(
            dp, hidden_mine, qkv_shard, w_out.T, jnp.stack(shards[:early]), g_local, gain_rows,
            cosine, sine, segc, segr,
        )
        normed, g_all, normed_mlp = (a.reshape(LEN, d) for a in (normed, g_all, normed_mlp))
        qkv_own, qkv_sib = qkv_full[0], qkv_full[1]
        out_own, out_sib = out_full[0], out_full[1]
        ff_sets = [ff_full[b].reshape(d, 3 * fb) for b in range(early)] + ff_sets
        gains = gains.reshape(2 * line, 16, d // dp)[:, :2].astype(F32)
        gain_one, gain_two = gains[:, 0].reshape(d), gains[:, 1].reshape(d)
        factor_two = norm_factor(middle)
    else:
        gains = lax.all_gather(jnp.stack([gain_attn, gain_mlp]), "dp", axis=0)
        gains = own_first(jnp.moveaxis(gains, 0, 1).reshape(2, d)).astype(F32)
        gain_one, gain_two = gains[0], gains[1]
        qkv_own, qkv_sib = line_gather(qkv_shard)
        out_own, out_sib = line_gather(w_out.T)
        normed = gather_rows((inputs * factor_one * gain_one).astype(BF16))
        g_all = gather_rows(g_local)
        query, keys, values, mixed, lse = attn_forward(
            blocks, key, normed, qkv_own, qkv_sib, cosine, sine, segc, segr
        )
        attended = jnp.concatenate(
            [dot_nt(mixed, out_own).astype(BF16), dot_nt(mixed, out_sib).astype(BF16)], axis=1
        )
        middle = inputs + scatter_rows(attended)
        factor_two = norm_factor(middle)
        normed_mlp = gather_rows((middle * factor_two * gain_two).astype(BF16))

    down_sum = jnp.zeros((LEN, d), F32)
    back_sum = jnp.zeros((LEN, d), F32)
    ff_grads = []
    for b in range(FF_BLOCKS):
        gate_w, up_w, down_w = jnp.split(ff_sets[b], 3, axis=1)
        gate_pre = dot_nn(normed_mlp, gate_w)
        upward = dot_nn(normed_mlp, up_w)
        grad_hidden = dot_nn(g_all, down_w)
        sig = jax.nn.sigmoid(gate_pre)
        activated = gate_pre * sig
        hidden = (activated * upward).astype(BF16)
        grad_gate_pre = (grad_hidden * upward * sig * (1.0 + gate_pre * (1.0 - sig))).astype(BF16)
        grad_upward = (grad_hidden * activated).astype(BF16)
        down_sum = down_sum + dot_nt(hidden, down_w)
        back_sum = back_sum + dot_nt(grad_gate_pre, gate_w) + dot_nt(grad_upward, up_w)
        grad = jnp.concatenate(
            [
                dot_tn(normed_mlp, grad_gate_pre).astype(BF16),
                dot_tn(normed_mlp, grad_upward).astype(BF16),
                dot_tn(g_all, hidden).astype(BF16),
            ],
            axis=1,
        )
        ff_grads.append(line_scatter(grad[: d // 2], grad[d // 2 :]))
    grad_norm_two = scatter_rows(back_sum.astype(BF16))
    output = true_order((middle + scatter_rows(down_sum.astype(BF16))).astype(BF16))
    grad_mid_norm, gain_two_part = norm_back(middle, factor_two, gain_two, grad_norm_two)
    grad_middle = g_local.astype(F32) + grad_mid_norm
    grad_mid_all = gather_rows(grad_middle.astype(BF16))

    dq, dk, dv = attn_backward(
        blocks, key, grad_mid_all, out_own, out_sib, query, keys, values, lse, cosine, sine,
        segc, segr,
    )
    grad = jnp.concatenate(
        [dot_tn(normed, dq), dot_tn(normed, dk), dot_tn(normed, dv), dot_tn(grad_mid_all, mixed)],
        axis=1,
    ).astype(BF16)
    attn_grads = line_scatter(grad[: d // 2], grad[d // 2 :])
    rows_grad = jnp.concatenate([dq, dk, dv], axis=1)
    back = jnp.concatenate(
        [
            dot_nt(rows_grad, qkv_own).astype(BF16),
            dot_nt(rows_grad, qkv_sib).astype(BF16),
        ],
        axis=1,
    )
    grad_in_norm, gain_one_part = norm_back(inputs, factor_one, gain_one, scatter_rows(back))
    input_grad = true_order(grad_middle + grad_in_norm)

    parts = true_order(jnp.stack([gain_one_part, gain_two_part])).reshape(2 * d)
    shares = lax.all_gather(parts, ("dp", "tensor"), axis=0)
    gain_sum = jnp.sum(shares, axis=0).reshape(2, d)
    share = d // (dp * tensor)
    first = (lax.axis_index("dp") * tensor + place) * share
    gain_sum = lax.dynamic_slice_in_dim(gain_sum, first, share, 1)

    return (
        output,
        input_grad,
        gain_sum[0],
        attn_grads[:, :cols],
        attn_grads[:, cols : 2 * cols],
        attn_grads[:, 2 * cols : 3 * cols],
        attn_grads[:, 3 * cols :].T,
        gain_sum[1],
        jnp.concatenate([g[:, :fb] for g in ff_grads], axis=1),
        jnp.concatenate([g[:, fb : 2 * fb] for g in ff_grads], axis=1),
        jnp.concatenate([g[:, 2 * fb :] for g in ff_grads], axis=1).T,
    )


def solution(mesh):
    shape = dict(mesh.shape)
    return jax.shard_map(
        functools.partial(on_device, shape["dp"], shape["tensor"]),
        mesh=mesh,
        in_specs=(
            P(("dp", "tensor"), None),
            P("dp", None),
            P("dp"),
            P("dp", "tensor"),
            P("dp", "tensor"),
            P("dp", "tensor"),
            P("tensor", "dp"),
            P("dp"),
            P("dp", "tensor"),
            P("dp", "tensor"),
            P("tensor", "dp"),
            P(("dp", "tensor"), None),
        ),
        out_specs=(
            P(("dp", "tensor"), None),
            P(("dp", "tensor"), None),
            P(("dp", "tensor")),
            P("dp", "tensor"),
            P("dp", "tensor"),
            P("dp", "tensor"),
            P("tensor", "dp"),
            P(("dp", "tensor")),
            P("dp", "tensor"),
            P("dp", "tensor"),
            P("tensor", "dp"),
        ),
        check_vma=False,
    )
```

```python
import functools

import jax
import jax.numpy as jnp
from jax import lax
from jax.experimental import pallas as pl
from jax.experimental.pallas import tpu as pltpu
from jax.sharding import PartitionSpec as P

HEAD_DIM = 64
LEN = 1024
MOST = 512
EPSILON = 1e-05
ROPE_BASE = 130000.0
NEG = -1e30
GROUP = 256
FF_BLOCKS = 8
FF_EARLY = 4
TICK_AFTER = (3, 5, 6)
F32 = jnp.float32
BF16 = jnp.bfloat16
VMEM_BYTES = 60 * 1024 * 1024


def dot_nn(a, b):
    return jnp.dot(a, b, preferred_element_type=F32)


def dot_tn(a, b):
    return lax.dot_general(a, b, (((0,), (0,)), ((), ())), preferred_element_type=F32)


def dot_nt(a, b):
    return lax.dot_general(a, b, (((1,), (1,)), ((), ())), preferred_element_type=F32)


def norm_factor(values):
    return lax.rsqrt(jnp.mean(values * values, axis=-1, keepdims=True) + EPSILON)


def norm_back(values, factor, gain, grads):
    scaled = grads * gain
    grad_in = factor * scaled - values * factor * factor * factor * jnp.mean(
        scaled * values, axis=-1, keepdims=True
    )
    return grad_in, jnp.sum(grads * values * factor, axis=0)


def doc_tables(doc_lengths, tokens):
    ends = jnp.cumsum(doc_lengths, axis=1)[0]
    passed = tokens[:, None] >= ends[None, :]
    segment = jnp.sum(passed.astype(jnp.int32), axis=1)
    start = jnp.sum(jnp.where(passed, doc_lengths, 0), axis=1)
    return segment, tokens - start


def rotary_tables(position):
    half = HEAD_DIM // 2
    inverse = jnp.power(ROPE_BASE, -jnp.arange(half, dtype=F32) * 2.0 / HEAD_DIM)
    angles = position.astype(F32)[:, None] * inverse
    cosine, sine = jnp.cos(angles), jnp.sin(angles)
    heads = GROUP // HEAD_DIM
    return (
        jnp.tile(jnp.concatenate([cosine, cosine], axis=1), (1, heads)),
        jnp.tile(jnp.concatenate([-sine, sine], axis=1), (1, heads)),
    )


def swap_halves(v):
    half, width = HEAD_DIM // 2, v.shape[1]
    lane = lax.broadcasted_iota(jnp.int32, v.shape, 1)
    ahead = pltpu.roll(v, width - half, 1)
    behind = pltpu.roll(v, half, 1)
    return jnp.where(lane % HEAD_DIM < half, ahead, behind)


def key_blocks(i, rows):
    reach = -(-(MOST - 1) // rows)
    return list(range(max(0, i - reach), i + 1))


def fill_bias(bias_ref, seg_col, seg_ref, i, places):
    rows = seg_col.shape[0]
    for n, (j, place) in enumerate(places):
        same = seg_col == seg_ref[place][0:1, :]
        if j == i:
            row = lax.broadcasted_iota(jnp.int32, (rows, rows), 0)
            col = lax.broadcasted_iota(jnp.int32, (rows, rows), 1)
            same = same & (col <= row)
        bias_ref[n] = jnp.where(same, 0.0, NEG)


def attn_forward_kernel(
    blocks, key_ref, x_ref, qo, qs, ko, ks, vo, vs, cos_ref, sin_ref, segc_ref, segr_ref,
    q_ref, k_ref, v_ref, mixed_ref, lse_ref, bias_ref,
):
    rows = LEN // blocks
    half = x_ref.shape[1] // 2
    key = key_ref[0]

    @pl.loop(0, blocks)
    def _(b):
        at = pl.ds(pl.multiple_of(b * rows, rows), rows)
        left, right = x_ref[at, :half], x_ref[at, half:]
        cosine, sine = cos_ref[at, :], sin_ref[at, :]
        query = dot_nn(left, qo[...]) + dot_nn(right, qs[...])
        q_ref[at, :] = (query * cosine + swap_halves(query) * sine).astype(BF16)
        keys = dot_nn(left, ko[...]) + dot_nn(right, ks[...])
        k_ref[at, :] = (keys * cosine + swap_halves(keys) * sine).astype(BF16)
        v_ref[at, :] = (dot_nn(left, vo[...]) + dot_nn(right, vs[...])).astype(BF16)

    head_lane = lax.broadcasted_iota(jnp.int32, (rows, 128), 1)
    for i in range(blocks):
        places = [(j, j ^ key) for j in key_blocks(i, rows)]
        at = pl.ds(pl.multiple_of((i ^ key) * rows, rows), rows)
        fill_bias(bias_ref, segc_ref[at, 0:1], segr_ref, i, places)
        spots = [pl.ds(pl.multiple_of(p * rows, rows), rows) for _, p in places]

        @pl.loop(0, GROUP // 128)
        def _(pair, at=at, spots=spots):
            first = pl.program_id(0) * (GROUP // HEAD_DIM)
            attend(pair, first, at, spots, head_lane, q_ref, k_ref, v_ref, mixed_ref, lse_ref, bias_ref)


def attn_forward(blocks, key, x, own, sib, cosine, sine, segc, segr):
    d = x.shape[1]
    cols = own.shape[1] // 3
    steps = cols // GROUP
    rows = LEN // blocks

    def weight(part):
        return pl.BlockSpec((d // 2, GROUP), lambda i, part=part: (0, part * steps + i))

    def whole(shape):
        return pl.BlockSpec(shape, lambda i: (0,) * len(shape))

    col_block = pl.BlockSpec((LEN, GROUP), lambda i: (0, i))
    slab = jax.ShapeDtypeStruct((LEN, cols), BF16)
    return pl.pallas_call(
        functools.partial(attn_forward_kernel, blocks),
        grid=(steps,),
        in_specs=[pl.BlockSpec(memory_space=pltpu.SMEM), whole((LEN, d))]
        + [weight(p) for p in (0, 0, 1, 1, 2, 2)]
        + [whole((LEN, GROUP))] * 2
        + [whole((LEN, 128)), whole(segr.shape)],
        out_specs=[col_block] * 4 + [whole((LEN, 128))],
        out_shape=[slab] * 4 + [jax.ShapeDtypeStruct((LEN, 128), F32)],
        scratch_shapes=[pltpu.VMEM((blocks, rows, rows), F32)],
        compiler_params=pltpu.CompilerParams(vmem_limit_bytes=VMEM_BYTES),
        name="attn_forward",
    )(key, x, own, sib, own, sib, own, sib, cosine, sine, segc, segr)


def attn_backward_kernel(
    blocks, key_ref, g_ref, wo, ws, q_ref, k_ref, v_ref, lse_ref, cos_ref, sin_ref, segc_ref,
    segr_ref, dq_ref, dk_ref, dv_ref, dm_ref, dqa_ref, dka_ref, dva_ref, bias_ref,
):
    rows = LEN // blocks
    half = g_ref.shape[1] // 2
    key = key_ref[0]

    @pl.loop(0, blocks)
    def _(b):
        at = pl.ds(pl.multiple_of(b * rows, rows), rows)
        dm_ref[at, :] = (dot_nn(g_ref[at, :half], wo[...]) + dot_nn(g_ref[at, half:], ws[...])).astype(BF16)
        dka_ref[at, :] = jnp.zeros((rows, GROUP), F32)
        dva_ref[at, :] = jnp.zeros((rows, GROUP), F32)

    head_lane = lax.broadcasted_iota(jnp.int32, (rows, 128), 1)
    scale = HEAD_DIM**-0.5
    for i in range(blocks):
        places = [(j, j ^ key) for j in key_blocks(i, rows)]
        at = pl.ds(pl.multiple_of((i ^ key) * rows, rows), rows)
        fill_bias(bias_ref, segc_ref[at, 0:1], segr_ref, i, places)
        spots = [pl.ds(pl.multiple_of(p * rows, rows), rows) for _, p in places]

        @pl.loop(0, GROUP // 128)
        def _(pair, at=at, spots=spots):
            lanes = pl.ds(pl.multiple_of(pair * 128, 128), 128)
            first = pl.program_id(0) * (GROUP // HEAD_DIM)
            query, grad = q_ref[at, lanes], dm_ref[at, lanes]
            logs = lse_ref[at, :]
            outs = []
            for h in range(2):
                mine = (head_lane < HEAD_DIM) if h == 0 else (head_lane >= HEAD_DIM)
                qm = jnp.where(mine, query, 0) * jnp.asarray(scale, BF16)
                gm = jnp.where(mine, grad, 0)
                log = jnp.sum(
                    jnp.where(head_lane == first + pair * 2 + h, logs, 0.0), axis=1, keepdims=True
                )
                weights = [
                    jnp.exp(dot_nt(qm, k_ref[s, lanes]) + bias_ref[n] - log)
                    for n, s in enumerate(spots)
                ]
                grads = [dot_nt(gm, v_ref[s, lanes]) for s in spots]
                inner = sum(
                    jnp.sum(w * g, axis=1, keepdims=True) for w, g in zip(weights, grads)
                )
                dq = jnp.zeros((rows, 128), F32)
                for w, g, s in zip(weights, grads, spots):
                    ds = (w * (g - inner)).astype(BF16)
                    dva_ref[s, lanes] += dot_tn(w.astype(BF16), gm)
                    dka_ref[s, lanes] += dot_tn(ds, qm)
                    dq = dq + dot_nn(ds, k_ref[s, lanes])
                outs.append(dq)
            dqa_ref[at, lanes] = jnp.where(head_lane < HEAD_DIM, outs[0], outs[1]) * scale

    @pl.loop(0, blocks)
    def _(b):
        at = pl.ds(pl.multiple_of(b * rows, rows), rows)
        cosine, sine = cos_ref[at, :], sin_ref[at, :]
        dq = dqa_ref[at, :]
        dq_ref[at, :] = (dq * cosine - swap_halves(dq) * sine).astype(BF16)
        dk = dka_ref[at, :]
        dk_ref[at, :] = (dk * cosine - swap_halves(dk) * sine).astype(BF16)
        dv_ref[at, :] = dva_ref[at, :].astype(BF16)


def attn_backward(blocks, key, g, own, sib, q, k, v, lse, cosine, sine, segc, segr):
    d = g.shape[1]
    cols = q.shape[1]
    steps = cols // GROUP
    rows = LEN // blocks

    def whole(shape):
        return pl.BlockSpec(shape, lambda i: (0,) * len(shape))

    col_block = pl.BlockSpec((LEN, GROUP), lambda i: (0, i))
    weight = pl.BlockSpec((d // 2, GROUP), lambda i: (0, i))
    slab = jax.ShapeDtypeStruct((LEN, cols), BF16)
    return pl.pallas_call(
        functools.partial(attn_backward_kernel, blocks),
        grid=(steps,),
        in_specs=[pl.BlockSpec(memory_space=pltpu.SMEM), whole((LEN, d)), weight, weight]
        + [col_block] * 3
        + [whole((LEN, 128))]
        + [whole((LEN, GROUP))] * 2
        + [whole((LEN, 128)), whole(segr.shape)],
        out_specs=[col_block] * 3,
        out_shape=[slab] * 3,
        scratch_shapes=[
            pltpu.VMEM((LEN, GROUP), BF16),
            pltpu.VMEM((LEN, GROUP), F32),
            pltpu.VMEM((LEN, GROUP), F32),
            pltpu.VMEM((LEN, GROUP), F32),
            pltpu.VMEM((blocks, rows, rows), F32),
        ],
        compiler_params=pltpu.CompilerParams(vmem_limit_bytes=VMEM_BYTES),
        name="attn_backward",
    )(key, g, own, sib, q, k, v, lse, cosine, sine, segc, segr)


class LineGather:
    def __init__(self, me, src, full, sems):
        self.me, self.src, self.full, self.sems = me, src, full, sems
        self.rows = src.shape[0]

    def spot(self, side, s):
        return self.full.at[side, pl.ds(pl.multiple_of(s * self.rows, self.rows), self.rows)]

    def to_line(self, src, s, way):
        device = self.me.up if way == 0 else self.me.down
        return remote(src, self.spot(0, s), self.sems.at[way, s], self.sems.at[3, s], device)

    def to_core(self, src, s):
        return remote(src, self.spot(1, s), self.sems.at[2, s], self.sems.at[4, s], self.me.other)

    def keep(self):
        return pltpu.make_async_copy(self.src, self.spot(0, self.me.z), self.sems.at[5, 0])

    def start(self):
        z, line = self.me.z, self.me.line

        @pl.when(z + 1 < line)
        def _():
            self.to_line(self.src, z, 0).start()

        @pl.when(z >= 1)
        def _():
            self.to_line(self.src, z, 1).start()

        self.to_core(self.src, z).start()
        self.keep().start()

    def hop(self, h):
        z, line = self.me.z, self.me.line
        for s, arrives, goes_on, way in (
            (z - h, z >= h, z + 1 < line, 0),
            (z + h, z + h < line, z >= 1, 1),
        ):

            @pl.when(arrives)
            def _(s=s, goes_on=goes_on, way=way):
                here = self.spot(0, s)
                self.to_line(here, s, way).wait_recv()

                @pl.when(goes_on)
                def _():
                    self.to_line(here, s, way).start()

                self.to_core(here, s).start()

    def arrived(self):
        self.keep().wait()
        for s in range(self.me.line):
            self.to_core(self.spot(0, s), s).wait_recv()

    def done(self):
        z, line = self.me.z, self.me.line
        for s in range(line):
            here = self.spot(0, s)
            self.to_core(here, s).wait_send()

            @pl.when((s <= z) & (z + 1 < line))
            def _(s=s, here=here):
                self.to_line(here, s, 0).wait_send()

            @pl.when((s >= z) & (z >= 1))
            def _(s=s, here=here):
                self.to_line(here, s, 1).wait_send()


class SquareGather:
    def __init__(self, me, full, sems):
        self.me, self.full, self.sems = me, full, sems
        self.half = full.shape[1] // 2

    def copies(self):
        me, full, sems, half = self.me, self.full, self.sems, self.half
        top, bottom = pl.ds(0, half), pl.ds(half, half)
        return (
            remote(full.at[0], full.at[1], sems.at[0], sems.at[1], me.x),
            remote(full.at[0], full.at[2], sems.at[2], sems.at[3], me.y),
            remote(full.at[1, top], full.at[3, top], sems.at[4], sems.at[5], me.y),
            remote(full.at[2, bottom], full.at[3, bottom], sems.at[6], sems.at[7], me.x),
        )

    def start(self):
        x, y, _, _ = self.copies()
        x.start()
        y.start()

    def forward(self):
        x, y, top, bottom = self.copies()
        x.wait_recv()
        top.start()
        y.wait_recv()
        bottom.start()

    def arrived(self):
        _, _, top, bottom = self.copies()
        top.wait_recv()
        bottom.wait_recv()

    def done(self):
        for copy in self.copies():
            copy.wait_send()


class SquareScatter:
    def __init__(self, me, stage, landed, sems):
        self.me, self.stage, self.landed, self.sems = me, stage, landed, sems
        self.half = stage.shape[1] // 2
        self.top, self.bottom = pl.ds(0, self.half), pl.ds(self.half, self.half)

    def copies(self):
        me, stage, landed, sems = self.me, self.stage, self.landed, self.sems
        top, bottom = self.top, self.bottom
        return (
            remote(stage.at[2, top], landed.at[2, top], sems.at[0], sems.at[1], me.y),
            remote(stage.at[2, bottom], landed.at[2, bottom], sems.at[2], sems.at[3], me.x),
            remote(stage.at[0, bottom], landed.at[0, bottom], sems.at[4], sems.at[5], me.x),
            remote(stage.at[1, top], landed.at[1, top], sems.at[6], sems.at[7], me.y),
            remote(stage.at[0, top], landed.at[0, top], sems.at[8], sems.at[9], me.x),
            remote(stage.at[1, bottom], landed.at[1, bottom], sems.at[10], sems.at[11], me.y),
        )

    def diagonal_ready(self):
        copies = self.copies()
        copies[0].start()
        copies[1].start()

    def sides_ready(self):
        copies = self.copies()
        copies[2].start()
        copies[3].start()

    def combine(self):
        copies = self.copies()
        for n, slot, at in ((0, 0, self.top), (1, 1, self.bottom)):
            copies[n].wait_recv()
            add_rows(self.stage, slot, at, self.landed)
            copies[4 + n].start()

    def arrived(self):
        for copy in self.copies()[2:]:
            copy.wait_recv()

    def done(self):
        for copy in self.copies():
            copy.wait_send()


def add_rows(stage, slot, at, landed):
    step = 32

    @pl.loop(0, at.size // step)
    def _(n):
        here = pl.ds(pl.multiple_of(at.start + n * step, step), step)
        total = stage[slot, here, :].astype(F32) + landed[2, here, :].astype(F32)
        stage[slot, here, :] = total.astype(BF16)


def remote(src, dst, send_sem, recv_sem, device):
    return pltpu.make_async_remote_copy(
        src_ref=src, dst_ref=dst, send_sem=send_sem, recv_sem=recv_sem, device_id=device,
        device_id_type=pl.DeviceIdType.MESH,
    )


class Place:
    def __init__(self, dp):
        index = lax.axis_index("dp")
        self.line = dp // 2
        self.z, self.core = index // 2, index % 2
        self.t = lax.axis_index("tensor")
        tx, ty = self.t % 2, self.t // 2
        self.other = {"dp": index + 1 - 2 * self.core}
        self.up, self.down = {"dp": index + 2}, {"dp": index - 2}
        self.next, self.far = {"dp": index + 2 - 4 * (self.z % 2)}, {"dp": index + 4 - 8 * (self.z // 2)}
        self.x = {"tensor": self.t + 1 - 2 * tx}
        self.y = {"tensor": self.t + 2 - 4 * ty}
        self.spots = [
            (tx if i % 2 == 0 else 1 - tx) + 2 * (ty if i // 2 == 0 else 1 - ty) for i in range(4)
        ]

    def greet(self, far=False):
        barrier = pltpu.get_barrier_semaphore()

        def signal(device):
            pl.semaphore_signal(
                barrier, inc=1, device_id=device, device_id_type=pl.DeviceIdType.MESH
            )

        for device in (self.other, self.x, self.y) + ((self.far,) if far else ()):
            signal(device)
        pl.when(self.z + 1 < self.line)(lambda: signal(self.up))
        pl.when(self.z >= 1)(lambda: signal(self.down))
        ends = (self.z == 0) | (self.z == self.line - 1)
        pl.when(ends)(lambda: pl.semaphore_wait(barrier, 4 + far))
        pl.when(jnp.logical_not(ends))(lambda: pl.semaphore_wait(barrier, 5 + far))


def norm_rows(count, body, step=32):
    @pl.loop(0, count // step)
    def _(n):
        body(pl.ds(pl.multiple_of(n * step, step), step))


def forward_kernel(
    dp, x_ref, wa_ref, wo_ref, wf_ref, g_ref, gain_ref, cos_ref, sin_ref, segc_ref, segr_ref,
    normed_ref, gall_ref, normed_mlp_ref, q_ref, k_ref, v_ref, mixed_ref, lse_ref, middle_ref,
    wa_full, wo_full, wf_full, gains_ref,
    bias_ref, local_ref, stage_ref, landed_ref,
    sem_gain, sem_a, sem_o, sem_f, sem_n, sem_g, sem_s, sem_m, sem_c,
):
    me = Place(dp)
    me.greet()
    nf = wf_ref.shape[0]
    gain = LineGather(me, gain_ref, gains_ref, sem_gain)
    wa = LineGather(me, wa_ref, wa_full, sem_a)
    wo = LineGather(me, wo_ref, wo_full, sem_o)
    wf = [LineGather(me, wf_ref.at[b], wf_full.at[b], sem_f.at[b]) for b in range(nf)]
    normed = SquareGather(me, normed_ref, sem_n)
    grads = SquareGather(me, gall_ref, sem_g)
    normed_mlp = SquareGather(me, normed_mlp_ref, sem_m)
    hops = range(1, me.line)
    acts = []
    for n, one in enumerate([wo] + wf):
        for h in hops:

            def act(n=n, one=one, h=h):
                one.hop(h)
                if h == 1 and n < nf:
                    wf[n].start()

            acts.append(act)

    def poll(count=1):
        for _ in range(min(count, len(acts))):
            acts.pop(0)()

    gain.start()
    wa.start()
    keep_g = pltpu.make_async_copy(g_ref, gall_ref.at[0], sem_c.at[0])
    keep_g.start()
    for h in hops:
        gain.hop(h)
    gain.arrived()

    half = x_ref.shape[1] // 2
    shard = gain_ref.shape[1]

    def gain_row(which, width):
        return jnp.concatenate(
            [
                gains_ref[side, pl.ds(s * 16 + which, 1), :].astype(F32)
                for side in range(2)
                for s in range(me.line)
            ],
            axis=1,
        )

    gain_one, gain_two = gain_row(0, shard), gain_row(1, shard)

    def first_norm(at):
        values = x_ref[at, :].astype(F32)
        normed_ref[0, at, :] = (values * norm_factor(values) * gain_one).astype(BF16)

    norm_rows(x_ref.shape[0], first_norm)
    normed.start()
    wa.hop(1)
    normed.forward()
    wa.hop(2)
    for h in range(3, me.line):
        wa.hop(h)
    wo.start()
    keep_g.wait()
    grads.start()
    normed.arrived()
    wa.arrived()

    rows = LEN // 4
    cols = q_ref.shape[1]
    groups = cols // GROUP

    @pl.loop(0, 4 * groups)
    def _(n):
        b, group = n // groups, n % groups
        at = pl.ds(pl.multiple_of(b * rows, rows), rows)
        lanes = pl.ds(pl.multiple_of(group * GROUP, GROUP), GROUP)
        left, right = normed_ref[b, :, :half], normed_ref[b, :, half:]
        cosine, sine = cos_ref[at, :], sin_ref[at, :]

        def product(part):
            here = pl.ds(pl.multiple_of(part * cols + group * GROUP, GROUP), GROUP)
            return dot_nn(left, wa_full[0, :, here]) + dot_nn(right, wa_full[1, :, here])

        query = product(0)
        q_ref[at, lanes] = (query * cosine + swap_halves(query) * sine).astype(BF16)
        keys = product(1)
        k_ref[at, lanes] = (keys * cosine + swap_halves(keys) * sine).astype(BF16)
        v_ref[at, lanes] = product(2).astype(BF16)

    poll()
    head_lane = lax.broadcasted_iota(jnp.int32, (rows, 128), 1)
    for i in range(4):
        places = [(j, me.spots[j]) for j in key_blocks(i, rows)]
        at = pl.ds(pl.multiple_of(me.spots[i] * rows, rows), rows)
        fill_bias(bias_ref, segc_ref[at, 0:1], segr_ref, i, places)
        spots = [pl.ds(pl.multiple_of(p * rows, rows), rows) for _, p in places]

        @pl.loop(0, cols // 128)
        def _(pair, at=at, spots=spots):
            attend(pair, 0, at, spots, head_lane, q_ref, k_ref, v_ref, mixed_ref, lse_ref, bias_ref)

        poll()
        if i == 1:
            grads.forward()

    wo.arrived()
    scatter = SquareScatter(me, stage_ref, landed_ref, sem_s)

    def out_rows(b, slot):
        at = pl.ds(b * rows, rows)

        @pl.loop(0, 2)
        def _(side):
            @pl.loop(0, half // GROUP)
            def _(n):
                here = pl.ds(pl.multiple_of(n * GROUP, GROUP), GROUP)
                there = pl.ds(pl.multiple_of(side * half + n * GROUP, GROUP), GROUP)
                total = dot_nt(mixed_ref[at, :], wo_full[side, here, :])
                if slot is None:
                    middle_ref[:, there] = total
                else:
                    stage_ref[slot, :, there] = total.astype(BF16)

    out_rows(3, 2)
    scatter.diagonal_ready()
    out_rows(1, 0)
    out_rows(2, 1)
    scatter.sides_ready()
    out_rows(0, None)
    poll()
    scatter.combine()
    poll(2)
    scatter.arrived()

    def second_norm(at):
        total = middle_ref[at, :] + landed_ref[0, at, :].astype(F32)
        total = total + landed_ref[1, at, :].astype(F32)
        middle = x_ref[at, :].astype(F32) + total
        middle_ref[at, :] = middle
        local_ref[at, :] = (middle * norm_factor(middle) * gain_two).astype(BF16)

    norm_rows(x_ref.shape[0], second_norm)
    keep_m = pltpu.make_async_copy(local_ref, normed_mlp_ref.at[0], sem_c.at[1])
    keep_m.start()
    keep_m.wait()
    normed_mlp.start()
    poll(3)
    normed_mlp.forward()
    poll(2)
    normed_mlp.arrived()
    poll(len(acts))
    grads.arrived()
    for one in wf:
        one.arrived()
    for one in (gain, wa, wo, *wf, normed, grads, normed_mlp, scatter):
        one.done()


def attend(pair, first, at, spots, head_lane, q_ref, k_ref, v_ref, mixed_ref, lse_ref, bias_ref):
    lanes = pl.ds(pl.multiple_of(pair * 128, 128), 128)
    query = q_ref[at, lanes]
    outs, stats = [], []
    for h in range(2):
        mine = (head_lane < HEAD_DIM) if h == 0 else (head_lane >= HEAD_DIM)
        qm = jnp.where(mine, query, 0) * jnp.asarray(HEAD_DIM**-0.5, BF16)
        scores = [dot_nt(qm, k_ref[s, lanes]) + bias_ref[n] for n, s in enumerate(spots)]
        top = functools.reduce(jnp.maximum, [jnp.max(s, axis=1, keepdims=True) for s in scores])
        weights = [jnp.exp(s - top) for s in scores]
        total = sum(jnp.sum(w, axis=1, keepdims=True) for w in weights)
        out = sum(dot_nn(w.astype(BF16), v_ref[s, lanes]) for w, s in zip(weights, spots))
        outs.append(out / total)
        stats.append(top + jnp.log(total))
    mixed_ref[at, lanes] = jnp.where(head_lane < HEAD_DIM, outs[0], outs[1]).astype(BF16)
    kept = jnp.where(pair + first == 0, 0.0, lse_ref[at, :])
    for h in range(2):
        kept = jnp.where(head_lane == first + pair * 2 + h, stats[h], kept)
    lse_ref[at, :] = kept


def forward(dp, x, wa, wo, wf, g, gains, cosine, sine, segc, segr):
    line = dp // 2
    local, d = x.shape
    cols = wo.shape[1]
    nf, _, fcols = wf.shape
    vmem, hbm = pl.BlockSpec(memory_space=pltpu.VMEM), pl.BlockSpec(memory_space=pl.ANY)
    S = jax.ShapeDtypeStruct
    slab = S((LEN, cols), BF16)
    rows = LEN // 4
    dma = pltpu.SemaphoreType.DMA
    return pl.pallas_call(
        functools.partial(forward_kernel, dp),
        in_specs=[vmem, vmem, vmem, hbm, hbm, vmem, vmem, vmem, vmem, vmem],
        out_specs=[vmem, hbm, hbm, vmem, vmem, vmem, vmem, vmem, vmem, vmem, vmem, hbm, vmem],
        out_shape=[
            S((4, local, d), BF16), S((4, local, d), BF16), S((4, local, d), BF16),
            slab, slab, slab, slab, S((LEN, 128), F32), S((local, d), F32),
            S((2, d // 2, 3 * cols), BF16), S((2, d // 2, cols), BF16),
            S((nf, 2, d // 2, fcols), BF16), S((2, line * 16, d // dp), BF16),
        ],
        scratch_shapes=[
            pltpu.VMEM((3, rows, rows), F32),
            pltpu.VMEM((local, d), BF16),
            pltpu.VMEM((3, local, d), BF16),
            pltpu.VMEM((3, local, d), BF16),
            dma((6, line)), dma((6, line)), dma((6, line)), dma((nf, 6, line)),
            dma((8,)), dma((8,)), dma((12,)), dma((8,)), dma((2,)),
        ],
        compiler_params=pltpu.CompilerParams(
            vmem_limit_bytes=VMEM_BYTES, collective_id=0, has_side_effects=True
        ),
        name="forward",
    )(x, wa, wo, wf, g, gains, cosine, sine, segc, segr)


def add_into(total, other, rows, step=64):
    @pl.loop(0, rows // step)
    def _(n):
        at = pl.ds(pl.multiple_of(n * step, step), step)
        total[at, :] = (total[at, :].astype(F32) + other[at, :].astype(F32)).astype(total.dtype)


class LineScatter:
    def __init__(self, me, rows, mine, theirs, swapped, kept, landed, work, sems):
        cut = lambda ref: ref.at[:, pl.ds(0, rows)]
        self.me, self.rows = me, rows
        self.mine, self.theirs, self.swapped = cut(mine), cut(theirs), cut(swapped)
        self.kept, self.landed, self.work = cut(kept), cut(landed), cut(work)
        self.sems = sems

    def swap(self):
        return remote(
            self.theirs, self.swapped, self.sems.at[0], self.sems.at[1], self.me.other
        )

    def keep(self):
        return pltpu.make_async_copy(self.mine, self.kept, self.sems.at[2])

    def send(self, src, s, upward, z):
        line = self.me.line
        if upward:
            slot, device = s, self.me.up
        else:
            slot, device = (s if s < z - 1 else line), self.me.down
        return remote(
            src, self.landed.at[slot], self.sems.at[3 + s], self.sems.at[3 + line + slot], device
        )

    def landing(self, slot):
        line = self.me.line
        return remote(
            self.landed.at[slot], self.landed.at[slot], self.sems.at[3],
            self.sems.at[3 + line + slot], self.me.other,
        )

    def load(self, src, n):
        return pltpu.make_async_copy(src, self.work.at[n], self.sems.at[4 + 2 * self.me.line + n])

    def reduce(self, free_sem):
        line = self.me.line
        self.swap().wait_recv()
        for s in range(line):
            add_into(self.mine.at[s], self.swapped.at[s], self.rows)
        pl.semaphore_signal(
            free_sem, inc=1, device_id=self.me.other, device_id_type=pl.DeviceIdType.MESH
        )
        self.keep().start()
        self.swap().wait_send()
        self.keep().wait()
        for end, upward in ((0, True), (line - 1, False)):

            @pl.when(self.me.z == end)
            def _(end=end, upward=upward):
                order = range(line - 1, end, -1) if upward else range(end)
                for s in order:
                    self.send(self.kept.at[s], s, upward, end).start()

    def going(self, p):
        line = self.me.line
        for z, upward in ((p, True), (line - 1 - p, False)):
            targets = list(range(line - 1, z, -1)) if upward else list(range(z))
            yield z, upward, targets

    def load_phase(self, p, first):
        for z, upward, targets in self.going(p):

            @pl.when(self.me.z == z)
            def _(targets=targets):
                for n, s in enumerate(targets):
                    self.landing(s).wait_recv()
                    self.load(self.landed.at[s], first + 2 * n).start()
                    self.load(self.kept.at[s], first + 2 * n + 1).start()

    def run_phase(self, p, first):
        for z, upward, targets in self.going(p):

            @pl.when(self.me.z == z)
            def _(z=z, upward=upward, targets=targets):
                for n, s in enumerate(targets):
                    a, b = first + 2 * n, first + 2 * n + 1
                    self.load(self.landed.at[s], a).wait()
                    self.load(self.kept.at[s], b).wait()
                    add_into(self.work.at[a], self.work.at[b], self.rows)
                    self.send(self.work.at[a], s, upward, z).start()

    def sent_phase(self, p, first):
        for z, upward, targets in self.going(p):

            @pl.when(self.me.z == z)
            def _(z=z, upward=upward, targets=targets):
                for n, s in enumerate(targets):
                    self.send(self.work.at[first + 2 * n], s, upward, z).wait_send()

    def load_last(self, first):
        me = self.me
        self.load(self.kept.at[me.z], first).start()

        @pl.when(me.z >= 1)
        def _():
            self.landing(me.z).wait_recv()
            self.load(self.landed.at[me.z], first + 1).start()

        @pl.when(me.z < me.line - 1)
        def _():
            self.landing(me.line).wait_recv()
            self.load(self.landed.at[me.line], first + 2).start()

    def run_last(self, first, total):
        me = self.me
        here = total.at[pl.ds(0, self.rows)]
        self.load(self.kept.at[me.z], first).wait()

        def put(n, step=64):
            @pl.loop(0, self.rows // step)
            def _(i):
                at = pl.ds(pl.multiple_of(i * step, step), step)
                if n == first:
                    here[at, :] = self.work[n, at, :].astype(F32)
                else:
                    here[at, :] += self.work[n, at, :].astype(F32)

        put(first)

        @pl.when(me.z >= 1)
        def _():
            self.load(self.landed.at[me.z], first + 1).wait()
            put(first + 1)

        @pl.when(me.z < me.line - 1)
        def _():
            self.load(self.landed.at[me.line], first + 2).wait()
            put(first + 2)

    def done(self):
        line = self.me.line
        for end, upward in ((0, True), (line - 1, False)):

            @pl.when(self.me.z == end)
            def _(end=end, upward=upward):
                for s in range(line - 1, end, -1) if upward else range(end):
                    self.send(self.kept.at[s], s, upward, end).wait_send()


class Ticks:
    def __init__(self, chunks, total, writers):
        self.chunks, self.total, self.writers = chunks, total, writers
        self.k = 0

    def jobs(self, k):
        count = len(self.chunks)
        out = []
        if 0 <= k < count:
            out.append((self.chunks[k], 1, 0))
        if 0 <= k - 1 < count:
            out.append((self.chunks[k - 1], 2, 4))
        return out

    def tick(self):
        k = self.k
        for chunk, p, first in self.jobs(k - 1):
            chunk.sent_phase(p, first)
        last = self.chunks[k - 2] if 0 <= k - 2 < len(self.chunks) else None
        for chunk, p, first in self.jobs(k):
            chunk.load_phase(p, first)
        if last is not None:
            last.load_last(6)
        for chunk, p, first in self.jobs(k):
            chunk.run_phase(p, first)
        if last is not None:
            if k - 2 > 0:
                self.writers[k - 3].wait()
            last.run_last(6, self.total)
            self.writers[k - 2].start()
        self.k += 1

    def rest(self):
        while self.k < len(self.chunks) + 2:
            self.tick()
        self.writers[-1].wait()
        for chunk in self.chunks:
            chunk.done()


class Writer:
    def __init__(self, total, turned, parts, sem):
        self.total, self.turned, self.parts, self.sem = total, turned, parts, sem

    def copies(self):
        for n, (dst, flip) in enumerate(self.parts):
            rows = dst.shape[0] if not flip else dst.shape[1]
            src = self.turned.at[n] if flip else self.total.at[pl.ds(n * 256, rows)]
            yield pltpu.make_async_copy(src, dst, self.sem.at[n])

    def start(self):
        for n, (_, flip) in enumerate(self.parts):
            if flip:
                self.turned[n] = self.total[pl.ds(n * 256, 256), :].T
        for copy in self.copies():
            copy.start()

    def wait(self):
        for copy in self.copies():
            copy.wait()


def norm_back_rows(count, gain, values_of, grads_of, gain_ref, row, put, step=32):
    @pl.loop(0, count // step)
    def _(n):
        at = pl.ds(pl.multiple_of(n * step, step), step)
        values, grads = values_of(at), grads_of(at)
        factor = norm_factor(values)
        scaled = grads * gain
        back = factor * scaled - values * factor * factor * factor * jnp.mean(
            scaled * values, axis=-1, keepdims=True
        )
        gain_ref[row : row + 1, :] += jnp.sum(grads * values * factor, axis=0, keepdims=True)
        put(at, back)


def backward_kernel(
    dp, x_ref, g_all, normed_all, mlp_all, middle_ref, gains_ref, wf_early, wf_late, qkv_full, out_full,
    q_all, k_all, v_all, mixed_all, lse_all, cos_all, sin_all, segc_all, segr_all,
    output_ref, input_grad_ref, gain_out_ref, gate_out, up_out, down_out, q_out, k_out, v_out, o_out,
    late_full, hidden_all, kept_all, landed_all, y_all,
    theirs, swapped, mine, work, total, turned, stage, landed, g2, own, gm, gp, gp_landed,
    sem_late, sem_line, sem_write, sem_s, sem_g2, sem_gain, sem_c, sem_w, free_core, free_x, free_y,
):
    me = Place(dp)
    me.greet(far=True)
    early, late = wf_early.shape[0], wf_late.shape[0]
    blocks = early + late
    line, half = me.line, mlp_all.shape[2] // 2
    local = x_ref.shape[0]
    shard = half // line
    rows = LEN // 4
    fw = wf_late.shape[2] // 3
    cols = q_all.shape[1]
    groups = cols // GROUP
    gathers = [LineGather(me, wf_late.at[b], late_full.at[b], sem_late.at[b]) for b in range(late)]
    acts = []
    for b in range(late):
        def first(b=b):
            gathers[b].hop(1)
            if b + 1 < late:
                gathers[b + 1].start()
        acts.append(first)
        for h in range(2, line):
            acts.append(functools.partial(gathers[b].hop, h))
    gathers[0].start()

    def poll(count=1):
        for _ in range(count):
            if acts:
                acts.pop(0)()

    sizes = [3 * fw] * blocks + [cols] + [3 * GROUP] * groups
    chunks = [
        LineScatter(me, size, mine, theirs, swapped, kept_all.at[n], landed_all.at[n], work, sem_line.at[n])
        for n, size in enumerate(sizes)
    ]
    writers = []
    for n in range(blocks):
        here = pl.ds(n * fw, fw)
        parts = [(gate_out.at[:, here], True), (up_out.at[:, here], True), (down_out.at[here], False)]
        writers.append(Writer(total, turned, parts, sem_write.at[n]))
    writers.append(Writer(total, turned, [(o_out, False)], sem_write.at[blocks]))
    for n in range(groups):
        here = pl.ds(n * GROUP, GROUP)
        parts = [(ref.at[:, here], True) for ref in (q_out, k_out, v_out)]
        writers.append(Writer(total, turned, parts, sem_write.at[blocks + 1 + n]))
    ticks = Ticks(chunks, total, writers)

    def swap(n):
        if n >= 1:
            pl.semaphore_wait(free_core, 1)
        chunks[n].swap().start()

    def gain_row(which):
        return jnp.concatenate(
            [
                gains_ref[side, pl.ds(s * 16 + which, 1), :].astype(F32)
                for side in range(2)
                for s in range(line)
            ],
            axis=1,
        )

    def products(left_of, right, first, size):
        @pl.loop(0, line)
        def _(s):
            for side, dst in ((0, mine), (1, theirs)):
                here = pl.ds(pl.multiple_of(side * half + s * shard, shard), shard)
                dst[s, pl.ds(first, size), :] = dot_nn(left_of[...], right[:, here]).astype(BF16)

    scatter = SquareScatter(me, stage, landed, sem_s)

    def mlp(xs, gs, wb, sums, dgu_t, hid_t, hid):
        loads = [
            pltpu.make_async_copy(mlp_all.at[b], xs.at[pl.ds(b * rows, rows)], sem_c.at[b])
            for b in range(4)
        ] + [
            pltpu.make_async_copy(g_all.at[b], gs.at[pl.ds(b * rows, rows)], sem_c.at[4 + b])
            for b in range(4)
        ]

        def weights(n):
            src = wf_early.at[n] if n < early else late_full.at[n - early]
            return [
                pltpu.make_async_copy(
                    src.at[side], wb.at[n % 2, pl.ds(side * half, half)], sem_w.at[n % 2, side]
                )
                for side in range(2)
            ]

        def hidden_copy(n):
            return pltpu.make_async_copy(
                hid.at[n % 2], hidden_all.at[n], sem_c.at[8 + n % 2]
            )

        for copy in loads + weights(0):
            copy.start()

        @pl.loop(0, LEN // 64)
        def _(i):
            at = pl.ds(pl.multiple_of(i * 64, 64), 64)
            sums[at, :] = jnp.zeros((64, 2 * half), F32)

        for copy in loads:
            copy.wait()
        for n in range(blocks):
            if n >= early:
                while len(acts) > (blocks - 1 - n) * (line - 1):
                    poll()
                gathers[n - early].arrived()
                for copy in weights(n):
                    copy.start()
            for copy in weights(n):
                copy.wait()
            if n + 1 < early:
                for copy in weights(n + 1):
                    copy.start()
            if n >= 2:
                hidden_copy(n - 2).wait()
            w = wb.at[n % 2]
            gu_w, down_w = w.at[:, pl.ds(0, 2 * fw)], w.at[:, pl.ds(2 * fw, fw)]

            @pl.loop(0, 4)
            def _(r, n=n, gu_w=gu_w, down_w=down_w):
                at = pl.ds(pl.multiple_of(r * rows, rows), rows)
                gu = dot_nn(xs[at, :], gu_w[...])
                grad_hidden = dot_nn(gs[at, :], down_w[...])
                gate_pre, upward = gu[:, :fw], gu[:, fw:]
                sig = jax.nn.sigmoid(gate_pre)
                activated = gate_pre * sig
                hidden = (activated * upward).astype(BF16)
                hid[n % 2, at, :] = hidden
                hid_t[:, at] = hidden.T
                grad_gate = grad_hidden * upward * sig * (1.0 + gate_pre * (1.0 - sig))
                grad_up = grad_hidden * activated
                dgu = jnp.concatenate([grad_gate, grad_up], axis=1).astype(BF16)
                dgu_t[:, at] = dgu.T

                @pl.loop(0, 4)
                def _(c):
                    here = pl.ds(pl.multiple_of(c * (half // 2), half // 2), half // 2)
                    sums[at, here] += dot_nt(dgu, gu_w[here, :])

            hidden_copy(n).start()
            if n >= 1:
                chunks[n - 1].reduce(free_core)
            products(dgu_t, xs, 0, 2 * fw)
            products(hid_t, gs, 2 * fw, fw)
            swap(n)
            if n < early:
                poll()
            if n in TICK_AFTER:
                ticks.tick()
        for n in range(max(0, blocks - 2), blocks):
            hidden_copy(n).wait()

        def to_stage(b, slot):
            @pl.loop(0, rows // 64)
            def _(i):
                at = pl.ds(pl.multiple_of(i * 64, 64), 64)
                there = pl.ds(pl.multiple_of(b * rows + i * 64, 64), 64)
                if slot is None:
                    own[at, :] = sums[there, :]
                else:
                    stage[slot, at, :] = sums[there, :].astype(BF16)

        to_stage(3, 2)
        scatter.diagonal_ready()
        to_stage(1, 0)
        to_stage(2, 1)
        scatter.sides_ready()
        to_stage(0, None)

    pl.run_scoped(
        mlp,
        pltpu.VMEM((LEN, 2 * half), BF16),
        pltpu.VMEM((LEN, 2 * half), BF16),
        pltpu.VMEM((2, 2 * half, 3 * fw), BF16),
        pltpu.VMEM((LEN, 2 * half), F32),
        pltpu.VMEM((2 * fw, LEN), BF16),
        pltpu.VMEM((fw, LEN), BF16),
        pltpu.VMEM((2, LEN, fw), BF16),
    )
    gain_one, gain_two = gain_row(0), gain_row(1)
    gp[...] = jnp.zeros(gp.shape, F32)
    square = SquareGather(me, g2, sem_g2)

    def free_landed():
        for device, sem in ((me.x, free_x), (me.y, free_y)):
            pl.semaphore_signal(
                sem, inc=1, device_id=device, device_id_type=pl.DeviceIdType.MESH
            )

    def wait_free():
        pl.semaphore_wait(free_x, 1)
        pl.semaphore_wait(free_y, 1)

    def summed(at):
        return own[at, :] + landed[0, at, :].astype(F32) + landed[1, at, :].astype(F32)

    def down(hidden, dw, rest):
        hid_in = [
            pltpu.make_async_copy(hidden_all.at[n], hidden.at[n], sem_c.at[n]) for n in range(blocks)
        ]
        dw_in = []
        for n in range(blocks):
            src = wf_early.at[n] if n < early else late_full.at[n - early]
            for side in range(2):
                dw_in.append(
                    pltpu.make_async_copy(
                        src.at[side, :, pl.ds(2 * fw, fw)], dw.at[n, pl.ds(side * half, half)],
                        sem_c.at[8 + 2 * n + side],
                    )
                )
        for copy in hid_in + dw_in:
            copy.start()
        chunks[blocks - 1].reduce(free_core)
        ticks.tick()
        for copy in hid_in + dw_in:
            copy.wait()

        @pl.loop(0, 4)
        def _(b):
            at = pl.ds(pl.multiple_of(b * rows, rows), rows)

            @pl.loop(0, 2 * half // GROUP)
            def _(c):
                here = pl.ds(pl.multiple_of(c * GROUP, GROUP), GROUP)
                value = sum(dot_nt(hidden[n, at, :], dw[n, here, :]) for n in range(blocks))
                rest[b, :, here] = value.astype(BF16)

        out = pltpu.make_async_copy(rest, y_all, sem_c.at[0])
        out.start()
        out.wait()

    pl.run_scoped(
        down,
        pltpu.VMEM((blocks, LEN, fw), BF16),
        pltpu.VMEM((blocks, 2 * half, fw), BF16),
        pltpu.VMEM((4, local, 2 * half), BF16),
    )
    scatter.combine()

    def attention(
        rows_grad, q_ref, k_ref, v_ref, mixed_t, mixed, lse_ref, cos_ref, sin_ref, segc_ref, segr_ref,
        normed, out_w, dm_ref, dqa_ref, dka_ref, dva_ref, part_t, bias_ref, middle, y_mine,
    ):
        ins = [
            (middle_ref, middle), (g_all.at[0], g2.at[0]), (mixed_all, mixed), (q_all, q_ref),
            (k_all, k_ref), (v_all, v_ref), (lse_all, lse_ref), (cos_all, cos_ref), (sin_all, sin_ref),
            (segc_all, segc_ref), (segr_all, segr_ref), (out_full, out_w), (y_all.at[0], y_mine),
        ] + [(normed_all.at[b], normed.at[pl.ds(b * rows, rows)]) for b in range(4)]
        loads = [pltpu.make_async_copy(a, b, sem_c.at[n]) for n, (a, b) in enumerate(ins)]
        for copy in loads:
            copy.start()
        ticks.tick()
        scatter.arrived()

        def second_norm_back(at, back):
            grad = g2[0, at, :].astype(F32) + back
            gm[at, :] = grad
            g2[0, at, :] = grad.astype(BF16)

        loads[0].wait()
        loads[1].wait()
        norm_back_rows(
            local, gain_two, lambda at: middle[at, :], summed, gp, 1, second_norm_back
        )
        square.start()
        free_landed()
        scatter.done()
        stage_in = [
            pltpu.make_async_copy(y_all.at[b], stage.at[slot], sem_w.at[0, n])
            for n, (b, slot) in enumerate(((3, 2), (1, 0)))
        ] + [pltpu.make_async_copy(y_all.at[2], stage.at[1], sem_w.at[1, 0])]
        for copy in stage_in:
            copy.start()
        for copy in loads[2:]:
            copy.wait()
        mixed_t[...] = mixed[...].T
        square.forward()
        ticks.tick()
        for copy in stage_in:
            copy.wait()
        wait_free()
        square.arrived()
        scatter.diagonal_ready()
        scatter.sides_ready()

        @pl.loop(0, 4)
        def _(b):
            at = pl.ds(pl.multiple_of(b * rows, rows), rows)
            dm_ref[at, :] = (
                dot_nn(g2[b, :, :half], out_w[0]) + dot_nn(g2[b, :, half:], out_w[1])
            ).astype(BF16)

        @pl.loop(0, line)
        def _(s):
            for side, dst in ((0, mine), (1, theirs)):
                here = pl.ds(pl.multiple_of(side * half + s * shard, shard), shard)
                value = sum(
                    dot_nn(mixed_t[:, pl.ds(b * rows, rows)], g2[b, :, here]) for b in range(4)
                )
                dst[s, pl.ds(0, cols), :] = value.astype(BF16)

        swap(blocks)
        head_lane = lax.broadcasted_iota(jnp.int32, (rows, 128), 1)
        for group in range(groups):

            @pl.loop(0, 4)
            def _(b):
                at = pl.ds(pl.multiple_of(b * rows, rows), rows)
                dka_ref[at, :] = jnp.zeros((rows, GROUP), F32)
                dva_ref[at, :] = jnp.zeros((rows, GROUP), F32)

            for i in range(4):
                places = [(j, me.spots[j]) for j in key_blocks(i, rows)]
                at = pl.ds(pl.multiple_of(me.spots[i] * rows, rows), rows)
                fill_bias(bias_ref, segc_ref[at, 0:1], segr_ref, i, places)
                spots = [pl.ds(pl.multiple_of(p * rows, rows), rows) for _, p in places]

                @pl.loop(0, GROUP // 128)
                def _(pair, at=at, spots=spots, group=group):
                    attend_back(
                        pair, group * (GROUP // 128), at, spots, head_lane, q_ref, k_ref, v_ref,
                        dm_ref, lse_ref, bias_ref, dqa_ref, dka_ref, dva_ref,
                    )

                if i == 1:
                    chunks[blocks + group].reduce(free_core)
                if i == 3 and group == 0:
                    scatter.combine()

            @pl.loop(0, 4)
            def _(b, group=group):
                at = pl.ds(pl.multiple_of(b * rows, rows), rows)
                cosine, sine = cos_ref[at, :], sin_ref[at, :]
                for part, ref in enumerate((dqa_ref, dka_ref, dva_ref)):
                    value = ref[at, :]
                    if part < 2:
                        value = value * cosine - swap_halves(value) * sine
                    value = value.astype(BF16)
                    rows_grad[at, pl.ds(part * cols + group * GROUP, GROUP)] = value
                    part_t[pl.ds(part * GROUP, GROUP), at] = value.T

            products(part_t, normed, 0, 3 * GROUP)
            swap(blocks + 1 + group)
            ticks.tick()
        scatter.arrived()

        def output_rows(at):
            total = middle[at, :] + y_mine[at, :].astype(F32)
            total = total + landed[0, at, :].astype(F32) + landed[1, at, :].astype(F32)
            output_ref[at, :] = total.astype(BF16)

        norm_rows(local, output_rows)
        free_landed()
        scatter.done()

    def normed_grads(rows_grad, qkv_w):
        load = pltpu.make_async_copy(qkv_full, qkv_w, sem_c.at[0])
        load.start()
        chunks[blocks + groups].reduce(free_core)
        load.wait()
        wait_free()

        def normed_grad(b, slot):
            at = pl.ds(b * rows, rows)

            @pl.loop(0, 2)
            def _(side):
                @pl.loop(0, half // GROUP)
                def _(n):
                    here = pl.ds(pl.multiple_of(n * GROUP, GROUP), GROUP)
                    there = pl.ds(pl.multiple_of(side * half + n * GROUP, GROUP), GROUP)
                    value = dot_nt(rows_grad[at, :], qkv_w[side, here, :])
                    if slot is None:
                        own[:, there] = value
                    else:
                        stage[slot, :, there] = value.astype(BF16)

        normed_grad(3, 2)
        scatter.diagonal_ready()
        normed_grad(1, 0)
        normed_grad(2, 1)
        scatter.sides_ready()
        normed_grad(0, None)

    vmem = pltpu.VMEM
    slab = vmem((LEN, cols), BF16)
    table = vmem((LEN, GROUP), F32)

    def heads(rows_grad):
        pl.run_scoped(
            functools.partial(attention, rows_grad),
            slab, slab, slab, vmem((cols, LEN), BF16), slab, vmem((LEN, 128), F32), table, table,
            vmem(segc_all.shape, jnp.int32), vmem(segr_all.shape, jnp.int32),
            vmem((LEN, 2 * half), BF16), vmem(out_full.shape, BF16), slab, table, table, table,
            vmem((3 * GROUP, LEN), BF16), vmem((3, rows, rows), F32), vmem((local, 2 * half), F32),
            vmem((local, 2 * half), BF16),
        )
        pl.run_scoped(functools.partial(normed_grads, rows_grad), vmem(qkv_full.shape, BF16))

    pl.run_scoped(heads, vmem((LEN, 3 * cols), BF16))
    ticks.tick()
    scatter.combine()
    ticks.tick()
    scatter.arrived()

    def first_norm_back(at, back):
        input_grad_ref[at, :] = gm[at, :] + back

    norm_back_rows(
        local, gain_one, lambda at: x_ref[at, :].astype(F32), summed, gp, 0, first_norm_back
    )
    scatter.done()
    for n, device in enumerate((me.x, me.y, me.other, me.next, me.far)):
        copy = remote(gp, gp_landed.at[n], sem_gain.at[n, 0], sem_gain.at[n, 1], device)
        copy.start()
        copy.wait()
        if device is me.other:
            gp[:, :half] += gp_landed[n, :, half:]
            gp[:, half:] += gp_landed[n, :, :half]
        else:
            gp[...] += gp_landed[n]
    gain_out_ref[...] = gp[...]
    ticks.rest()
    pl.semaphore_wait(free_core, 1)
    square.done()
    for one in gathers:
        one.done()


def backward(dp, x, g_all, normed_all, mlp_all, middle, gains, wf_early, wf_late, qkv, out, q, k, v, mixed, lse, cosine, sine, segc, segr):
    line = dp // 2
    local, d = x.shape
    cols = q.shape[1]
    early, late = wf_early.shape[0], wf_late.shape[0]
    fcols = wf_late.shape[2]
    fw = fcols // 3
    blocks = early + late
    groups = cols // GROUP
    count = blocks + 1 + groups
    shard = d // dp
    ff = blocks * fw
    most = max(fcols, cols, 3 * GROUP)
    vm, hbm = pl.BlockSpec(memory_space=pltpu.VMEM), pl.BlockSpec(memory_space=pl.ANY)
    S, vmem, dma = jax.ShapeDtypeStruct, pltpu.VMEM, pltpu.SemaphoreType.DMA
    regular = pltpu.SemaphoreType.REGULAR
    return pl.pallas_call(
        functools.partial(backward_kernel, dp),
        in_specs=[vm, hbm, hbm, hbm, hbm, vm] + [hbm] * 13,
        out_specs=[vm, vm, vm] + [hbm] * 12,
        out_shape=[
            S((local, d), BF16), S((local, d), F32), S((8, d), F32),
            S((shard, ff), F32), S((shard, ff), F32), S((ff, shard), F32),
            S((shard, cols), F32), S((shard, cols), F32), S((shard, cols), F32), S((cols, shard), F32),
            S((late, 2, d // 2, fcols), BF16), S((blocks, LEN, fw), BF16),
            S((count, line, most, shard), BF16), S((count, line + 1, most, shard), BF16),
            S((4, local, d), BF16),
        ],
        scratch_shapes=[
            vmem((line, most, shard), BF16), vmem((line, most, shard), BF16),
            vmem((line, most, shard), BF16), vmem((9, most, shard), BF16),
            vmem((most, shard), F32), vmem((3, shard, 256), F32),
            vmem((3, local, d), BF16), vmem((3, local, d), BF16), vmem((4, local, d), BF16),
            vmem((local, d), F32), vmem((local, d), F32), vmem((8, d), F32), vmem((5, 8, d), F32),
            dma((late, 6, line)), dma((count, 4 + 2 * line + 9)), dma((count, 3)), dma((12,)),
            dma((8,)), dma((5, 2)), dma((8 + 2 * blocks,)), dma((2, 2)), regular, regular, regular,
        ],
        compiler_params=pltpu.CompilerParams(
            vmem_limit_bytes=VMEM_BYTES, collective_id=1, has_side_effects=True
        ),
        name="backward",
    )(x, g_all, normed_all, mlp_all, middle, gains, wf_early, wf_late, qkv, out, q, k, v, mixed, lse, cosine, sine, segc, segr)


def attend_back(
    pair, first, at, spots, head_lane, q_ref, k_ref, v_ref, dm_ref, lse_ref, bias_ref, dqa_ref, dka_ref, dva_ref
):
    scale = HEAD_DIM**-0.5
    rows = at.size
    lanes = pl.ds(pl.multiple_of((first + pair) * 128, 128), 128)
    there = pl.ds(pl.multiple_of(pair * 128, 128), 128)
    query, grad = q_ref[at, lanes], dm_ref[at, lanes]
    logs = lse_ref[at, :]
    outs = []
    for h in range(2):
        mine = (head_lane < HEAD_DIM) if h == 0 else (head_lane >= HEAD_DIM)
        qm = jnp.where(mine, query, 0) * jnp.asarray(scale, BF16)
        gm = jnp.where(mine, grad, 0)
        log = jnp.sum(
            jnp.where(head_lane == (first + pair) * 2 + h, logs, 0.0), axis=1, keepdims=True
        )
        weights = [
            jnp.exp(dot_nt(qm, k_ref[s, lanes]) + bias_ref[n] - log) for n, s in enumerate(spots)
        ]
        grads = [dot_nt(gm, v_ref[s, lanes]) for s in spots]
        inner = sum(jnp.sum(w * g, axis=1, keepdims=True) for w, g in zip(weights, grads))
        dq = jnp.zeros((rows, 128), F32)
        for w, g, s in zip(weights, grads, spots):
            ds = (w * (g - inner)).astype(BF16)
            dva_ref[s, there] += dot_tn(w.astype(BF16), gm)
            dka_ref[s, there] += dot_tn(ds, qm)
            dq = dq + dot_nn(ds, k_ref[s, lanes])
        outs.append(dq)
    dqa_ref[at, there] = jnp.where(head_lane < HEAD_DIM, outs[0], outs[1]) * scale


def on_device(
    dp, tensor, hidden_in, doc_lengths, gain_attn, w_query, w_key, w_value, w_out, gain_mlp,
    w_gate, w_up, w_down, cotangent,
):
    line = dp // 2
    core = lax.axis_index("dp") % 2
    place = lax.axis_index("tensor")
    square = tensor == 4 and dp == 8
    same_core = [[c + 2 * z for z in range(line)] for c in range(2)]
    sibling = [(i, i ^ 1) for i in range(dp)]
    d = hidden_in.shape[1]
    local = hidden_in.shape[0]

    def own_first(a):
        s = a.reshape(a.shape[:-1] + (line, 2, d // dp))
        even, odd = s[..., 0, :], s[..., 1, :]
        out = jnp.concatenate(
            [jnp.where(core == 0, even, odd), jnp.where(core == 0, odd, even)], axis=-2
        )
        return out.reshape(a.shape)

    def true_order(a):
        s = a.reshape(a.shape[:-1] + (2, line, d // dp))
        first, second = s[..., 0, :, :], s[..., 1, :, :]
        out = jnp.stack(
            [jnp.where(core == 0, first, second), jnp.where(core == 0, second, first)], axis=-2
        )
        return out.reshape(a.shape)

    def hop(a, step):
        return lax.ppermute(a, "tensor", [(i, i ^ step) for i in range(tensor)])

    def gather_rows(a):
        if not square:
            return lax.all_gather(a, "tensor", axis=0, tiled=True)
        half = a.shape[0] // 2
        from_x, from_y = hop(a, 1), hop(a, 2)
        top, bottom = hop(from_x[:half], 2), hop(from_y[half:], 1)
        return jnp.concatenate([a, from_x, from_y, top, bottom], axis=0)

    def scatter_rows(a):
        if not square:
            return lax.psum_scatter(a, "tensor", scatter_dimension=0, tiled=True).astype(F32)
        n = a.shape[0] // 4
        half = n // 2
        top = hop(a[3 * n : 3 * n + half], 2)
        bottom = hop(a[3 * n + half :], 1)
        for_x = jnp.concatenate([a[n : n + half] + top, a[n + half : 2 * n]], axis=0)
        for_y = jnp.concatenate([a[2 * n : 2 * n + half], a[2 * n + half : 3 * n] + bottom], axis=0)
        return (a[:n].astype(F32) + hop(for_x, 1).astype(F32)) + hop(for_y, 2).astype(F32)

    def line_gather(a):
        own = lax.all_gather(a, "dp", axis=0, axis_index_groups=same_core, tiled=True)
        return own, lax.ppermute(own, "dp", sibling)

    def line_scatter(own, sib):
        mine = own + lax.ppermute(sib, "dp", sibling)
        return lax.psum_scatter(
            mine, "dp", scatter_dimension=0, axis_index_groups=same_core, tiled=True
        ).astype(F32)

    blocks = 4
    rows = LEN // blocks
    key = place if square else jnp.zeros((), jnp.int32)
    tokens = (
        (jnp.arange(blocks, dtype=jnp.int32) ^ key)[:, None] * rows
        + jnp.arange(rows, dtype=jnp.int32)[None, :]
    ).reshape(LEN)
    segment, position = doc_tables(doc_lengths, tokens)
    cosine, sine = rotary_tables(position)
    segc = jnp.broadcast_to(segment[:, None], (LEN, 128))
    segr = jnp.broadcast_to(segment.reshape(blocks, 1, rows), (blocks, 8, rows))
    key = key.reshape(1)

    ff = w_gate.shape[1]
    fb = ff // FF_BLOCKS
    down_t = w_down.T
    shards = [
        jnp.concatenate([w[:, b * fb : (b + 1) * fb] for w in (w_gate, w_up, down_t)], axis=1)
        for b in range(FF_BLOCKS)
    ]
    qkv_shard = jnp.concatenate([w_query, w_key, w_value], axis=1)
    cols = w_query.shape[1]
    hidden_mine = own_first(hidden_in)
    g_local = own_first(cotangent)
    inputs = hidden_mine.astype(F32)
    factor_one = norm_factor(inputs)
    if square:
        gain_rows = jnp.pad(jnp.stack([gain_attn, gain_mlp]), ((0, 14), (0, 0)))
        (
            normed, g_all, normed_mlp, query, keys, values, mixed, lse, middle, qkv_full,
            out_full, ff_full, gains,
        ) = forward(
            dp, hidden_mine, qkv_shard, w_out.T, jnp.stack(shards[:FF_EARLY]), g_local, gain_rows,
            cosine, sine, segc, segr,
        )
        (
            output, input_grad, gain_sum, grad_gate, grad_up, grad_down, grad_query, grad_key,
            grad_value, grad_out, *_,
        ) = backward(
            dp, hidden_mine, g_all, normed, normed_mlp, middle, gains, ff_full,
            jnp.stack(shards[FF_EARLY:]), qkv_full, out_full, query, keys, values, mixed, lse,
            cosine, sine, segc, segr,
        )
        share = d // (dp * tensor)
        first = (lax.axis_index("dp") // 2) * (d // dp) + place * share
        gain_sum = lax.dynamic_slice_in_dim(gain_sum, first, share, 1)
        return (
            true_order(output), true_order(input_grad), gain_sum[0], grad_query, grad_key,
            grad_value, grad_out, gain_sum[1], grad_gate, grad_up, grad_down,
        )
    gains = lax.all_gather(jnp.stack([gain_attn, gain_mlp]), "dp", axis=0)
    gains = own_first(jnp.moveaxis(gains, 0, 1).reshape(2, d)).astype(F32)
    gain_one, gain_two = gains[0], gains[1]
    qkv_own, qkv_sib = line_gather(qkv_shard)
    out_own, out_sib = line_gather(w_out.T)
    normed = gather_rows((inputs * factor_one * gain_one).astype(BF16))
    g_all = gather_rows(g_local)
    query, keys, values, mixed, lse = attn_forward(
        blocks, key, normed, qkv_own, qkv_sib, cosine, sine, segc, segr
    )
    attended = jnp.concatenate(
        [dot_nt(mixed, out_own).astype(BF16), dot_nt(mixed, out_sib).astype(BF16)], axis=1
    )
    middle = inputs + scatter_rows(attended)
    factor_two = norm_factor(middle)
    normed_mlp = gather_rows((middle * factor_two * gain_two).astype(BF16))
    ff_sets = [jnp.concatenate(line_gather(shard), axis=0) for shard in shards]

    down_sum = jnp.zeros((LEN, d), F32)
    back_sum = jnp.zeros((LEN, d), F32)
    ff_grads = []
    for b in range(FF_BLOCKS):
        gate_w, up_w, down_w = jnp.split(ff_sets[b], 3, axis=1)
        gate_pre = dot_nn(normed_mlp, gate_w)
        upward = dot_nn(normed_mlp, up_w)
        grad_hidden = dot_nn(g_all, down_w)
        sig = jax.nn.sigmoid(gate_pre)
        activated = gate_pre * sig
        hidden = (activated * upward).astype(BF16)
        grad_gate_pre = (grad_hidden * upward * sig * (1.0 + gate_pre * (1.0 - sig))).astype(BF16)
        grad_upward = (grad_hidden * activated).astype(BF16)
        down_sum = down_sum + dot_nt(hidden, down_w)
        back_sum = back_sum + dot_nt(grad_gate_pre, gate_w) + dot_nt(grad_upward, up_w)
        grad = jnp.concatenate(
            [
                dot_tn(normed_mlp, grad_gate_pre).astype(BF16),
                dot_tn(normed_mlp, grad_upward).astype(BF16),
                dot_tn(g_all, hidden).astype(BF16),
            ],
            axis=1,
        )
        ff_grads.append(line_scatter(grad[: d // 2], grad[d // 2 :]))
    grad_norm_two = scatter_rows(back_sum.astype(BF16))
    output = true_order((middle + scatter_rows(down_sum.astype(BF16))).astype(BF16))
    grad_mid_norm, gain_two_part = norm_back(middle, factor_two, gain_two, grad_norm_two)
    grad_middle = g_local.astype(F32) + grad_mid_norm
    grad_mid_all = gather_rows(grad_middle.astype(BF16))

    dq, dk, dv = attn_backward(
        blocks, key, grad_mid_all, out_own, out_sib, query, keys, values, lse, cosine, sine,
        segc, segr,
    )
    grad = jnp.concatenate(
        [dot_tn(normed, dq), dot_tn(normed, dk), dot_tn(normed, dv), dot_tn(grad_mid_all, mixed)],
        axis=1,
    ).astype(BF16)
    attn_grads = line_scatter(grad[: d // 2], grad[d // 2 :])
    rows_grad = jnp.concatenate([dq, dk, dv], axis=1)
    back = jnp.concatenate(
        [
            dot_nt(rows_grad, qkv_own).astype(BF16),
            dot_nt(rows_grad, qkv_sib).astype(BF16),
        ],
        axis=1,
    )
    grad_in_norm, gain_one_part = norm_back(inputs, factor_one, gain_one, scatter_rows(back))
    input_grad = true_order(grad_middle + grad_in_norm)

    parts = true_order(jnp.stack([gain_one_part, gain_two_part])).reshape(2 * d)
    shares = lax.all_gather(parts, ("dp", "tensor"), axis=0)
    gain_sum = jnp.sum(shares, axis=0).reshape(2, d)
    share = d // (dp * tensor)
    first = (lax.axis_index("dp") * tensor + place) * share
    gain_sum = lax.dynamic_slice_in_dim(gain_sum, first, share, 1)

    return (
        output,
        input_grad,
        gain_sum[0],
        attn_grads[:, :cols],
        attn_grads[:, cols : 2 * cols],
        attn_grads[:, 2 * cols : 3 * cols],
        attn_grads[:, 3 * cols :].T,
        gain_sum[1],
        jnp.concatenate([g[:, :fb] for g in ff_grads], axis=1),
        jnp.concatenate([g[:, fb : 2 * fb] for g in ff_grads], axis=1),
        jnp.concatenate([g[:, 2 * fb :] for g in ff_grads], axis=1).T,
    )


def solution(mesh):
    shape = dict(mesh.shape)
    return jax.shard_map(
        functools.partial(on_device, shape["dp"], shape["tensor"]),
        mesh=mesh,
        in_specs=(
            P(("dp", "tensor"), None),
            P("dp", None),
            P("dp"),
            P("dp", "tensor"),
            P("dp", "tensor"),
            P("dp", "tensor"),
            P("tensor", "dp"),
            P("dp"),
            P("dp", "tensor"),
            P("dp", "tensor"),
            P("tensor", "dp"),
            P(("dp", "tensor"), None),
        ),
        out_specs=(
            P(("dp", "tensor"), None),
            P(("dp", "tensor"), None),
            P(("dp", "tensor")),
            P("dp", "tensor"),
            P("dp", "tensor"),
            P("dp", "tensor"),
            P("tensor", "dp"),
            P(("dp", "tensor")),
            P("dp", "tensor"),
            P("dp", "tensor"),
            P("tensor", "dp"),
        ),
        check_vma=False,
    )
```

```python
import functools

import jax
import jax.numpy as jnp
from jax import lax
from jax.experimental import pallas as pl
from jax.experimental.pallas import tpu as pltpu
from jax.sharding import PartitionSpec as P

HEAD_DIM = 64
LEN = 1024
MOST = 512
EPSILON = 1e-05
ROPE_BASE = 130000.0
NEG = -1e30
GROUP = 256
FF_BLOCKS = 8
F32 = jnp.float32
BF16 = jnp.bfloat16
VMEM_BYTES = 60 * 1024 * 1024


def dot_nn(a, b):
    return jnp.dot(a, b, preferred_element_type=F32)


def dot_tn(a, b):
    return lax.dot_general(a, b, (((0,), (0,)), ((), ())), preferred_element_type=F32)


def dot_nt(a, b):
    return lax.dot_general(a, b, (((1,), (1,)), ((), ())), preferred_element_type=F32)


def norm_factor(values):
    return lax.rsqrt(jnp.mean(values * values, axis=-1, keepdims=True) + EPSILON)


def norm_back(values, factor, gain, grads):
    scaled = grads * gain
    grad_in = factor * scaled - values * factor * factor * factor * jnp.mean(
        scaled * values, axis=-1, keepdims=True
    )
    return grad_in, jnp.sum(grads * values * factor, axis=0)


def doc_tables(doc_lengths, tokens):
    ends = jnp.cumsum(doc_lengths, axis=1)[0]
    passed = tokens[:, None] >= ends[None, :]
    segment = jnp.sum(passed.astype(jnp.int32), axis=1)
    start = jnp.sum(jnp.where(passed, doc_lengths, 0), axis=1)
    return segment, tokens - start


def rotary_tables(position):
    half = HEAD_DIM // 2
    inverse = jnp.power(ROPE_BASE, -jnp.arange(half, dtype=F32) * 2.0 / HEAD_DIM)
    angles = position.astype(F32)[:, None] * inverse
    cosine, sine = jnp.cos(angles), jnp.sin(angles)
    heads = 128 // HEAD_DIM
    return (
        jnp.tile(jnp.concatenate([cosine, cosine], axis=1), (1, heads)),
        jnp.tile(jnp.concatenate([-sine, sine], axis=1), (1, heads)),
    )


def swap_halves(v):
    half, width = HEAD_DIM // 2, v.shape[1]
    lane = lax.broadcasted_iota(jnp.int32, v.shape, 1)
    ahead = pltpu.roll(v, width - half, 1)
    behind = pltpu.roll(v, half, 1)
    return jnp.where(lane % HEAD_DIM < half, ahead, behind)


def key_blocks(i, rows):
    reach = -(-(MOST - 1) // rows)
    return list(range(max(0, i - reach), i + 1))


def fill_bias(bias_ref, seg_col, seg_ref, i, places):
    rows = seg_col.shape[0]
    for n, (j, place) in enumerate(places):
        same = seg_col == seg_ref[place][0:1, :]
        if j == i:
            row = lax.broadcasted_iota(jnp.int32, (rows, rows), 0)
            col = lax.broadcasted_iota(jnp.int32, (rows, rows), 1)
            same = same & (col <= row)
        bias_ref[n] = jnp.where(same, 0.0, NEG)


def attn_forward_kernel(
    blocks, key_ref, x_ref, qo, qs, ko, ks, vo, vs, cos_ref, sin_ref, segc_ref, segr_ref,
    q_ref, k_ref, v_ref, mixed_ref, lse_ref, bias_ref,
):
    rows = LEN // blocks
    half = x_ref.shape[1] // 2
    key = key_ref[0]

    @pl.loop(0, blocks)
    def _(b):
        at = pl.ds(pl.multiple_of(b * rows, rows), rows)
        left, right = x_ref[at, :half], x_ref[at, half:]
        cosine, sine = cos_ref[at, :], sin_ref[at, :]
        query = dot_nn(left, qo[...]) + dot_nn(right, qs[...])
        q_ref[at, :] = (query * cosine + swap_halves(query) * sine).astype(BF16)
        keys = dot_nn(left, ko[...]) + dot_nn(right, ks[...])
        k_ref[at, :] = (keys * cosine + swap_halves(keys) * sine).astype(BF16)
        v_ref[at, :] = (dot_nn(left, vo[...]) + dot_nn(right, vs[...])).astype(BF16)

    head_lane = lax.broadcasted_iota(jnp.int32, (rows, 128), 1)
    for i in range(blocks):
        places = [(j, j ^ key) for j in key_blocks(i, rows)]
        at = pl.ds(pl.multiple_of((i ^ key) * rows, rows), rows)
        fill_bias(bias_ref, segc_ref[at, 0:1], segr_ref, i, places)
        spots = [pl.ds(pl.multiple_of(p * rows, rows), rows) for _, p in places]

        @pl.loop(0, GROUP // 128)
        def _(pair, at=at, spots=spots):
            first = pl.program_id(0) * (GROUP // HEAD_DIM)
            attend(pair, first, at, spots, head_lane, q_ref, k_ref, v_ref, mixed_ref, lse_ref, bias_ref)


def attn_forward(blocks, key, x, own, sib, cosine, sine, segc, segr):
    d = x.shape[1]
    cols = own.shape[1] // 3
    steps = cols // GROUP
    rows = LEN // blocks

    def weight(part):
        return pl.BlockSpec((d // 2, GROUP), lambda i, part=part: (0, part * steps + i))

    def whole(shape):
        return pl.BlockSpec(shape, lambda i: (0,) * len(shape))

    col_block = pl.BlockSpec((LEN, GROUP), lambda i: (0, i))
    slab = jax.ShapeDtypeStruct((LEN, cols), BF16)
    return pl.pallas_call(
        functools.partial(attn_forward_kernel, blocks),
        grid=(steps,),
        in_specs=[pl.BlockSpec(memory_space=pltpu.SMEM), whole((LEN, d))]
        + [weight(p) for p in (0, 0, 1, 1, 2, 2)]
        + [whole((LEN, GROUP))] * 2
        + [whole((LEN, 128)), whole(segr.shape)],
        out_specs=[col_block] * 4 + [whole((LEN, 128))],
        out_shape=[slab] * 4 + [jax.ShapeDtypeStruct((LEN, 128), F32)],
        scratch_shapes=[pltpu.VMEM((blocks, rows, rows), F32)],
        compiler_params=pltpu.CompilerParams(vmem_limit_bytes=VMEM_BYTES),
        name="attn_forward",
    )(key, x, own, sib, own, sib, own, sib, cosine, sine, segc, segr)


def attn_backward_kernel(
    blocks, key_ref, g_ref, wo, ws, q_ref, k_ref, v_ref, lse_ref, cos_ref, sin_ref, segc_ref,
    segr_ref, dq_ref, dk_ref, dv_ref, dm_ref, dqa_ref, dka_ref, dva_ref, bias_ref,
):
    rows = LEN // blocks
    half = g_ref.shape[1] // 2
    key = key_ref[0]

    @pl.loop(0, blocks)
    def _(b):
        at = pl.ds(pl.multiple_of(b * rows, rows), rows)
        dm_ref[at, :] = (dot_nn(g_ref[at, :half], wo[...]) + dot_nn(g_ref[at, half:], ws[...])).astype(BF16)
        dka_ref[at, :] = jnp.zeros((rows, GROUP), F32)
        dva_ref[at, :] = jnp.zeros((rows, GROUP), F32)

    head_lane = lax.broadcasted_iota(jnp.int32, (rows, 128), 1)
    scale = HEAD_DIM**-0.5
    for i in range(blocks):
        places = [(j, j ^ key) for j in key_blocks(i, rows)]
        at = pl.ds(pl.multiple_of((i ^ key) * rows, rows), rows)
        fill_bias(bias_ref, segc_ref[at, 0:1], segr_ref, i, places)
        spots = [pl.ds(pl.multiple_of(p * rows, rows), rows) for _, p in places]

        @pl.loop(0, GROUP // 128)
        def _(pair, at=at, spots=spots):
            lanes = pl.ds(pl.multiple_of(pair * 128, 128), 128)
            first = pl.program_id(0) * (GROUP // HEAD_DIM)
            query, grad = q_ref[at, lanes], dm_ref[at, lanes]
            logs = lse_ref[at, :]
            outs = []
            for h in range(2):
                mine = (head_lane < HEAD_DIM) if h == 0 else (head_lane >= HEAD_DIM)
                qm = jnp.where(mine, query, 0) * jnp.asarray(scale, BF16)
                gm = jnp.where(mine, grad, 0)
                log = jnp.sum(
                    jnp.where(head_lane == first + pair * 2 + h, logs, 0.0), axis=1, keepdims=True
                )
                weights = [
                    jnp.exp(dot_nt(qm, k_ref[s, lanes]) + bias_ref[n] - log)
                    for n, s in enumerate(spots)
                ]
                grads = [dot_nt(gm, v_ref[s, lanes]) for s in spots]
                inner = sum(
                    jnp.sum(w * g, axis=1, keepdims=True) for w, g in zip(weights, grads)
                )
                dq = jnp.zeros((rows, 128), F32)
                for w, g, s in zip(weights, grads, spots):
                    ds = (w * (g - inner)).astype(BF16)
                    dva_ref[s, lanes] += dot_tn(w.astype(BF16), gm)
                    dka_ref[s, lanes] += dot_tn(ds, qm)
                    dq = dq + dot_nn(ds, k_ref[s, lanes])
                outs.append(dq)
            dqa_ref[at, lanes] = jnp.where(head_lane < HEAD_DIM, outs[0], outs[1]) * scale

    @pl.loop(0, blocks)
    def _(b):
        at = pl.ds(pl.multiple_of(b * rows, rows), rows)
        cosine, sine = cos_ref[at, :], sin_ref[at, :]
        dq = dqa_ref[at, :]
        dq_ref[at, :] = (dq * cosine - swap_halves(dq) * sine).astype(BF16)
        dk = dka_ref[at, :]
        dk_ref[at, :] = (dk * cosine - swap_halves(dk) * sine).astype(BF16)
        dv_ref[at, :] = dva_ref[at, :].astype(BF16)


def attn_backward(blocks, key, g, own, sib, q, k, v, lse, cosine, sine, segc, segr):
    d = g.shape[1]
    cols = q.shape[1]
    steps = cols // GROUP
    rows = LEN // blocks

    def whole(shape):
        return pl.BlockSpec(shape, lambda i: (0,) * len(shape))

    col_block = pl.BlockSpec((LEN, GROUP), lambda i: (0, i))
    weight = pl.BlockSpec((d // 2, GROUP), lambda i: (0, i))
    slab = jax.ShapeDtypeStruct((LEN, cols), BF16)
    return pl.pallas_call(
        functools.partial(attn_backward_kernel, blocks),
        grid=(steps,),
        in_specs=[pl.BlockSpec(memory_space=pltpu.SMEM), whole((LEN, d)), weight, weight]
        + [col_block] * 3
        + [whole((LEN, 128))]
        + [whole((LEN, GROUP))] * 2
        + [whole((LEN, 128)), whole(segr.shape)],
        out_specs=[col_block] * 3,
        out_shape=[slab] * 3,
        scratch_shapes=[
            pltpu.VMEM((LEN, GROUP), BF16),
            pltpu.VMEM((LEN, GROUP), F32),
            pltpu.VMEM((LEN, GROUP), F32),
            pltpu.VMEM((LEN, GROUP), F32),
            pltpu.VMEM((blocks, rows, rows), F32),
        ],
        compiler_params=pltpu.CompilerParams(vmem_limit_bytes=VMEM_BYTES),
        name="attn_backward",
    )(key, g, own, sib, q, k, v, lse, cosine, sine, segc, segr)


class LineGather:
    def __init__(self, me, src, full, sems):
        self.me, self.src, self.full, self.sems = me, src, full, sems
        self.rows = src.shape[0]

    def spot(self, side, s):
        return self.full.at[side, pl.ds(pl.multiple_of(s * self.rows, self.rows), self.rows)]

    def to_line(self, src, s, way):
        device = self.me.up if way == 0 else self.me.down
        return remote(src, self.spot(0, s), self.sems.at[way, s], self.sems.at[3, s], device)

    def to_core(self, src, s):
        return remote(src, self.spot(1, s), self.sems.at[2, s], self.sems.at[4, s], self.me.other)

    def keep(self):
        return pltpu.make_async_copy(self.src, self.spot(0, self.me.z), self.sems.at[5, 0])

    def start(self):
        z, line = self.me.z, self.me.line

        @pl.when(z + 1 < line)
        def _():
            self.to_line(self.src, z, 0).start()

        @pl.when(z >= 1)
        def _():
            self.to_line(self.src, z, 1).start()

        self.to_core(self.src, z).start()
        self.keep().start()

    def hop(self, h):
        z, line = self.me.z, self.me.line
        for s, arrives, goes_on, way in (
            (z - h, z >= h, z + 1 < line, 0),
            (z + h, z + h < line, z >= 1, 1),
        ):

            @pl.when(arrives)
            def _(s=s, goes_on=goes_on, way=way):
                here = self.spot(0, s)
                self.to_line(here, s, way).wait_recv()

                @pl.when(goes_on)
                def _():
                    self.to_line(here, s, way).start()

                self.to_core(here, s).start()

    def arrived(self):
        self.keep().wait()
        for s in range(self.me.line):
            self.to_core(self.spot(0, s), s).wait_recv()

    def done(self):
        z, line = self.me.z, self.me.line
        for s in range(line):
            here = self.spot(0, s)
            self.to_core(here, s).wait_send()

            @pl.when((s <= z) & (z + 1 < line))
            def _(s=s, here=here):
                self.to_line(here, s, 0).wait_send()

            @pl.when((s >= z) & (z >= 1))
            def _(s=s, here=here):
                self.to_line(here, s, 1).wait_send()


class SquareGather:
    def __init__(self, me, full, sems):
        self.me, self.full, self.sems = me, full, sems
        self.rows = full.shape[0] // 4

    def copies(self):
        me, full, sems, rows = self.me, self.full, self.sems, self.rows
        half = rows // 2

        def part(first, size):
            return full.at[pl.ds(first, size)]

        return (
            remote(part(0, rows), part(rows, rows), sems.at[0], sems.at[1], me.x),
            remote(part(0, rows), part(2 * rows, rows), sems.at[2], sems.at[3], me.y),
            remote(part(rows, half), part(3 * rows, half), sems.at[4], sems.at[5], me.y),
            remote(
                part(2 * rows + half, half), part(3 * rows + half, half), sems.at[6], sems.at[7], me.x
            ),
        )

    def start(self):
        x, y, _, _ = self.copies()
        x.start()
        y.start()

    def forward(self):
        x, y, top, bottom = self.copies()
        x.wait_recv()
        top.start()
        y.wait_recv()
        bottom.start()

    def arrived(self):
        _, _, top, bottom = self.copies()
        top.wait_recv()
        bottom.wait_recv()

    def done(self):
        for copy in self.copies():
            copy.wait_send()


class SquareScatter:
    def __init__(self, me, stage, landed, sems):
        self.me, self.stage, self.landed, self.sems = me, stage, landed, sems
        self.half = stage.shape[1] // 2
        self.top, self.bottom = pl.ds(0, self.half), pl.ds(self.half, self.half)

    def copies(self):
        me, stage, landed, sems = self.me, self.stage, self.landed, self.sems
        top, bottom = self.top, self.bottom
        return (
            remote(stage.at[2, top], landed.at[2, top], sems.at[0], sems.at[1], me.y),
            remote(stage.at[2, bottom], landed.at[2, bottom], sems.at[2], sems.at[3], me.x),
            remote(stage.at[0, bottom], landed.at[0, bottom], sems.at[4], sems.at[5], me.x),
            remote(stage.at[1, top], landed.at[1, top], sems.at[6], sems.at[7], me.y),
            remote(stage.at[0, top], landed.at[0, top], sems.at[8], sems.at[9], me.x),
            remote(stage.at[1, bottom], landed.at[1, bottom], sems.at[10], sems.at[11], me.y),
        )

    def diagonal_ready(self):
        copies = self.copies()
        copies[0].start()
        copies[1].start()

    def sides_ready(self):
        copies = self.copies()
        copies[2].start()
        copies[3].start()

    def combine(self):
        copies = self.copies()
        for n, slot, at in ((0, 0, self.top), (1, 1, self.bottom)):
            copies[n].wait_recv()
            add_rows(self.stage, slot, at, self.landed)
            copies[4 + n].start()

    def arrived(self):
        for copy in self.copies()[2:]:
            copy.wait_recv()

    def done(self):
        for copy in self.copies():
            copy.wait_send()


def add_rows(stage, slot, at, landed):
    step = 32

    @pl.loop(0, at.size // step)
    def _(n):
        here = pl.ds(pl.multiple_of(at.start + n * step, step), step)
        total = stage[slot, here, :].astype(F32) + landed[2, here, :].astype(F32)
        stage[slot, here, :] = total.astype(BF16)


def remote(src, dst, send_sem, recv_sem, device):
    return pltpu.make_async_remote_copy(
        src_ref=src, dst_ref=dst, send_sem=send_sem, recv_sem=recv_sem, device_id=device,
        device_id_type=pl.DeviceIdType.MESH,
    )


class Place:
    def __init__(self, dp):
        index = lax.axis_index("dp")
        self.index, self.dp = index, dp
        self.line = dp // 2
        self.z, self.core = index // 2, index % 2
        self.t = lax.axis_index("tensor")
        tx, ty = self.t % 2, self.t // 2
        self.other = {"dp": index + 1 - 2 * self.core}
        self.up, self.down = {"dp": index + 2}, {"dp": index - 2}
        self.next, self.far = {"dp": index + 2 - 4 * (self.z % 2)}, {"dp": index + 4 - 8 * (self.z // 2)}
        self.x = {"tensor": self.t + 1 - 2 * tx}
        self.y = {"tensor": self.t + 2 - 4 * ty}
        self.spots = [
            (tx if i % 2 == 0 else 1 - tx) + 2 * (ty if i // 2 == 0 else 1 - ty) for i in range(4)
        ]

    def greet(self):
        barrier = pltpu.get_barrier_semaphore()
        peers = [self.x, self.y] + [{"dp": (self.index + k) % self.dp} for k in range(1, self.dp)]
        for device in peers:
            pl.semaphore_signal(
                barrier, inc=1, device_id=device, device_id_type=pl.DeviceIdType.MESH
            )
        pl.semaphore_wait(barrier, len(peers))


def norm_rows(count, body, step=32):
    @pl.loop(0, count // step)
    def _(n):
        body(pl.ds(pl.multiple_of(n * step, step), step))


def attend(pair, first, at, spots, head_lane, q_ref, k_ref, v_ref, mixed_ref, lse_ref, bias_ref):
    lanes = pl.ds(pl.multiple_of(pair * 128, 128), 128)
    query = q_ref[at, lanes]
    outs, stats = [], []
    for h in range(2):
        mine = (head_lane < HEAD_DIM) if h == 0 else (head_lane >= HEAD_DIM)
        qm = jnp.where(mine, query, 0) * jnp.asarray(HEAD_DIM**-0.5, BF16)
        scores = [dot_nt(qm, k_ref[s, lanes]) + bias_ref[n] for n, s in enumerate(spots)]
        top = functools.reduce(jnp.maximum, [jnp.max(s, axis=1, keepdims=True) for s in scores])
        weights = [jnp.exp(s - top) for s in scores]
        total = sum(jnp.sum(w, axis=1, keepdims=True) for w in weights)
        out = sum(dot_nn(w.astype(BF16), v_ref[s, lanes]) for w, s in zip(weights, spots))
        outs.append(out / total)
        stats.append(top + jnp.log(total))
    mixed_ref[at, lanes] = jnp.where(head_lane < HEAD_DIM, outs[0], outs[1]).astype(BF16)
    kept = jnp.where(pair + first == 0, 0.0, lse_ref[at, :])
    for h in range(2):
        kept = jnp.where(head_lane == first + pair * 2 + h, stats[h], kept)
    lse_ref[at, :] = kept


def add_into(total, other, rows, step=64):
    @pl.loop(0, rows // step)
    def _(n):
        at = pl.ds(pl.multiple_of(n * step, step), step)
        total[at, :] = (total[at, :].astype(F32) + other[at, :].astype(F32)).astype(total.dtype)


class LineScatter:
    def __init__(self, me, rows, mine, theirs, swapped, kept, landed, work, sems):
        cut = lambda ref: ref.at[:, pl.ds(0, rows)]
        self.me, self.rows = me, rows
        self.mine, self.theirs, self.swapped = cut(mine), cut(theirs), cut(swapped)
        self.kept, self.landed, self.work = cut(kept), cut(landed), cut(work)
        self.sems = sems

    def swap(self):
        return remote(
            self.theirs, self.swapped, self.sems.at[0], self.sems.at[1], self.me.other
        )

    def keep(self):
        return pltpu.make_async_copy(self.mine, self.kept, self.sems.at[2])

    def send(self, src, s, upward, z):
        line = self.me.line
        if upward:
            slot, device = s, self.me.up
        else:
            slot, device = (s if s < z - 1 else line), self.me.down
        return remote(
            src, self.landed.at[slot], self.sems.at[3 + s], self.sems.at[3 + line + slot], device
        )

    def landing(self, slot):
        line = self.me.line
        return remote(
            self.landed.at[slot], self.landed.at[slot], self.sems.at[3],
            self.sems.at[3 + line + slot], self.me.other,
        )

    def load(self, src, n):
        return pltpu.make_async_copy(src, self.work.at[n], self.sems.at[4 + 2 * self.me.line + n])

    def reduce(self, free_sem):
        line = self.me.line
        self.swap().wait_recv()
        for s in range(line):
            add_into(self.mine.at[s], self.swapped.at[s], self.rows)
        pl.semaphore_signal(
            free_sem, inc=1, device_id=self.me.other, device_id_type=pl.DeviceIdType.MESH
        )
        self.keep().start()
        self.swap().wait_send()
        self.keep().wait()
        for end, upward in ((0, True), (line - 1, False)):

            @pl.when(self.me.z == end)
            def _(end=end, upward=upward):
                order = range(line - 1, end, -1) if upward else range(end)
                for s in order:
                    self.send(self.kept.at[s], s, upward, end).start()

    def going(self, p):
        line = self.me.line
        for z, upward in ((p, True), (line - 1 - p, False)):
            targets = list(range(line - 1, z, -1)) if upward else list(range(z))
            yield z, upward, targets

    def load_phase(self, p, first):
        for z, upward, targets in self.going(p):

            @pl.when(self.me.z == z)
            def _(targets=targets):
                for n, s in enumerate(targets):
                    self.landing(s).wait_recv()
                    self.load(self.landed.at[s], first + 2 * n).start()
                    self.load(self.kept.at[s], first + 2 * n + 1).start()

    def run_phase(self, p, first):
        for z, upward, targets in self.going(p):

            @pl.when(self.me.z == z)
            def _(z=z, upward=upward, targets=targets):
                for n, s in enumerate(targets):
                    a, b = first + 2 * n, first + 2 * n + 1
                    self.load(self.landed.at[s], a).wait()
                    self.load(self.kept.at[s], b).wait()
                    add_into(self.work.at[a], self.work.at[b], self.rows)
                    self.send(self.work.at[a], s, upward, z).start()

    def sent_phase(self, p, first):
        for z, upward, targets in self.going(p):

            @pl.when(self.me.z == z)
            def _(z=z, upward=upward, targets=targets):
                for n, s in enumerate(targets):
                    self.send(self.work.at[first + 2 * n], s, upward, z).wait_send()

    def load_last(self, first):
        me = self.me
        self.load(self.kept.at[me.z], first).start()

        @pl.when(me.z >= 1)
        def _():
            self.landing(me.z).wait_recv()
            self.load(self.landed.at[me.z], first + 1).start()

        @pl.when(me.z < me.line - 1)
        def _():
            self.landing(me.line).wait_recv()
            self.load(self.landed.at[me.line], first + 2).start()

    def run_last(self, first, total):
        me = self.me
        here = total.at[pl.ds(0, self.rows)]
        self.load(self.kept.at[me.z], first).wait()

        def put(n, step=64):
            @pl.loop(0, self.rows // step)
            def _(i):
                at = pl.ds(pl.multiple_of(i * step, step), step)
                if n == first:
                    here[at, :] = self.work[n, at, :].astype(F32)
                else:
                    here[at, :] += self.work[n, at, :].astype(F32)

        put(first)

        @pl.when(me.z >= 1)
        def _():
            self.load(self.landed.at[me.z], first + 1).wait()
            put(first + 1)

        @pl.when(me.z < me.line - 1)
        def _():
            self.load(self.landed.at[me.line], first + 2).wait()
            put(first + 2)

    def done(self):
        line = self.me.line
        for end, upward in ((0, True), (line - 1, False)):

            @pl.when(self.me.z == end)
            def _(end=end, upward=upward):
                for s in range(line - 1, end, -1) if upward else range(end):
                    self.send(self.kept.at[s], s, upward, end).wait_send()


class Ticks:
    def __init__(self, chunks, total, writers):
        self.chunks, self.total, self.writers = chunks, total, writers
        self.k = 0

    def jobs(self, k):
        count = len(self.chunks)
        out = []
        if 0 <= k < count:
            out.append((self.chunks[k], 1, 0))
        if 0 <= k - 1 < count:
            out.append((self.chunks[k - 1], 2, 4))
        return out

    def tick(self):
        k = self.k
        for chunk, p, first in self.jobs(k - 1):
            chunk.sent_phase(p, first)
        last = self.chunks[k - 2] if 0 <= k - 2 < len(self.chunks) else None
        for chunk, p, first in self.jobs(k):
            chunk.load_phase(p, first)
        if last is not None:
            last.load_last(6)
        for chunk, p, first in self.jobs(k):
            chunk.run_phase(p, first)
        if last is not None:
            if k - 2 > 0:
                self.writers[k - 3].wait()
            last.run_last(6, self.total)
            self.writers[k - 2].start()
        self.k += 1

    def rest(self):
        while self.k < len(self.chunks) + 2:
            self.tick()
        self.writers[-1].wait()
        for chunk in self.chunks:
            chunk.done()


class Writer:
    def __init__(self, total, turned, parts, sem):
        self.total, self.turned, self.parts, self.sem = total, turned, parts, sem

    def copies(self):
        for n, (dst, _) in enumerate(self.parts):
            yield pltpu.make_async_copy(self.turned.at[n], dst, self.sem.at[n])

    def start(self):
        for n, (_, flip) in enumerate(self.parts):
            block = self.total[pl.ds(n * 256, 256), :]
            self.turned[n] = (block.T if flip else block).astype(BF16)
        for copy in self.copies():
            copy.start()

    def wait(self):
        for copy in self.copies():
            copy.wait()


def norm_back_rows(count, gain, values_of, grads_of, gain_ref, row, put, step=32):
    @pl.loop(0, count // step)
    def _(n):
        at = pl.ds(pl.multiple_of(n * step, step), step)
        values, grads = values_of(at), grads_of(at)
        factor = norm_factor(values)
        scaled = grads * gain
        back = factor * scaled - values * factor * factor * factor * jnp.mean(
            scaled * values, axis=-1, keepdims=True
        )
        gain_ref[row : row + 1, :] += jnp.sum(grads * values * factor, axis=0, keepdims=True)
        put(at, back)


def attend_back(
    pair, first, at, spots, head_lane, q_ref, k_ref, v_ref, dm_ref, lse_ref, bias_ref, dqa_ref, dka_ref, dva_ref
):
    scale = HEAD_DIM**-0.5
    rows = at.size
    lanes = pl.ds(pl.multiple_of((first + pair) * 128, 128), 128)
    there = pl.ds(pl.multiple_of(pair * 128, 128), 128)
    query, grad = q_ref[at, lanes], dm_ref[at, lanes]
    logs = lse_ref[at, :]
    outs = []
    for h in range(2):
        mine = (head_lane < HEAD_DIM) if h == 0 else (head_lane >= HEAD_DIM)
        qm = jnp.where(mine, query, 0) * jnp.asarray(scale, BF16)
        gm = jnp.where(mine, grad, 0)
        log = jnp.sum(
            jnp.where(head_lane == (first + pair) * 2 + h, logs, 0.0), axis=1, keepdims=True
        )
        weights = [
            jnp.exp(dot_nt(qm, k_ref[s, lanes]) + bias_ref[n] - log) for n, s in enumerate(spots)
        ]
        grads = [dot_nt(gm, v_ref[s, lanes]) for s in spots]
        inner = sum(jnp.sum(w * g, axis=1, keepdims=True) for w, g in zip(weights, grads))
        dq = jnp.zeros((rows, 128), F32)
        for w, g, s in zip(weights, grads, spots):
            ds = (w * (g - inner)).astype(BF16)
            dva_ref[s, there] += dot_tn(w.astype(BF16), gm)
            dka_ref[s, there] += dot_tn(ds, qm)
            dq = dq + dot_nn(ds, k_ref[s, lanes])
        outs.append(dq)
    dqa_ref[at, there] = jnp.where(head_lane < HEAD_DIM, outs[0], outs[1]) * scale


TICK_AFTER = (2, 4, 6)


def layer_kernel(
    dp, x_in, g_in, gain_ref, wq_in, wk_in, wv_in, wo_in, gate_in, up_in, down_in, cos_all, sin_all,
    segc_all, segr_all,
    output_out, input_grad_out, gain_out, gate_out, up_out, down_out, q_out, k_out, v_out, o_out,
    wa_full, wo_full, wf_full, hidden_all, kept_all, landed_all, y_all, normed_all, q_all, k_all, v_all,
    mixed_all, lse_all,
    x_ref, wa_src, wo_src, wf_src, gains_full, rows_a, rows_m, rows_g,
    theirs, swapped, mine, work, total, turned, stage, landed, own, gm, middle, gp, gp_landed,
    sem_in, sem_gains, sem_a, sem_o, sem_f, sem_n, sem_m, sem_g, sem_g2, sem_s, sem_line, sem_write,
    sem_gain, sem_c, sem_w, free_core, free_x, free_y,
):
    me = Place(dp)
    line = me.line
    d = x_in.shape[1]
    half, local = d // 2, x_in.shape[0]
    shard = half // line
    rows = LEN // 4
    blocks = wf_src.shape[0]
    fw = wf_src.shape[2] // 3
    cols = wq_in.shape[1]
    groups = cols // GROUP

    def at_block(b):
        return pl.ds(pl.multiple_of(b * rows, rows), rows)

    def true_columns(side, s):
        core = me.core if side == 0 else 1 - me.core
        return pl.ds(pl.multiple_of((2 * s + core) * shard, shard), shard)

    def own_columns(side, s):
        return pl.ds(side * half + s * shard, shard)

    sides = [(side, s) for side in range(2) for s in range(line)]
    x_loads = [
        pltpu.make_async_copy(
            x_in.at[:, true_columns(*p)], x_ref.at[:, own_columns(*p)], sem_in.at[n]
        )
        for n, p in enumerate(sides)
    ]
    g_loads = [
        pltpu.make_async_copy(
            g_in.at[:, true_columns(*p)], rows_g.at[pl.ds(0, local), own_columns(*p)],
            sem_in.at[2 * line + n],
        )
        for n, p in enumerate(sides)
    ]
    first_sem = 4 * line
    a_loads = [
        pltpu.make_async_copy(ref, wa_src.at[:, pl.ds(n * cols, cols)], sem_in.at[first_sem + n])
        for n, ref in enumerate((wq_in, wk_in, wv_in))
    ]
    f_loads = [
        pltpu.make_async_copy(
            ref.at[:, pl.ds(n * fw, fw)], wf_src.at[n, :, pl.ds(part * fw, fw)],
            sem_in.at[first_sem + 3 + 2 * n + part],
        )
        for n in range(blocks)
        for part, ref in enumerate((gate_in, up_in))
    ]
    for copy in a_loads + x_loads + g_loads + f_loads:
        copy.start()
    gains_full[0, pl.ds(pl.multiple_of(me.z * 16, 16), 16), :] = gain_ref[...]
    me.greet()

    def gain_copy(k, sender):
        place = gains_full.at[k % 2, pl.ds(pl.multiple_of(sender // 2 * 16, 16), 16)]
        return remote(
            gain_ref, place, sem_gains.at[0, k], sem_gains.at[1, k], {"dp": (me.index + k) % dp}
        )

    for k in range(1, dp):
        gain_copy(k, me.index).start()

    wa = LineGather(me, wa_src, wa_full, sem_a)
    wo = LineGather(me, wo_src, wo_full, sem_o)
    gathers = [LineGather(me, wf_src.at[n], wf_full.at[n], sem_f.at[n]) for n in range(blocks)]
    order = [wa, wo] + gathers
    acts = []
    for n, one in enumerate(order):
        for h in range(1, line):

            def act(n=n, one=one, h=h):
                one.hop(h)
                if h == 1 and n == 0:
                    wo.start()
                if h == 2 and n == 0:
                    gathers[0].start()
                if h == 1 and 1 <= n < blocks:
                    order[n + 2].start()

            acts.append(act)

    def poll(count=1):
        for _ in range(min(count, len(acts))):
            acts.pop(0)()

    def hops_done(n):
        return len(acts) <= (blocks - 1 - n) * (line - 1)

    for copy in a_loads:
        copy.wait()
    wa.start()
    for k in range(1, dp):
        gain_copy(k, (me.index + dp - k) % dp).wait_recv()
    for copy in x_loads:
        copy.wait()

    def gain_row(which):
        return jnp.concatenate(
            [
                gains_full[side, pl.ds(s * 16 + which, 1), :].astype(F32)
                for side in range(2)
                for s in range(line)
            ],
            axis=1,
        )

    gain_one, gain_two = gain_row(0), gain_row(1)

    def first_norm(at):
        values = x_ref[at, :].astype(F32)
        rows_a[at, :] = (values * norm_factor(values) * gain_one).astype(BF16)

    norm_rows(local, first_norm)
    normed = SquareGather(me, rows_a, sem_n)
    grads = SquareGather(me, rows_g, sem_g)
    normed_mlp = SquareGather(me, rows_m, sem_m)
    square = SquareGather(me, rows_a, sem_g2)
    scatter = SquareScatter(me, stage, landed, sem_s)
    normed.start()
    for n in range(cols // 256):
        wo_src[:, pl.ds(n * 256, 256)] = wo_in[pl.ds(n * 256, 256), :].T
    for n in range(blocks):
        wf_src[n, :, pl.ds(2 * fw, fw)] = down_in[pl.ds(n * fw, fw), :].T
    for copy in f_loads:
        copy.wait()
    poll()
    for copy in g_loads:
        copy.wait()
    normed.forward()
    grads.start()
    poll(line - 2)
    normed.arrived()
    wa.arrived()

    def free_landed():
        for device, sem in ((me.x, free_x), (me.y, free_y)):
            pl.semaphore_signal(
                sem, inc=1, device_id=device, device_id_type=pl.DeviceIdType.MESH
            )

    def wait_free():
        pl.semaphore_wait(free_x, 1)
        pl.semaphore_wait(free_y, 1)

    def summed(at):
        return own[at, :] + landed[0, at, :].astype(F32) + landed[1, at, :].astype(F32)

    def doubled(ref, at):
        part = ref[at, :]
        return jnp.concatenate([part] * (GROUP // 128), axis=1)

    head_lane = lax.broadcasted_iota(jnp.int32, (rows, 128), 1)

    def forward(
        wa_v, wo_v, q_ref, k_ref, v_ref, mixed_ref, lse_ref, cos_ref, sin_ref, segc_ref, segr_ref, bias_ref
    ):
        ins = [(cos_all, cos_ref), (sin_all, sin_ref), (segc_all, segc_ref), (segr_all, segr_ref)] + [
            (wa_full.at[side], wa_v.at[pl.ds(side * half, half)]) for side in range(2)
        ]
        loads = [pltpu.make_async_copy(a, b, sem_c.at[n]) for n, (a, b) in enumerate(ins)]
        for copy in loads:
            copy.start()
        for copy in loads:
            copy.wait()

        @pl.loop(0, 4 * groups)
        def _(n):
            b, group = n // groups, n % groups
            at = at_block(b)
            lanes = pl.ds(pl.multiple_of(group * GROUP, GROUP), GROUP)
            cosine, sine = doubled(cos_ref, at), doubled(sin_ref, at)

            def product(part):
                here = pl.ds(pl.multiple_of(part * cols + group * GROUP, GROUP), GROUP)
                return dot_nn(rows_a[at, :], wa_v[:, here])

            query = product(0)
            q_ref[at, lanes] = (query * cosine + swap_halves(query) * sine).astype(BF16)
            keys = product(1)
            k_ref[at, lanes] = (keys * cosine + swap_halves(keys) * sine).astype(BF16)
            v_ref[at, lanes] = product(2).astype(BF16)

        outs = [(q_ref, q_all), (k_ref, k_all), (v_ref, v_all), (rows_a, normed_all)]
        stores = [pltpu.make_async_copy(a, b, sem_c.at[n]) for n, (a, b) in enumerate(outs)]
        for copy in stores:
            copy.start()
        poll(2)
        for i in range(4):
            places = [(j, me.spots[j]) for j in key_blocks(i, rows)]
            at = at_block(me.spots[i])
            fill_bias(bias_ref, segc_ref[at, 0:1], segr_ref, i, places)
            spots = [at_block(p) for _, p in places]

            @pl.loop(0, cols // 128)
            def _(pair, at=at, spots=spots):
                attend(pair, 0, at, spots, head_lane, q_ref, k_ref, v_ref, mixed_ref, lse_ref, bias_ref)

            if i == 0:
                poll(line - 3)
            if i == 1:
                grads.forward()
            if i == 2:
                wo.arrived()
                wo_load = [
                    pltpu.make_async_copy(wo_full.at[side], wo_v.at[pl.ds(side * half, half)], sem_w.at[0, side])
                    for side in range(2)
                ]
                for copy in wo_load:
                    copy.start()
                poll()
        for n, (a, b) in enumerate(((mixed_ref, mixed_all), (lse_ref, lse_all))):
            stores.append(pltpu.make_async_copy(a, b, sem_c.at[len(outs) + n]))
            stores[-1].start()
        for copy in wo_load:
            copy.wait()

        def out_rows(b, slot):
            at = pl.ds(b * rows, rows)
            wide = d // 4

            @pl.loop(0, 4)
            def _(n):
                here = pl.ds(pl.multiple_of(n * wide, wide), wide)
                value = dot_nt(mixed_ref[at, :], wo_v[here, :])
                if slot is None:
                    own[:, here] = value
                else:
                    stage[slot, :, here] = value.astype(BF16)

        out_rows(3, 2)
        scatter.diagonal_ready()
        out_rows(1, 0)
        out_rows(2, 1)
        scatter.sides_ready()
        out_rows(0, None)
        poll(2)
        scatter.combine()
        poll(2)
        for copy in stores:
            copy.wait()
        normed.done()
        scatter.arrived()

    V = pltpu.VMEM
    slab = V((LEN, cols), BF16)
    table, wide_table = V((LEN, 128), F32), V((LEN, GROUP), F32)
    bias = V((3, rows, rows), F32)
    segs = (V(segc_all.shape, jnp.int32), V(segr_all.shape, jnp.int32))
    pl.run_scoped(
        forward, V((d, 3 * cols), BF16), V((d, cols), BF16), slab, slab, slab, slab, table, table, table,
        *segs, bias,
    )

    def second_norm(at):
        values = x_ref[at, :].astype(F32) + summed(at)
        middle[at, :] = values
        rows_m[at, :] = (values * norm_factor(values) * gain_two).astype(BF16)

    norm_rows(local, second_norm)
    normed_mlp.start()
    free_landed()
    scatter.done()
    poll(3)
    normed_mlp.forward()
    poll()
    grads.arrived()
    normed_mlp.arrived()

    sizes = [3 * fw] * blocks + [cols] + [3 * GROUP] * groups
    chunks = [
        LineScatter(me, size, mine, theirs, swapped, kept_all.at[n], landed_all.at[n], work, sem_line.at[n])
        for n, size in enumerate(sizes)
    ]
    writers = []
    for n in range(blocks):
        here = pl.ds(n * fw, fw)
        parts = [(gate_out.at[:, here], True), (up_out.at[:, here], True), (down_out.at[here], False)]
        writers.append(Writer(total, turned, parts, sem_write.at[n]))
    parts = [(o_out.at[pl.ds(n * 256, 256)], False) for n in range(cols // 256)]
    writers.append(Writer(total, turned, parts, sem_write.at[blocks]))
    for n in range(groups):
        here = pl.ds(n * GROUP, GROUP)
        parts = [(ref.at[:, here], True) for ref in (q_out, k_out, v_out)]
        writers.append(Writer(total, turned, parts, sem_write.at[blocks + 1 + n]))
    ticks = Ticks(chunks, total, writers)

    def swap(n):
        if n >= 1:
            pl.semaphore_wait(free_core, 1)
        chunks[n].swap().start()

    def products(left, right, first, size):
        @pl.loop(0, line)
        def _(s):
            for side, dst in ((0, mine), (1, theirs)):
                here = pl.ds(pl.multiple_of(side * half + s * shard, shard), shard)
                dst[s, pl.ds(first, size), :] = dot_nn(left[...], right[:, here]).astype(BF16)

    def mlp(wb, sums, dgu_t, hid_t, hid):
        def weights(n):
            return [
                pltpu.make_async_copy(
                    wf_full.at[n, side], wb.at[n % 2, pl.ds(side * half, half)], sem_w.at[n % 2, side]
                )
                for side in range(2)
            ]

        def hidden_copy(n):
            return pltpu.make_async_copy(hid.at[n % 2], hidden_all.at[n], sem_c.at[n % 2])

        fetched = [False] * (blocks + 1)

        def fetch(n):
            if n < blocks and not fetched[n]:
                while not hops_done(n):
                    poll()
                gathers[n].arrived()
                for copy in weights(n):
                    copy.start()
                fetched[n] = True

        for n in range(blocks):
            fetch(n)
            if n == 0:

                @pl.loop(0, LEN // 64)
                def _(i):
                    at = pl.ds(pl.multiple_of(i * 64, 64), 64)
                    sums[at, :] = jnp.zeros((64, d), F32)

            for copy in weights(n):
                copy.wait()
            if n == 1:
                chunks[0].reduce(free_core)
            if n + 1 < blocks and hops_done(n + 1):
                fetch(n + 1)
            if n >= 2:
                hidden_copy(n - 2).wait()
            w = wb.at[n % 2]
            gu_w, down_w = w.at[:, pl.ds(0, 2 * fw)], w.at[:, pl.ds(2 * fw, fw)]

            @pl.loop(0, 4)
            def _(r, n=n, gu_w=gu_w, down_w=down_w):
                at = at_block(r)
                gu = dot_nn(rows_m[at, :], gu_w[...])
                grad_hidden = dot_nn(rows_g[at, :], down_w[...])
                gate_pre, upward = gu[:, :fw], gu[:, fw:]
                sig = jax.nn.sigmoid(gate_pre)
                activated = gate_pre * sig
                hidden = (activated * upward).astype(BF16)
                hid[n % 2, at, :] = hidden
                hid_t[:, at] = hidden.T
                grad_gate = grad_hidden * upward * sig * (1.0 + gate_pre * (1.0 - sig))
                grad_up = grad_hidden * activated
                dgu = jnp.concatenate([grad_gate, grad_up], axis=1).astype(BF16)
                dgu_t[:, at] = dgu.T

                @pl.loop(0, 4)
                def _(c):
                    here = pl.ds(pl.multiple_of(c * (half // 2), half // 2), half // 2)
                    sums[at, here] += dot_nt(dgu, gu_w[here, :])

            hidden_copy(n).start()
            poll()
            if n >= 2:
                chunks[n - 1].reduce(free_core)
            products(dgu_t, rows_m, 0, 2 * fw)
            products(hid_t, rows_g, 2 * fw, fw)
            swap(n)
            poll()
            if n in TICK_AFTER:
                ticks.tick()
        for n in range(max(0, blocks - 2), blocks):
            hidden_copy(n).wait()
        wait_free()

        def to_stage(b, slot):
            @pl.loop(0, rows // 64)
            def _(i):
                at = pl.ds(pl.multiple_of(i * 64, 64), 64)
                there = pl.ds(pl.multiple_of(b * rows + i * 64, 64), 64)
                if slot is None:
                    own[at, :] = sums[there, :]
                else:
                    stage[slot, at, :] = sums[there, :].astype(BF16)

        to_stage(3, 2)
        scatter.diagonal_ready()
        to_stage(1, 0)
        to_stage(2, 1)
        scatter.sides_ready()
        to_stage(0, None)

    pl.run_scoped(
        mlp, V((2, d, 3 * fw), BF16), V((LEN, d), F32), V((2 * fw, LEN), BF16), V((fw, LEN), BF16),
        V((2, LEN, fw), BF16),
    )
    gp[...] = jnp.zeros(gp.shape, F32)

    def down(hidden, dw, rest):
        ins = [(hidden_all.at[n], hidden.at[n]) for n in range(blocks)] + [
            (wf_full.at[n, side, :, pl.ds(2 * fw, fw)], dw.at[n, pl.ds(side * half, half)])
            for n in range(blocks)
            for side in range(2)
        ]
        loads = [pltpu.make_async_copy(a, b, sem_c.at[n]) for n, (a, b) in enumerate(ins)]
        for copy in loads:
            copy.start()
        chunks[blocks - 1].reduce(free_core)
        ticks.tick()
        for copy in loads:
            copy.wait()

        @pl.loop(0, 4)
        def _(b):
            at = at_block(b)

            @pl.loop(0, d // GROUP)
            def _(c):
                here = pl.ds(pl.multiple_of(c * GROUP, GROUP), GROUP)
                value = sum(dot_nt(hidden[n, at, :], dw[n, here, :]) for n in range(blocks))
                rest[b, :, here] = value.astype(BF16)

        out = pltpu.make_async_copy(rest, y_all, sem_c.at[0])
        out.start()
        out.wait()

    pl.run_scoped(
        down, V((blocks, LEN, fw), BF16), V((blocks, d, fw), BF16), V((4, local, d), BF16)
    )
    scatter.combine()
    normed_mlp.done()
    grads.done()

    def attention(
        q_ref, k_ref, v_ref, mixed_t, mixed, lse_ref, cos_ref, sin_ref, segc_ref, segr_ref, out_w,
        dqa_ref, dka_ref, dva_ref, part_t, bias_ref, y_mine,
    ):
        ins = [
            (mixed_all, mixed), (q_all, q_ref), (k_all, k_ref), (v_all, v_ref), (lse_all, lse_ref),
            (cos_all, cos_ref), (sin_all, sin_ref), (segc_all, segc_ref), (segr_all, segr_ref),
            (wo_full, out_w), (y_all.at[0], y_mine), (normed_all, rows_m),
        ]
        loads = [pltpu.make_async_copy(a, b, sem_c.at[n]) for n, (a, b) in enumerate(ins)]
        for copy in loads:
            copy.start()
        ticks.tick()
        scatter.arrived()

        def second_norm_back(at, back):
            grad = rows_g[at, :].astype(F32) + back
            gm[at, :] = grad
            rows_a[at, :] = grad.astype(BF16)

        norm_back_rows(local, gain_two, lambda at: middle[at, :], summed, gp, 1, second_norm_back)
        square.start()
        free_landed()
        scatter.done()
        stage_in = [
            pltpu.make_async_copy(y_all.at[b], stage.at[slot], sem_w.at[n // 2, n % 2])
            for n, (b, slot) in enumerate(((3, 2), (1, 0), (2, 1)))
        ]
        for copy in stage_in:
            copy.start()
        for copy in loads:
            copy.wait()
        mixed_t[...] = mixed[...].T
        square.forward()
        ticks.tick()
        for copy in stage_in:
            copy.wait()
        wait_free()
        square.arrived()
        scatter.diagonal_ready()
        scatter.sides_ready()

        @pl.loop(0, 4)
        def _(b):
            at = at_block(b)
            rows_g[at, pl.ds(3 * cols, cols)] = (
                dot_nn(rows_a[at, :half], out_w[0]) + dot_nn(rows_a[at, half:], out_w[1])
            ).astype(BF16)

        products(mixed_t, rows_a, 0, cols)
        swap(blocks)
        dm_ref = rows_g.at[:, pl.ds(3 * cols, cols)]
        for group in range(groups):

            @pl.loop(0, 4)
            def _(b):
                at = at_block(b)
                dka_ref[at, :] = jnp.zeros((rows, GROUP), F32)
                dva_ref[at, :] = jnp.zeros((rows, GROUP), F32)

            for i in range(4):
                places = [(j, me.spots[j]) for j in key_blocks(i, rows)]
                at = at_block(me.spots[i])
                fill_bias(bias_ref, segc_ref[at, 0:1], segr_ref, i, places)
                spots = [at_block(p) for _, p in places]

                @pl.loop(0, GROUP // 128)
                def _(pair, at=at, spots=spots, group=group):
                    attend_back(
                        pair, group * (GROUP // 128), at, spots, head_lane, q_ref, k_ref, v_ref,
                        dm_ref, lse_ref, bias_ref, dqa_ref, dka_ref, dva_ref,
                    )

                if i == 1:
                    chunks[blocks + group].reduce(free_core)
                if i == 2 and group == 0:
                    ticks.tick()
                if i == 3 and group == 0:
                    scatter.combine()

            @pl.loop(0, 4)
            def _(b, group=group):
                at = at_block(b)
                cosine, sine = doubled(cos_ref, at), doubled(sin_ref, at)
                for part, ref in enumerate((dqa_ref, dka_ref, dva_ref)):
                    value = ref[at, :]
                    if part < 2:
                        value = value * cosine - swap_halves(value) * sine
                    value = value.astype(BF16)
                    rows_g[at, pl.ds(part * cols + group * GROUP, GROUP)] = value
                    part_t[pl.ds(part * GROUP, GROUP), at] = value.T

            products(part_t, rows_m, 0, 3 * GROUP)
            swap(blocks + 1 + group)
            if group == 0:
                ticks.tick()
        scatter.arrived()

        def output_rows(at):
            value = middle[at, :] + y_mine[at, :].astype(F32)
            value = value + landed[0, at, :].astype(F32) + landed[1, at, :].astype(F32)
            y_mine[at, :] = value.astype(BF16)

        norm_rows(local, output_rows)
        free_landed()
        results = [
            pltpu.make_async_copy(
                y_mine.at[:, own_columns(*p)], output_out.at[:, true_columns(*p)], sem_in.at[n]
            )
            for n, p in enumerate(sides)
        ]
        for copy in results:
            copy.start()
        scatter.done()
        for copy in results:
            copy.wait()

    pl.run_scoped(
        attention, slab, slab, slab, V((cols, LEN), BF16), slab, table, table, table, *segs,
        V(wo_full.shape, BF16), wide_table, wide_table, wide_table, V((3 * GROUP, LEN), BF16), bias,
        V((local, d), BF16),
    )

    def normed_grads(qkv_w):
        loads = [
            pltpu.make_async_copy(wa_full.at[side], qkv_w.at[pl.ds(side * half, half)], sem_c.at[side])
            for side in range(2)
        ]
        for copy in loads:
            copy.start()
        chunks[blocks + groups].reduce(free_core)
        for copy in loads:
            copy.wait()
        wait_free()

        def normed_grad(b, slot):
            at = pl.ds(b * rows, rows)
            wide = d // 4

            @pl.loop(0, 4)
            def _(n):
                here = pl.ds(pl.multiple_of(n * wide, wide), wide)
                value = dot_nt(rows_g[at, pl.ds(0, 3 * cols)], qkv_w[here, :])
                if slot is None:
                    own[:, here] = value
                else:
                    stage[slot, :, here] = value.astype(BF16)

        normed_grad(3, 2)
        scatter.diagonal_ready()
        normed_grad(1, 0)
        normed_grad(2, 1)
        scatter.sides_ready()
        normed_grad(0, None)

    pl.run_scoped(normed_grads, V((d, 3 * cols), BF16))
    ticks.tick()
    scatter.combine()
    ticks.tick()
    scatter.arrived()

    def first_norm_back(at, back):
        gm[at, :] += back

    norm_back_rows(
        local, gain_one, lambda at: x_ref[at, :].astype(F32), summed, gp, 0, first_norm_back
    )
    results = [
        pltpu.make_async_copy(
            gm.at[:, own_columns(*p)], input_grad_out.at[:, true_columns(*p)], sem_in.at[n]
        )
        for n, p in enumerate(sides)
    ]
    for copy in results:
        copy.start()
    scatter.done()
    exchange = [
        remote(gp, gp_landed.at[n], sem_gain.at[n, 0], sem_gain.at[n, 1], device)
        for n, device in enumerate((me.x, me.y, me.other, me.next, me.far))
    ]

    def add_gains(n):
        exchange[n].wait()
        if n == 2:
            gp[:, :half] += gp_landed[n, :, half:]
            gp[:, half:] += gp_landed[n, :, :half]
        else:
            gp[...] += gp_landed[n]

    for n in range(3):
        exchange[n].start()
        add_gains(n)
    exchange[3].start()
    ticks.tick()
    add_gains(3)
    exchange[4].start()
    ticks.tick()
    add_gains(4)
    gain_out[...] = gp[...]
    ticks.rest()
    pl.semaphore_wait(free_core, 1)
    for k in range(1, dp):
        gain_copy(k, me.index).wait_send()
    for copy in results:
        copy.wait()
    for one in [wa, wo, square] + gathers:
        one.done()


def layer(dp, x, g, gains, wq, wk, wv, wo, gate, up, down, cosine, sine, segc, segr):
    line = dp // 2
    local, d = x.shape
    cols, ff = wq.shape[1], gate.shape[1]
    blocks, shard = FF_BLOCKS, d // dp
    fw = ff // blocks
    groups = cols // GROUP
    count = blocks + 1 + groups
    most = max(3 * fw, cols, 3 * GROUP)
    vm, hbm = pl.BlockSpec(memory_space=pltpu.VMEM), pl.BlockSpec(memory_space=pl.ANY)
    S, V, dma = jax.ShapeDtypeStruct, pltpu.VMEM, pltpu.SemaphoreType.DMA
    regular = pltpu.SemaphoreType.REGULAR
    slab = S((LEN, cols), BF16)
    piece = V((line, most, shard), BF16)
    return pl.pallas_call(
        functools.partial(layer_kernel, dp),
        in_specs=[hbm, hbm, vm, hbm, hbm, hbm, vm, hbm, hbm, vm, hbm, hbm, hbm, hbm],
        out_specs=[hbm, hbm, vm] + [hbm] * 20,
        out_shape=[
            S((local, d), BF16), S((local, d), F32), S((8, d), F32),
            S((shard, ff), BF16), S((shard, ff), BF16), S((ff, shard), BF16),
            S((shard, cols), BF16), S((shard, cols), BF16), S((shard, cols), BF16), S((cols, shard), BF16),
            S((2, d // 2, 3 * cols), BF16), S((2, d // 2, cols), BF16),
            S((blocks, 2, d // 2, 3 * fw), BF16), S((blocks, LEN, fw), BF16),
            S((count, line, most, shard), BF16), S((count, line + 1, most, shard), BF16),
            S((4, local, d), BF16), S((LEN, d), BF16), slab, slab, slab, slab, S((LEN, 128), F32),
        ],
        scratch_shapes=[
            V((local, d), BF16), V((shard, 3 * cols), BF16), V((shard, cols), BF16),
            V((blocks, shard, 3 * fw), BF16), V((2, line * 16, shard), BF16),
            V((LEN, d), BF16), V((LEN, d), BF16), V((LEN, d), BF16),
            piece, piece, piece, V((9, most, shard), BF16), V((most, shard), F32), V((3, shard, 256), BF16),
            V((3, local, d), BF16), V((3, local, d), BF16), V((local, d), F32), V((local, d), F32),
            V((local, d), F32), V((8, d), F32), V((5, 8, d), F32),
            dma((4 * line + 3 + 2 * blocks,)), dma((2, dp)), dma((6, line)), dma((6, line)),
            dma((blocks, 6, line)), dma((8,)), dma((8,)), dma((8,)), dma((8,)), dma((12,)),
            dma((count, 4 + 2 * line + 9)), dma((count, 3)), dma((5, 2)), dma((3 * blocks,)), dma((2, 2)),
            regular, regular, regular,
        ],
        compiler_params=pltpu.CompilerParams(
            vmem_limit_bytes=VMEM_BYTES, collective_id=0, has_side_effects=True
        ),
        name="layer",
    )(x, g, gains, wq, wk, wv, wo, gate, up, down, cosine, sine, segc, segr)


def on_device(
    dp, tensor, hidden_in, doc_lengths, gain_attn, w_query, w_key, w_value, w_out, gain_mlp,
    w_gate, w_up, w_down, cotangent,
):
    line = dp // 2
    core = lax.axis_index("dp") % 2
    place = lax.axis_index("tensor")
    square = tensor == 4 and dp == 8
    same_core = [[c + 2 * z for z in range(line)] for c in range(2)]
    sibling = [(i, i ^ 1) for i in range(dp)]
    d = hidden_in.shape[1]
    local = hidden_in.shape[0]

    def own_first(a):
        s = a.reshape(a.shape[:-1] + (line, 2, d // dp))
        even, odd = s[..., 0, :], s[..., 1, :]
        out = jnp.concatenate(
            [jnp.where(core == 0, even, odd), jnp.where(core == 0, odd, even)], axis=-2
        )
        return out.reshape(a.shape)

    def true_order(a):
        s = a.reshape(a.shape[:-1] + (2, line, d // dp))
        first, second = s[..., 0, :, :], s[..., 1, :, :]
        out = jnp.stack(
            [jnp.where(core == 0, first, second), jnp.where(core == 0, second, first)], axis=-2
        )
        return out.reshape(a.shape)

    def hop(a, step):
        return lax.ppermute(a, "tensor", [(i, i ^ step) for i in range(tensor)])

    def gather_rows(a):
        if not square:
            return lax.all_gather(a, "tensor", axis=0, tiled=True)
        half = a.shape[0] // 2
        from_x, from_y = hop(a, 1), hop(a, 2)
        top, bottom = hop(from_x[:half], 2), hop(from_y[half:], 1)
        return jnp.concatenate([a, from_x, from_y, top, bottom], axis=0)

    def scatter_rows(a):
        if not square:
            return lax.psum_scatter(a, "tensor", scatter_dimension=0, tiled=True).astype(F32)
        n = a.shape[0] // 4
        half = n // 2
        top = hop(a[3 * n : 3 * n + half], 2)
        bottom = hop(a[3 * n + half :], 1)
        for_x = jnp.concatenate([a[n : n + half] + top, a[n + half : 2 * n]], axis=0)
        for_y = jnp.concatenate([a[2 * n : 2 * n + half], a[2 * n + half : 3 * n] + bottom], axis=0)
        return (a[:n].astype(F32) + hop(for_x, 1).astype(F32)) + hop(for_y, 2).astype(F32)

    def line_gather(a):
        own = lax.all_gather(a, "dp", axis=0, axis_index_groups=same_core, tiled=True)
        return own, lax.ppermute(own, "dp", sibling)

    def line_scatter(own, sib):
        mine = own + lax.ppermute(sib, "dp", sibling)
        return lax.psum_scatter(
            mine, "dp", scatter_dimension=0, axis_index_groups=same_core, tiled=True
        ).astype(F32)

    blocks = 4
    rows = LEN // blocks
    key = place if square else jnp.zeros((), jnp.int32)
    tokens = (
        (jnp.arange(blocks, dtype=jnp.int32) ^ key)[:, None] * rows
        + jnp.arange(rows, dtype=jnp.int32)[None, :]
    ).reshape(LEN)
    segment, position = doc_tables(doc_lengths, tokens)
    cosine, sine = rotary_tables(position)
    segc = jnp.broadcast_to(segment[:, None], (LEN, 128))
    segr = jnp.broadcast_to(segment.reshape(blocks, 1, rows), (blocks, 8, rows))
    key = key.reshape(1)
    cols = w_query.shape[1]
    if square:
        gain_rows = jnp.pad(
            jnp.concatenate([gain_attn, gain_mlp]), (0, 14 * gain_attn.shape[0])
        ).reshape(16, -1)
        (
            output, input_grad, gain_sum, grad_gate, grad_up, grad_down, grad_query, grad_key,
            grad_value, grad_out, *_,
        ) = layer(
            dp, hidden_in, cotangent, gain_rows, w_query, w_key, w_value, w_out, w_gate, w_up,
            w_down, cosine, sine, segc, segr,
        )
        share = d // (dp * tensor)
        first = (lax.axis_index("dp") // 2) * (d // dp) + place * share
        gain_sum = lax.dynamic_slice_in_dim(gain_sum, first, share, 1)
        return (
            output, input_grad, gain_sum[0], grad_query.astype(F32), grad_key.astype(F32),
            grad_value.astype(F32), grad_out.astype(F32), gain_sum[1], grad_gate.astype(F32),
            grad_up.astype(F32), grad_down.astype(F32),
        )

    cosine, sine = (jnp.tile(a, (1, GROUP // 128)) for a in (cosine, sine))
    ff = w_gate.shape[1]
    fb = ff // FF_BLOCKS
    down_t = w_down.T
    shards = [
        jnp.concatenate([w[:, b * fb : (b + 1) * fb] for w in (w_gate, w_up, down_t)], axis=1)
        for b in range(FF_BLOCKS)
    ]
    qkv_shard = jnp.concatenate([w_query, w_key, w_value], axis=1)
    g_local = own_first(cotangent)
    inputs = own_first(hidden_in).astype(F32)
    factor_one = norm_factor(inputs)
    gains = lax.all_gather(jnp.stack([gain_attn, gain_mlp]), "dp", axis=0)
    gains = own_first(jnp.moveaxis(gains, 0, 1).reshape(2, d)).astype(F32)
    gain_one, gain_two = gains[0], gains[1]
    qkv_own, qkv_sib = line_gather(qkv_shard)
    out_own, out_sib = line_gather(w_out.T)
    normed = gather_rows((inputs * factor_one * gain_one).astype(BF16))
    g_all = gather_rows(g_local)
    query, keys, values, mixed, lse = attn_forward(
        blocks, key, normed, qkv_own, qkv_sib, cosine, sine, segc, segr
    )
    attended = jnp.concatenate(
        [dot_nt(mixed, out_own).astype(BF16), dot_nt(mixed, out_sib).astype(BF16)], axis=1
    )
    middle = inputs + scatter_rows(attended)
    factor_two = norm_factor(middle)
    normed_mlp = gather_rows((middle * factor_two * gain_two).astype(BF16))
    ff_sets = [jnp.concatenate(line_gather(shard), axis=0) for shard in shards]

    down_sum = jnp.zeros((LEN, d), F32)
    back_sum = jnp.zeros((LEN, d), F32)
    ff_grads = []
    for b in range(FF_BLOCKS):
        gate_w, up_w, down_w = jnp.split(ff_sets[b], 3, axis=1)
        gate_pre = dot_nn(normed_mlp, gate_w)
        upward = dot_nn(normed_mlp, up_w)
        grad_hidden = dot_nn(g_all, down_w)
        sig = jax.nn.sigmoid(gate_pre)
        activated = gate_pre * sig
        hidden = (activated * upward).astype(BF16)
        grad_gate_pre = (grad_hidden * upward * sig * (1.0 + gate_pre * (1.0 - sig))).astype(BF16)
        grad_upward = (grad_hidden * activated).astype(BF16)
        down_sum = down_sum + dot_nt(hidden, down_w)
        back_sum = back_sum + dot_nt(grad_gate_pre, gate_w) + dot_nt(grad_upward, up_w)
        grad = jnp.concatenate(
            [
                dot_tn(normed_mlp, grad_gate_pre).astype(BF16),
                dot_tn(normed_mlp, grad_upward).astype(BF16),
                dot_tn(g_all, hidden).astype(BF16),
            ],
            axis=1,
        )
        ff_grads.append(line_scatter(grad[: d // 2], grad[d // 2 :]))
    grad_norm_two = scatter_rows(back_sum.astype(BF16))
    output = true_order((middle + scatter_rows(down_sum.astype(BF16))).astype(BF16))
    grad_mid_norm, gain_two_part = norm_back(middle, factor_two, gain_two, grad_norm_two)
    grad_middle = g_local.astype(F32) + grad_mid_norm
    grad_mid_all = gather_rows(grad_middle.astype(BF16))

    dq, dk, dv = attn_backward(
        blocks, key, grad_mid_all, out_own, out_sib, query, keys, values, lse, cosine, sine,
        segc, segr,
    )
    grad = jnp.concatenate(
        [dot_tn(normed, dq), dot_tn(normed, dk), dot_tn(normed, dv), dot_tn(grad_mid_all, mixed)],
        axis=1,
    ).astype(BF16)
    attn_grads = line_scatter(grad[: d // 2], grad[d // 2 :])
    rows_grad = jnp.concatenate([dq, dk, dv], axis=1)
    back = jnp.concatenate(
        [
            dot_nt(rows_grad, qkv_own).astype(BF16),
            dot_nt(rows_grad, qkv_sib).astype(BF16),
        ],
        axis=1,
    )
    grad_in_norm, gain_one_part = norm_back(inputs, factor_one, gain_one, scatter_rows(back))
    input_grad = true_order(grad_middle + grad_in_norm)

    parts = true_order(jnp.stack([gain_one_part, gain_two_part])).reshape(2 * d)
    shares = lax.all_gather(parts, ("dp", "tensor"), axis=0)
    gain_sum = jnp.sum(shares, axis=0).reshape(2, d)
    share = d // (dp * tensor)
    first = (lax.axis_index("dp") * tensor + place) * share
    gain_sum = lax.dynamic_slice_in_dim(gain_sum, first, share, 1)

    return (
        output,
        input_grad,
        gain_sum[0],
        attn_grads[:, :cols],
        attn_grads[:, cols : 2 * cols],
        attn_grads[:, 2 * cols : 3 * cols],
        attn_grads[:, 3 * cols :].T,
        gain_sum[1],
        jnp.concatenate([g[:, :fb] for g in ff_grads], axis=1),
        jnp.concatenate([g[:, fb : 2 * fb] for g in ff_grads], axis=1),
        jnp.concatenate([g[:, 2 * fb :] for g in ff_grads], axis=1).T,
    )


def solution(mesh):
    shape = dict(mesh.shape)
    return jax.shard_map(
        functools.partial(on_device, shape["dp"], shape["tensor"]),
        mesh=mesh,
        in_specs=(
            P(("dp", "tensor"), None),
            P("dp", None),
            P("dp"),
            P("dp", "tensor"),
            P("dp", "tensor"),
            P("dp", "tensor"),
            P("tensor", "dp"),
            P("dp"),
            P("dp", "tensor"),
            P("dp", "tensor"),
            P("tensor", "dp"),
            P(("dp", "tensor"), None),
        ),
        out_specs=(
            P(("dp", "tensor"), None),
            P(("dp", "tensor"), None),
            P(("dp", "tensor")),
            P("dp", "tensor"),
            P("dp", "tensor"),
            P("dp", "tensor"),
            P("tensor", "dp"),
            P(("dp", "tensor")),
            P("dp", "tensor"),
            P("dp", "tensor"),
            P("tensor", "dp"),
        ),
        check_vma=False,
    )
```

```python
import functools

import jax
import jax.numpy as jnp
from jax import lax
from jax.experimental import pallas as pl
from jax.experimental.pallas import tpu as pltpu
from jax.sharding import PartitionSpec as P

HEAD_DIM = 64
LEN = 1024
MOST = 512
EPSILON = 1e-05
ROPE_BASE = 130000.0
NEG = -1e30
GROUP = 256
FF_BLOCKS = 8
F32 = jnp.float32
BF16 = jnp.bfloat16
VMEM_BYTES = 63 * 1024 * 1024


def dot_nn(a, b):
    return jnp.dot(a, b, preferred_element_type=F32)


def dot_tn(a, b):
    return lax.dot_general(a, b, (((0,), (0,)), ((), ())), preferred_element_type=F32)


def dot_nt(a, b):
    return lax.dot_general(a, b, (((1,), (1,)), ((), ())), preferred_element_type=F32)


def norm_factor(values):
    return lax.rsqrt(jnp.mean(values * values, axis=-1, keepdims=True) + EPSILON)


def norm_back(values, factor, gain, grads):
    scaled = grads * gain
    grad_in = factor * scaled - values * factor * factor * factor * jnp.mean(
        scaled * values, axis=-1, keepdims=True
    )
    return grad_in, jnp.sum(grads * values * factor, axis=0)


def doc_tables(doc_lengths, tokens):
    ends = jnp.cumsum(doc_lengths, axis=1)[0]
    passed = tokens[:, None] >= ends[None, :]
    segment = jnp.sum(passed.astype(jnp.int32), axis=1)
    start = jnp.sum(jnp.where(passed, doc_lengths, 0), axis=1)
    return segment, tokens - start


def rotary_tables(position):
    half = HEAD_DIM // 2
    inverse = jnp.power(ROPE_BASE, -jnp.arange(half, dtype=F32) * 2.0 / HEAD_DIM)
    angles = position.astype(F32)[:, None] * inverse
    cosine, sine = jnp.cos(angles), jnp.sin(angles)
    heads = 128 // HEAD_DIM
    return (
        jnp.tile(jnp.concatenate([cosine, cosine], axis=1), (1, heads)),
        jnp.tile(jnp.concatenate([-sine, sine], axis=1), (1, heads)),
    )


def swap_halves(v):
    half, width = HEAD_DIM // 2, v.shape[1]
    lane = lax.broadcasted_iota(jnp.int32, v.shape, 1)
    ahead = pltpu.roll(v, width - half, 1)
    behind = pltpu.roll(v, half, 1)
    return jnp.where(lane % HEAD_DIM < half, ahead, behind)


def key_blocks(i, rows):
    reach = -(-(MOST - 1) // rows)
    return list(range(max(0, i - reach), i + 1))


def fill_bias(bias_ref, seg_col, seg_ref, i, places):
    rows = seg_col.shape[0]
    for n, (j, place) in enumerate(places):
        same = seg_col == seg_ref[place][0:1, :]
        if j == i:
            row = lax.broadcasted_iota(jnp.int32, (rows, rows), 0)
            col = lax.broadcasted_iota(jnp.int32, (rows, rows), 1)
            same = same & (col <= row)
        bias_ref[n] = jnp.where(same, 0.0, NEG)


def attn_forward_kernel(
    blocks, key_ref, x_ref, qo, qs, ko, ks, vo, vs, cos_ref, sin_ref, segc_ref, segr_ref,
    q_ref, k_ref, v_ref, mixed_ref, lse_ref, bias_ref,
):
    rows = LEN // blocks
    half = x_ref.shape[1] // 2
    key = key_ref[0]

    @pl.loop(0, blocks)
    def _(b):
        at = pl.ds(pl.multiple_of(b * rows, rows), rows)
        left, right = x_ref[at, :half], x_ref[at, half:]
        cosine, sine = cos_ref[at, :], sin_ref[at, :]
        query = dot_nn(left, qo[...]) + dot_nn(right, qs[...])
        q_ref[at, :] = (query * cosine + swap_halves(query) * sine).astype(BF16)
        keys = dot_nn(left, ko[...]) + dot_nn(right, ks[...])
        k_ref[at, :] = (keys * cosine + swap_halves(keys) * sine).astype(BF16)
        v_ref[at, :] = (dot_nn(left, vo[...]) + dot_nn(right, vs[...])).astype(BF16)

    head_lane = lax.broadcasted_iota(jnp.int32, (rows, 128), 1)
    for i in range(blocks):
        places = [(j, j ^ key) for j in key_blocks(i, rows)]
        at = pl.ds(pl.multiple_of((i ^ key) * rows, rows), rows)
        fill_bias(bias_ref, segc_ref[at, 0:1], segr_ref, i, places)
        spots = [pl.ds(pl.multiple_of(p * rows, rows), rows) for _, p in places]

        @pl.loop(0, GROUP // 128)
        def _(pair, at=at, spots=spots):
            first = pl.program_id(0) * (GROUP // HEAD_DIM)
            attend(pair, first, at, spots, head_lane, q_ref, k_ref, v_ref, mixed_ref, lse_ref, bias_ref)


def attn_forward(blocks, key, x, own, sib, cosine, sine, segc, segr):
    d = x.shape[1]
    cols = own.shape[1] // 3
    steps = cols // GROUP
    rows = LEN // blocks

    def weight(part):
        return pl.BlockSpec((d // 2, GROUP), lambda i, part=part: (0, part * steps + i))

    def whole(shape):
        return pl.BlockSpec(shape, lambda i: (0,) * len(shape))

    col_block = pl.BlockSpec((LEN, GROUP), lambda i: (0, i))
    slab = jax.ShapeDtypeStruct((LEN, cols), BF16)
    return pl.pallas_call(
        functools.partial(attn_forward_kernel, blocks),
        grid=(steps,),
        in_specs=[pl.BlockSpec(memory_space=pltpu.SMEM), whole((LEN, d))]
        + [weight(p) for p in (0, 0, 1, 1, 2, 2)]
        + [whole((LEN, GROUP))] * 2
        + [whole((LEN, 128)), whole(segr.shape)],
        out_specs=[col_block] * 4 + [whole((LEN, 128))],
        out_shape=[slab] * 4 + [jax.ShapeDtypeStruct((LEN, 128), F32)],
        scratch_shapes=[pltpu.VMEM((blocks, rows, rows), F32)],
        compiler_params=pltpu.CompilerParams(vmem_limit_bytes=VMEM_BYTES),
        name="attn_forward",
    )(key, x, own, sib, own, sib, own, sib, cosine, sine, segc, segr)


def attn_backward_kernel(
    blocks, key_ref, g_ref, wo, ws, q_ref, k_ref, v_ref, lse_ref, cos_ref, sin_ref, segc_ref,
    segr_ref, dq_ref, dk_ref, dv_ref, dm_ref, dqa_ref, dka_ref, dva_ref, bias_ref,
):
    rows = LEN // blocks
    half = g_ref.shape[1] // 2
    key = key_ref[0]

    @pl.loop(0, blocks)
    def _(b):
        at = pl.ds(pl.multiple_of(b * rows, rows), rows)
        dm_ref[at, :] = (dot_nn(g_ref[at, :half], wo[...]) + dot_nn(g_ref[at, half:], ws[...])).astype(BF16)
        dka_ref[at, :] = jnp.zeros((rows, GROUP), F32)
        dva_ref[at, :] = jnp.zeros((rows, GROUP), F32)

    head_lane = lax.broadcasted_iota(jnp.int32, (rows, 128), 1)
    scale = HEAD_DIM**-0.5
    for i in range(blocks):
        places = [(j, j ^ key) for j in key_blocks(i, rows)]
        at = pl.ds(pl.multiple_of((i ^ key) * rows, rows), rows)
        fill_bias(bias_ref, segc_ref[at, 0:1], segr_ref, i, places)
        spots = [pl.ds(pl.multiple_of(p * rows, rows), rows) for _, p in places]

        @pl.loop(0, GROUP // 128)
        def _(pair, at=at, spots=spots):
            lanes = pl.ds(pl.multiple_of(pair * 128, 128), 128)
            first = pl.program_id(0) * (GROUP // HEAD_DIM)
            query, grad = q_ref[at, lanes], dm_ref[at, lanes]
            logs = lse_ref[at, :]
            outs = []
            for h in range(2):
                mine = (head_lane < HEAD_DIM) if h == 0 else (head_lane >= HEAD_DIM)
                qm = jnp.where(mine, query, 0) * jnp.asarray(scale, BF16)
                gm = jnp.where(mine, grad, 0)
                log = jnp.sum(
                    jnp.where(head_lane == first + pair * 2 + h, logs, 0.0), axis=1, keepdims=True
                )
                weights = [
                    jnp.exp(dot_nt(qm, k_ref[s, lanes]) + bias_ref[n] - log)
                    for n, s in enumerate(spots)
                ]
                grads = [dot_nt(gm, v_ref[s, lanes]) for s in spots]
                inner = sum(
                    jnp.sum(w * g, axis=1, keepdims=True) for w, g in zip(weights, grads)
                )
                dq = jnp.zeros((rows, 128), F32)
                for w, g, s in zip(weights, grads, spots):
                    ds = (w * (g - inner)).astype(BF16)
                    dva_ref[s, lanes] += dot_tn(w.astype(BF16), gm)
                    dka_ref[s, lanes] += dot_tn(ds, qm)
                    dq = dq + dot_nn(ds, k_ref[s, lanes])
                outs.append(dq)
            dqa_ref[at, lanes] = jnp.where(head_lane < HEAD_DIM, outs[0], outs[1]) * scale

    @pl.loop(0, blocks)
    def _(b):
        at = pl.ds(pl.multiple_of(b * rows, rows), rows)
        cosine, sine = cos_ref[at, :], sin_ref[at, :]
        dq = dqa_ref[at, :]
        dq_ref[at, :] = (dq * cosine - swap_halves(dq) * sine).astype(BF16)
        dk = dka_ref[at, :]
        dk_ref[at, :] = (dk * cosine - swap_halves(dk) * sine).astype(BF16)
        dv_ref[at, :] = dva_ref[at, :].astype(BF16)


def attn_backward(blocks, key, g, own, sib, q, k, v, lse, cosine, sine, segc, segr):
    d = g.shape[1]
    cols = q.shape[1]
    steps = cols // GROUP
    rows = LEN // blocks

    def whole(shape):
        return pl.BlockSpec(shape, lambda i: (0,) * len(shape))

    col_block = pl.BlockSpec((LEN, GROUP), lambda i: (0, i))
    weight = pl.BlockSpec((d // 2, GROUP), lambda i: (0, i))
    slab = jax.ShapeDtypeStruct((LEN, cols), BF16)
    return pl.pallas_call(
        functools.partial(attn_backward_kernel, blocks),
        grid=(steps,),
        in_specs=[pl.BlockSpec(memory_space=pltpu.SMEM), whole((LEN, d)), weight, weight]
        + [col_block] * 3
        + [whole((LEN, 128))]
        + [whole((LEN, GROUP))] * 2
        + [whole((LEN, 128)), whole(segr.shape)],
        out_specs=[col_block] * 3,
        out_shape=[slab] * 3,
        scratch_shapes=[
            pltpu.VMEM((LEN, GROUP), BF16),
            pltpu.VMEM((LEN, GROUP), F32),
            pltpu.VMEM((LEN, GROUP), F32),
            pltpu.VMEM((LEN, GROUP), F32),
            pltpu.VMEM((blocks, rows, rows), F32),
        ],
        compiler_params=pltpu.CompilerParams(vmem_limit_bytes=VMEM_BYTES),
        name="attn_backward",
    )(key, g, own, sib, q, k, v, lse, cosine, sine, segc, segr)


class LineGather:
    def __init__(self, me, src, full, sems):
        self.me, self.src, self.full, self.sems = me, src, full, sems
        self.rows = src.shape[0]

    def spot(self, side, s):
        return self.full.at[side, pl.ds(pl.multiple_of(s * self.rows, self.rows), self.rows)]

    def to_line(self, src, s, way):
        device = self.me.up if way == 0 else self.me.down
        return remote(src, self.spot(0, s), self.sems.at[way, s], self.sems.at[3, s], device)

    def to_core(self, src, s):
        return remote(src, self.spot(1, s), self.sems.at[2, s], self.sems.at[4, s], self.me.other)

    def keep(self):
        return pltpu.make_async_copy(self.src, self.spot(0, self.me.z), self.sems.at[5, 0])

    def start(self):
        z, line = self.me.z, self.me.line

        @pl.when(z + 1 < line)
        def _():
            self.to_line(self.src, z, 0).start()

        @pl.when(z >= 1)
        def _():
            self.to_line(self.src, z, 1).start()

        self.to_core(self.src, z).start()
        self.keep().start()

    def hop(self, h):
        z, line = self.me.z, self.me.line
        for s, arrives, goes_on, way in (
            (z - h, z >= h, z + 1 < line, 0),
            (z + h, z + h < line, z >= 1, 1),
        ):

            @pl.when(arrives)
            def _(s=s, goes_on=goes_on, way=way):
                here = self.spot(0, s)
                self.to_line(here, s, way).wait_recv()

                @pl.when(goes_on)
                def _():
                    self.to_line(here, s, way).start()

                self.to_core(here, s).start()

    def arrived(self):
        self.keep().wait()
        for s in range(self.me.line):
            self.to_core(self.spot(0, s), s).wait_recv()

    def done(self):
        z, line = self.me.z, self.me.line
        for s in range(line):
            here = self.spot(0, s)
            self.to_core(here, s).wait_send()

            @pl.when((s <= z) & (z + 1 < line))
            def _(s=s, here=here):
                self.to_line(here, s, 0).wait_send()

            @pl.when((s >= z) & (z >= 1))
            def _(s=s, here=here):
                self.to_line(here, s, 1).wait_send()


class SquareGather:
    def __init__(self, me, full, sems):
        self.me, self.full, self.sems = me, full, sems
        self.rows = full.shape[0] // 4

    def copies(self):
        me, full, sems, rows = self.me, self.full, self.sems, self.rows
        half = rows // 2

        def part(first, size):
            return full.at[pl.ds(first, size)]

        return (
            remote(part(0, rows), part(rows, rows), sems.at[0], sems.at[1], me.x),
            remote(part(0, rows), part(2 * rows, rows), sems.at[2], sems.at[3], me.y),
            remote(part(rows, half), part(3 * rows, half), sems.at[4], sems.at[5], me.y),
            remote(
                part(2 * rows + half, half), part(3 * rows + half, half), sems.at[6], sems.at[7], me.x
            ),
        )

    def start(self):
        x, y, _, _ = self.copies()
        x.start()
        y.start()

    def forward(self):
        x, y, top, bottom = self.copies()
        x.wait_recv()
        top.start()
        y.wait_recv()
        bottom.start()

    def arrived(self):
        _, _, top, bottom = self.copies()
        top.wait_recv()
        bottom.wait_recv()

    def done(self):
        for copy in self.copies():
            copy.wait_send()


class SquareScatter:
    def __init__(self, me, stage, landed, sems):
        self.me, self.stage, self.landed, self.sems = me, stage, landed, sems
        self.half = stage.shape[1] // 2
        self.top, self.bottom = pl.ds(0, self.half), pl.ds(self.half, self.half)

    def copies(self):
        me, stage, landed, sems = self.me, self.stage, self.landed, self.sems
        top, bottom = self.top, self.bottom
        return (
            remote(stage.at[2, top], landed.at[2, top], sems.at[0], sems.at[1], me.y),
            remote(stage.at[2, bottom], landed.at[2, bottom], sems.at[2], sems.at[3], me.x),
            remote(stage.at[0, bottom], landed.at[0, bottom], sems.at[4], sems.at[5], me.x),
            remote(stage.at[1, top], landed.at[1, top], sems.at[6], sems.at[7], me.y),
            remote(stage.at[0, top], landed.at[0, top], sems.at[8], sems.at[9], me.x),
            remote(stage.at[1, bottom], landed.at[1, bottom], sems.at[10], sems.at[11], me.y),
        )

    def diagonal_ready(self):
        copies = self.copies()
        copies[0].start()
        copies[1].start()

    def sides_ready(self):
        copies = self.copies()
        copies[2].start()
        copies[3].start()

    def combine(self):
        copies = self.copies()
        for n, slot, at in ((0, 0, self.top), (1, 1, self.bottom)):
            copies[n].wait_recv()
            add_rows(self.stage, slot, at, self.landed)
            copies[4 + n].start()

    def arrived(self):
        for copy in self.copies()[2:]:
            copy.wait_recv()

    def done(self):
        for copy in self.copies():
            copy.wait_send()


def add_rows(stage, slot, at, landed):
    step = 32

    @pl.loop(0, at.size // step)
    def _(n):
        here = pl.ds(pl.multiple_of(at.start + n * step, step), step)
        total = stage[slot, here, :].astype(F32) + landed[2, here, :].astype(F32)
        stage[slot, here, :] = total.astype(BF16)


def remote(src, dst, send_sem, recv_sem, device):
    return pltpu.make_async_remote_copy(
        src_ref=src, dst_ref=dst, send_sem=send_sem, recv_sem=recv_sem, device_id=device,
        device_id_type=pl.DeviceIdType.MESH,
    )


class Place:
    def __init__(self, dp):
        index = lax.axis_index("dp")
        self.index, self.dp = index, dp
        self.line = dp // 2
        self.z, self.core = index // 2, index % 2
        self.at_end = (self.z == 0) | (self.z == self.line - 1)
        self.t = lax.axis_index("tensor")
        tx, ty = self.t % 2, self.t // 2
        self.other = {"dp": index + 1 - 2 * self.core}
        self.up, self.down = {"dp": index + 2}, {"dp": index - 2}
        self.next, self.far = {"dp": index + 2 - 4 * (self.z % 2)}, {"dp": index + 4 - 8 * (self.z // 2)}
        self.x = {"tensor": self.t + 1 - 2 * tx}
        self.y = {"tensor": self.t + 2 - 4 * ty}
        self.spots = [
            (tx if i % 2 == 0 else 1 - tx) + 2 * (ty if i // 2 == 0 else 1 - ty) for i in range(4)
        ]

    def window(self, i, rows, seg_col, seg_ref, bias_ref):
        spots = []
        for n in range(-(-(MOST - 1) // rows) + 1):
            j = jnp.maximum(i - n, 0)
            place = (j % 2 + self.t % 2) % 2 + 2 * ((j // 2 + self.t // 2) % 2)
            same = seg_col == seg_ref[place][0:1, :]
            if n == 0:
                row = lax.broadcasted_iota(jnp.int32, (rows, rows), 0)
                col = lax.broadcasted_iota(jnp.int32, (rows, rows), 1)
                bias_ref[n] = jnp.where(same & (col <= row), 0.0, NEG)
            else:
                bias_ref[n] = jnp.where(same, jnp.where(i >= n, 0.0, NEG), NEG)
            spots.append(pl.ds(pl.multiple_of(place * rows, rows), rows))
        return spots

    def greet(self):
        barrier = pltpu.get_barrier_semaphore()
        peers = [self.x, self.y] + [{"dp": (self.index + k) % self.dp} for k in range(1, self.dp)]
        for device in peers:
            pl.semaphore_signal(
                barrier, inc=1, device_id=device, device_id_type=pl.DeviceIdType.MESH
            )
        pl.semaphore_wait(barrier, len(peers))


def norm_rows(count, body, step=32):
    @pl.loop(0, count // step)
    def _(n):
        body(pl.ds(pl.multiple_of(n * step, step), step))


def attend(pair, first, at, spots, head_lane, q_ref, k_ref, v_ref, mixed_ref, lse_ref, bias_ref):
    lanes = pl.ds(pl.multiple_of(pair * 128, 128), 128)
    query = q_ref[at, lanes]
    outs, stats = [], []
    for h in range(2):
        mine = (head_lane < HEAD_DIM) if h == 0 else (head_lane >= HEAD_DIM)
        qm = jnp.where(mine, query, 0) * jnp.asarray(HEAD_DIM**-0.5, BF16)
        scores = [dot_nt(qm, k_ref[s, lanes]) + bias_ref[n] for n, s in enumerate(spots)]
        top = functools.reduce(jnp.maximum, [jnp.max(s, axis=1, keepdims=True) for s in scores])
        weights = [jnp.exp(s - top) for s in scores]
        total = sum(jnp.sum(w, axis=1, keepdims=True) for w in weights)
        out = sum(dot_nn(w.astype(BF16), v_ref[s, lanes]) for w, s in zip(weights, spots))
        outs.append(out / total)
        stats.append(top + jnp.log(total))
    mixed_ref[at, lanes] = jnp.where(head_lane < HEAD_DIM, outs[0], outs[1]).astype(BF16)
    kept = jnp.where(pair + first == 0, 0.0, lse_ref[at, :])
    for h in range(2):
        kept = jnp.where(head_lane == first + pair * 2 + h, stats[h], kept)
    lse_ref[at, :] = kept


def add_into(total, other, rows, step=64):
    @pl.loop(0, rows // step)
    def _(n):
        at = pl.ds(pl.multiple_of(n * step, step), step)
        total[at, :] = (total[at, :].astype(F32) + other[at, :].astype(F32)).astype(total.dtype)


class LineScatter:
    def __init__(self, me, rows, mine, theirs, swapped, kept, landed, work, sems):
        cut = lambda ref: ref.at[:, pl.ds(0, rows)]
        self.me, self.rows = me, rows
        self.mine, self.theirs, self.swapped = cut(mine), cut(theirs), cut(swapped)
        self.kept, self.landed, self.work = cut(kept), cut(landed), cut(work)
        self.sems = sems

    def swap(self):
        return remote(
            self.theirs, self.swapped, self.sems.at[0], self.sems.at[1], self.me.other
        )

    def keep(self):
        return pltpu.make_async_copy(self.mine, self.kept, self.sems.at[2])

    def send(self, src, s, upward, z):
        line = self.me.line
        if upward:
            slot, device = s, self.me.up
        else:
            slot, device = (s if s < z - 1 else line), self.me.down
        return remote(
            src, self.landed.at[slot], self.sems.at[3 + s], self.sems.at[3 + line + slot], device
        )

    def landing(self, slot):
        line = self.me.line
        return remote(
            self.landed.at[slot], self.landed.at[slot], self.sems.at[3],
            self.sems.at[3 + line + slot], self.me.other,
        )

    def load(self, src, n):
        return pltpu.make_async_copy(src, self.work.at[n], self.sems.at[4 + 2 * self.me.line + n])

    def reduce(self, free_sem):
        line = self.me.line
        self.swap().wait_recv()
        for s in range(line):
            add_into(self.mine.at[s], self.swapped.at[s], self.rows)
        pl.semaphore_signal(
            free_sem, inc=1, device_id=self.me.other, device_id_type=pl.DeviceIdType.MESH
        )
        self.keep().start()
        self.swap().wait_send()
        self.keep().wait()
        for end, upward in ((0, True), (line - 1, False)):

            @pl.when(self.me.z == end)
            def _(end=end, upward=upward):
                order = range(line - 1, end, -1) if upward else range(end)
                for s in order:
                    self.send(self.kept.at[s], s, upward, end).start()

    def going(self, p):
        line = self.me.line
        for z, upward in ((p, True), (line - 1 - p, False)):
            targets = list(range(line - 1, z, -1)) if upward else list(range(z))
            yield z, upward, targets

    def run_phase(self, p, first):
        for z, upward, targets in self.going(p):

            @pl.when(self.me.z == z)
            def _(z=z, upward=upward, targets=targets):
                for n, s in enumerate(targets):
                    self.load(self.kept.at[s], first + 2 * n + 1).start()
                for n, s in enumerate(targets):
                    a, b = first + 2 * n, first + 2 * n + 1
                    self.landing(s).wait_recv()
                    self.load(self.landed.at[s], a).start()
                    self.load(self.kept.at[s], b).wait()
                    self.load(self.landed.at[s], a).wait()
                    add_into(self.work.at[a], self.work.at[b], self.rows)
                    self.send(self.work.at[a], s, upward, z).start()

    def sent_phase(self, p, first):
        for z, upward, targets in self.going(p):

            @pl.when(self.me.z == z)
            def _(z=z, upward=upward, targets=targets):
                for n, s in enumerate(targets):
                    self.send(self.work.at[first + 2 * n], s, upward, z).wait_send()

    def load_last(self, first):
        me = self.me
        self.load(self.kept.at[me.z], first).start()

        @pl.when(me.z >= 1)
        def _():
            self.landing(me.z).wait_recv()
            self.load(self.landed.at[me.z], first + 1).start()

        @pl.when(me.z < me.line - 1)
        def _():
            self.landing(me.line).wait_recv()
            self.load(self.landed.at[me.line], first + 2).start()

    def run_last(self, first, total):
        me = self.me
        here = total.at[pl.ds(0, self.rows)]
        self.load(self.kept.at[me.z], first).wait()

        def put(n, step=64):
            @pl.loop(0, self.rows // step)
            def _(i):
                at = pl.ds(pl.multiple_of(i * step, step), step)
                if n == first:
                    here[at, :] = self.work[n, at, :].astype(F32)
                else:
                    here[at, :] += self.work[n, at, :].astype(F32)

        put(first)

        @pl.when(me.z >= 1)
        def _():
            self.load(self.landed.at[me.z], first + 1).wait()
            put(first + 1)

        @pl.when(me.z < me.line - 1)
        def _():
            self.load(self.landed.at[me.line], first + 2).wait()
            put(first + 2)

    def done(self):
        line = self.me.line
        for end, upward in ((0, True), (line - 1, False)):

            @pl.when(self.me.z == end)
            def _(end=end, upward=upward):
                for s in range(line - 1, end, -1) if upward else range(end):
                    self.send(self.kept.at[s], s, upward, end).wait_send()


WORK_SLOTS = (0, 4, 8, 10)


class Ticks:
    def __init__(self, chunks, total, writers, held):
        self.chunks, self.total, self.writers, self.held = chunks, total, writers, held
        self.k, self.second, self.last, self.written = 0, 0, 0, 0
        self.sent = [None] * len(WORK_SLOTS)

    def run(self, chunk, p, group):
        first = WORK_SLOTS[group]
        if self.sent[group] is not None:
            self.sent[group].sent_phase(p, first)
        chunk.run_phase(p, first)
        self.sent[group] = chunk

    def finish(self, n):
        self.chunks[n].load_last(12)
        if n > 0:
            self.writers[n - 1].wait()
        self.chunks[n].run_last(12, self.total)
        self.writers[n].start()

    def tick(self, most=2):
        k, count = self.k, len(self.chunks)
        if k < count:
            self.run(self.chunks[k], 1, k % 2)
        ready, done = min(k, count), self.second
        if k >= self.held:
            for _ in range(most):
                if self.second < ready:
                    self.run(self.chunks[self.second], 2, 2 + self.second % 2)
                    self.second += 1
            for _ in range(most):
                if self.last < done:
                    self.finish(self.last)
                    self.last += 1
        self.k += 1

    def rest(self):
        while self.last < len(self.chunks):
            self.tick(3)

    def done(self):
        self.writers[-1].wait()
        for group, p in ((0, 1), (1, 1), (2, 2), (3, 2)):
            self.sent[group].sent_phase(p, WORK_SLOTS[group])
        for chunk in self.chunks:
            chunk.done()


class Writer:
    def __init__(self, total, turned, parts, sem):
        self.total, self.turned, self.parts, self.sem = total, turned, parts, sem

    def copies(self):
        for n, (dst, _) in enumerate(self.parts):
            yield pltpu.make_async_copy(self.turned.at[n], dst, self.sem.at[n])

    def start(self):
        for n, (_, flip) in enumerate(self.parts):
            block = self.total[pl.ds(n * 256, 256), :]
            self.turned[n] = (block.T if flip else block).astype(BF16)
        for copy in self.copies():
            copy.start()

    def wait(self):
        for copy in self.copies():
            copy.wait()


def norm_back_rows(count, gain, values_of, grads_of, gain_ref, row, put, step=32):
    @pl.loop(0, count // step)
    def _(n):
        at = pl.ds(pl.multiple_of(n * step, step), step)
        values, grads = values_of(at), grads_of(at)
        factor = norm_factor(values)
        scaled = grads * gain
        back = factor * scaled - values * factor * factor * factor * jnp.mean(
            scaled * values, axis=-1, keepdims=True
        )
        gain_ref[row : row + 1, :] += jnp.sum(grads * values * factor, axis=0, keepdims=True)
        put(at, back)


def attend_back(
    pair, at, spots, head_lane, q_ref, k_ref, v_ref, dm_ref, lse_ref, bias_ref, dqa_ref, dka_ref, dva_ref
):
    scale = HEAD_DIM**-0.5
    rows = at.size
    lanes = pl.ds(pl.multiple_of(pair * 128, 128), 128)
    query, grad = q_ref[at, lanes], dm_ref[at, lanes]
    logs = lse_ref[at, :]
    outs = []
    for h in range(2):
        mine = (head_lane < HEAD_DIM) if h == 0 else (head_lane >= HEAD_DIM)
        qm = jnp.where(mine, query, 0) * jnp.asarray(scale, BF16)
        gm = jnp.where(mine, grad, 0)
        log = jnp.sum(
            jnp.where(head_lane == pair * 2 + h, logs, 0.0), axis=1, keepdims=True
        )
        weights = [
            jnp.exp(dot_nt(qm, k_ref[s, lanes]) + bias_ref[n] - log) for n, s in enumerate(spots)
        ]
        grads = [dot_nt(gm, v_ref[s, lanes]) for s in spots]
        inner = sum(jnp.sum(w * g, axis=1, keepdims=True) for w, g in zip(weights, grads))
        dq = jnp.zeros((rows, 128), F32)
        for w, g, s in zip(weights, grads, spots):
            ds = (w * (g - inner)).astype(BF16)
            dva_ref[s, lanes] += dot_tn(w.astype(BF16), gm)
            dka_ref[s, lanes] += dot_tn(ds, qm)
            dq = dq + dot_nn(ds, k_ref[s, lanes])
        outs.append(dq)
    dqa_ref[:, lanes] = jnp.where(head_lane < HEAD_DIM, outs[0], outs[1]) * scale


TICK_AFTER = (2, 3, 5, 6)
TICK_HELD = 3


def layer_kernel(
    dp, x_in, g_in, gain_ref, wq_in, wk_in, wv_in, wo_in, gate_in, up_in, down_in, cos_all, sin_all,
    segc_all, segr_all,
    output_out, input_grad_out, gain_out, gate_out, up_out, down_out, q_out, k_out, v_out, o_out,
    wa_full, wo_full, wf_full, hidden_all, kept_all, landed_all, y_all, normed_all, q_all, k_all, v_all,
    mixed_all, lse_all,
    x_ref, wa_src, wo_src, wf_src, gains_full, rows_a, rows_m, rows_g,
    theirs, swapped, mine, work, total, turned, stage, landed, own, gm, middle, gp, gp_landed,
    sem_in, sem_gains, sem_a, sem_o, sem_f, sem_n, sem_m, sem_g, sem_g2, sem_s, sem_line, sem_write,
    sem_gain, sem_c, sem_w, free_core, free_x, free_y,
):
    me = Place(dp)
    line = me.line
    d = x_in.shape[1]
    half, local = d // 2, x_in.shape[0]
    shard = half // line
    rows = LEN // 4
    blocks = wf_src.shape[0]
    fw = wf_src.shape[2] // 3
    cols = wq_in.shape[1]
    groups = cols // GROUP

    def at_block(b):
        return pl.ds(pl.multiple_of(b * rows, rows), rows)

    def true_columns(side, s):
        core = me.core if side == 0 else 1 - me.core
        return pl.ds(pl.multiple_of((2 * s + core) * shard, shard), shard)

    def own_columns(side, s):
        return pl.ds(side * half + s * shard, shard)

    sides = [(side, s) for side in range(2) for s in range(line)]
    x_loads = [
        pltpu.make_async_copy(
            x_in.at[:, true_columns(*p)], x_ref.at[:, own_columns(*p)], sem_in.at[n]
        )
        for n, p in enumerate(sides)
    ]
    g_loads = [
        pltpu.make_async_copy(
            g_in.at[:, true_columns(*p)], rows_g.at[pl.ds(0, local), own_columns(*p)],
            sem_in.at[2 * line + n],
        )
        for n, p in enumerate(sides)
    ]
    first_sem = 4 * line
    a_loads = [
        pltpu.make_async_copy(ref, wa_src.at[:, pl.ds(n * cols, cols)], sem_in.at[first_sem + n])
        for n, ref in enumerate((wq_in, wk_in, wv_in))
    ]
    f_loads = [
        pltpu.make_async_copy(
            ref.at[:, pl.ds(n * fw, fw)], wf_src.at[n, :, pl.ds(part * fw, fw)],
            sem_in.at[first_sem + 3 + 2 * n + part],
        )
        for n in range(blocks)
        for part, ref in enumerate((gate_in, up_in))
    ]
    for copy in a_loads + x_loads + g_loads + f_loads:
        copy.start()
    gains_full[0, pl.ds(pl.multiple_of(me.z * 16, 16), 16), :] = gain_ref[...]
    me.greet()

    def gain_copy(k, sender):
        place = gains_full.at[k % 2, pl.ds(pl.multiple_of(sender // 2 * 16, 16), 16)]
        return remote(
            gain_ref, place, sem_gains.at[0, k], sem_gains.at[1, k], {"dp": (me.index + k) % dp}
        )

    for k in range(1, dp):
        gain_copy(k, me.index).start()

    wa = LineGather(me, wa_src, wa_full, sem_a)
    wo = LineGather(me, wo_src, wo_full, sem_o)
    gathers = [LineGather(me, wf_src.at[n], wf_full.at[n], sem_f.at[n]) for n in range(blocks)]
    order = [wa, wo] + gathers

    def start_all():
        for one in gathers:
            one.start()

    acts = []
    for n, one in enumerate(order):
        for h in range(1, line):

            def act(n=n, one=one, h=h):
                one.hop(h)
                if h == 2 and n == 0:
                    wo.start()
                    pl.when(me.at_end)(start_all)
                if n == 1 and h <= 2:
                    pl.when(jnp.logical_not(me.at_end))(gathers[h - 1].start)
                if h == 1 and 2 <= n < blocks:
                    pl.when(jnp.logical_not(me.at_end))(order[n + 2].start)

            acts.append(act)

    def poll(count=1):
        for _ in range(min(count, len(acts))):
            acts.pop(0)()

    def hops_done(n):
        return len(acts) <= (blocks - 1 - n) * (line - 1)

    for copy in a_loads:
        copy.wait()
    wa.start()
    for k in range(1, dp):
        gain_copy(k, (me.index + dp - k) % dp).wait_recv()
    for copy in x_loads:
        copy.wait()

    def gain_row(which):
        return jnp.concatenate(
            [
                gains_full[side, pl.ds(s * 16 + which, 1), :].astype(F32)
                for side in range(2)
                for s in range(line)
            ],
            axis=1,
        )

    gain_one, gain_two = gain_row(0), gain_row(1)

    def first_norm(at):
        values = x_ref[at, :].astype(F32)
        rows_a[at, :] = (values * norm_factor(values) * gain_one).astype(BF16)

    norm_rows(local, first_norm)
    normed = SquareGather(me, rows_a, sem_n)
    grads = SquareGather(me, rows_g, sem_g)
    normed_mlp = SquareGather(me, rows_m, sem_m)
    square = SquareGather(me, rows_a, sem_g2)
    scatter = SquareScatter(me, stage, landed, sem_s)
    normed.start()
    for n in range(cols // 256):
        wo_src[:, pl.ds(n * 256, 256)] = wo_in[pl.ds(n * 256, 256), :].T
    for n in range(blocks):
        wf_src[n, :, pl.ds(2 * fw, fw)] = down_in[pl.ds(n * fw, fw), :].T
    for copy in f_loads:
        copy.wait()
    poll()
    for copy in g_loads:
        copy.wait()
    normed.forward()
    grads.start()
    poll(line - 2)
    normed.arrived()
    wa.arrived()

    def free_landed():
        for device, sem in ((me.x, free_x), (me.y, free_y)):
            pl.semaphore_signal(
                sem, inc=1, device_id=device, device_id_type=pl.DeviceIdType.MESH
            )

    def wait_free():
        pl.semaphore_wait(free_x, 1)
        pl.semaphore_wait(free_y, 1)

    def summed(at):
        return own[at, :] + landed[0, at, :].astype(F32) + landed[1, at, :].astype(F32)

    def doubled(ref, at):
        part = ref[at, :]
        return jnp.concatenate([part] * (GROUP // 128), axis=1)

    head_lane = lax.broadcasted_iota(jnp.int32, (rows, 128), 1)

    def forward(
        wa_v, wo_v, q_ref, k_ref, v_ref, mixed_ref, mixed_t, lse_ref, cos_ref, sin_ref, segc_ref, segr_ref, bias_ref
    ):
        ins = [(cos_all, cos_ref), (sin_all, sin_ref), (segc_all, segc_ref), (segr_all, segr_ref)] + [
            (wa_full.at[side], wa_v.at[pl.ds(side * half, half)]) for side in range(2)
        ]
        loads = [pltpu.make_async_copy(a, b, sem_c.at[n]) for n, (a, b) in enumerate(ins)]
        for copy in loads:
            copy.start()
        for copy in loads:
            copy.wait()

        @pl.loop(0, 4 * groups)
        def _(n):
            b, group = n // groups, n % groups
            at = at_block(b)
            lanes = pl.ds(pl.multiple_of(group * GROUP, GROUP), GROUP)
            cosine, sine = doubled(cos_ref, at), doubled(sin_ref, at)

            def product(part):
                here = pl.ds(pl.multiple_of(part * cols + group * GROUP, GROUP), GROUP)
                return dot_nn(rows_a[at, :], wa_v[:, here])

            query = product(0)
            q_ref[at, lanes] = (query * cosine + swap_halves(query) * sine).astype(BF16)
            keys = product(1)
            k_ref[at, lanes] = (keys * cosine + swap_halves(keys) * sine).astype(BF16)
            v_ref[at, lanes] = product(2).astype(BF16)

        outs = [(q_ref, q_all), (k_ref, k_all), (v_ref, v_all), (rows_a, normed_all)]
        stores = [pltpu.make_async_copy(a, b, sem_c.at[n]) for n, (a, b) in enumerate(outs)]
        for copy in stores:
            copy.start()
        poll(2)
        for i in range(4):
            places = [(j, me.spots[j]) for j in key_blocks(i, rows)]
            at = at_block(me.spots[i])
            fill_bias(bias_ref, segc_ref[at, 0:1], segr_ref, i, places)
            spots = [at_block(p) for _, p in places]

            @pl.loop(0, cols // 128)
            def _(pair, at=at, spots=spots):
                attend(pair, 0, at, spots, head_lane, q_ref, k_ref, v_ref, mixed_ref, lse_ref, bias_ref)

            if i == 0:
                poll(line - 3)
            if i == 1:
                grads.forward()
            if i == 2:
                wo.arrived()
                wo_load = [
                    pltpu.make_async_copy(wo_full.at[side], wo_v.at[pl.ds(side * half, half)], sem_w.at[0, side])
                    for side in range(2)
                ]
                for copy in wo_load:
                    copy.start()
                poll()
        mixed_t[...] = mixed_ref[...].T
        for n, (a, b) in enumerate(((mixed_t, mixed_all), (lse_ref, lse_all))):
            stores.append(pltpu.make_async_copy(a, b, sem_c.at[len(outs) + n]))
            stores[-1].start()
        for copy in wo_load:
            copy.wait()

        def out_rows(b, slot):
            at = pl.ds(b * rows, rows)
            wide = d // 4

            @pl.loop(0, 4)
            def _(n):
                here = pl.ds(pl.multiple_of(n * wide, wide), wide)
                value = dot_nt(mixed_ref[at, :], wo_v[here, :])
                if slot is None:
                    own[:, here] = value
                else:
                    stage[slot, :, here] = value.astype(BF16)

        out_rows(3, 2)
        scatter.diagonal_ready()
        out_rows(1, 0)
        out_rows(2, 1)
        scatter.sides_ready()
        out_rows(0, None)
        poll(2)
        scatter.combine()
        poll(2)
        for copy in stores:
            copy.wait()
        normed.done()
        scatter.arrived()

    V = pltpu.VMEM
    slab = V((LEN, cols), BF16)
    table, wide_table = V((LEN, 128), F32), V((LEN, GROUP), F32)
    bias = V((3, rows, rows), F32)
    segs = (V(segc_all.shape, jnp.int32), V(segr_all.shape, jnp.int32))
    pl.run_scoped(
        forward, V((d, 3 * cols), BF16), V((d, cols), BF16), slab, slab, slab, slab, V((cols, LEN), BF16), table, table, table,
        *segs, bias,
    )

    def second_norm(at):
        values = x_ref[at, :].astype(F32) + summed(at)
        middle[at, :] = values
        rows_m[at, :] = (values * norm_factor(values) * gain_two).astype(BF16)

    norm_rows(local, second_norm)
    normed_mlp.start()
    free_landed()
    scatter.done()
    poll(2)
    grads.arrived()

    sizes = [3 * fw] * blocks + [cols] + [3 * GROUP] * groups
    chunks = [
        LineScatter(me, size, mine, theirs, swapped, kept_all.at[n], landed_all.at[n], work, sem_line.at[n])
        for n, size in enumerate(sizes)
    ]
    writers = []
    for n in range(blocks):
        here = pl.ds(n * fw, fw)
        parts = [(gate_out.at[:, here], True), (up_out.at[:, here], True), (down_out.at[here], False)]
        writers.append(Writer(total, turned, parts, sem_write.at[n]))
    parts = [(o_out.at[pl.ds(n * 256, 256)], False) for n in range(cols // 256)]
    writers.append(Writer(total, turned, parts, sem_write.at[blocks]))
    for n in range(groups):
        here = pl.ds(n * GROUP, GROUP)
        parts = [(ref.at[:, here], True) for ref in (q_out, k_out, v_out)]
        writers.append(Writer(total, turned, parts, sem_write.at[blocks + 1 + n]))
    ticks = Ticks(chunks, total, writers, TICK_HELD)

    def swap(n):
        if n >= 1:
            pl.semaphore_wait(free_core, 1)
        chunks[n].swap().start()

    def products(left, right, first, size):
        @pl.loop(0, line)
        def _(s):
            for side, dst in ((0, mine), (1, theirs)):
                here = pl.ds(pl.multiple_of(side * half + s * shard, shard), shard)
                dst[s, pl.ds(first, size), :] = dot_nn(left[...], right[:, here]).astype(BF16)

    def mlp(wb, sums, dgu_t, hid_t, hid):
        def weights(n):
            return [
                pltpu.make_async_copy(
                    wf_full.at[n, side], wb.at[n % 2, pl.ds(side * half, half)], sem_w.at[n % 2, side]
                )
                for side in range(2)
            ]

        def hidden_copy(n):
            return pltpu.make_async_copy(hid.at[n % 2], hidden_all.at[n], sem_c.at[n % 2])

        fetched = [False] * (blocks + 1)

        def to_stage(b, slot):
            @pl.loop(0, rows // 64)
            def _(i):
                at = pl.ds(pl.multiple_of(i * 64, 64), 64)
                there = pl.ds(pl.multiple_of(b * rows + i * 64, 64), 64)
                if slot is None:
                    own[at, :] = sums[there, :]
                else:
                    stage[slot, at, :] = sums[there, :].astype(BF16)

        def fetch(n):
            if n < blocks and not fetched[n]:
                while not hops_done(n):
                    poll()
                gathers[n].arrived()
                for copy in weights(n):
                    copy.start()
                fetched[n] = True

        for n in range(blocks):
            fetch(n)
            if n == 0:

                @pl.loop(0, LEN // 64)
                def _(i):
                    at = pl.ds(pl.multiple_of(i * 64, 64), 64)
                    sums[at, :] = jnp.zeros((64, d), F32)

            for copy in weights(n):
                copy.wait()
            if n == 1:
                chunks[0].reduce(free_core)
            if n + 1 < blocks and hops_done(n + 1):
                fetch(n + 1)
            if n >= 2:
                hidden_copy(n - 2).wait()
            w = wb.at[n % 2]
            gu_w, down_w = w.at[:, pl.ds(0, 2 * fw)], w.at[:, pl.ds(2 * fw, fw)]

            def one_block(r, n=n, gu_w=gu_w, down_w=down_w):
                at = at_block(r)
                gu = dot_nn(rows_m[at, :], gu_w[...])
                grad_hidden = dot_nn(rows_g[at, :], down_w[...])
                gate_pre, upward = gu[:, :fw], gu[:, fw:]
                sig = jax.nn.sigmoid(gate_pre)
                activated = gate_pre * sig
                hidden = (activated * upward).astype(BF16)
                hid[n % 2, at, :] = hidden
                hid_t[:, at] = hidden.T
                grad_gate = grad_hidden * upward * sig * (1.0 + gate_pre * (1.0 - sig))
                grad_up = grad_hidden * activated
                dgu = jnp.concatenate([grad_gate, grad_up], axis=1).astype(BF16)
                dgu_t[:, at] = dgu.T

                @pl.loop(0, 4)
                def _(c):
                    here = pl.ds(pl.multiple_of(c * (half // 2), half // 2), half // 2)
                    sums[at, here] += dot_nt(dgu, gu_w[here, :])

            if n == 0:
                one_block(0)
                poll()
                normed_mlp.forward()
                pl.loop(1, 3)(one_block)
                normed_mlp.arrived()
                one_block(3)
                poll()
            elif n == blocks - 1:
                wait_free()
                one_block(3)
                to_stage(3, 2)
                scatter.diagonal_ready()
                one_block(1)
                to_stage(1, 0)
                one_block(2)
                to_stage(2, 1)
                scatter.sides_ready()
                one_block(0)
                to_stage(0, None)
            else:
                pl.loop(0, 4)(one_block)
            hidden_copy(n).start()
            poll()
            if n >= 2:
                chunks[n - 1].reduce(free_core)
            products(dgu_t, rows_m, 0, 2 * fw)
            products(hid_t, rows_g, 2 * fw, fw)
            swap(n)
            poll()
            if n in TICK_AFTER:
                ticks.tick()
        for n in range(max(0, blocks - 2), blocks):
            hidden_copy(n).wait()

    pl.run_scoped(
        mlp, V((2, d, 3 * fw), BF16), V((LEN, d), F32), V((2 * fw, LEN), BF16), V((fw, LEN), BF16),
        V((2, LEN, fw), BF16),
    )
    gp[...] = jnp.zeros(gp.shape, F32)

    def down(hidden, dw, rest):
        ins = [(hidden_all.at[n], hidden.at[:, pl.ds(n * fw, fw)]) for n in range(blocks)] + [
            (
                wf_full.at[n, side, :, pl.ds(2 * fw, fw)],
                dw.at[pl.ds(side * half, half), pl.ds(n * fw, fw)],
            )
            for n in range(blocks)
            for side in range(2)
        ]
        loads = [pltpu.make_async_copy(a, b, sem_c.at[n]) for n, (a, b) in enumerate(ins)]
        for copy in loads:
            copy.start()
        scatter.combine()
        for copy in loads:
            copy.wait()

        @pl.loop(0, 4)
        def _(b):
            at = at_block(b)

            @pl.loop(0, 4)
            def _(c):
                here = pl.ds(pl.multiple_of(c * (d // 4), d // 4), d // 4)
                rest[b, :, here] = dot_nt(hidden[at, :], dw[here, :]).astype(BF16)

        out = pltpu.make_async_copy(rest, y_all, sem_c.at[0])
        out.start()
        out.wait()

    pl.run_scoped(
        down, V((LEN, blocks * fw), BF16), V((d, blocks * fw), BF16), V((4, local, d), BF16)
    )
    normed_mlp.done()
    grads.done()

    def attention(
        q_ref, k_ref, v_ref, mixed_t, lse_ref, cos_ref, sin_ref, segc_ref, segr_ref, out_w,
        dqa_ref, dka_ref, dva_ref, part_t, bias_ref,
    ):
        ins = [
            (q_all, q_ref), (k_all, k_ref), (v_all, v_ref), (lse_all, lse_ref), (cos_all, cos_ref),
            (sin_all, sin_ref), (segc_all, segc_ref), (segr_all, segr_ref), (wo_full, out_w),
            (mixed_all, mixed_t), (normed_all, rows_m),
        ]
        loads = [pltpu.make_async_copy(a, b, sem_c.at[n]) for n, (a, b) in enumerate(ins)]
        for copy in loads:
            copy.start()
        scatter.arrived()

        def second_norm_back(at, back):
            grad = rows_g[at, :].astype(F32) + back
            gm[at, :] = grad
            rows_a[at, :] = grad.astype(BF16)

        norm_back_rows(local, gain_two, lambda at: middle[at, :], summed, gp, 1, second_norm_back)
        square.start()
        free_landed()
        scatter.done()
        stage_in = [
            pltpu.make_async_copy(y_all.at[b], stage.at[slot], sem_w.at[n // 2, n % 2])
            for n, (b, slot) in enumerate(((3, 2), (1, 0), (2, 1)))
        ]
        for copy in stage_in:
            copy.start()
        chunks[blocks - 1].reduce(free_core)
        ticks.tick()
        for copy in loads:
            copy.wait()

        @pl.loop(0, 4)
        def _(b):
            at = at_block(b)
            dka_ref[at, :] = jnp.zeros((rows, cols), F32)
            dva_ref[at, :] = jnp.zeros((rows, cols), F32)

        dm_ref = rows_g.at[:, pl.ds(3 * cols, cols)]

        def query_block(p, between=lambda: None):
            at = pl.ds(p * rows, rows)
            dm_ref[at, :] = (
                dot_nn(rows_a[at, :half], out_w[0]) + dot_nn(rows_a[at, half:], out_w[1])
            ).astype(BF16)
            spots = me.window(me.spots[p], rows, segc_ref[at, 0:1], segr_ref, bias_ref)

            def one_pair(pair):
                attend_back(
                    pair, at, spots, head_lane, q_ref, k_ref, v_ref, dm_ref, lse_ref, bias_ref,
                    dqa_ref, dka_ref, dva_ref,
                )

            middle_pair = cols // 256
            pl.loop(0, middle_pair)(one_pair)
            between()
            pl.loop(middle_pair, cols // 128)(one_pair)
            for group in range(groups):
                lanes = pl.ds(group * GROUP, GROUP)
                value = dqa_ref[:, lanes]
                value = value * doubled(cos_ref, at) - swap_halves(value) * doubled(sin_ref, at)
                rows_g[at, lanes] = value.astype(BF16)

        query_block(0)
        ticks.tick()
        square.forward()
        query_block(1)
        query_block(2)
        ticks.tick()
        for copy in stage_in:
            copy.wait()
        wait_free()
        square.arrived()
        scatter.diagonal_ready()
        scatter.sides_ready()
        products(mixed_t, rows_a, 0, cols)
        swap(blocks)
        query_block(3, lambda: chunks[blocks].reduce(free_core))

        def turn(group):
            @pl.loop(0, 4)
            def _(b):
                at = at_block(b)
                cosine, sine = doubled(cos_ref, at), doubled(sin_ref, at)
                for part, ref in enumerate((None, dka_ref, dva_ref)):
                    lanes = pl.ds(group * GROUP, GROUP)
                    there = pl.ds(part * cols + group * GROUP, GROUP)
                    if part == 0:
                        value = rows_g[at, there]
                    else:
                        value = ref[at, lanes]
                        if part == 1:
                            value = value * cosine - swap_halves(value) * sine
                        value = value.astype(BF16)
                        rows_g[at, there] = value
                    part_t[pl.ds(part * GROUP, GROUP), at] = value.T

        for group in range(groups):
            turn(group)
            if group > 0:
                chunks[blocks + group].reduce(free_core)
            products(part_t, rows_m, 0, 3 * GROUP)
            swap(blocks + 1 + group)
            if group == 0:
                scatter.combine()
                ticks.tick()

    pl.run_scoped(
        attention, slab, slab, slab, V((cols, LEN), BF16), table, table, table, *segs,
        V(wo_full.shape, BF16), V((rows, cols), F32), V((LEN, cols), F32), V((LEN, cols), F32),
        V((3 * GROUP, LEN), BF16), bias,
    )

    def normed_grads(qkv_w, stage_two, y_mine):
        ins = [(wa_full.at[side], qkv_w.at[pl.ds(side * half, half)]) for side in range(2)]
        ins.append((y_all.at[0], y_mine))
        loads = [pltpu.make_async_copy(a, b, sem_c.at[n]) for n, (a, b) in enumerate(ins)]
        for copy in loads:
            copy.start()
        chunks[blocks + groups].reduce(free_core)
        ticks.tick()
        for copy in loads:
            copy.wait()

        def normed_grad(b, slot):
            at = pl.ds(b * rows, rows)
            wide = d // 4

            @pl.loop(0, 4)
            def _(n):
                here = pl.ds(pl.multiple_of(n * wide, wide), wide)
                value = dot_nt(rows_g[at, pl.ds(0, 3 * cols)], qkv_w[here, :])
                if slot is None:
                    own[:, here] = value
                else:
                    stage_two[slot, :, here] = value.astype(BF16)

        for b, slot in ((3, 2), (1, 0), (2, 1), (0, None)):
            normed_grad(b, slot)
        scatter.arrived()

        def output_rows(at):
            value = middle[at, :] + y_mine[at, :].astype(F32)
            value = value + landed[0, at, :].astype(F32) + landed[1, at, :].astype(F32)
            y_mine[at, :] = value.astype(BF16)

        norm_rows(local, output_rows)
        free_landed()
        results = [
            pltpu.make_async_copy(
                y_mine.at[:, own_columns(*p)], output_out.at[:, true_columns(*p)], sem_in.at[n]
            )
            for n, p in enumerate(sides)
        ]
        for copy in results:
            copy.start()
        scatter.done()
        wait_free()
        scatter_two = SquareScatter(me, stage_two, landed, sem_s)
        scatter_two.diagonal_ready()
        scatter_two.sides_ready()
        for copy in results:
            copy.wait()
        ticks.tick(3)
        scatter_two.combine()
        ticks.tick(3)
        ticks.tick(3)
        scatter_two.arrived()
        scatter_two.done()

    pl.run_scoped(
        normed_grads, V((d, 3 * cols), BF16), V((3, local, d), BF16), V((local, d), BF16)
    )

    def first_norm_back(at, back):
        gm[at, :] += back

    norm_back_rows(
        local, gain_one, lambda at: x_ref[at, :].astype(F32), summed, gp, 0, first_norm_back
    )
    results = [
        pltpu.make_async_copy(
            gm.at[:, own_columns(*p)], input_grad_out.at[:, true_columns(*p)], sem_in.at[n]
        )
        for n, p in enumerate(sides)
    ]
    for copy in results:
        copy.start()
    exchange = [
        remote(gp, gp_landed.at[n], sem_gain.at[n, 0], sem_gain.at[n, 1], device)
        for n, device in enumerate((me.x, me.y, me.other, me.next, me.far))
    ]

    def add_gains(n):
        exchange[n].wait()
        if n == 2:
            gp[:, :half] += gp_landed[n, :, half:]
            gp[:, half:] += gp_landed[n, :, :half]
        else:
            gp[...] += gp_landed[n]

    for n in range(3):
        exchange[n].start()
        add_gains(n)
    exchange[3].start()
    ticks.rest()
    add_gains(3)
    exchange[4].start()
    add_gains(4)
    gain_out[...] = gp[...]
    ticks.done()
    pl.semaphore_wait(free_core, 1)
    for k in range(1, dp):
        gain_copy(k, me.index).wait_send()
    for copy in results:
        copy.wait()
    for one in [wa, wo, square] + gathers:
        one.done()


def layer(dp, x, g, gains, wq, wk, wv, wo, gate, up, down, cosine, sine, segc, segr):
    line = dp // 2
    local, d = x.shape
    cols, ff = wq.shape[1], gate.shape[1]
    blocks, shard = FF_BLOCKS, d // dp
    fw = ff // blocks
    groups = cols // GROUP
    count = blocks + 1 + groups
    most = max(3 * fw, cols, 3 * GROUP)
    vm, hbm = pl.BlockSpec(memory_space=pltpu.VMEM), pl.BlockSpec(memory_space=pl.ANY)
    S, V, dma = jax.ShapeDtypeStruct, pltpu.VMEM, pltpu.SemaphoreType.DMA
    regular = pltpu.SemaphoreType.REGULAR
    slab = S((LEN, cols), BF16)
    piece = V((line, most, shard), BF16)
    return pl.pallas_call(
        functools.partial(layer_kernel, dp),
        in_specs=[hbm, hbm, vm, hbm, hbm, hbm, vm, hbm, hbm, vm, hbm, hbm, hbm, hbm],
        out_specs=[hbm, hbm, vm] + [hbm] * 20,
        out_shape=[
            S((local, d), BF16), S((local, d), F32), S((8, d), F32),
            S((shard, ff), BF16), S((shard, ff), BF16), S((ff, shard), BF16),
            S((shard, cols), BF16), S((shard, cols), BF16), S((shard, cols), BF16), S((cols, shard), BF16),
            S((2, d // 2, 3 * cols), BF16), S((2, d // 2, cols), BF16),
            S((blocks, 2, d // 2, 3 * fw), BF16), S((blocks, LEN, fw), BF16),
            S((count, line, most, shard), BF16), S((count, line + 1, most, shard), BF16),
            S((4, local, d), BF16), S((LEN, d), BF16), slab, slab, slab, S((cols, LEN), BF16), S((LEN, 128), F32),
        ],
        scratch_shapes=[
            V((local, d), BF16), V((shard, 3 * cols), BF16), V((shard, cols), BF16),
            V((blocks, shard, 3 * fw), BF16), V((2, line * 16, shard), BF16),
            V((LEN, d), BF16), V((LEN, d), BF16), V((LEN, d), BF16),
            piece, piece, piece, V((15, most, shard), BF16), V((most, shard), F32), V((3, shard, 256), BF16),
            V((3, local, d), BF16), V((3, local, d), BF16), V((local, d), F32), V((local, d), F32),
            V((local, d), F32), V((8, d), F32), V((5, 8, d), F32),
            dma((4 * line + 3 + 2 * blocks,)), dma((2, dp)), dma((6, line)), dma((6, line)),
            dma((blocks, 6, line)), dma((8,)), dma((8,)), dma((8,)), dma((8,)), dma((12,)),
            dma((count, 4 + 2 * line + 15)), dma((count, 3)), dma((5, 2)), dma((3 * blocks,)), dma((2, 2)),
            regular, regular, regular,
        ],
        compiler_params=pltpu.CompilerParams(
            vmem_limit_bytes=VMEM_BYTES, collective_id=0, has_side_effects=True
        ),
        name="layer",
    )(x, g, gains, wq, wk, wv, wo, gate, up, down, cosine, sine, segc, segr)


def widen_kernel(*refs):
    count = (len(refs) - 2) // 4
    ins, outs = refs[:count], refs[count : 2 * count]
    here, wide = refs[2 * count : 3 * count], refs[3 * count : 4 * count]
    sem_in, sem_out = refs[-2:]
    loads = [pltpu.make_async_copy(a, b, sem_in.at[n]) for n, (a, b) in enumerate(zip(ins, here))]
    stores = [pltpu.make_async_copy(a, b, sem_out.at[n]) for n, (a, b) in enumerate(zip(wide, outs))]
    for copy in loads:
        copy.start()
    for n, (load, store) in enumerate(zip(loads, stores)):
        load.wait()
        rows = here[n].shape[0]
        step = min(rows, 64)

        @pl.loop(0, rows // step)
        def _(i, n=n, step=step):
            at = pl.ds(pl.multiple_of(i * step, step), step)
            wide[n][at, :] = here[n][at, :].astype(wide[n].dtype)

        store.start()
    for store in stores:
        store.wait()


def widen(arrays, dtypes):
    hbm = pl.BlockSpec(memory_space=pl.ANY)
    return pl.pallas_call(
        widen_kernel,
        in_specs=[hbm] * len(arrays),
        out_specs=[hbm] * len(arrays),
        out_shape=[jax.ShapeDtypeStruct(a.shape, t) for a, t in zip(arrays, dtypes)],
        scratch_shapes=[pltpu.VMEM(a.shape, a.dtype) for a in arrays]
        + [pltpu.VMEM(a.shape, t) for a, t in zip(arrays, dtypes)]
        + [pltpu.SemaphoreType.DMA((len(arrays),))] * 2,
        compiler_params=pltpu.CompilerParams(vmem_limit_bytes=VMEM_BYTES),
        name="widen",
    )(*arrays)


def on_device(
    dp, tensor, hidden_in, doc_lengths, gain_attn, w_query, w_key, w_value, w_out, gain_mlp,
    w_gate, w_up, w_down, cotangent,
):
    line = dp // 2
    core = lax.axis_index("dp") % 2
    place = lax.axis_index("tensor")
    square = tensor == 4 and dp == 8
    same_core = [[c + 2 * z for z in range(line)] for c in range(2)]
    sibling = [(i, i ^ 1) for i in range(dp)]
    d = hidden_in.shape[1]
    local = hidden_in.shape[0]

    def own_first(a):
        s = a.reshape(a.shape[:-1] + (line, 2, d // dp))
        even, odd = s[..., 0, :], s[..., 1, :]
        out = jnp.concatenate(
            [jnp.where(core == 0, even, odd), jnp.where(core == 0, odd, even)], axis=-2
        )
        return out.reshape(a.shape)

    def true_order(a):
        s = a.reshape(a.shape[:-1] + (2, line, d // dp))
        first, second = s[..., 0, :, :], s[..., 1, :, :]
        out = jnp.stack(
            [jnp.where(core == 0, first, second), jnp.where(core == 0, second, first)], axis=-2
        )
        return out.reshape(a.shape)

    def hop(a, step):
        return lax.ppermute(a, "tensor", [(i, i ^ step) for i in range(tensor)])

    def gather_rows(a):
        if not square:
            return lax.all_gather(a, "tensor", axis=0, tiled=True)
        half = a.shape[0] // 2
        from_x, from_y = hop(a, 1), hop(a, 2)
        top, bottom = hop(from_x[:half], 2), hop(from_y[half:], 1)
        return jnp.concatenate([a, from_x, from_y, top, bottom], axis=0)

    def scatter_rows(a):
        if not square:
            return lax.psum_scatter(a, "tensor", scatter_dimension=0, tiled=True).astype(F32)
        n = a.shape[0] // 4
        half = n // 2
        top = hop(a[3 * n : 3 * n + half], 2)
        bottom = hop(a[3 * n + half :], 1)
        for_x = jnp.concatenate([a[n : n + half] + top, a[n + half : 2 * n]], axis=0)
        for_y = jnp.concatenate([a[2 * n : 2 * n + half], a[2 * n + half : 3 * n] + bottom], axis=0)
        return (a[:n].astype(F32) + hop(for_x, 1).astype(F32)) + hop(for_y, 2).astype(F32)

    def line_gather(a):
        own = lax.all_gather(a, "dp", axis=0, axis_index_groups=same_core, tiled=True)
        return own, lax.ppermute(own, "dp", sibling)

    def line_scatter(own, sib):
        mine = own + lax.ppermute(sib, "dp", sibling)
        return lax.psum_scatter(
            mine, "dp", scatter_dimension=0, axis_index_groups=same_core, tiled=True
        ).astype(F32)

    blocks = 4
    rows = LEN // blocks
    key = place if square else jnp.zeros((), jnp.int32)
    tokens = (
        (jnp.arange(blocks, dtype=jnp.int32) ^ key)[:, None] * rows
        + jnp.arange(rows, dtype=jnp.int32)[None, :]
    ).reshape(LEN)
    segment, position = doc_tables(doc_lengths, tokens)
    cosine, sine = rotary_tables(position)
    segc = jnp.broadcast_to(segment[:, None], (LEN, 128))
    segr = jnp.broadcast_to(segment.reshape(blocks, 1, rows), (blocks, 8, rows))
    key = key.reshape(1)
    cols = w_query.shape[1]
    if square:
        gain_rows = jnp.pad(
            jnp.concatenate([gain_attn, gain_mlp]), (0, 14 * gain_attn.shape[0])
        ).reshape(16, -1)
        (
            output, input_grad, gain_sum, grad_gate, grad_up, grad_down, grad_query, grad_key,
            grad_value, grad_out, *_,
        ) = layer(
            dp, hidden_in, cotangent, gain_rows, w_query, w_key, w_value, w_out, w_gate, w_up,
            w_down, cosine, sine, segc, segr,
        )
        share = d // (dp * tensor)
        first = (lax.axis_index("dp") // 2) * (d // dp) + place * share
        gain_sum = lax.dynamic_slice_in_dim(gain_sum, first, share, 1)
        grads = (grad_gate, grad_up, grad_down, grad_query, grad_key, grad_value, grad_out)
        (
            output, input_grad, grad_gate, grad_up, grad_down, grad_query, grad_key, grad_value, grad_out
        ) = widen((output, input_grad) + grads, (BF16,) + (F32,) * 8)
        return (
            output, input_grad, gain_sum[0], grad_query, grad_key, grad_value, grad_out, gain_sum[1],
            grad_gate, grad_up, grad_down,
        )

    cosine, sine = (jnp.tile(a, (1, GROUP // 128)) for a in (cosine, sine))
    ff = w_gate.shape[1]
    fb = ff // FF_BLOCKS
    down_t = w_down.T
    shards = [
        jnp.concatenate([w[:, b * fb : (b + 1) * fb] for w in (w_gate, w_up, down_t)], axis=1)
        for b in range(FF_BLOCKS)
    ]
    qkv_shard = jnp.concatenate([w_query, w_key, w_value], axis=1)
    g_local = own_first(cotangent)
    inputs = own_first(hidden_in).astype(F32)
    factor_one = norm_factor(inputs)
    gains = lax.all_gather(jnp.stack([gain_attn, gain_mlp]), "dp", axis=0)
    gains = own_first(jnp.moveaxis(gains, 0, 1).reshape(2, d)).astype(F32)
    gain_one, gain_two = gains[0], gains[1]
    qkv_own, qkv_sib = line_gather(qkv_shard)
    out_own, out_sib = line_gather(w_out.T)
    normed = gather_rows((inputs * factor_one * gain_one).astype(BF16))
    g_all = gather_rows(g_local)
    query, keys, values, mixed, lse = attn_forward(
        blocks, key, normed, qkv_own, qkv_sib, cosine, sine, segc, segr
    )
    attended = jnp.concatenate(
        [dot_nt(mixed, out_own).astype(BF16), dot_nt(mixed, out_sib).astype(BF16)], axis=1
    )
    middle = inputs + scatter_rows(attended)
    factor_two = norm_factor(middle)
    normed_mlp = gather_rows((middle * factor_two * gain_two).astype(BF16))
    ff_sets = [jnp.concatenate(line_gather(shard), axis=0) for shard in shards]

    down_sum = jnp.zeros((LEN, d), F32)
    back_sum = jnp.zeros((LEN, d), F32)
    ff_grads = []
    for b in range(FF_BLOCKS):
        gate_w, up_w, down_w = jnp.split(ff_sets[b], 3, axis=1)
        gate_pre = dot_nn(normed_mlp, gate_w)
        upward = dot_nn(normed_mlp, up_w)
        grad_hidden = dot_nn(g_all, down_w)
        sig = jax.nn.sigmoid(gate_pre)
        activated = gate_pre * sig
        hidden = (activated * upward).astype(BF16)
        grad_gate_pre = (grad_hidden * upward * sig * (1.0 + gate_pre * (1.0 - sig))).astype(BF16)
        grad_upward = (grad_hidden * activated).astype(BF16)
        down_sum = down_sum + dot_nt(hidden, down_w)
        back_sum = back_sum + dot_nt(grad_gate_pre, gate_w) + dot_nt(grad_upward, up_w)
        grad = jnp.concatenate(
            [
                dot_tn(normed_mlp, grad_gate_pre).astype(BF16),
                dot_tn(normed_mlp, grad_upward).astype(BF16),
                dot_tn(g_all, hidden).astype(BF16),
            ],
            axis=1,
        )
        ff_grads.append(line_scatter(grad[: d // 2], grad[d // 2 :]))
    grad_norm_two = scatter_rows(back_sum.astype(BF16))
    output = true_order((middle + scatter_rows(down_sum.astype(BF16))).astype(BF16))
    grad_mid_norm, gain_two_part = norm_back(middle, factor_two, gain_two, grad_norm_two)
    grad_middle = g_local.astype(F32) + grad_mid_norm
    grad_mid_all = gather_rows(grad_middle.astype(BF16))

    dq, dk, dv = attn_backward(
        blocks, key, grad_mid_all, out_own, out_sib, query, keys, values, lse, cosine, sine,
        segc, segr,
    )
    grad = jnp.concatenate(
        [dot_tn(normed, dq), dot_tn(normed, dk), dot_tn(normed, dv), dot_tn(grad_mid_all, mixed)],
        axis=1,
    ).astype(BF16)
    attn_grads = line_scatter(grad[: d // 2], grad[d // 2 :])
    rows_grad = jnp.concatenate([dq, dk, dv], axis=1)
    back = jnp.concatenate(
        [
            dot_nt(rows_grad, qkv_own).astype(BF16),
            dot_nt(rows_grad, qkv_sib).astype(BF16),
        ],
        axis=1,
    )
    grad_in_norm, gain_one_part = norm_back(inputs, factor_one, gain_one, scatter_rows(back))
    input_grad = true_order(grad_middle + grad_in_norm)

    parts = true_order(jnp.stack([gain_one_part, gain_two_part])).reshape(2 * d)
    shares = lax.all_gather(parts, ("dp", "tensor"), axis=0)
    gain_sum = jnp.sum(shares, axis=0).reshape(2, d)
    share = d // (dp * tensor)
    first = (lax.axis_index("dp") * tensor + place) * share
    gain_sum = lax.dynamic_slice_in_dim(gain_sum, first, share, 1)

    return (
        output,
        input_grad,
        gain_sum[0],
        attn_grads[:, :cols],
        attn_grads[:, cols : 2 * cols],
        attn_grads[:, 2 * cols : 3 * cols],
        attn_grads[:, 3 * cols :].T,
        gain_sum[1],
        jnp.concatenate([g[:, :fb] for g in ff_grads], axis=1),
        jnp.concatenate([g[:, fb : 2 * fb] for g in ff_grads], axis=1),
        jnp.concatenate([g[:, 2 * fb :] for g in ff_grads], axis=1).T,
    )


def solution(mesh):
    shape = dict(mesh.shape)
    return jax.shard_map(
        functools.partial(on_device, shape["dp"], shape["tensor"]),
        mesh=mesh,
        in_specs=(
            P(("dp", "tensor"), None),
            P("dp", None),
            P("dp"),
            P("dp", "tensor"),
            P("dp", "tensor"),
            P("dp", "tensor"),
            P("tensor", "dp"),
            P("dp"),
            P("dp", "tensor"),
            P("dp", "tensor"),
            P("tensor", "dp"),
            P(("dp", "tensor"), None),
        ),
        out_specs=(
            P(("dp", "tensor"), None),
            P(("dp", "tensor"), None),
            P(("dp", "tensor")),
            P("dp", "tensor"),
            P("dp", "tensor"),
            P("dp", "tensor"),
            P("tensor", "dp"),
            P(("dp", "tensor")),
            P("dp", "tensor"),
            P("dp", "tensor"),
            P("tensor", "dp"),
        ),
        check_vma=False,
    )
```

```python
import functools
import math

import jax
import jax.numpy as jnp
from jax import lax
from jax.experimental import pallas as pl
from jax.experimental.pallas import tpu as pltpu
from jax.sharding import PartitionSpec as P

HEAD_DIM = 64
LEN = 1024
MOST = 512
EPSILON = 1e-05
ROPE_BASE = 130000.0
NEG = -1e30
GROUP = 256
FF_BLOCKS = 8
F32 = jnp.float32
BF16 = jnp.bfloat16
VMEM_BYTES = 63 * 1024 * 1024


def dot_nn(a, b):
    return jnp.dot(a, b, preferred_element_type=F32)


def dot_tn(a, b):
    return lax.dot_general(a, b, (((0,), (0,)), ((), ())), preferred_element_type=F32)


def dot_nt(a, b):
    return lax.dot_general(a, b, (((1,), (1,)), ((), ())), preferred_element_type=F32)


def norm_factor(values):
    return lax.rsqrt(jnp.mean(values * values, axis=-1, keepdims=True) + EPSILON)


def norm_back(values, factor, gain, grads):
    scaled = grads * gain
    grad_in = factor * scaled - values * factor * factor * factor * jnp.mean(
        scaled * values, axis=-1, keepdims=True
    )
    return grad_in, jnp.sum(grads * values * factor, axis=0)


def doc_tables(doc_lengths, tokens):
    ends = jnp.cumsum(doc_lengths, axis=1)[0]
    passed = tokens[:, None] >= ends[None, :]
    segment = jnp.sum(passed.astype(jnp.int32), axis=1)
    start = jnp.sum(jnp.where(passed, doc_lengths, 0), axis=1)
    return segment, tokens - start


def rotary_tables(position):
    half = HEAD_DIM // 2
    inverse = jnp.power(ROPE_BASE, -jnp.arange(half, dtype=F32) * 2.0 / HEAD_DIM)
    angles = position.astype(F32)[:, None] * inverse
    cosine, sine = jnp.cos(angles), jnp.sin(angles)
    heads = 128 // HEAD_DIM
    return (
        jnp.tile(jnp.concatenate([cosine, cosine], axis=1), (1, heads)),
        jnp.tile(jnp.concatenate([-sine, sine], axis=1), (1, heads)),
    )


def swap_halves(v):
    half, width = HEAD_DIM // 2, v.shape[1]
    lane = lax.broadcasted_iota(jnp.int32, v.shape, 1)
    ahead = pltpu.roll(v, width - half, 1)
    behind = pltpu.roll(v, half, 1)
    return jnp.where(lane % HEAD_DIM < half, ahead, behind)


def key_blocks(i, rows):
    reach = -(-(MOST - 1) // rows)
    return list(range(max(0, i - reach), i + 1))


def fill_bias(bias_ref, seg_col, seg_ref, i, places):
    rows = seg_col.shape[0]
    for n, (j, place) in enumerate(places):
        same = seg_col == seg_ref[place][0:1, :]
        if j == i:
            row = lax.broadcasted_iota(jnp.int32, (rows, rows), 0)
            col = lax.broadcasted_iota(jnp.int32, (rows, rows), 1)
            same = same & (col <= row)
        bias_ref[n] = jnp.where(same, 0.0, NEG)


def attn_forward_kernel(
    blocks, key_ref, x_ref, qo, qs, ko, ks, vo, vs, cos_ref, sin_ref, segc_ref, segr_ref,
    q_ref, k_ref, v_ref, mixed_ref, lse_ref, bias_ref,
):
    rows = LEN // blocks
    half = x_ref.shape[1] // 2
    key = key_ref[0]

    @pl.loop(0, blocks)
    def _(b):
        at = pl.ds(pl.multiple_of(b * rows, rows), rows)
        left, right = x_ref[at, :half], x_ref[at, half:]
        cosine, sine = cos_ref[at, :], sin_ref[at, :]
        query = dot_nn(left, qo[...]) + dot_nn(right, qs[...])
        q_ref[at, :] = (query * cosine + swap_halves(query) * sine).astype(BF16)
        keys = dot_nn(left, ko[...]) + dot_nn(right, ks[...])
        k_ref[at, :] = (keys * cosine + swap_halves(keys) * sine).astype(BF16)
        v_ref[at, :] = (dot_nn(left, vo[...]) + dot_nn(right, vs[...])).astype(BF16)

    head_lane = lax.broadcasted_iota(jnp.int32, (rows, 128), 1)
    for i in range(blocks):
        places = [(j, j ^ key) for j in key_blocks(i, rows)]
        at = pl.ds(pl.multiple_of((i ^ key) * rows, rows), rows)
        fill_bias(bias_ref, segc_ref[at, 0:1], segr_ref, i, places)
        spots = [pl.ds(pl.multiple_of(p * rows, rows), rows) for _, p in places]

        @pl.loop(0, GROUP // 128)
        def _(pair, at=at, spots=spots):
            first = pl.program_id(0) * (GROUP // HEAD_DIM)
            attend(pair, first, at, spots, head_lane, q_ref, k_ref, v_ref, mixed_ref, lse_ref, bias_ref)


def attn_forward(blocks, key, x, own, sib, cosine, sine, segc, segr):
    d = x.shape[1]
    cols = own.shape[1] // 3
    steps = cols // GROUP
    rows = LEN // blocks

    def weight(part):
        return pl.BlockSpec((d // 2, GROUP), lambda i, part=part: (0, part * steps + i))

    def whole(shape):
        return pl.BlockSpec(shape, lambda i: (0,) * len(shape))

    col_block = pl.BlockSpec((LEN, GROUP), lambda i: (0, i))
    slab = jax.ShapeDtypeStruct((LEN, cols), BF16)
    return pl.pallas_call(
        functools.partial(attn_forward_kernel, blocks),
        grid=(steps,),
        in_specs=[pl.BlockSpec(memory_space=pltpu.SMEM), whole((LEN, d))]
        + [weight(p) for p in (0, 0, 1, 1, 2, 2)]
        + [whole((LEN, GROUP))] * 2
        + [whole((LEN, 128)), whole(segr.shape)],
        out_specs=[col_block] * 4 + [whole((LEN, 128))],
        out_shape=[slab] * 4 + [jax.ShapeDtypeStruct((LEN, 128), F32)],
        scratch_shapes=[pltpu.VMEM((blocks, rows, rows), F32)],
        compiler_params=pltpu.CompilerParams(vmem_limit_bytes=VMEM_BYTES),
        name="attn_forward",
    )(key, x, own, sib, own, sib, own, sib, cosine, sine, segc, segr)


def attn_backward_kernel(
    blocks, key_ref, g_ref, wo, ws, q_ref, k_ref, v_ref, lse_ref, cos_ref, sin_ref, segc_ref,
    segr_ref, dq_ref, dk_ref, dv_ref, dm_ref, dqa_ref, dka_ref, dva_ref, bias_ref,
):
    rows = LEN // blocks
    half = g_ref.shape[1] // 2
    key = key_ref[0]

    @pl.loop(0, blocks)
    def _(b):
        at = pl.ds(pl.multiple_of(b * rows, rows), rows)
        dm_ref[at, :] = (dot_nn(g_ref[at, :half], wo[...]) + dot_nn(g_ref[at, half:], ws[...])).astype(BF16)
        dka_ref[at, :] = jnp.zeros((rows, GROUP), F32)
        dva_ref[at, :] = jnp.zeros((rows, GROUP), F32)

    head_lane = lax.broadcasted_iota(jnp.int32, (rows, 128), 1)
    scale = HEAD_DIM**-0.5
    for i in range(blocks):
        places = [(j, j ^ key) for j in key_blocks(i, rows)]
        at = pl.ds(pl.multiple_of((i ^ key) * rows, rows), rows)
        fill_bias(bias_ref, segc_ref[at, 0:1], segr_ref, i, places)
        spots = [pl.ds(pl.multiple_of(p * rows, rows), rows) for _, p in places]

        @pl.loop(0, GROUP // 128)
        def _(pair, at=at, spots=spots):
            lanes = pl.ds(pl.multiple_of(pair * 128, 128), 128)
            first = pl.program_id(0) * (GROUP // HEAD_DIM)
            query, grad = q_ref[at, lanes], dm_ref[at, lanes]
            logs = lse_ref[at, :]
            outs = []
            for h in range(2):
                mine = (head_lane < HEAD_DIM) if h == 0 else (head_lane >= HEAD_DIM)
                qm = jnp.where(mine, query, 0) * jnp.asarray(scale, BF16)
                gm = jnp.where(mine, grad, 0)
                log = jnp.sum(
                    jnp.where(head_lane == first + pair * 2 + h, logs, 0.0), axis=1, keepdims=True
                )
                weights = [
                    jnp.exp(dot_nt(qm, k_ref[s, lanes]) + bias_ref[n] - log)
                    for n, s in enumerate(spots)
                ]
                grads = [dot_nt(gm, v_ref[s, lanes]) for s in spots]
                inner = sum(
                    jnp.sum(w * g, axis=1, keepdims=True) for w, g in zip(weights, grads)
                )
                dq = jnp.zeros((rows, 128), F32)
                for w, g, s in zip(weights, grads, spots):
                    ds = (w * (g - inner)).astype(BF16)
                    dva_ref[s, lanes] += dot_tn(w.astype(BF16), gm)
                    dka_ref[s, lanes] += dot_tn(ds, qm)
                    dq = dq + dot_nn(ds, k_ref[s, lanes])
                outs.append(dq)
            dqa_ref[at, lanes] = jnp.where(head_lane < HEAD_DIM, outs[0], outs[1]) * scale

    @pl.loop(0, blocks)
    def _(b):
        at = pl.ds(pl.multiple_of(b * rows, rows), rows)
        cosine, sine = cos_ref[at, :], sin_ref[at, :]
        dq = dqa_ref[at, :]
        dq_ref[at, :] = (dq * cosine - swap_halves(dq) * sine).astype(BF16)
        dk = dka_ref[at, :]
        dk_ref[at, :] = (dk * cosine - swap_halves(dk) * sine).astype(BF16)
        dv_ref[at, :] = dva_ref[at, :].astype(BF16)


def attn_backward(blocks, key, g, own, sib, q, k, v, lse, cosine, sine, segc, segr):
    d = g.shape[1]
    cols = q.shape[1]
    steps = cols // GROUP
    rows = LEN // blocks

    def whole(shape):
        return pl.BlockSpec(shape, lambda i: (0,) * len(shape))

    col_block = pl.BlockSpec((LEN, GROUP), lambda i: (0, i))
    weight = pl.BlockSpec((d // 2, GROUP), lambda i: (0, i))
    slab = jax.ShapeDtypeStruct((LEN, cols), BF16)
    return pl.pallas_call(
        functools.partial(attn_backward_kernel, blocks),
        grid=(steps,),
        in_specs=[pl.BlockSpec(memory_space=pltpu.SMEM), whole((LEN, d)), weight, weight]
        + [col_block] * 3
        + [whole((LEN, 128))]
        + [whole((LEN, GROUP))] * 2
        + [whole((LEN, 128)), whole(segr.shape)],
        out_specs=[col_block] * 3,
        out_shape=[slab] * 3,
        scratch_shapes=[
            pltpu.VMEM((LEN, GROUP), BF16),
            pltpu.VMEM((LEN, GROUP), F32),
            pltpu.VMEM((LEN, GROUP), F32),
            pltpu.VMEM((LEN, GROUP), F32),
            pltpu.VMEM((blocks, rows, rows), F32),
        ],
        compiler_params=pltpu.CompilerParams(vmem_limit_bytes=VMEM_BYTES),
        name="attn_backward",
    )(key, g, own, sib, q, k, v, lse, cosine, sine, segc, segr)


class LineGather:
    def __init__(self, me, src, full, sems):
        self.me, self.src, self.full, self.sems = me, src, full, sems
        self.rows = src.shape[0]

    def spot(self, side, s):
        return self.full.at[side, pl.ds(pl.multiple_of(s * self.rows, self.rows), self.rows)]

    def to_line(self, src, s, way):
        device = self.me.up if way == 0 else self.me.down
        return remote(src, self.spot(0, s), self.sems.at[way, s], self.sems.at[3, s], device)

    def to_core(self, src, s):
        return remote(src, self.spot(1, s), self.sems.at[2, s], self.sems.at[4, s], self.me.other)

    def keep(self):
        return pltpu.make_async_copy(self.src, self.spot(0, self.me.z), self.sems.at[5, 0])

    def start(self):
        z, line = self.me.z, self.me.line

        @pl.when(z + 1 < line)
        def _():
            self.to_line(self.src, z, 0).start()

        @pl.when(z >= 1)
        def _():
            self.to_line(self.src, z, 1).start()

        self.to_core(self.src, z).start()
        self.keep().start()

    def hop(self, h):
        z, line = self.me.z, self.me.line
        for s, arrives, goes_on, way in (
            (z - h, z >= h, z + 1 < line, 0),
            (z + h, z + h < line, z >= 1, 1),
        ):

            @pl.when(arrives)
            def _(s=s, goes_on=goes_on, way=way):
                here = self.spot(0, s)
                self.to_line(here, s, way).wait_recv()

                @pl.when(goes_on)
                def _():
                    self.to_line(here, s, way).start()

                self.to_core(here, s).start()

    def arrived(self):
        self.keep().wait()
        for s in range(self.me.line):
            self.to_core(self.spot(0, s), s).wait_recv()

    def done(self):
        z, line = self.me.z, self.me.line
        for s in range(line):
            here = self.spot(0, s)
            self.to_core(here, s).wait_send()

            @pl.when((s <= z) & (z + 1 < line))
            def _(s=s, here=here):
                self.to_line(here, s, 0).wait_send()

            @pl.when((s >= z) & (z >= 1))
            def _(s=s, here=here):
                self.to_line(here, s, 1).wait_send()


class SquareGather:
    def __init__(self, me, full, sems):
        self.me, self.full, self.sems = me, full, sems
        self.rows = full.shape[0] // 4

    def copies(self):
        me, full, sems, rows = self.me, self.full, self.sems, self.rows
        half = rows // 2

        def part(first, size):
            return full.at[pl.ds(first, size)]

        return (
            remote(part(0, rows), part(rows, rows), sems.at[0], sems.at[1], me.x),
            remote(part(0, rows), part(2 * rows, rows), sems.at[2], sems.at[3], me.y),
            remote(part(rows, half), part(3 * rows, half), sems.at[4], sems.at[5], me.y),
            remote(
                part(2 * rows + half, half), part(3 * rows + half, half), sems.at[6], sems.at[7], me.x
            ),
        )

    def start(self):
        x, y, _, _ = self.copies()
        x.start()
        y.start()

    def forward(self):
        x, y, top, bottom = self.copies()
        x.wait_recv()
        top.start()
        y.wait_recv()
        bottom.start()

    def arrived(self):
        _, _, top, bottom = self.copies()
        top.wait_recv()
        bottom.wait_recv()

    def done(self):
        for copy in self.copies():
            copy.wait_send()


class SquareScatter:
    def __init__(self, me, stage, landed, sems):
        self.me, self.stage, self.landed, self.sems = me, stage, landed, sems
        self.half = stage.shape[1] // 2
        self.top, self.bottom = pl.ds(0, self.half), pl.ds(self.half, self.half)

    def copies(self):
        me, stage, landed, sems = self.me, self.stage, self.landed, self.sems
        top, bottom = self.top, self.bottom
        return (
            remote(stage.at[2, top], landed.at[2, top], sems.at[0], sems.at[1], me.y),
            remote(stage.at[2, bottom], landed.at[2, bottom], sems.at[2], sems.at[3], me.x),
            remote(stage.at[0, bottom], landed.at[0, bottom], sems.at[4], sems.at[5], me.x),
            remote(stage.at[1, top], landed.at[1, top], sems.at[6], sems.at[7], me.y),
            remote(stage.at[0, top], landed.at[0, top], sems.at[8], sems.at[9], me.x),
            remote(stage.at[1, bottom], landed.at[1, bottom], sems.at[10], sems.at[11], me.y),
        )

    def diagonal_ready(self):
        copies = self.copies()
        copies[0].start()
        copies[1].start()

    def sides_ready(self):
        copies = self.copies()
        copies[2].start()
        copies[3].start()

    def combine(self):
        copies = self.copies()
        for n, slot, at in ((0, 0, self.top), (1, 1, self.bottom)):
            copies[n].wait_recv()
            add_rows(self.stage, slot, at, self.landed)
            copies[4 + n].start()

    def arrived(self):
        for copy in self.copies()[2:]:
            copy.wait_recv()

    def done(self):
        for copy in self.copies():
            copy.wait_send()


def add_rows(stage, slot, at, landed):
    step = 32

    @pl.loop(0, at.size // step)
    def _(n):
        here = pl.ds(pl.multiple_of(at.start + n * step, step), step)
        total = stage[slot, here, :].astype(F32) + landed[2, here, :].astype(F32)
        stage[slot, here, :] = total.astype(BF16)


def remote(src, dst, send_sem, recv_sem, device):
    return pltpu.make_async_remote_copy(
        src_ref=src, dst_ref=dst, send_sem=send_sem, recv_sem=recv_sem, device_id=device,
        device_id_type=pl.DeviceIdType.MESH,
    )


class Place:
    def __init__(self, dp):
        index = lax.axis_index("dp")
        self.index, self.dp = index, dp
        self.line = dp // 2
        self.z, self.core = index // 2, index % 2
        self.at_end = (self.z == 0) | (self.z == self.line - 1)
        self.t = lax.axis_index("tensor")
        tx, ty = self.t % 2, self.t // 2
        self.other = {"dp": index + 1 - 2 * self.core}
        self.up, self.down = {"dp": index + 2}, {"dp": index - 2}
        self.next, self.far = {"dp": index + 2 - 4 * (self.z % 2)}, {"dp": index + 4 - 8 * (self.z // 2)}
        self.x = {"tensor": self.t + 1 - 2 * tx}
        self.y = {"tensor": self.t + 2 - 4 * ty}
        self.spots = [
            (tx if i % 2 == 0 else 1 - tx) + 2 * (ty if i // 2 == 0 else 1 - ty) for i in range(4)
        ]

    def window(self, i, rows, seg_col, seg_ref, bias_ref):
        spots = []
        for n in range(-(-(MOST - 1) // rows) + 1):
            j = jnp.maximum(i - n, 0)
            place = (j % 2 + self.t % 2) % 2 + 2 * ((j // 2 + self.t // 2) % 2)
            same = seg_col == seg_ref[place][0:1, :]
            if n == 0:
                row = lax.broadcasted_iota(jnp.int32, (rows, rows), 0)
                col = lax.broadcasted_iota(jnp.int32, (rows, rows), 1)
                bias_ref[n] = jnp.where(same & (col <= row), 0.0, NEG)
            else:
                bias_ref[n] = jnp.where(same, jnp.where(i >= n, 0.0, NEG), NEG)
            spots.append(pl.ds(pl.multiple_of(place * rows, rows), rows))
        return spots

    def greet(self):
        barrier = pltpu.get_barrier_semaphore()
        peers = [self.x, self.y] + [{"dp": (self.index + k) % self.dp} for k in range(1, self.dp)]
        for device in peers:
            pl.semaphore_signal(
                barrier, inc=1, device_id=device, device_id_type=pl.DeviceIdType.MESH
            )
        pl.semaphore_wait(barrier, len(peers))


def norm_rows(count, body, step=32):
    @pl.loop(0, count // step)
    def _(n):
        body(pl.ds(pl.multiple_of(n * step, step), step))


def attend(pair, first, at, spots, head_lane, q_ref, k_ref, v_ref, mixed_ref, lse_ref, bias_ref):
    lanes = pl.ds(pl.multiple_of(pair * 128, 128), 128)
    query = q_ref[at, lanes]
    outs, stats = [], []
    for h in range(2):
        mine = (head_lane < HEAD_DIM) if h == 0 else (head_lane >= HEAD_DIM)
        qm = jnp.where(mine, query, 0) * jnp.asarray(HEAD_DIM**-0.5, BF16)
        scores = [dot_nt(qm, k_ref[s, lanes]) + bias_ref[n] for n, s in enumerate(spots)]
        top = functools.reduce(jnp.maximum, [jnp.max(s, axis=1, keepdims=True) for s in scores])
        weights = [jnp.exp(s - top) for s in scores]
        total = sum(jnp.sum(w, axis=1, keepdims=True) for w in weights)
        out = sum(dot_nn(w.astype(BF16), v_ref[s, lanes]) for w, s in zip(weights, spots))
        outs.append(out / total)
        stats.append(top + jnp.log(total))
    mixed_ref[at, lanes] = jnp.where(head_lane < HEAD_DIM, outs[0], outs[1]).astype(BF16)
    kept = jnp.where(pair + first == 0, 0.0, lse_ref[at, :])
    for h in range(2):
        kept = jnp.where(head_lane == first + pair * 2 + h, stats[h], kept)
    lse_ref[at, :] = kept


def add_into(total, other, rows, step=64):
    @pl.loop(0, rows // step)
    def _(n):
        at = pl.ds(pl.multiple_of(n * step, step), step)
        total[at, :] = (total[at, :].astype(F32) + other[at, :].astype(F32)).astype(total.dtype)


KEPT_SLOT = 6


class LineScatter:
    def __init__(self, me, rows, mine, theirs, swapped, kept, landed, work, sems, step_sems):
        cut = lambda ref: ref.at[:, pl.ds(0, rows)]
        self.me, self.rows = me, rows
        self.mine, self.theirs, self.swapped = cut(mine), cut(theirs), cut(swapped)
        self.kept, self.landed, self.work = cut(kept), cut(landed), cut(work)
        self.sems, self.step_sems = sems, step_sems

    def swap(self):
        return remote(
            self.theirs, self.swapped, self.step_sems.at[0], self.step_sems.at[1], self.me.other
        )

    def keep(self):
        return pltpu.make_async_copy(self.mine, self.kept, self.step_sems.at[2])

    def send(self, src, s, upward, z):
        line = self.me.line
        if upward:
            slot, device = s, self.me.up
        else:
            slot, device = (s if s < z - 1 else line), self.me.down
        return remote(
            src, self.landed.at[slot], self.sems.at[s], self.sems.at[line + slot], device
        )

    def landing(self, slot):
        line = self.me.line
        return remote(
            self.landed.at[slot], self.landed.at[slot], self.sems.at[0],
            self.sems.at[line + slot], self.me.other,
        )

    def load(self, src, n):
        return pltpu.make_async_copy(src, self.work.at[n], self.step_sems.at[3 + n])

    def reduce(self, free_sem):
        line = self.me.line
        self.swap().wait_recv()
        for s in range(line):
            add_into(self.mine.at[s], self.swapped.at[s], self.rows)
        pl.semaphore_signal(
            free_sem, inc=1, device_id=self.me.other, device_id_type=pl.DeviceIdType.MESH
        )
        self.keep().start()
        self.swap().wait_send()
        self.keep().wait()
        for end, upward in ((0, True), (line - 1, False)):

            @pl.when(self.me.z == end)
            def _(end=end, upward=upward):
                order = range(line - 1, end, -1) if upward else range(end)
                for s in order:
                    self.send(self.kept.at[s], s, upward, end).start()

    def going(self, p):
        line = self.me.line
        for z, upward in ((p, True), (line - 1 - p, False)):
            targets = list(range(line - 1, z, -1)) if upward else list(range(z))
            yield z, upward, targets

    def run_phase(self, p, first):
        for z, upward, targets in self.going(p):

            @pl.when(self.me.z == z)
            def _(z=z, upward=upward, targets=targets):
                for n, s in enumerate(targets):
                    self.load(self.kept.at[s], KEPT_SLOT + n).start()
                for n, s in enumerate(targets):
                    a, b = first + n, KEPT_SLOT + n
                    self.landing(s).wait_recv()
                    self.load(self.landed.at[s], a).start()
                    self.load(self.kept.at[s], b).wait()
                    self.load(self.landed.at[s], a).wait()
                    add_into(self.work.at[a], self.work.at[b], self.rows)
                    self.send(self.work.at[a], s, upward, z).start()

    def sent_phase(self, p, first):
        for z, upward, targets in self.going(p):

            @pl.when(self.me.z == z)
            def _(z=z, upward=upward, targets=targets):
                for n, s in enumerate(targets):
                    self.send(self.work.at[first + n], s, upward, z).wait_send()

    def load_last(self, first):
        me = self.me
        self.load(self.kept.at[me.z], first).start()

        @pl.when(me.z >= 1)
        def _():
            self.landing(me.z).wait_recv()
            self.load(self.landed.at[me.z], first + 1).start()

        @pl.when(me.z < me.line - 1)
        def _():
            self.landing(me.line).wait_recv()
            self.load(self.landed.at[me.line], first + 2).start()

    def run_last(self, first, total):
        me = self.me
        here = total.at[pl.ds(0, self.rows)]
        self.load(self.kept.at[me.z], first).wait()

        def put(n, step=64):
            @pl.loop(0, self.rows // step)
            def _(i):
                at = pl.ds(pl.multiple_of(i * step, step), step)
                if n == first:
                    here[at, :] = self.work[n, at, :].astype(F32)
                else:
                    here[at, :] += self.work[n, at, :].astype(F32)

        put(first)

        @pl.when(me.z >= 1)
        def _():
            self.load(self.landed.at[me.z], first + 1).wait()
            put(first + 1)

        @pl.when(me.z < me.line - 1)
        def _():
            self.load(self.landed.at[me.line], first + 2).wait()
            put(first + 2)

    def done(self):
        line = self.me.line
        for end, upward in ((0, True), (line - 1, False)):

            @pl.when(self.me.z == end)
            def _(end=end, upward=upward):
                for s in range(line - 1, end, -1) if upward else range(end):
                    self.send(self.kept.at[s], s, upward, end).wait_send()


WORK_SLOTS = (0, 2, 4, 5)


class Ticks:
    def __init__(self, chunks, total, writers, held):
        self.chunks, self.total, self.writers, self.held = chunks, total, writers, held
        self.k, self.second, self.last, self.written = 0, 0, 0, 0
        self.sent = [None] * len(WORK_SLOTS)

    def run(self, chunk, p, group):
        first = WORK_SLOTS[group]
        if self.sent[group] is not None:
            self.sent[group].sent_phase(p, first)
        chunk.run_phase(p, first)
        self.sent[group] = chunk

    def finish(self, n):
        self.chunks[n].load_last(KEPT_SLOT)
        if n > 0:
            self.writers[n - 1].wait()
        self.chunks[n].run_last(KEPT_SLOT, self.total)
        self.writers[n].start()

    def tick(self, most=2, last=2):
        k, count = self.k, len(self.chunks)
        ready, done = min(k, count), self.second
        if k >= self.held:
            for _ in range(most):
                if self.second < ready:
                    self.run(self.chunks[self.second], 2, 2 + self.second % 2)
                    self.second += 1
        if k < count:
            self.run(self.chunks[k], 1, k % 2)
        if k >= self.held:
            for _ in range(last):
                if self.last < done:
                    self.finish(self.last)
                    self.last += 1
        self.k += 1

    def rest(self):
        while self.last < len(self.chunks):
            self.tick(3, 3)

    def done(self):
        self.writers[-1].wait()
        for group, p in ((0, 1), (1, 1), (2, 2), (3, 2)):
            self.sent[group].sent_phase(p, WORK_SLOTS[group])
        for chunk in self.chunks:
            chunk.done()


class Writer:
    def __init__(self, total, turned, parts, sem):
        self.total, self.turned, self.parts, self.sem = total, turned, parts, sem

    def copies(self):
        for n, (dst, _) in enumerate(self.parts):
            yield pltpu.make_async_copy(self.turned.at[n], dst, self.sem.at[n])

    def start(self):
        for n, (_, flip) in enumerate(self.parts):
            block = self.total[pl.ds(n * 256, 256), :]
            self.turned[n] = (block.T if flip else block).astype(BF16)
        for copy in self.copies():
            copy.start()

    def wait(self):
        for copy in self.copies():
            copy.wait()


def norm_back_rows(count, gain, values_of, grads_of, gain_ref, row, put, step=32):
    @pl.loop(0, count // step)
    def _(n):
        at = pl.ds(pl.multiple_of(n * step, step), step)
        values, grads = values_of(at), grads_of(at)
        factor = norm_factor(values)
        scaled = grads * gain
        back = factor * scaled - values * factor * factor * factor * jnp.mean(
            scaled * values, axis=-1, keepdims=True
        )
        gain_ref[row : row + 1, :] += jnp.sum(grads * values * factor, axis=0, keepdims=True)
        put(at, back)


def attend_back(
    pair, at, spots, head_lane, q_ref, k_ref, v_ref, dm_ref, lse_ref, bias_ref, dqa_ref, dka_ref, dva_ref
):
    scale = HEAD_DIM**-0.5
    rows = at.size
    lanes = pl.ds(pl.multiple_of(pair * 128, 128), 128)
    query, grad = q_ref[at, lanes], dm_ref[at, lanes]
    logs = lse_ref[at, :]
    outs = []
    for h in range(2):
        mine = (head_lane < HEAD_DIM) if h == 0 else (head_lane >= HEAD_DIM)
        qm = jnp.where(mine, query, 0) * jnp.asarray(scale, BF16)
        gm = jnp.where(mine, grad, 0)
        log = jnp.sum(
            jnp.where(head_lane == pair * 2 + h, logs, 0.0), axis=1, keepdims=True
        )
        weights = [
            jnp.exp(dot_nt(qm, k_ref[s, lanes]) + bias_ref[n] - log) for n, s in enumerate(spots)
        ]
        grads = [dot_nt(gm, v_ref[s, lanes]) for s in spots]
        inner = sum(jnp.sum(w * g, axis=1, keepdims=True) for w, g in zip(weights, grads))
        dq = jnp.zeros((rows, 128), F32)
        for w, g, s in zip(weights, grads, spots):
            ds = (w * (g - inner)).astype(BF16)
            dva_ref[s, lanes] += dot_tn(w.astype(BF16), gm)
            dka_ref[s, lanes] += dot_tn(ds, qm)
            dq = dq + dot_nn(ds, k_ref[s, lanes])
        outs.append(dq)
    dqa_ref[:, lanes] = jnp.where(head_lane < HEAD_DIM, outs[0], outs[1]) * scale


TICK_AFTER = (3, 5, 6)
TICK_HELD = 3


def layer_kernel(
    dp, x_in, g_in, gain_ref, wq_in, wk_in, wv_in, wo_in, gate_in, up_in, down_in, doc_ref,
    output_out, input_grad_out, gain_out, gate_out, up_out, down_out, q_out, k_out, v_out, o_out,
    wa_full, wo_full, wf_full, hidden_all, kept_all, landed_all, y_all, normed_all, q_all, k_all, v_all,
    mixed_all, lse_all, cos_all, sin_all, segc_all, segr_all,
    x_ref, wa_src, wo_src, wf_src, gains_full, rows_a, rows_m, rows_g,
    theirs, swapped, mine, work, total, turned, stage, landed, own, gm, middle, gp, gp_landed,
    sem_in, sem_gains, sem_a, sem_o, sem_f, sem_n, sem_m, sem_g, sem_g2, sem_s, sem_line, sem_step, sem_write,
    sem_gain, sem_c, sem_w, free_core, free_x, free_y,
):
    me = Place(dp)
    line = me.line
    d = x_in.shape[1]
    half, local = d // 2, x_in.shape[0]
    shard = half // line
    rows = LEN // 4
    blocks = wf_src.shape[0]
    fw = wf_src.shape[2] // 3
    cols = wq_in.shape[1]
    groups = cols // GROUP

    def at_block(b):
        return pl.ds(pl.multiple_of(b * rows, rows), rows)

    def true_columns(side, s):
        core = me.core if side == 0 else 1 - me.core
        return pl.ds(pl.multiple_of((2 * s + core) * shard, shard), shard)

    def own_columns(side, s):
        return pl.ds(side * half + s * shard, shard)

    sides = [(side, s) for side in range(2) for s in range(line)]
    x_loads = [
        pltpu.make_async_copy(
            x_in.at[:, true_columns(*p)], x_ref.at[:, own_columns(*p)], sem_in.at[n]
        )
        for n, p in enumerate(sides)
    ]
    g_loads = [
        pltpu.make_async_copy(
            g_in.at[:, true_columns(*p)], rows_g.at[pl.ds(0, local), own_columns(*p)],
            sem_in.at[2 * line + n],
        )
        for n, p in enumerate(sides)
    ]
    first_sem = 4 * line
    a_loads = [
        pltpu.make_async_copy(ref, wa_src.at[:, pl.ds(n * cols, cols)], sem_in.at[first_sem + n])
        for n, ref in enumerate((wq_in, wk_in, wv_in))
    ]
    f_loads = [
        pltpu.make_async_copy(
            ref.at[:, pl.ds(n * fw, fw)], wf_src.at[n, :, pl.ds(part * fw, fw)],
            sem_in.at[first_sem + 3 + 2 * n + part],
        )
        for n in range(blocks)
        for part, ref in enumerate((gate_in, up_in))
    ]
    for copy in a_loads + x_loads + g_loads + f_loads:
        copy.start()
    gains_full[0, pl.ds(pl.multiple_of(me.z * 16, 16), 16), :] = gain_ref[...]
    me.greet()

    def gain_copy(k, sender):
        place = gains_full.at[k % 2, pl.ds(pl.multiple_of(sender // 2 * 16, 16), 16)]
        return remote(
            gain_ref, place, sem_gains.at[0, k], sem_gains.at[1, k], {"dp": (me.index + k) % dp}
        )

    for k in range(1, dp):
        gain_copy(k, me.index).start()

    wa = LineGather(me, wa_src, wa_full, sem_a)
    wo = LineGather(me, wo_src, wo_full, sem_o)
    gathers = [LineGather(me, wf_src.at[n], wf_full.at[n], sem_f.at[n]) for n in range(blocks)]
    order = [wa, wo] + gathers

    def start_all():
        for one in gathers:
            one.start()

    acts = []
    for n, one in enumerate(order):
        for h in range(1, line):

            def act(n=n, one=one, h=h):
                one.hop(h)
                if h == 2 and n == 0:
                    wo.start()
                    pl.when(me.at_end)(start_all)
                if n == 1 and h == 2:
                    pl.when(jnp.logical_not(me.at_end))(gathers[0].start)
                    pl.when(jnp.logical_not(me.at_end))(gathers[1].start)
                if h == 1 and 2 <= n < blocks:
                    pl.when(jnp.logical_not(me.at_end))(order[n + 2].start)

            acts.append(act)

    def poll(count=1):
        for _ in range(min(count, len(acts))):
            acts.pop(0)()

    def hops_done(n):
        return len(acts) <= (blocks - 1 - n) * (line - 1)

    for copy in a_loads:
        copy.wait()
    wa.start()
    for k in range(1, dp):
        gain_copy(k, (me.index + dp - k) % dp).wait_recv()
    for copy in x_loads:
        copy.wait()

    def gain_row(which):
        return jnp.concatenate(
            [
                gains_full[side, pl.ds(s * 16 + which, 1), :].astype(F32)
                for side in range(2)
                for s in range(line)
            ],
            axis=1,
        )

    gain_one, gain_two = gain_row(0), gain_row(1)

    def first_norm(at):
        values = x_ref[at, :].astype(F32)
        rows_a[at, :] = (values * norm_factor(values) * gain_one).astype(BF16)

    norm_rows(local, first_norm)
    normed = SquareGather(me, rows_a, sem_n)
    grads = SquareGather(me, rows_g, sem_g)
    normed_mlp = SquareGather(me, rows_m, sem_m)
    square = SquareGather(me, rows_a, sem_g2)
    scatter = SquareScatter(me, stage, landed, sem_s)
    normed.start()
    for n in range(cols // 256):
        wo_src[:, pl.ds(n * 256, 256)] = wo_in[pl.ds(n * 256, 256), :].T
    for n in range(blocks):
        wf_src[n, :, pl.ds(2 * fw, fw)] = down_in[pl.ds(n * fw, fw), :].T

    def tables(cos_ref, sin_ref, segc_ref, segr_ref):
        ends = []
        for k in range(doc_ref.shape[1]):
            length = doc_ref[0:1, k : k + 1]
            ends.append((length, length + ends[-1][1] if ends else length))

        def place_of(token):
            segment, first = jnp.zeros_like(token), jnp.zeros_like(token)
            for length, end in ends:
                passed = token >= end
                segment = segment + jnp.where(passed, 1, 0)
                first = first + jnp.where(passed, length, 0)
            return segment, token - first

        lane = lax.broadcasted_iota(jnp.int32, (1, 128), 1)
        pair = (lane % (HEAD_DIM // 2)).astype(F32)
        inverse = jnp.exp(pair * (-2.0 / HEAD_DIM * math.log(ROPE_BASE)))
        sign = jnp.where(lane % HEAD_DIM < HEAD_DIM // 2, -1.0, 1.0)
        for p in range(4):
            at = pl.ds(p * rows, rows)
            begin = me.spots[p] * rows
            segment, position = place_of(begin + lax.broadcasted_iota(jnp.int32, (rows, 128), 0))
            segc_ref[at, :] = segment
            angle = position.astype(F32) * inverse
            cos_ref[at, :] = jnp.cos(angle)
            sin_ref[at, :] = jnp.sin(angle) * sign
            segr_ref[p] = place_of(begin + lax.broadcasted_iota(jnp.int32, (8, rows), 1))[0]
        out = [
            pltpu.make_async_copy(a, b, sem_c.at[n])
            for n, (a, b) in enumerate(
                ((cos_ref, cos_all), (sin_ref, sin_all), (segc_ref, segc_all), (segr_ref, segr_all))
            )
        ]
        for copy in out:
            copy.start()
        for copy in out:
            copy.wait()

    table = pltpu.VMEM((LEN, 128), F32)
    segs = (pltpu.VMEM(segc_all.shape, jnp.int32), pltpu.VMEM(segr_all.shape, jnp.int32))
    pl.run_scoped(tables, table, table, *segs)
    for copy in f_loads:
        copy.wait()
    poll()
    for copy in g_loads:
        copy.wait()
    normed.forward()
    grads.start()
    poll(line - 2)
    normed.arrived()
    wa.arrived()

    def free_landed():
        for device, sem in ((me.x, free_x), (me.y, free_y)):
            pl.semaphore_signal(
                sem, inc=1, device_id=device, device_id_type=pl.DeviceIdType.MESH
            )

    def wait_free():
        pl.semaphore_wait(free_x, 1)
        pl.semaphore_wait(free_y, 1)

    def summed(at):
        return own[at, :] + landed[0, at, :].astype(F32) + landed[1, at, :].astype(F32)

    def doubled(ref, at):
        part = ref[at, :]
        return jnp.concatenate([part] * (GROUP // 128), axis=1)

    head_lane = lax.broadcasted_iota(jnp.int32, (rows, 128), 1)

    def forward(
        wa_v, wo_v, q_ref, k_ref, v_ref, mixed_ref, mixed_t, lse_ref, cos_ref, sin_ref, segc_ref, segr_ref, bias_ref
    ):
        ins = [(cos_all, cos_ref), (sin_all, sin_ref), (segc_all, segc_ref), (segr_all, segr_ref)] + [
            (wa_full.at[side], wa_v.at[pl.ds(side * half, half)]) for side in range(2)
        ]
        loads = [pltpu.make_async_copy(a, b, sem_c.at[n]) for n, (a, b) in enumerate(ins)]
        for copy in loads:
            copy.start()
        for copy in loads:
            copy.wait()

        @pl.loop(0, 2)
        def _(r):
            at = pl.ds(pl.multiple_of(r * 2 * rows, 2 * rows), 2 * rows)
            cosine = jnp.concatenate([cos_ref[at, :]] * (cols // 128), axis=1)
            sine = jnp.concatenate([sin_ref[at, :]] * (cols // 128), axis=1)

            def product(part):
                return dot_nn(rows_a[at, :], wa_v[:, pl.ds(part * cols, cols)])

            query = product(0)
            q_ref[at, :] = (query * cosine + swap_halves(query) * sine).astype(BF16)
            keys = product(1)
            k_ref[at, :] = (keys * cosine + swap_halves(keys) * sine).astype(BF16)
            v_ref[at, :] = product(2).astype(BF16)

        outs = [(q_ref, q_all), (k_ref, k_all), (v_ref, v_all), (rows_a, normed_all)]
        stores = [pltpu.make_async_copy(a, b, sem_c.at[n]) for n, (a, b) in enumerate(outs)]
        for copy in stores:
            copy.start()
        poll(2)
        for i in range(4):
            places = [(j, me.spots[j]) for j in key_blocks(i, rows)]
            at = at_block(me.spots[i])
            fill_bias(bias_ref, segc_ref[at, 0:1], segr_ref, i, places)
            spots = [at_block(p) for _, p in places]

            @pl.loop(0, cols // 128)
            def _(pair, at=at, spots=spots):
                attend(pair, 0, at, spots, head_lane, q_ref, k_ref, v_ref, mixed_ref, lse_ref, bias_ref)

            if i == 0:
                poll(line - 3)
            if i == 1:
                grads.forward()
            if i == 2:
                wo.arrived()
                wo_load = [
                    pltpu.make_async_copy(wo_full.at[side], wo_v.at[pl.ds(side * half, half)], sem_w.at[0, side])
                    for side in range(2)
                ]
                for copy in wo_load:
                    copy.start()
                poll()
        mixed_t[...] = mixed_ref[...].T
        for n, (a, b) in enumerate(((mixed_t, mixed_all), (lse_ref, lse_all))):
            stores.append(pltpu.make_async_copy(a, b, sem_c.at[len(outs) + n]))
            stores[-1].start()
        for copy in wo_load:
            copy.wait()

        def out_rows(b, slot, count=1):
            at = pl.ds(b * rows, count * rows)
            for side in range(2):
                here = pl.ds(side * half, half)
                value = dot_nt(mixed_ref[at, :], wo_v[here, :])
                if slot is None:
                    own[:, here] = value
                else:
                    for k in range(count):
                        stage[slot + k, :, here] = value[k * rows : (k + 1) * rows].astype(BF16)

        out_rows(3, 2)
        scatter.diagonal_ready()
        out_rows(1, 0, 2)
        scatter.sides_ready()
        out_rows(0, None)
        poll()
        scatter.combine()
        poll(3)
        for copy in stores:
            copy.wait()
        normed.done()
        scatter.arrived()

    V = pltpu.VMEM
    slab = V((LEN, cols), BF16)
    bias = V((3, rows, rows), F32)
    pl.run_scoped(
        forward, V((d, 3 * cols), BF16), V((d, cols), BF16), slab, slab, slab, slab, V((cols, LEN), BF16), table, table, table,
        *segs, bias,
    )

    def second_norm(at):
        values = x_ref[at, :].astype(F32) + summed(at)
        middle[at, :] = values
        rows_m[at, :] = (values * norm_factor(values) * gain_two).astype(BF16)

    norm_rows(local, second_norm)
    normed_mlp.start()
    free_landed()
    scatter.done()
    poll(2)
    grads.arrived()

    sizes = [3 * fw] * blocks + [cols] + [3 * GROUP] * groups
    chunks = [
        LineScatter(me, size, mine, theirs, swapped, kept_all.at[n], landed_all.at[n], work, sem_line.at[n], sem_step)
        for n, size in enumerate(sizes)
    ]
    writers = []
    for n in range(blocks):
        here = pl.ds(n * fw, fw)
        parts = [(gate_out.at[:, here], True), (up_out.at[:, here], True), (down_out.at[here], False)]
        writers.append(Writer(total, turned, parts, sem_write))
    parts = [(o_out.at[pl.ds(n * 256, 256)], False) for n in range(cols // 256)]
    writers.append(Writer(total, turned, parts, sem_write))
    for n in range(groups):
        here = pl.ds(n * GROUP, GROUP)
        parts = [(ref.at[:, here], True) for ref in (q_out, k_out, v_out)]
        writers.append(Writer(total, turned, parts, sem_write))
    ticks = Ticks(chunks, total, writers, TICK_HELD)

    def swap(n):
        if n >= 1:
            pl.semaphore_wait(free_core, 1)
        chunks[n].swap().start()

    def products(left, right, first, size):
        for side, dst in ((0, mine), (1, theirs)):
            value = dot_nn(left[...], right[:, pl.ds(side * half, half)]).astype(BF16)
            for s in range(line):
                dst[s, pl.ds(first, size), :] = value[:, s * shard : (s + 1) * shard]

    def mlp(wb, sums, dgu_t, hid_t, hid):
        def weights(n):
            return [
                pltpu.make_async_copy(
                    wf_full.at[n, side], wb.at[n % 2, pl.ds(side * half, half)], sem_w.at[n % 2, side]
                )
                for side in range(2)
            ]

        def hidden_copy(n):
            return pltpu.make_async_copy(hid.at[n % 2], hidden_all.at[n], sem_c.at[n % 2])

        fetched = [False] * (blocks + 1)

        def to_stage(b, slot):
            @pl.loop(0, rows // 64)
            def _(i):
                at = pl.ds(pl.multiple_of(i * 64, 64), 64)
                there = pl.ds(pl.multiple_of(b * rows + i * 64, 64), 64)
                if slot is None:
                    own[at, :] = sums[there, :]
                else:
                    stage[slot, at, :] = sums[there, :].astype(BF16)

        def fetch(n):
            if n < blocks and not fetched[n]:
                while not hops_done(n):
                    poll()
                gathers[n].arrived()
                for copy in weights(n):
                    copy.start()
                fetched[n] = True

        for n in range(blocks):
            fetch(n)
            if n == 0:

                @pl.loop(0, LEN // 64)
                def _(i):
                    at = pl.ds(pl.multiple_of(i * 64, 64), 64)
                    sums[at, :] = jnp.zeros((64, d), F32)

            for copy in weights(n):
                copy.wait()
            if n == 1:
                chunks[0].reduce(free_core)
            if n + 1 < blocks and hops_done(n + 1):
                fetch(n + 1)
            if n >= 2:
                hidden_copy(n - 2).wait()
            w = wb.at[n % 2]
            gu_w, down_w = w.at[:, pl.ds(0, 2 * fw)], w.at[:, pl.ds(2 * fw, fw)]

            def block_rows(at, n=n, gu_w=gu_w, down_w=down_w):
                gu = dot_nn(rows_m[at, :], gu_w[...])
                grad_hidden = dot_nn(rows_g[at, :], down_w[...])
                gate_pre, upward = gu[:, :fw], gu[:, fw:]
                sig = jax.nn.sigmoid(gate_pre)
                activated = gate_pre * sig
                hidden = (activated * upward).astype(BF16)
                hid[n % 2, at, :] = hidden
                hid_t[:, at] = hidden.T
                grad_gate = grad_hidden * upward * sig * (1.0 + gate_pre * (1.0 - sig))
                grad_up = grad_hidden * activated
                dgu = jnp.concatenate([grad_gate, grad_up], axis=1).astype(BF16)
                dgu_t[:, at] = dgu.T

                @pl.loop(0, 2)
                def _(c):
                    here = pl.ds(pl.multiple_of(c * half, half), half)
                    sums[at, here] += dot_nt(dgu, gu_w[here, :])

            if n == 0:
                block_rows(pl.ds(0, rows))
                poll()
                normed_mlp.forward()
                block_rows(pl.ds(rows, 2 * rows))
                normed_mlp.arrived()
                block_rows(pl.ds(3 * rows, rows))
                poll()
            elif n == blocks - 1:
                wait_free()
                block_rows(pl.ds(3 * rows, rows))
                to_stage(3, 2)
                scatter.diagonal_ready()
                block_rows(pl.ds(rows, 2 * rows))
                to_stage(1, 0)
                to_stage(2, 1)
                scatter.sides_ready()
                block_rows(pl.ds(0, rows))
                to_stage(0, None)
            else:
                @pl.loop(0, 2)
                def _(r, block_rows=block_rows):
                    block_rows(pl.ds(pl.multiple_of(r * 2 * rows, 2 * rows), 2 * rows))
            hidden_copy(n).start()
            if n % 2 == 1:
                poll()
            if n >= 2:
                chunks[n - 1].reduce(free_core)
            products(dgu_t, rows_m, 0, 2 * fw)
            products(hid_t, rows_g, 2 * fw, fw)
            swap(n)
            poll()
            if n in TICK_AFTER:
                ticks.tick()
        for n in range(max(0, blocks - 2), blocks):
            hidden_copy(n).wait()

    pl.run_scoped(
        mlp, V((2, d, 3 * fw), BF16), V((LEN, d), F32), V((2 * fw, LEN), BF16), V((fw, LEN), BF16),
        V((2, LEN, fw), BF16),
    )
    gp[...] = jnp.zeros(gp.shape, F32)

    def down(hidden, dw, rest):
        ins = [(hidden_all.at[n], hidden.at[:, pl.ds(n * fw, fw)]) for n in range(blocks)] + [
            (
                wf_full.at[n, side, :, pl.ds(2 * fw, fw)],
                dw.at[pl.ds(side * half, half), pl.ds(n * fw, fw)],
            )
            for n in range(blocks)
            for side in range(2)
        ]
        loads = [pltpu.make_async_copy(a, b, sem_c.at[n]) for n, (a, b) in enumerate(ins)]
        for copy in loads:
            copy.start()
        scatter.combine()
        ticks.tick()
        for copy in loads:
            copy.wait()

        @pl.loop(0, 4)
        def _(n):
            at = pl.ds(pl.multiple_of(n // 2 * 2 * rows, 2 * rows), 2 * rows)
            here = pl.ds(pl.multiple_of(n % 2 * half, half), half)
            rest[at, here] = dot_nt(hidden[at, :], dw[here, :]).astype(BF16)

        out = pltpu.make_async_copy(rest, y_all, sem_c.at[0])
        out.start()
        out.wait()

    pl.run_scoped(
        down, V((LEN, blocks * fw), BF16), V((d, blocks * fw), BF16), V((LEN, d), BF16)
    )
    normed_mlp.done()
    grads.done()

    def attention(
        q_ref, k_ref, v_ref, mixed_t, lse_ref, cos_ref, sin_ref, segc_ref, segr_ref, out_w,
        dqa_ref, dka_ref, dva_ref, part_t, bias_ref,
    ):
        ins = [
            (q_all, q_ref), (k_all, k_ref), (v_all, v_ref), (lse_all, lse_ref), (cos_all, cos_ref),
            (sin_all, sin_ref), (segc_all, segc_ref), (segr_all, segr_ref), (wo_full, out_w),
            (mixed_all, mixed_t), (normed_all, rows_m),
        ]
        loads = [pltpu.make_async_copy(a, b, sem_c.at[n]) for n, (a, b) in enumerate(ins)]
        for copy in loads:
            copy.start()
        scatter.arrived()

        def second_norm_back(at, back):
            grad = rows_g[at, :].astype(F32) + back
            gm[at, :] = grad
            rows_a[at, :] = grad.astype(BF16)

        norm_back_rows(local, gain_two, lambda at: middle[at, :], summed, gp, 1, second_norm_back)
        square.start()
        free_landed()
        scatter.done()
        stage_in = [
            pltpu.make_async_copy(y_all.at[pl.ds(b * rows, rows)], stage.at[slot], sem_w.at[n // 2, n % 2])
            for n, (b, slot) in enumerate(((3, 2), (1, 0), (2, 1)))
        ]
        for copy in stage_in:
            copy.start()
        chunks[blocks - 1].reduce(free_core)
        ticks.tick()
        for copy in loads:
            copy.wait()

        @pl.loop(0, 4)
        def _(b):
            at = at_block(b)
            dka_ref[at, :] = jnp.zeros((rows, cols), F32)
            dva_ref[at, :] = jnp.zeros((rows, cols), F32)

        dm_ref = rows_g.at[:, pl.ds(3 * cols, cols)]

        def query_block(p, between=None):
            at = pl.ds(p * rows, rows)
            dm_ref[at, :] = (
                dot_nn(rows_a[at, :half], out_w[0]) + dot_nn(rows_a[at, half:], out_w[1])
            ).astype(BF16)
            spots = me.window(me.spots[p], rows, segc_ref[at, 0:1], segr_ref, bias_ref)

            def one_pair(pair):
                attend_back(
                    pair, at, spots, head_lane, q_ref, k_ref, v_ref, dm_ref, lse_ref, bias_ref,
                    dqa_ref, dka_ref, dva_ref,
                )

            pairs = GROUP // 128
            if between is None:
                pl.loop(0, cols // 128)(one_pair)
            for group in range(groups):
                if between is not None:
                    pl.loop(group * pairs, (group + 1) * pairs)(one_pair)
                lanes = pl.ds(group * GROUP, GROUP)
                value = dqa_ref[:, lanes]
                value = value * doubled(cos_ref, at) - swap_halves(value) * doubled(sin_ref, at)
                rows_g[at, lanes] = value.astype(BF16)
                if between is not None:
                    between(group)

        query_block(0)
        ticks.tick()
        square.forward()
        query_block(1)
        query_block(2)
        ticks.tick()
        for copy in stage_in:
            copy.wait()
        wait_free()
        square.arrived()
        scatter.diagonal_ready()
        scatter.sides_ready()
        products(mixed_t, rows_a, 0, cols)
        swap(blocks)
        def turn(group):
            @pl.loop(0, 4)
            def _(b):
                at = at_block(b)
                cosine, sine = doubled(cos_ref, at), doubled(sin_ref, at)
                for part, ref in enumerate((None, dka_ref, dva_ref)):
                    lanes = pl.ds(group * GROUP, GROUP)
                    there = pl.ds(part * cols + group * GROUP, GROUP)
                    if part == 0:
                        value = rows_g[at, there]
                    else:
                        value = ref[at, lanes]
                        if part == 1:
                            value = value * cosine - swap_halves(value) * sine
                        value = value.astype(BF16)
                        rows_g[at, there] = value
                    part_t[pl.ds(part * GROUP, GROUP), at] = value.T

        def finish_group(group):
            chunks[blocks + group].reduce(free_core)
            turn(group)
            products(part_t, rows_m, 0, 3 * GROUP)
            swap(blocks + 1 + group)
            if group == 0:
                scatter.combine()
                ticks.tick()

        query_block(3, finish_group)

    pl.run_scoped(
        attention, slab, slab, slab, V((cols, LEN), BF16), table, table, table, *segs,
        V(wo_full.shape, BF16), V((rows, cols), F32), V((LEN, cols), F32), V((LEN, cols), F32),
        V((3 * GROUP, LEN), BF16), bias,
    )

    def normed_grads(qkv_w, stage_two, y_mine):
        ins = [(wa_full.at[side], qkv_w.at[pl.ds(side * half, half)]) for side in range(2)]
        ins.append((y_all.at[pl.ds(0, rows)], y_mine))
        loads = [pltpu.make_async_copy(a, b, sem_c.at[n]) for n, (a, b) in enumerate(ins)]
        for copy in loads:
            copy.start()
        for copy in loads:
            copy.wait()

        def normed_grad(b, slot, count=1):
            at = pl.ds(b * rows, count * rows)
            for side in range(2):
                here = pl.ds(side * half, half)
                value = dot_nt(rows_g[at, pl.ds(0, 3 * cols)], qkv_w[here, :])
                if slot is None:
                    own[:, here] = value
                else:
                    for k in range(count):
                        stage_two[slot + k, :, here] = value[k * rows : (k + 1) * rows].astype(BF16)

        normed_grad(3, 2)
        normed_grad(1, 0, 2)
        normed_grad(0, None)
        scatter.arrived()

        def output_rows(at):
            value = middle[at, :] + y_mine[at, :].astype(F32)
            value = value + landed[0, at, :].astype(F32) + landed[1, at, :].astype(F32)
            y_mine[at, :] = value.astype(BF16)

        norm_rows(local, output_rows)
        free_landed()
        results = [
            pltpu.make_async_copy(
                y_mine.at[:, own_columns(*p)], output_out.at[:, true_columns(*p)], sem_in.at[n]
            )
            for n, p in enumerate(sides)
        ]
        for copy in results:
            copy.start()
        scatter.done()
        wait_free()
        scatter_two = SquareScatter(me, stage_two, landed, sem_s)
        scatter_two.diagonal_ready()
        scatter_two.sides_ready()
        chunks[blocks + groups].reduce(free_core)
        ticks.tick(2, 2)
        for copy in results:
            copy.wait()
        scatter_two.combine()
        ticks.tick(3, 2)
        ticks.tick(3, 0)
        ticks.tick(3, 0)
        scatter_two.arrived()
        scatter_two.done()

    pl.run_scoped(
        normed_grads, V((d, 3 * cols), BF16), V((3, local, d), BF16), V((local, d), BF16)
    )

    def first_norm_back(at, back):
        gm[at, :] += back

    norm_back_rows(
        local, gain_one, lambda at: x_ref[at, :].astype(F32), summed, gp, 0, first_norm_back
    )
    results = [
        pltpu.make_async_copy(
            gm.at[:, own_columns(*p)], input_grad_out.at[:, true_columns(*p)], sem_in.at[n]
        )
        for n, p in enumerate(sides)
    ]
    for copy in results:
        copy.start()
    peers = [me.x, me.y] + [{"dp": (me.index + k) % dp} for k in range(1, dp)]
    exchange = [
        remote(gp, gp_landed.at[n], sem_gain.at[n, 0], sem_gain.at[n, 1], device)
        for n, device in enumerate(peers)
    ]
    for n in range(2):
        exchange[n].start()
        exchange[n].wait()
        gp[...] += gp_landed[n]
    for copy in exchange[2:]:
        copy.start()
    ticks.rest()
    for copy in exchange[2:]:
        copy.wait()
    for k in range(1, dp):
        if k % 2 == 1:
            gp[:, :half] += gp_landed[1 + k, :, half:]
            gp[:, half:] += gp_landed[1 + k, :, :half]
        else:
            gp[...] += gp_landed[1 + k]
    gain_out[...] = gp[...]
    ticks.done()
    pl.semaphore_wait(free_core, 1)
    for k in range(1, dp):
        gain_copy(k, me.index).wait_send()
    for copy in results:
        copy.wait()
    for one in [wa, wo, square] + gathers:
        one.done()


def layer(dp, x, g, gains, wq, wk, wv, wo, gate, up, down, docs):
    line = dp // 2
    local, d = x.shape
    cols, ff = wq.shape[1], gate.shape[1]
    blocks, shard = FF_BLOCKS, d // dp
    fw = ff // blocks
    groups = cols // GROUP
    count = blocks + 1 + groups
    most = max(3 * fw, cols, 3 * GROUP)
    vm, hbm = pl.BlockSpec(memory_space=pltpu.VMEM), pl.BlockSpec(memory_space=pl.ANY)
    S, V, dma = jax.ShapeDtypeStruct, pltpu.VMEM, pltpu.SemaphoreType.DMA
    regular = pltpu.SemaphoreType.REGULAR
    slab = S((LEN, cols), BF16)
    piece = V((line, most, shard), BF16)
    return pl.pallas_call(
        functools.partial(layer_kernel, dp),
        in_specs=[hbm, hbm, vm, hbm, hbm, hbm, vm, hbm, hbm, vm, vm],
        out_specs=[hbm, hbm, vm] + [hbm] * 24,
        out_shape=[
            S((local, d), BF16), S((local, d), F32), S((8, d), F32),
            S((shard, ff), BF16), S((shard, ff), BF16), S((ff, shard), BF16),
            S((shard, cols), BF16), S((shard, cols), BF16), S((shard, cols), BF16), S((cols, shard), BF16),
            S((2, d // 2, 3 * cols), BF16), S((2, d // 2, cols), BF16),
            S((blocks, 2, d // 2, 3 * fw), BF16), S((blocks, LEN, fw), BF16),
            S((count, line, most, shard), BF16), S((count, line + 1, most, shard), BF16),
            S((LEN, d), BF16), S((LEN, d), BF16), slab, slab, slab, S((cols, LEN), BF16), S((LEN, 128), F32),
            S((LEN, 128), F32), S((LEN, 128), F32), S((LEN, 128), jnp.int32), S((4, 8, LEN // 4), jnp.int32),
        ],
        scratch_shapes=[
            V((local, d), BF16), V((shard, 3 * cols), BF16), V((shard, cols), BF16),
            V((blocks, shard, 3 * fw), BF16), V((2, line * 16, shard), BF16),
            V((LEN, d), BF16), V((LEN, d), BF16), V((LEN, d), BF16),
            piece, piece, piece, V((9, most, shard), BF16), V((most, shard), F32), V((3, shard, 256), BF16),
            V((3, local, d), BF16), V((3, local, d), BF16), V((local, d), F32), V((local, d), F32),
            V((local, d), F32), V((8, d), F32), V((dp + 1, 8, d), F32),
            dma((4 * line + 3 + 2 * blocks,)), dma((2, dp)), dma((6, line)), dma((6, line)),
            dma((blocks, 6, line)), dma((8,)), dma((8,)), dma((8,)), dma((8,)), dma((12,)),
            dma((count, 2 * line + 1)), dma((12,)), dma((3,)), dma((dp + 1, 2)), dma((3 * blocks,)), dma((2, 2)),
            regular, regular, regular,
        ],
        compiler_params=pltpu.CompilerParams(
            vmem_limit_bytes=VMEM_BYTES, collective_id=0, has_side_effects=True
        ),
        name="layer",
    )(x, g, gains, wq, wk, wv, wo, gate, up, down, docs)


def widen_kernel(*refs):
    count = (len(refs) - 2) // 4
    ins, outs = refs[:count], refs[count : 2 * count]
    here, wide = refs[2 * count : 3 * count], refs[3 * count : 4 * count]
    sem_in, sem_out = refs[-2:]
    loads = [pltpu.make_async_copy(a, b, sem_in.at[n]) for n, (a, b) in enumerate(zip(ins, here))]
    stores = [pltpu.make_async_copy(a, b, sem_out.at[n]) for n, (a, b) in enumerate(zip(wide, outs))]
    for copy in loads:
        copy.start()
    for n, (load, store) in enumerate(zip(loads, stores)):
        load.wait()
        rows = here[n].shape[0]
        step = min(rows, 64)

        @pl.loop(0, rows // step)
        def _(i, n=n, step=step):
            at = pl.ds(pl.multiple_of(i * step, step), step)
            wide[n][at, :] = here[n][at, :].astype(wide[n].dtype)

        store.start()
    for store in stores:
        store.wait()


def widen(arrays, dtypes):
    hbm = pl.BlockSpec(memory_space=pl.ANY)
    return pl.pallas_call(
        widen_kernel,
        in_specs=[hbm] * len(arrays),
        out_specs=[hbm] * len(arrays),
        out_shape=[jax.ShapeDtypeStruct(a.shape, t) for a, t in zip(arrays, dtypes)],
        scratch_shapes=[pltpu.VMEM(a.shape, a.dtype) for a in arrays]
        + [pltpu.VMEM(a.shape, t) for a, t in zip(arrays, dtypes)]
        + [pltpu.SemaphoreType.DMA((len(arrays),))] * 2,
        compiler_params=pltpu.CompilerParams(vmem_limit_bytes=VMEM_BYTES),
        name="widen",
    )(*arrays)


def on_device(
    dp, tensor, hidden_in, doc_lengths, gain_attn, w_query, w_key, w_value, w_out, gain_mlp,
    w_gate, w_up, w_down, cotangent,
):
    line = dp // 2
    core = lax.axis_index("dp") % 2
    place = lax.axis_index("tensor")
    square = tensor == 4 and dp == 8
    same_core = [[c + 2 * z for z in range(line)] for c in range(2)]
    sibling = [(i, i ^ 1) for i in range(dp)]
    d = hidden_in.shape[1]
    local = hidden_in.shape[0]

    def own_first(a):
        s = a.reshape(a.shape[:-1] + (line, 2, d // dp))
        even, odd = s[..., 0, :], s[..., 1, :]
        out = jnp.concatenate(
            [jnp.where(core == 0, even, odd), jnp.where(core == 0, odd, even)], axis=-2
        )
        return out.reshape(a.shape)

    def true_order(a):
        s = a.reshape(a.shape[:-1] + (2, line, d // dp))
        first, second = s[..., 0, :, :], s[..., 1, :, :]
        out = jnp.stack(
            [jnp.where(core == 0, first, second), jnp.where(core == 0, second, first)], axis=-2
        )
        return out.reshape(a.shape)

    def hop(a, step):
        return lax.ppermute(a, "tensor", [(i, i ^ step) for i in range(tensor)])

    def gather_rows(a):
        if not square:
            return lax.all_gather(a, "tensor", axis=0, tiled=True)
        half = a.shape[0] // 2
        from_x, from_y = hop(a, 1), hop(a, 2)
        top, bottom = hop(from_x[:half], 2), hop(from_y[half:], 1)
        return jnp.concatenate([a, from_x, from_y, top, bottom], axis=0)

    def scatter_rows(a):
        if not square:
            return lax.psum_scatter(a, "tensor", scatter_dimension=0, tiled=True).astype(F32)
        n = a.shape[0] // 4
        half = n // 2
        top = hop(a[3 * n : 3 * n + half], 2)
        bottom = hop(a[3 * n + half :], 1)
        for_x = jnp.concatenate([a[n : n + half] + top, a[n + half : 2 * n]], axis=0)
        for_y = jnp.concatenate([a[2 * n : 2 * n + half], a[2 * n + half : 3 * n] + bottom], axis=0)
        return (a[:n].astype(F32) + hop(for_x, 1).astype(F32)) + hop(for_y, 2).astype(F32)

    def line_gather(a):
        own = lax.all_gather(a, "dp", axis=0, axis_index_groups=same_core, tiled=True)
        return own, lax.ppermute(own, "dp", sibling)

    def line_scatter(own, sib):
        mine = own + lax.ppermute(sib, "dp", sibling)
        return lax.psum_scatter(
            mine, "dp", scatter_dimension=0, axis_index_groups=same_core, tiled=True
        ).astype(F32)

    blocks = 4
    rows = LEN // blocks
    key = place if square else jnp.zeros((), jnp.int32)
    tokens = (
        (jnp.arange(blocks, dtype=jnp.int32) ^ key)[:, None] * rows
        + jnp.arange(rows, dtype=jnp.int32)[None, :]
    ).reshape(LEN)
    segment, position = doc_tables(doc_lengths, tokens)
    cosine, sine = rotary_tables(position)
    segc = jnp.broadcast_to(segment[:, None], (LEN, 128))
    segr = jnp.broadcast_to(segment.reshape(blocks, 1, rows), (blocks, 8, rows))
    key = key.reshape(1)
    cols = w_query.shape[1]
    if square:
        gain_rows = jnp.pad(
            jnp.concatenate([gain_attn, gain_mlp]), (0, 14 * gain_attn.shape[0])
        ).reshape(16, -1)
        (
            output, input_grad, gain_sum, grad_gate, grad_up, grad_down, grad_query, grad_key,
            grad_value, grad_out, *_,
        ) = layer(
            dp, hidden_in, cotangent, gain_rows, w_query, w_key, w_value, w_out, w_gate, w_up,
            w_down, doc_lengths,
        )
        share = d // (dp * tensor)
        first = (lax.axis_index("dp") // 2) * (d // dp) + place * share
        gain_sum = lax.dynamic_slice_in_dim(gain_sum, first, share, 1)
        grads = (grad_gate, grad_up, grad_down, grad_query, grad_key, grad_value, grad_out)
        (
            output, input_grad, grad_gate, grad_up, grad_down, grad_query, grad_key, grad_value, grad_out
        ) = widen((output, input_grad) + grads, (BF16,) + (F32,) * 8)
        return (
            output, input_grad, gain_sum[0], grad_query, grad_key, grad_value, grad_out, gain_sum[1],
            grad_gate, grad_up, grad_down,
        )

    cosine, sine = (jnp.tile(a, (1, GROUP // 128)) for a in (cosine, sine))
    ff = w_gate.shape[1]
    fb = ff // FF_BLOCKS
    down_t = w_down.T
    shards = [
        jnp.concatenate([w[:, b * fb : (b + 1) * fb] for w in (w_gate, w_up, down_t)], axis=1)
        for b in range(FF_BLOCKS)
    ]
    qkv_shard = jnp.concatenate([w_query, w_key, w_value], axis=1)
    g_local = own_first(cotangent)
    inputs = own_first(hidden_in).astype(F32)
    factor_one = norm_factor(inputs)
    gains = lax.all_gather(jnp.stack([gain_attn, gain_mlp]), "dp", axis=0)
    gains = own_first(jnp.moveaxis(gains, 0, 1).reshape(2, d)).astype(F32)
    gain_one, gain_two = gains[0], gains[1]
    qkv_own, qkv_sib = line_gather(qkv_shard)
    out_own, out_sib = line_gather(w_out.T)
    normed = gather_rows((inputs * factor_one * gain_one).astype(BF16))
    g_all = gather_rows(g_local)
    query, keys, values, mixed, lse = attn_forward(
        blocks, key, normed, qkv_own, qkv_sib, cosine, sine, segc, segr
    )
    attended = jnp.concatenate(
        [dot_nt(mixed, out_own).astype(BF16), dot_nt(mixed, out_sib).astype(BF16)], axis=1
    )
    middle = inputs + scatter_rows(attended)
    factor_two = norm_factor(middle)
    normed_mlp = gather_rows((middle * factor_two * gain_two).astype(BF16))
    ff_sets = [jnp.concatenate(line_gather(shard), axis=0) for shard in shards]

    down_sum = jnp.zeros((LEN, d), F32)
    back_sum = jnp.zeros((LEN, d), F32)
    ff_grads = []
    for b in range(FF_BLOCKS):
        gate_w, up_w, down_w = jnp.split(ff_sets[b], 3, axis=1)
        gate_pre = dot_nn(normed_mlp, gate_w)
        upward = dot_nn(normed_mlp, up_w)
        grad_hidden = dot_nn(g_all, down_w)
        sig = jax.nn.sigmoid(gate_pre)
        activated = gate_pre * sig
        hidden = (activated * upward).astype(BF16)
        grad_gate_pre = (grad_hidden * upward * sig * (1.0 + gate_pre * (1.0 - sig))).astype(BF16)
        grad_upward = (grad_hidden * activated).astype(BF16)
        down_sum = down_sum + dot_nt(hidden, down_w)
        back_sum = back_sum + dot_nt(grad_gate_pre, gate_w) + dot_nt(grad_upward, up_w)
        grad = jnp.concatenate(
            [
                dot_tn(normed_mlp, grad_gate_pre).astype(BF16),
                dot_tn(normed_mlp, grad_upward).astype(BF16),
                dot_tn(g_all, hidden).astype(BF16),
            ],
            axis=1,
        )
        ff_grads.append(line_scatter(grad[: d // 2], grad[d // 2 :]))
    grad_norm_two = scatter_rows(back_sum.astype(BF16))
    output = true_order((middle + scatter_rows(down_sum.astype(BF16))).astype(BF16))
    grad_mid_norm, gain_two_part = norm_back(middle, factor_two, gain_two, grad_norm_two)
    grad_middle = g_local.astype(F32) + grad_mid_norm
    grad_mid_all = gather_rows(grad_middle.astype(BF16))

    dq, dk, dv = attn_backward(
        blocks, key, grad_mid_all, out_own, out_sib, query, keys, values, lse, cosine, sine,
        segc, segr,
    )
    grad = jnp.concatenate(
        [dot_tn(normed, dq), dot_tn(normed, dk), dot_tn(normed, dv), dot_tn(grad_mid_all, mixed)],
        axis=1,
    ).astype(BF16)
    attn_grads = line_scatter(grad[: d // 2], grad[d // 2 :])
    rows_grad = jnp.concatenate([dq, dk, dv], axis=1)
    back = jnp.concatenate(
        [
            dot_nt(rows_grad, qkv_own).astype(BF16),
            dot_nt(rows_grad, qkv_sib).astype(BF16),
        ],
        axis=1,
    )
    grad_in_norm, gain_one_part = norm_back(inputs, factor_one, gain_one, scatter_rows(back))
    input_grad = true_order(grad_middle + grad_in_norm)

    parts = true_order(jnp.stack([gain_one_part, gain_two_part])).reshape(2 * d)
    shares = lax.all_gather(parts, ("dp", "tensor"), axis=0)
    gain_sum = jnp.sum(shares, axis=0).reshape(2, d)
    share = d // (dp * tensor)
    first = (lax.axis_index("dp") * tensor + place) * share
    gain_sum = lax.dynamic_slice_in_dim(gain_sum, first, share, 1)

    return (
        output,
        input_grad,
        gain_sum[0],
        attn_grads[:, :cols],
        attn_grads[:, cols : 2 * cols],
        attn_grads[:, 2 * cols : 3 * cols],
        attn_grads[:, 3 * cols :].T,
        gain_sum[1],
        jnp.concatenate([g[:, :fb] for g in ff_grads], axis=1),
        jnp.concatenate([g[:, fb : 2 * fb] for g in ff_grads], axis=1),
        jnp.concatenate([g[:, 2 * fb :] for g in ff_grads], axis=1).T,
    )


def solution(mesh):
    shape = dict(mesh.shape)
    return jax.shard_map(
        functools.partial(on_device, shape["dp"], shape["tensor"]),
        mesh=mesh,
        in_specs=(
            P(("dp", "tensor"), None),
            P("dp", None),
            P("dp"),
            P("dp", "tensor"),
            P("dp", "tensor"),
            P("dp", "tensor"),
            P("tensor", "dp"),
            P("dp"),
            P("dp", "tensor"),
            P("dp", "tensor"),
            P("tensor", "dp"),
            P(("dp", "tensor"), None),
        ),
        out_specs=(
            P(("dp", "tensor"), None),
            P(("dp", "tensor"), None),
            P(("dp", "tensor")),
            P("dp", "tensor"),
            P("dp", "tensor"),
            P("dp", "tensor"),
            P("tensor", "dp"),
            P(("dp", "tensor")),
            P("dp", "tensor"),
            P("dp", "tensor"),
            P("tensor", "dp"),
        ),
        check_vma=False,
    )
```

```python
import functools
import math

import jax
import jax.numpy as jnp
from jax import lax
from jax.experimental import pallas as pl
from jax.experimental.pallas import tpu as pltpu
from jax.sharding import PartitionSpec as P

HEAD_DIM = 64
LEN = 1024
MOST = 512
EPSILON = 1e-05
ROPE_BASE = 130000.0
NEG = -1e30
GROUP = 256
FF_BLOCKS = 8
F32 = jnp.float32
BF16 = jnp.bfloat16
VMEM_BYTES = 63 * 1024 * 1024


def dot_nn(a, b):
    return jnp.dot(a, b, preferred_element_type=F32)


def dot_tn(a, b):
    return lax.dot_general(a, b, (((0,), (0,)), ((), ())), preferred_element_type=F32)


def dot_nt(a, b):
    return lax.dot_general(a, b, (((1,), (1,)), ((), ())), preferred_element_type=F32)


def norm_factor(values):
    return lax.rsqrt(jnp.mean(values * values, axis=-1, keepdims=True) + EPSILON)


def norm_back(values, factor, gain, grads):
    scaled = grads * gain
    grad_in = factor * scaled - values * factor * factor * factor * jnp.mean(
        scaled * values, axis=-1, keepdims=True
    )
    return grad_in, jnp.sum(grads * values * factor, axis=0)


def doc_tables(doc_lengths, tokens):
    ends = jnp.cumsum(doc_lengths, axis=1)[0]
    passed = tokens[:, None] >= ends[None, :]
    segment = jnp.sum(passed.astype(jnp.int32), axis=1)
    start = jnp.sum(jnp.where(passed, doc_lengths, 0), axis=1)
    return segment, tokens - start


def rotary_tables(position):
    half = HEAD_DIM // 2
    inverse = jnp.power(ROPE_BASE, -jnp.arange(half, dtype=F32) * 2.0 / HEAD_DIM)
    angles = position.astype(F32)[:, None] * inverse
    cosine, sine = jnp.cos(angles), jnp.sin(angles)
    heads = 128 // HEAD_DIM
    return (
        jnp.tile(jnp.concatenate([cosine, cosine], axis=1), (1, heads)),
        jnp.tile(jnp.concatenate([-sine, sine], axis=1), (1, heads)),
    )


def swap_halves(v):
    half, width = HEAD_DIM // 2, v.shape[1]
    lane = lax.broadcasted_iota(jnp.int32, v.shape, 1)
    ahead = pltpu.roll(v, width - half, 1)
    behind = pltpu.roll(v, half, 1)
    return jnp.where(lane % HEAD_DIM < half, ahead, behind)


def key_blocks(i, rows):
    reach = -(-(MOST - 1) // rows)
    return list(range(max(0, i - reach), i + 1))


def fill_bias(bias_ref, seg_col, seg_ref, i, places):
    rows = seg_col.shape[0]
    for n, (j, place) in enumerate(places):
        same = seg_col == seg_ref[place][0:1, :]
        if j == i:
            row = lax.broadcasted_iota(jnp.int32, (rows, rows), 0)
            col = lax.broadcasted_iota(jnp.int32, (rows, rows), 1)
            same = same & (col <= row)
        bias_ref[n] = jnp.where(same, 0.0, NEG)


def attn_forward_kernel(
    blocks, key_ref, x_ref, qo, qs, ko, ks, vo, vs, cos_ref, sin_ref, segc_ref, segr_ref,
    q_ref, k_ref, v_ref, mixed_ref, lse_ref, bias_ref,
):
    rows = LEN // blocks
    half = x_ref.shape[1] // 2
    key = key_ref[0]

    @pl.loop(0, blocks)
    def _(b):
        at = pl.ds(pl.multiple_of(b * rows, rows), rows)
        left, right = x_ref[at, :half], x_ref[at, half:]
        cosine, sine = cos_ref[at, :], sin_ref[at, :]
        query = dot_nn(left, qo[...]) + dot_nn(right, qs[...])
        q_ref[at, :] = (query * cosine + swap_halves(query) * sine).astype(BF16)
        keys = dot_nn(left, ko[...]) + dot_nn(right, ks[...])
        k_ref[at, :] = (keys * cosine + swap_halves(keys) * sine).astype(BF16)
        v_ref[at, :] = (dot_nn(left, vo[...]) + dot_nn(right, vs[...])).astype(BF16)

    head_lane = lax.broadcasted_iota(jnp.int32, (rows, 128), 1)
    for i in range(blocks):
        places = [(j, j ^ key) for j in key_blocks(i, rows)]
        at = pl.ds(pl.multiple_of((i ^ key) * rows, rows), rows)
        fill_bias(bias_ref, segc_ref[at, 0:1], segr_ref, i, places)
        spots = [pl.ds(pl.multiple_of(p * rows, rows), rows) for _, p in places]

        @pl.loop(0, GROUP // 128)
        def _(pair, at=at, spots=spots):
            first = pl.program_id(0) * (GROUP // HEAD_DIM)
            attend(pair, first, at, spots, head_lane, q_ref, k_ref, v_ref, mixed_ref, lse_ref, bias_ref)


def attn_forward(blocks, key, x, own, sib, cosine, sine, segc, segr):
    d = x.shape[1]
    cols = own.shape[1] // 3
    steps = cols // GROUP
    rows = LEN // blocks

    def weight(part):
        return pl.BlockSpec((d // 2, GROUP), lambda i, part=part: (0, part * steps + i))

    def whole(shape):
        return pl.BlockSpec(shape, lambda i: (0,) * len(shape))

    col_block = pl.BlockSpec((LEN, GROUP), lambda i: (0, i))
    slab = jax.ShapeDtypeStruct((LEN, cols), BF16)
    return pl.pallas_call(
        functools.partial(attn_forward_kernel, blocks),
        grid=(steps,),
        in_specs=[pl.BlockSpec(memory_space=pltpu.SMEM), whole((LEN, d))]
        + [weight(p) for p in (0, 0, 1, 1, 2, 2)]
        + [whole((LEN, GROUP))] * 2
        + [whole((LEN, 128)), whole(segr.shape)],
        out_specs=[col_block] * 4 + [whole((LEN, 128))],
        out_shape=[slab] * 4 + [jax.ShapeDtypeStruct((LEN, 128), F32)],
        scratch_shapes=[pltpu.VMEM((blocks, rows, rows), F32)],
        compiler_params=pltpu.CompilerParams(vmem_limit_bytes=VMEM_BYTES),
        name="attn_forward",
    )(key, x, own, sib, own, sib, own, sib, cosine, sine, segc, segr)


def attn_backward_kernel(
    blocks, key_ref, g_ref, wo, ws, q_ref, k_ref, v_ref, lse_ref, cos_ref, sin_ref, segc_ref,
    segr_ref, dq_ref, dk_ref, dv_ref, dm_ref, dqa_ref, dka_ref, dva_ref, bias_ref,
):
    rows = LEN // blocks
    half = g_ref.shape[1] // 2
    key = key_ref[0]

    @pl.loop(0, blocks)
    def _(b):
        at = pl.ds(pl.multiple_of(b * rows, rows), rows)
        dm_ref[at, :] = (dot_nn(g_ref[at, :half], wo[...]) + dot_nn(g_ref[at, half:], ws[...])).astype(BF16)
        dka_ref[at, :] = jnp.zeros((rows, GROUP), F32)
        dva_ref[at, :] = jnp.zeros((rows, GROUP), F32)

    head_lane = lax.broadcasted_iota(jnp.int32, (rows, 128), 1)
    scale = HEAD_DIM**-0.5
    for i in range(blocks):
        places = [(j, j ^ key) for j in key_blocks(i, rows)]
        at = pl.ds(pl.multiple_of((i ^ key) * rows, rows), rows)
        fill_bias(bias_ref, segc_ref[at, 0:1], segr_ref, i, places)
        spots = [pl.ds(pl.multiple_of(p * rows, rows), rows) for _, p in places]

        @pl.loop(0, GROUP // 128)
        def _(pair, at=at, spots=spots):
            lanes = pl.ds(pl.multiple_of(pair * 128, 128), 128)
            first = pl.program_id(0) * (GROUP // HEAD_DIM)
            query, grad = q_ref[at, lanes], dm_ref[at, lanes]
            logs = lse_ref[at, :]
            outs = []
            for h in range(2):
                mine = (head_lane < HEAD_DIM) if h == 0 else (head_lane >= HEAD_DIM)
                qm = jnp.where(mine, query, 0) * jnp.asarray(scale, BF16)
                gm = jnp.where(mine, grad, 0)
                log = jnp.sum(
                    jnp.where(head_lane == first + pair * 2 + h, logs, 0.0), axis=1, keepdims=True
                )
                weights = [
                    jnp.exp(dot_nt(qm, k_ref[s, lanes]) + bias_ref[n] - log)
                    for n, s in enumerate(spots)
                ]
                grads = [dot_nt(gm, v_ref[s, lanes]) for s in spots]
                inner = sum(
                    jnp.sum(w * g, axis=1, keepdims=True) for w, g in zip(weights, grads)
                )
                dq = jnp.zeros((rows, 128), F32)
                for w, g, s in zip(weights, grads, spots):
                    ds = (w * (g - inner)).astype(BF16)
                    dva_ref[s, lanes] += dot_tn(w.astype(BF16), gm)
                    dka_ref[s, lanes] += dot_tn(ds, qm)
                    dq = dq + dot_nn(ds, k_ref[s, lanes])
                outs.append(dq)
            dqa_ref[at, lanes] = jnp.where(head_lane < HEAD_DIM, outs[0], outs[1]) * scale

    @pl.loop(0, blocks)
    def _(b):
        at = pl.ds(pl.multiple_of(b * rows, rows), rows)
        cosine, sine = cos_ref[at, :], sin_ref[at, :]
        dq = dqa_ref[at, :]
        dq_ref[at, :] = (dq * cosine - swap_halves(dq) * sine).astype(BF16)
        dk = dka_ref[at, :]
        dk_ref[at, :] = (dk * cosine - swap_halves(dk) * sine).astype(BF16)
        dv_ref[at, :] = dva_ref[at, :].astype(BF16)


def attn_backward(blocks, key, g, own, sib, q, k, v, lse, cosine, sine, segc, segr):
    d = g.shape[1]
    cols = q.shape[1]
    steps = cols // GROUP
    rows = LEN // blocks

    def whole(shape):
        return pl.BlockSpec(shape, lambda i: (0,) * len(shape))

    col_block = pl.BlockSpec((LEN, GROUP), lambda i: (0, i))
    weight = pl.BlockSpec((d // 2, GROUP), lambda i: (0, i))
    slab = jax.ShapeDtypeStruct((LEN, cols), BF16)
    return pl.pallas_call(
        functools.partial(attn_backward_kernel, blocks),
        grid=(steps,),
        in_specs=[pl.BlockSpec(memory_space=pltpu.SMEM), whole((LEN, d)), weight, weight]
        + [col_block] * 3
        + [whole((LEN, 128))]
        + [whole((LEN, GROUP))] * 2
        + [whole((LEN, 128)), whole(segr.shape)],
        out_specs=[col_block] * 3,
        out_shape=[slab] * 3,
        scratch_shapes=[
            pltpu.VMEM((LEN, GROUP), BF16),
            pltpu.VMEM((LEN, GROUP), F32),
            pltpu.VMEM((LEN, GROUP), F32),
            pltpu.VMEM((LEN, GROUP), F32),
            pltpu.VMEM((blocks, rows, rows), F32),
        ],
        compiler_params=pltpu.CompilerParams(vmem_limit_bytes=VMEM_BYTES),
        name="attn_backward",
    )(key, g, own, sib, q, k, v, lse, cosine, sine, segc, segr)


class LineGather:
    def __init__(self, me, src, full, sems):
        self.me, self.src, self.full, self.sems = me, src, full, sems
        self.rows = src.shape[0]

    def spot(self, side, s):
        return self.full.at[side, pl.ds(pl.multiple_of(s * self.rows, self.rows), self.rows)]

    def to_line(self, src, s, way):
        device = self.me.up if way == 0 else self.me.down
        return remote(src, self.spot(0, s), self.sems.at[way, s], self.sems.at[3, s], device)

    def to_core(self, src, s):
        return remote(src, self.spot(1, s), self.sems.at[2, s], self.sems.at[4, s], self.me.other)

    def keep(self):
        return pltpu.make_async_copy(self.src, self.spot(0, self.me.z), self.sems.at[5, 0])

    def start(self):
        z, line = self.me.z, self.me.line

        @pl.when(z + 1 < line)
        def _():
            self.to_line(self.src, z, 0).start()

        @pl.when(z >= 1)
        def _():
            self.to_line(self.src, z, 1).start()

        self.to_core(self.src, z).start()
        self.keep().start()

    def hop(self, h):
        z, line = self.me.z, self.me.line
        for s, arrives, goes_on, way in (
            (z - h, z >= h, z + 1 < line, 0),
            (z + h, z + h < line, z >= 1, 1),
        ):

            @pl.when(arrives)
            def _(s=s, goes_on=goes_on, way=way):
                here = self.spot(0, s)
                self.to_line(here, s, way).wait_recv()

                @pl.when(goes_on)
                def _():
                    self.to_line(here, s, way).start()

                self.to_core(here, s).start()

    def arrived(self):
        self.keep().wait()
        for s in range(self.me.line):
            self.to_core(self.spot(0, s), s).wait_recv()

    def done(self):
        z, line = self.me.z, self.me.line
        for s in range(line):
            here = self.spot(0, s)
            self.to_core(here, s).wait_send()

            @pl.when((s <= z) & (z + 1 < line))
            def _(s=s, here=here):
                self.to_line(here, s, 0).wait_send()

            @pl.when((s >= z) & (z >= 1))
            def _(s=s, here=here):
                self.to_line(here, s, 1).wait_send()


class SquareGather:
    def __init__(self, me, full, sems):
        self.me, self.full, self.sems = me, full, sems
        self.rows = full.shape[0] // 4

    def copies(self):
        me, full, sems, rows = self.me, self.full, self.sems, self.rows
        half = rows // 2

        def part(first, size):
            return full.at[pl.ds(first, size)]

        return (
            remote(part(0, rows), part(rows, rows), sems.at[0], sems.at[1], me.x),
            remote(part(0, rows), part(2 * rows, rows), sems.at[2], sems.at[3], me.y),
            remote(part(rows, half), part(3 * rows, half), sems.at[4], sems.at[5], me.y),
            remote(
                part(2 * rows + half, half), part(3 * rows + half, half), sems.at[6], sems.at[7], me.x
            ),
        )

    def start(self):
        x, y, _, _ = self.copies()
        x.start()
        y.start()

    def forward(self):
        x, y, top, bottom = self.copies()
        x.wait_recv()
        top.start()
        y.wait_recv()
        bottom.start()

    def arrived(self):
        _, _, top, bottom = self.copies()
        top.wait_recv()
        bottom.wait_recv()

    def done(self):
        for copy in self.copies():
            copy.wait_send()


class SquareScatter:
    def __init__(self, me, stage, landed, sems):
        self.me, self.stage, self.landed, self.sems = me, stage, landed, sems
        self.half = stage.shape[1] // 2
        self.top, self.bottom = pl.ds(0, self.half), pl.ds(self.half, self.half)

    def copies(self):
        me, stage, landed, sems = self.me, self.stage, self.landed, self.sems
        top, bottom = self.top, self.bottom
        return (
            remote(stage.at[2, top], landed.at[2, top], sems.at[0], sems.at[1], me.y),
            remote(stage.at[2, bottom], landed.at[2, bottom], sems.at[2], sems.at[3], me.x),
            remote(stage.at[0, bottom], landed.at[0, bottom], sems.at[4], sems.at[5], me.x),
            remote(stage.at[1, top], landed.at[1, top], sems.at[6], sems.at[7], me.y),
            remote(stage.at[0, top], landed.at[0, top], sems.at[8], sems.at[9], me.x),
            remote(stage.at[1, bottom], landed.at[1, bottom], sems.at[10], sems.at[11], me.y),
        )

    def diagonal_ready(self):
        copies = self.copies()
        copies[0].start()
        copies[1].start()

    def side_ready(self, slot):
        self.copies()[2 + slot].start()

    def sides_ready(self):
        self.side_ready(0)
        self.side_ready(1)

    def combine(self):
        copies = self.copies()
        for n, slot, at in ((0, 0, self.top), (1, 1, self.bottom)):
            copies[n].wait_recv()
            add_rows(self.stage, slot, at, self.landed)
            copies[4 + n].start()

    def arrived(self):
        for copy in self.copies()[2:]:
            copy.wait_recv()

    def done(self):
        for copy in self.copies():
            copy.wait_send()


def add_rows(stage, slot, at, landed):
    step = 32

    @pl.loop(0, at.size // step)
    def _(n):
        here = pl.ds(pl.multiple_of(at.start + n * step, step), step)
        total = stage[slot, here, :].astype(F32) + landed[2, here, :].astype(F32)
        stage[slot, here, :] = total.astype(BF16)


def remote(src, dst, send_sem, recv_sem, device):
    return pltpu.make_async_remote_copy(
        src_ref=src, dst_ref=dst, send_sem=send_sem, recv_sem=recv_sem, device_id=device,
        device_id_type=pl.DeviceIdType.MESH,
    )


class Place:
    def __init__(self, dp):
        index = lax.axis_index("dp")
        self.index, self.dp = index, dp
        self.line = dp // 2
        self.z, self.core = index // 2, index % 2
        self.at_end = (self.z == 0) | (self.z == self.line - 1)
        self.t = lax.axis_index("tensor")
        tx, ty = self.t % 2, self.t // 2
        self.other = {"dp": index + 1 - 2 * self.core}
        self.up, self.down = {"dp": index + 2}, {"dp": index - 2}
        self.next, self.far = {"dp": index + 2 - 4 * (self.z % 2)}, {"dp": index + 4 - 8 * (self.z // 2)}
        self.x = {"tensor": self.t + 1 - 2 * tx}
        self.y = {"tensor": self.t + 2 - 4 * ty}
        self.spots = [
            (tx if i % 2 == 0 else 1 - tx) + 2 * (ty if i // 2 == 0 else 1 - ty) for i in range(4)
        ]

    def window(self, i, rows, seg_col, seg_ref, bias_ref):
        spots = []
        for n in range(-(-(MOST - 1) // rows) + 1):
            j = jnp.maximum(i - n, 0)
            place = (j % 2 + self.t % 2) % 2 + 2 * ((j // 2 + self.t // 2) % 2)
            same = seg_col == seg_ref[place][0:1, :]
            if n == 0:
                row = lax.broadcasted_iota(jnp.int32, (rows, rows), 0)
                col = lax.broadcasted_iota(jnp.int32, (rows, rows), 1)
                bias_ref[n] = jnp.where(same & (col <= row), 0.0, NEG)
            else:
                bias_ref[n] = jnp.where(same, jnp.where(i >= n, 0.0, NEG), NEG)
            spots.append(pl.ds(pl.multiple_of(place * rows, rows), rows))
        return spots

    def greet(self):
        barrier = pltpu.get_barrier_semaphore()
        peers = [self.x, self.y] + [{"dp": (self.index + k) % self.dp} for k in range(1, self.dp)]
        for device in peers:
            pl.semaphore_signal(
                barrier, inc=1, device_id=device, device_id_type=pl.DeviceIdType.MESH
            )
        pl.semaphore_wait(barrier, len(peers))


def norm_rows(count, body, step=32):
    @pl.loop(0, count // step)
    def _(n):
        body(pl.ds(pl.multiple_of(n * step, step), step))


def attend(pair, first, at, spots, head_lane, q_ref, k_ref, v_ref, mixed_ref, lse_ref, bias_ref):
    lanes = pl.ds(pl.multiple_of(pair * 128, 128), 128)
    query = q_ref[at, lanes]
    outs, stats = [], []
    for h in range(2):
        mine = (head_lane < HEAD_DIM) if h == 0 else (head_lane >= HEAD_DIM)
        qm = jnp.where(mine, query, 0) * jnp.asarray(HEAD_DIM**-0.5, BF16)
        scores = [dot_nt(qm, k_ref[s, lanes]) + bias_ref[n] for n, s in enumerate(spots)]
        top = functools.reduce(jnp.maximum, [jnp.max(s, axis=1, keepdims=True) for s in scores])
        weights = [jnp.exp(s - top) for s in scores]
        total = sum(jnp.sum(w, axis=1, keepdims=True) for w in weights)
        out = sum(dot_nn(w.astype(BF16), v_ref[s, lanes]) for w, s in zip(weights, spots))
        outs.append(out / total)
        stats.append(top + jnp.log(total))
    mixed_ref[at, lanes] = jnp.where(head_lane < HEAD_DIM, outs[0], outs[1]).astype(BF16)
    kept = jnp.where(pair + first == 0, 0.0, lse_ref[at, :])
    for h in range(2):
        kept = jnp.where(head_lane == first + pair * 2 + h, stats[h], kept)
    lse_ref[at, :] = kept


def add_into(total, other, rows, step=64):
    @pl.loop(0, rows // step)
    def _(n):
        at = pl.ds(pl.multiple_of(n * step, step), step)
        total[at, :] = (total[at, :].astype(F32) + other[at, :].astype(F32)).astype(total.dtype)


KEPT_SLOT = 6


class LineScatter:
    def __init__(self, me, rows, mine, theirs, swapped, kept, landed, work, sems, step_sems):
        cut = lambda ref: ref.at[:, pl.ds(0, rows)]
        self.me, self.rows = me, rows
        self.mine, self.theirs, self.swapped = cut(mine), cut(theirs), cut(swapped)
        self.kept, self.landed, self.work = cut(kept), cut(landed), cut(work)
        self.sems, self.step_sems = sems, step_sems

    def swap(self):
        return remote(
            self.theirs, self.swapped, self.step_sems.at[0], self.step_sems.at[1], self.me.other
        )

    def keep(self):
        return pltpu.make_async_copy(self.mine, self.kept, self.step_sems.at[2])

    def send(self, src, s, upward, z):
        line = self.me.line
        if upward:
            slot, device = s, self.me.up
        else:
            slot, device = (s if s < z - 1 else line), self.me.down
        return remote(
            src, self.landed.at[slot], self.sems.at[s], self.sems.at[line + slot], device
        )

    def landing(self, slot):
        line = self.me.line
        return remote(
            self.landed.at[slot], self.landed.at[slot], self.sems.at[0],
            self.sems.at[line + slot], self.me.other,
        )

    def load(self, src, n):
        return pltpu.make_async_copy(src, self.work.at[n], self.step_sems.at[3 + n])

    def reduce(self, free_sem):
        line = self.me.line
        self.swap().wait_recv()
        for s in range(line):
            add_into(self.mine.at[s], self.swapped.at[s], self.rows)
        pl.semaphore_signal(
            free_sem, inc=1, device_id=self.me.other, device_id_type=pl.DeviceIdType.MESH
        )
        self.keep().start()
        self.swap().wait_send()
        self.keep().wait()
        for end, upward in ((0, True), (line - 1, False)):

            @pl.when(self.me.z == end)
            def _(end=end, upward=upward):
                order = range(line - 1, end, -1) if upward else range(end)
                for s in order:
                    self.send(self.kept.at[s], s, upward, end).start()

    def going(self, p):
        line = self.me.line
        for z, upward in ((p, True), (line - 1 - p, False)):
            targets = list(range(line - 1, z, -1)) if upward else list(range(z))
            yield z, upward, targets

    def run_phase(self, p, first):
        for z, upward, targets in self.going(p):

            @pl.when(self.me.z == z)
            def _(z=z, upward=upward, targets=targets):
                for n, s in enumerate(targets):
                    self.load(self.kept.at[s], KEPT_SLOT + n).start()
                for n, s in enumerate(targets):
                    a, b = first + n, KEPT_SLOT + n
                    self.landing(s).wait_recv()
                    self.load(self.landed.at[s], a).start()
                    self.load(self.kept.at[s], b).wait()
                    self.load(self.landed.at[s], a).wait()
                    add_into(self.work.at[a], self.work.at[b], self.rows)
                    self.send(self.work.at[a], s, upward, z).start()

    def sent_phase(self, p, first):
        for z, upward, targets in self.going(p):

            @pl.when(self.me.z == z)
            def _(z=z, upward=upward, targets=targets):
                for n, s in enumerate(targets):
                    self.send(self.work.at[first + n], s, upward, z).wait_send()

    def load_last(self, first):
        me = self.me
        self.load(self.kept.at[me.z], first).start()

        @pl.when(me.z >= 1)
        def _():
            self.landing(me.z).wait_recv()
            self.load(self.landed.at[me.z], first + 1).start()

        @pl.when(me.z < me.line - 1)
        def _():
            self.landing(me.line).wait_recv()
            self.load(self.landed.at[me.line], first + 2).start()

    def run_last(self, first, total):
        me = self.me
        here = total.at[pl.ds(0, self.rows)]
        self.load(self.kept.at[me.z], first).wait()

        def put(n, step=64):
            @pl.loop(0, self.rows // step)
            def _(i):
                at = pl.ds(pl.multiple_of(i * step, step), step)
                if n == first:
                    here[at, :] = self.work[n, at, :].astype(F32)
                else:
                    here[at, :] += self.work[n, at, :].astype(F32)

        put(first)

        @pl.when(me.z >= 1)
        def _():
            self.load(self.landed.at[me.z], first + 1).wait()
            put(first + 1)

        @pl.when(me.z < me.line - 1)
        def _():
            self.load(self.landed.at[me.line], first + 2).wait()
            put(first + 2)

    def done(self):
        line = self.me.line
        for end, upward in ((0, True), (line - 1, False)):

            @pl.when(self.me.z == end)
            def _(end=end, upward=upward):
                for s in range(line - 1, end, -1) if upward else range(end):
                    self.send(self.kept.at[s], s, upward, end).wait_send()


WORK_SLOTS = (0, 2, 4, 5)


class Ticks:
    def __init__(self, chunks, total, writers, held):
        self.chunks, self.total, self.writers, self.held = chunks, total, writers, held
        self.k, self.second, self.last, self.written = 0, 0, 0, 0
        self.sent = [None] * len(WORK_SLOTS)

    def run(self, chunk, p, group):
        first = WORK_SLOTS[group]
        if self.sent[group] is not None:
            self.sent[group].sent_phase(p, first)
        chunk.run_phase(p, first)
        self.sent[group] = chunk

    def finish(self, n):
        self.chunks[n].load_last(KEPT_SLOT)
        if n > 0:
            self.writers[n - 1].wait()
        self.chunks[n].run_last(KEPT_SLOT, self.total)
        self.writers[n].start()

    def tick(self, most=2, last=2):
        k, count = self.k, len(self.chunks)
        ready, done = min(k, count), self.second
        if k >= self.held:
            for _ in range(most):
                if self.second < ready:
                    self.run(self.chunks[self.second], 2, 2 + self.second % 2)
                    self.second += 1
        if k < count:
            self.run(self.chunks[k], 1, k % 2)
        if k >= self.held:
            for _ in range(last):
                if self.last < done:
                    self.finish(self.last)
                    self.last += 1
        self.k += 1

    def rest(self):
        while self.last < len(self.chunks):
            self.tick(3, 3)

    def done(self):
        self.writers[-1].wait()
        for group, p in ((0, 1), (1, 1), (2, 2), (3, 2)):
            self.sent[group].sent_phase(p, WORK_SLOTS[group])
        for chunk in self.chunks:
            chunk.done()


class Writer:
    def __init__(self, total, turned, parts, sem):
        self.total, self.turned, self.parts, self.sem = total, turned, parts, sem

    def copies(self):
        for n, (dst, _) in enumerate(self.parts):
            yield pltpu.make_async_copy(self.turned.at[n], dst, self.sem.at[n])

    def start(self):
        for n, (_, flip) in enumerate(self.parts):
            block = self.total[pl.ds(n * 256, 256), :]
            self.turned[n] = (block.T if flip else block).astype(BF16)
        for copy in self.copies():
            copy.start()

    def wait(self):
        for copy in self.copies():
            copy.wait()


def norm_back_rows(count, gain, values_of, grads_of, gain_ref, row, put, step=32):
    @pl.loop(0, count // step)
    def _(n):
        at = pl.ds(pl.multiple_of(n * step, step), step)
        values, grads = values_of(at), grads_of(at)
        factor = norm_factor(values)
        scaled = grads * gain
        back = factor * scaled - values * factor * factor * factor * jnp.mean(
            scaled * values, axis=-1, keepdims=True
        )
        gain_ref[row : row + 1, :] += jnp.sum(grads * values * factor, axis=0, keepdims=True)
        put(at, back)


def attend_back(
    pair, at, spots, head_lane, q_ref, k_ref, v_ref, dm_ref, lse_ref, bias_ref, dqa_ref, dka_ref, dva_ref
):
    scale = HEAD_DIM**-0.5
    rows = at.size
    lanes = pl.ds(pl.multiple_of(pair * 128, 128), 128)
    query, grad = q_ref[at, lanes], dm_ref[at, lanes]
    logs = lse_ref[at, :]
    outs = []
    for h in range(2):
        mine = (head_lane < HEAD_DIM) if h == 0 else (head_lane >= HEAD_DIM)
        qm = jnp.where(mine, query, 0) * jnp.asarray(scale, BF16)
        gm = jnp.where(mine, grad, 0)
        log = jnp.sum(
            jnp.where(head_lane == pair * 2 + h, logs, 0.0), axis=1, keepdims=True
        )
        weights = [
            jnp.exp(dot_nt(qm, k_ref[s, lanes]) + bias_ref[n] - log) for n, s in enumerate(spots)
        ]
        grads = [dot_nt(gm, v_ref[s, lanes]) for s in spots]
        inner = sum(jnp.sum(w * g, axis=1, keepdims=True) for w, g in zip(weights, grads))
        dq = jnp.zeros((rows, 128), F32)
        for w, g, s in zip(weights, grads, spots):
            ds = (w * (g - inner)).astype(BF16)
            dva_ref[s, lanes] += dot_tn(w.astype(BF16), gm)
            dka_ref[s, lanes] += dot_tn(ds, qm)
            dq = dq + dot_nn(ds, k_ref[s, lanes])
        outs.append(dq)
    dqa_ref[:, lanes] = jnp.where(head_lane < HEAD_DIM, outs[0], outs[1]) * scale


TICK_AFTER = (3, 5, 6)
TICK_HELD = 3


def layer_kernel(
    dp, x_in, g_in, gain_ref, wq_in, wk_in, wv_in, wo_in, gate_in, up_in, down_in, doc_ref,
    output_out, input_grad_out, gain_out, gate_out, up_out, down_out, q_out, k_out, v_out, o_out,
    wa_full, wo_full, wf_full, hidden_all, kept_all, landed_all, y_all, normed_all, q_all, k_all, v_all,
    mixed_all, lse_all, cos_all, sin_all, segc_all, segr_all,
    x_ref, wa_src, wo_src, wf_src, gains_full, rows_a, rows_m, rows_g,
    theirs, swapped, mine, work, total, turned, stage, landed, own, gm, middle, gp, gp_landed,
    sem_in, sem_gains, sem_a, sem_o, sem_f, sem_n, sem_m, sem_g, sem_g2, sem_s, sem_line, sem_step, sem_write,
    sem_gain, sem_c, sem_w, free_core, free_x, free_y,
):
    me = Place(dp)
    line = me.line
    d = x_in.shape[1]
    half, local = d // 2, x_in.shape[0]
    shard = half // line
    rows = LEN // 4
    blocks = wf_src.shape[0]
    fw = wf_src.shape[2] // 3
    cols = wq_in.shape[1]
    groups = cols // GROUP

    def at_block(b):
        return pl.ds(pl.multiple_of(b * rows, rows), rows)

    def true_columns(side, s):
        core = me.core if side == 0 else 1 - me.core
        return pl.ds(pl.multiple_of((2 * s + core) * shard, shard), shard)

    def own_columns(side, s):
        return pl.ds(side * half + s * shard, shard)

    sides = [(side, s) for side in range(2) for s in range(line)]
    x_loads = [
        pltpu.make_async_copy(
            x_in.at[:, true_columns(*p)], x_ref.at[:, own_columns(*p)], sem_in.at[n]
        )
        for n, p in enumerate(sides)
    ]
    g_loads = [
        pltpu.make_async_copy(
            g_in.at[:, true_columns(*p)], rows_g.at[pl.ds(0, local), own_columns(*p)],
            sem_in.at[2 * line + n],
        )
        for n, p in enumerate(sides)
    ]
    first_sem = 4 * line
    a_loads = [
        pltpu.make_async_copy(ref, wa_src.at[:, pl.ds(n * cols, cols)], sem_in.at[first_sem + n])
        for n, ref in enumerate((wq_in, wk_in, wv_in))
    ]
    f_loads = [
        pltpu.make_async_copy(
            ref.at[:, pl.ds(n * fw, fw)], wf_src.at[n, :, pl.ds(part * fw, fw)],
            sem_in.at[first_sem + 3 + 2 * n + part],
        )
        for n in range(blocks)
        for part, ref in enumerate((gate_in, up_in))
    ]
    for copy in a_loads + x_loads + g_loads + f_loads:
        copy.start()
    gains_full[0, pl.ds(pl.multiple_of(me.z * 16, 16), 16), :] = gain_ref[...]
    me.greet()

    def gain_copy(k, sender):
        place = gains_full.at[k % 2, pl.ds(pl.multiple_of(sender // 2 * 16, 16), 16)]
        return remote(
            gain_ref, place, sem_gains.at[0, k], sem_gains.at[1, k], {"dp": (me.index + k) % dp}
        )

    for k in range(1, dp):
        gain_copy(k, me.index).start()

    wa = LineGather(me, wa_src, wa_full, sem_a)
    wo = LineGather(me, wo_src, wo_full, sem_o)
    gathers = [LineGather(me, wf_src.at[n], wf_full.at[n], sem_f.at[n]) for n in range(blocks)]
    order = [wa, wo] + gathers

    def start_all():
        for one in gathers:
            one.start()

    acts = []
    for n, one in enumerate(order):
        for h in range(1, line):

            def act(n=n, one=one, h=h):
                one.hop(h)
                if h == 2 and n == 0:
                    wo.start()
                    pl.when(me.at_end)(start_all)
                if n == 1 and h == 2:
                    pl.when(jnp.logical_not(me.at_end))(gathers[0].start)
                    pl.when(jnp.logical_not(me.at_end))(gathers[1].start)
                if h == 1 and 2 <= n < blocks:
                    pl.when(jnp.logical_not(me.at_end))(order[n + 2].start)

            acts.append(act)

    def poll(count=1):
        for _ in range(min(count, len(acts))):
            acts.pop(0)()

    def hops_done(n):
        return len(acts) <= (blocks - 1 - n) * (line - 1)

    for copy in a_loads:
        copy.wait()
    wa.start()
    for k in range(1, dp):
        gain_copy(k, (me.index + dp - k) % dp).wait_recv()
    for copy in x_loads:
        copy.wait()

    def gain_row(which):
        return jnp.concatenate(
            [
                gains_full[side, pl.ds(s * 16 + which, 1), :].astype(F32)
                for side in range(2)
                for s in range(line)
            ],
            axis=1,
        )

    gain_one, gain_two = gain_row(0), gain_row(1)

    def first_norm(at):
        values = x_ref[at, :].astype(F32)
        rows_a[at, :] = (values * norm_factor(values) * gain_one).astype(BF16)

    norm_rows(local, first_norm)
    normed = SquareGather(me, rows_a, sem_n)
    grads = SquareGather(me, rows_g, sem_g)
    normed_mlp = SquareGather(me, rows_m, sem_m)
    square = SquareGather(me, rows_a, sem_g2)
    scatter = SquareScatter(me, stage, landed, sem_s)
    normed.start()
    for n in range(cols // 256):
        wo_src[:, pl.ds(n * 256, 256)] = wo_in[pl.ds(n * 256, 256), :].T
    for n in range(blocks):
        wf_src[n, :, pl.ds(2 * fw, fw)] = down_in[pl.ds(n * fw, fw), :].T

    def tables(cos_ref, sin_ref, segc_ref, segr_ref):
        ends = []
        for k in range(doc_ref.shape[1]):
            length = doc_ref[0:1, k : k + 1]
            ends.append((length, length + ends[-1][1] if ends else length))

        def place_of(token):
            segment, first = jnp.zeros_like(token), jnp.zeros_like(token)
            for length, end in ends:
                passed = token >= end
                segment = segment + jnp.where(passed, 1, 0)
                first = first + jnp.where(passed, length, 0)
            return segment, token - first

        lane = lax.broadcasted_iota(jnp.int32, (1, 128), 1)
        pair = (lane % (HEAD_DIM // 2)).astype(F32)
        inverse = jnp.exp(pair * (-2.0 / HEAD_DIM * math.log(ROPE_BASE)))
        sign = jnp.where(lane % HEAD_DIM < HEAD_DIM // 2, -1.0, 1.0)
        for p in range(4):
            at = pl.ds(p * rows, rows)
            begin = me.spots[p] * rows
            segment, position = place_of(begin + lax.broadcasted_iota(jnp.int32, (rows, 128), 0))
            segc_ref[at, :] = segment
            angle = position.astype(F32) * inverse
            cos_ref[at, :] = jnp.cos(angle)
            sin_ref[at, :] = jnp.sin(angle) * sign
            segr_ref[p] = place_of(begin + lax.broadcasted_iota(jnp.int32, (8, rows), 1))[0]
        out = [
            pltpu.make_async_copy(a, b, sem_c.at[n])
            for n, (a, b) in enumerate(
                ((cos_ref, cos_all), (sin_ref, sin_all), (segc_ref, segc_all), (segr_ref, segr_all))
            )
        ]
        for copy in out:
            copy.start()
        for copy in out:
            copy.wait()

    table = pltpu.VMEM((LEN, 128), F32)
    segs = (pltpu.VMEM(segc_all.shape, jnp.int32), pltpu.VMEM(segr_all.shape, jnp.int32))
    pl.run_scoped(tables, table, table, *segs)
    for copy in f_loads:
        copy.wait()
    poll()
    for copy in g_loads:
        copy.wait()
    normed.forward()
    grads.start()
    poll(line - 3)
    normed.arrived()
    pl.when(me.at_end)(grads.forward)
    poll()
    wa.arrived()

    def free_landed():
        for device, sem in ((me.x, free_x), (me.y, free_y)):
            pl.semaphore_signal(
                sem, inc=1, device_id=device, device_id_type=pl.DeviceIdType.MESH
            )

    def wait_free():
        pl.semaphore_wait(free_x, 1)
        pl.semaphore_wait(free_y, 1)

    def summed(at):
        return own[at, :] + landed[0, at, :].astype(F32) + landed[1, at, :].astype(F32)

    def doubled(ref, at):
        part = ref[at, :]
        return jnp.concatenate([part] * (GROUP // 128), axis=1)

    head_lane = lax.broadcasted_iota(jnp.int32, (rows, 128), 1)

    def forward(
        wa_v, wo_v, q_ref, k_ref, v_ref, mixed_ref, mixed_t, lse_ref, cos_ref, sin_ref, segc_ref, segr_ref, bias_ref
    ):
        ins = [(cos_all, cos_ref), (sin_all, sin_ref), (segc_all, segc_ref), (segr_all, segr_ref)] + [
            (wa_full.at[side], wa_v.at[pl.ds(side * half, half)]) for side in range(2)
        ]
        loads = [pltpu.make_async_copy(a, b, sem_c.at[n]) for n, (a, b) in enumerate(ins)]
        for copy in loads:
            copy.start()
        for copy in loads:
            copy.wait()

        @pl.loop(0, 2)
        def _(r):
            at = pl.ds(pl.multiple_of(r * 2 * rows, 2 * rows), 2 * rows)
            cosine = jnp.concatenate([cos_ref[at, :]] * (cols // 128), axis=1)
            sine = jnp.concatenate([sin_ref[at, :]] * (cols // 128), axis=1)

            def product(part):
                return dot_nn(rows_a[at, :], wa_v[:, pl.ds(part * cols, cols)])

            query = product(0)
            q_ref[at, :] = (query * cosine + swap_halves(query) * sine).astype(BF16)
            keys = product(1)
            k_ref[at, :] = (keys * cosine + swap_halves(keys) * sine).astype(BF16)
            v_ref[at, :] = product(2).astype(BF16)

        outs = [(q_ref, q_all), (k_ref, k_all), (v_ref, v_all), (rows_a, normed_all)]
        stores = [pltpu.make_async_copy(a, b, sem_c.at[n]) for n, (a, b) in enumerate(outs)]
        for copy in stores:
            copy.start()
        poll(2)
        def queries(p):
            at = pl.ds(p * rows, rows)
            spots = me.window(me.spots[p], rows, segc_ref[at, 0:1], segr_ref, bias_ref)

            @pl.loop(0, cols // 128)
            def _(pair):
                attend(pair, 0, at, spots, head_lane, q_ref, k_ref, v_ref, mixed_ref, lse_ref, bias_ref)

        def out_rows(b, slot):
            at = pl.ds(b * rows, rows)
            for side in range(2):
                here = pl.ds(side * half, half)
                value = dot_nt(mixed_ref[at, :], wo_v[here, :])
                if slot is None:
                    own[:, here] = value
                else:
                    stage[slot, :, here] = value.astype(BF16)

        queries(3)
        poll(line - 3)
        queries(1)
        wo.arrived()
        wo_load = [
            pltpu.make_async_copy(wo_full.at[side], wo_v.at[pl.ds(side * half, half)], sem_w.at[0, side])
            for side in range(2)
        ]
        for copy in wo_load:
            copy.start()
        pl.when(jnp.logical_not(me.at_end))(grads.forward)
        for copy in wo_load:
            copy.wait()
        out_rows(3, 2)
        scatter.diagonal_ready()
        out_rows(1, 0)
        scatter.side_ready(0)
        queries(2)
        out_rows(2, 1)
        scatter.side_ready(1)
        poll()
        queries(0)
        mixed_t[...] = mixed_ref[...].T
        for n, (a, b) in enumerate(((mixed_t, mixed_all), (lse_ref, lse_all))):
            stores.append(pltpu.make_async_copy(a, b, sem_c.at[len(outs) + n]))
            stores[-1].start()
        out_rows(0, None)
        scatter.combine()
        poll(4)
        for copy in stores:
            copy.wait()
        normed.done()
        scatter.arrived()

    V = pltpu.VMEM
    slab = V((LEN, cols), BF16)
    bias = V((3, rows, rows), F32)
    pl.run_scoped(
        forward, V((d, 3 * cols), BF16), V((d, cols), BF16), slab, slab, slab, slab, V((cols, LEN), BF16), table, table, table,
        *segs, bias,
    )

    def second_norm(at):
        values = x_ref[at, :].astype(F32) + summed(at)
        middle[at, :] = values
        rows_m[at, :] = (values * norm_factor(values) * gain_two).astype(BF16)

    norm_rows(local, second_norm)
    normed_mlp.start()
    free_landed()
    scatter.done()
    poll(2)
    grads.arrived()

    sizes = [3 * fw] * blocks + [cols] + [3 * GROUP] * groups
    chunks = [
        LineScatter(me, size, mine, theirs, swapped, kept_all.at[n], landed_all.at[n], work, sem_line.at[n], sem_step)
        for n, size in enumerate(sizes)
    ]
    writers = []
    for n in range(blocks):
        here = pl.ds(n * fw, fw)
        parts = [(gate_out.at[:, here], True), (up_out.at[:, here], True), (down_out.at[here], False)]
        writers.append(Writer(total, turned, parts, sem_write))
    parts = [(o_out.at[pl.ds(n * 256, 256)], False) for n in range(cols // 256)]
    writers.append(Writer(total, turned, parts, sem_write))
    for n in range(groups):
        here = pl.ds(n * GROUP, GROUP)
        parts = [(ref.at[:, here], True) for ref in (q_out, k_out, v_out)]
        writers.append(Writer(total, turned, parts, sem_write))
    ticks = Ticks(chunks, total, writers, TICK_HELD)

    def swap(n):
        if n >= 1:
            pl.semaphore_wait(free_core, 1)
        chunks[n].swap().start()

    def products(left, right, first, size):
        for side, dst in ((0, mine), (1, theirs)):
            value = dot_nn(left[...], right[:, pl.ds(side * half, half)]).astype(BF16)
            for s in range(line):
                dst[s, pl.ds(first, size), :] = value[:, s * shard : (s + 1) * shard]

    def mlp(wb, sums, dgu_t, hid_t, hid):
        def weights(n):
            return [
                pltpu.make_async_copy(
                    wf_full.at[n, side], wb.at[n % 2, pl.ds(side * half, half)], sem_w.at[n % 2, side]
                )
                for side in range(2)
            ]

        def hidden_copy(n):
            return pltpu.make_async_copy(hid.at[n % 2], hidden_all.at[n], sem_c.at[n % 2])

        fetched = [False] * (blocks + 1)

        def to_stage(b, slot):
            @pl.loop(0, rows // 64)
            def _(i):
                at = pl.ds(pl.multiple_of(i * 64, 64), 64)
                there = pl.ds(pl.multiple_of(b * rows + i * 64, 64), 64)
                if slot is None:
                    own[at, :] = sums[there, :]
                else:
                    stage[slot, at, :] = sums[there, :].astype(BF16)

        def fetch(n):
            if n < blocks and not fetched[n]:
                while not hops_done(n):
                    poll()
                gathers[n].arrived()
                for copy in weights(n):
                    copy.start()
                fetched[n] = True

        for n in range(blocks):
            fetch(n)
            if n == 0:

                @pl.loop(0, LEN // 64)
                def _(i):
                    at = pl.ds(pl.multiple_of(i * 64, 64), 64)
                    sums[at, :] = jnp.zeros((64, d), F32)

            for copy in weights(n):
                copy.wait()
            if n == 1:
                chunks[0].reduce(free_core)
            if n + 1 < blocks and hops_done(n + 1):
                fetch(n + 1)
            if n >= 2:
                hidden_copy(n - 2).wait()
            w = wb.at[n % 2]
            gu_w, down_w = w.at[:, pl.ds(0, 2 * fw)], w.at[:, pl.ds(2 * fw, fw)]

            def block_rows(at, n=n, gu_w=gu_w, down_w=down_w):
                gu = dot_nn(rows_m[at, :], gu_w[...])
                grad_hidden = dot_nn(rows_g[at, :], down_w[...])
                gate_pre, upward = gu[:, :fw], gu[:, fw:]
                sig = jax.nn.sigmoid(gate_pre)
                activated = gate_pre * sig
                hidden = (activated * upward).astype(BF16)
                hid[n % 2, at, :] = hidden
                hid_t[:, at] = hidden.T
                grad_gate = grad_hidden * upward * sig * (1.0 + gate_pre * (1.0 - sig))
                grad_up = grad_hidden * activated
                dgu = jnp.concatenate([grad_gate, grad_up], axis=1).astype(BF16)
                dgu_t[:, at] = dgu.T

                @pl.loop(0, 2)
                def _(c):
                    here = pl.ds(pl.multiple_of(c * half, half), half)
                    sums[at, here] += dot_nt(dgu, gu_w[here, :])

            if n == 0:
                block_rows(pl.ds(0, rows))
                poll()
                normed_mlp.forward()
                block_rows(pl.ds(rows, 2 * rows))
                normed_mlp.arrived()
                block_rows(pl.ds(3 * rows, rows))
                poll()
            elif n == blocks - 1:
                wait_free()
                block_rows(pl.ds(3 * rows, rows))
                to_stage(3, 2)
                scatter.diagonal_ready()
                block_rows(pl.ds(rows, 2 * rows))
                to_stage(1, 0)
                to_stage(2, 1)
                scatter.sides_ready()
                block_rows(pl.ds(0, rows))
                to_stage(0, None)
            else:
                @pl.loop(0, 2)
                def _(r, block_rows=block_rows):
                    block_rows(pl.ds(pl.multiple_of(r * 2 * rows, 2 * rows), 2 * rows))
            hidden_copy(n).start()
            if n % 2 == 1:
                poll()
            if n >= 2:
                chunks[n - 1].reduce(free_core)
            products(dgu_t, rows_m, 0, 2 * fw)
            products(hid_t, rows_g, 2 * fw, fw)
            swap(n)
            poll()
            if n in TICK_AFTER:
                ticks.tick()
        for n in range(max(0, blocks - 2), blocks):
            hidden_copy(n).wait()

    pl.run_scoped(
        mlp, V((2, d, 3 * fw), BF16), V((LEN, d), F32), V((2 * fw, LEN), BF16), V((fw, LEN), BF16),
        V((2, LEN, fw), BF16),
    )
    gp[...] = jnp.zeros(gp.shape, F32)

    def down(hidden, dw, rest):
        ins = [(hidden_all.at[n], hidden.at[:, pl.ds(n * fw, fw)]) for n in range(blocks)] + [
            (
                wf_full.at[n, side, :, pl.ds(2 * fw, fw)],
                dw.at[pl.ds(side * half, half), pl.ds(n * fw, fw)],
            )
            for n in range(blocks)
            for side in range(2)
        ]
        loads = [pltpu.make_async_copy(a, b, sem_c.at[n]) for n, (a, b) in enumerate(ins)]
        for copy in loads:
            copy.start()
        scatter.combine()
        ticks.tick()
        for copy in loads:
            copy.wait()

        @pl.loop(0, 4)
        def _(n):
            at = pl.ds(pl.multiple_of(n // 2 * 2 * rows, 2 * rows), 2 * rows)
            here = pl.ds(pl.multiple_of(n % 2 * half, half), half)
            rest[at, here] = dot_nt(hidden[at, :], dw[here, :]).astype(BF16)

        out = pltpu.make_async_copy(rest, y_all, sem_c.at[0])
        out.start()
        out.wait()

    pl.run_scoped(
        down, V((LEN, blocks * fw), BF16), V((d, blocks * fw), BF16), V((LEN, d), BF16)
    )
    normed_mlp.done()
    grads.done()

    def attention(
        q_ref, k_ref, v_ref, mixed_t, lse_ref, cos_ref, sin_ref, segc_ref, segr_ref, out_w,
        dqa_ref, dka_ref, dva_ref, part_t, bias_ref,
    ):
        ins = [
            (q_all, q_ref), (k_all, k_ref), (v_all, v_ref), (lse_all, lse_ref), (cos_all, cos_ref),
            (sin_all, sin_ref), (segc_all, segc_ref), (segr_all, segr_ref), (wo_full, out_w),
            (mixed_all, mixed_t), (normed_all, rows_m),
        ]
        loads = [pltpu.make_async_copy(a, b, sem_c.at[n]) for n, (a, b) in enumerate(ins)]
        for copy in loads:
            copy.start()
        scatter.arrived()

        def second_norm_back(at, back):
            grad = rows_g[at, :].astype(F32) + back
            gm[at, :] = grad
            rows_a[at, :] = grad.astype(BF16)

        norm_back_rows(local, gain_two, lambda at: middle[at, :], summed, gp, 1, second_norm_back)
        square.start()
        free_landed()
        scatter.done()
        stage_in = [
            pltpu.make_async_copy(y_all.at[pl.ds(b * rows, rows)], stage.at[slot], sem_w.at[n // 2, n % 2])
            for n, (b, slot) in enumerate(((3, 2), (1, 0), (2, 1)))
        ]
        for copy in stage_in:
            copy.start()
        chunks[blocks - 1].reduce(free_core)
        ticks.tick()
        for copy in loads:
            copy.wait()

        @pl.loop(0, 4)
        def _(b):
            at = at_block(b)
            dka_ref[at, :] = jnp.zeros((rows, cols), F32)
            dva_ref[at, :] = jnp.zeros((rows, cols), F32)

        dm_ref = rows_g.at[:, pl.ds(3 * cols, cols)]

        def query_block(p, between=None):
            at = pl.ds(p * rows, rows)
            dm_ref[at, :] = (
                dot_nn(rows_a[at, :half], out_w[0]) + dot_nn(rows_a[at, half:], out_w[1])
            ).astype(BF16)
            spots = me.window(me.spots[p], rows, segc_ref[at, 0:1], segr_ref, bias_ref)

            def one_pair(pair):
                attend_back(
                    pair, at, spots, head_lane, q_ref, k_ref, v_ref, dm_ref, lse_ref, bias_ref,
                    dqa_ref, dka_ref, dva_ref,
                )

            pairs = GROUP // 128
            if between is None:
                pl.loop(0, cols // 128)(one_pair)
            for group in range(groups):
                if between is not None:
                    pl.loop(group * pairs, (group + 1) * pairs)(one_pair)
                lanes = pl.ds(group * GROUP, GROUP)
                value = dqa_ref[:, lanes]
                value = value * doubled(cos_ref, at) - swap_halves(value) * doubled(sin_ref, at)
                rows_g[at, lanes] = value.astype(BF16)
                if between is not None:
                    between(group)

        query_block(0)
        ticks.tick()
        square.forward()
        query_block(1)
        query_block(2)
        ticks.tick()
        for copy in stage_in:
            copy.wait()
        wait_free()
        square.arrived()
        scatter.diagonal_ready()
        scatter.sides_ready()
        products(mixed_t, rows_a, 0, cols)
        swap(blocks)
        def turn(group):
            @pl.loop(0, 4)
            def _(b):
                at = at_block(b)
                cosine, sine = doubled(cos_ref, at), doubled(sin_ref, at)
                for part, ref in enumerate((None, dka_ref, dva_ref)):
                    lanes = pl.ds(group * GROUP, GROUP)
                    there = pl.ds(part * cols + group * GROUP, GROUP)
                    if part == 0:
                        value = rows_g[at, there]
                    else:
                        value = ref[at, lanes]
                        if part == 1:
                            value = value * cosine - swap_halves(value) * sine
                        value = value.astype(BF16)
                        rows_g[at, there] = value
                    part_t[pl.ds(part * GROUP, GROUP), at] = value.T

        def finish_group(group):
            chunks[blocks + group].reduce(free_core)
            turn(group)
            products(part_t, rows_m, 0, 3 * GROUP)
            swap(blocks + 1 + group)
            if group == 0:
                scatter.combine()
                ticks.tick()

        query_block(3, finish_group)

    pl.run_scoped(
        attention, slab, slab, slab, V((cols, LEN), BF16), table, table, table, *segs,
        V(wo_full.shape, BF16), V((rows, cols), F32), V((LEN, cols), F32), V((LEN, cols), F32),
        V((3 * GROUP, LEN), BF16), bias,
    )

    def normed_grads(qkv_w, stage_two, y_mine):
        ins = [(wa_full.at[side], qkv_w.at[pl.ds(side * half, half)]) for side in range(2)]
        ins.append((y_all.at[pl.ds(0, rows)], y_mine))
        loads = [pltpu.make_async_copy(a, b, sem_c.at[n]) for n, (a, b) in enumerate(ins)]
        for copy in loads:
            copy.start()
        for copy in loads:
            copy.wait()

        def normed_grad(b, slot, count=1):
            at = pl.ds(b * rows, count * rows)
            for side in range(2):
                here = pl.ds(side * half, half)
                value = dot_nt(rows_g[at, pl.ds(0, 3 * cols)], qkv_w[here, :])
                if slot is None:
                    own[:, here] = value
                else:
                    for k in range(count):
                        stage_two[slot + k, :, here] = value[k * rows : (k + 1) * rows].astype(BF16)

        normed_grad(3, 2)
        normed_grad(1, 0, 2)
        normed_grad(0, None)
        scatter.arrived()

        def output_rows(at):
            value = middle[at, :] + y_mine[at, :].astype(F32)
            value = value + landed[0, at, :].astype(F32) + landed[1, at, :].astype(F32)
            y_mine[at, :] = value.astype(BF16)

        norm_rows(local, output_rows)
        free_landed()
        results = [
            pltpu.make_async_copy(
                y_mine.at[:, own_columns(*p)], output_out.at[:, true_columns(*p)], sem_in.at[n]
            )
            for n, p in enumerate(sides)
        ]
        for copy in results:
            copy.start()
        scatter.done()
        wait_free()
        scatter_two = SquareScatter(me, stage_two, landed, sem_s)
        scatter_two.diagonal_ready()
        scatter_two.sides_ready()
        chunks[blocks + groups].reduce(free_core)
        ticks.tick(2, 2)
        for copy in results:
            copy.wait()
        scatter_two.combine()
        ticks.tick(3, 2)
        ticks.tick(3, 0)
        ticks.tick(3, 0)
        scatter_two.arrived()
        scatter_two.done()

    pl.run_scoped(
        normed_grads, V((d, 3 * cols), BF16), V((3, local, d), BF16), V((local, d), BF16)
    )

    def first_norm_back(at, back):
        gm[at, :] += back

    norm_back_rows(
        local, gain_one, lambda at: x_ref[at, :].astype(F32), summed, gp, 0, first_norm_back
    )
    results = [
        pltpu.make_async_copy(
            gm.at[:, own_columns(*p)], input_grad_out.at[:, true_columns(*p)], sem_in.at[n]
        )
        for n, p in enumerate(sides)
    ]
    for copy in results:
        copy.start()
    peers = [me.x, me.y] + [{"dp": (me.index + k) % dp} for k in range(1, dp)]
    exchange = [
        remote(gp, gp_landed.at[n], sem_gain.at[n, 0], sem_gain.at[n, 1], device)
        for n, device in enumerate(peers)
    ]
    for n in range(2):
        exchange[n].start()
        exchange[n].wait()
        gp[...] += gp_landed[n]
    for copy in exchange[2:]:
        copy.start()
    ticks.rest()
    for copy in exchange[2:]:
        copy.wait()
    for k in range(1, dp):
        if k % 2 == 1:
            gp[:, :half] += gp_landed[1 + k, :, half:]
            gp[:, half:] += gp_landed[1 + k, :, :half]
        else:
            gp[...] += gp_landed[1 + k]
    gain_out[...] = gp[...]
    ticks.done()
    pl.semaphore_wait(free_core, 1)
    for k in range(1, dp):
        gain_copy(k, me.index).wait_send()
    for copy in results:
        copy.wait()
    for one in [wa, wo, square] + gathers:
        one.done()


def layer(dp, x, g, gains, wq, wk, wv, wo, gate, up, down, docs):
    line = dp // 2
    local, d = x.shape
    cols, ff = wq.shape[1], gate.shape[1]
    blocks, shard = FF_BLOCKS, d // dp
    fw = ff // blocks
    groups = cols // GROUP
    count = blocks + 1 + groups
    most = max(3 * fw, cols, 3 * GROUP)
    vm, hbm = pl.BlockSpec(memory_space=pltpu.VMEM), pl.BlockSpec(memory_space=pl.ANY)
    S, V, dma = jax.ShapeDtypeStruct, pltpu.VMEM, pltpu.SemaphoreType.DMA
    regular = pltpu.SemaphoreType.REGULAR
    slab = S((LEN, cols), BF16)
    piece = V((line, most, shard), BF16)
    return pl.pallas_call(
        functools.partial(layer_kernel, dp),
        in_specs=[hbm, hbm, vm, hbm, hbm, hbm, vm, hbm, hbm, vm, vm],
        out_specs=[hbm, hbm, vm] + [hbm] * 24,
        out_shape=[
            S((local, d), BF16), S((local, d), F32), S((8, d), F32),
            S((shard, ff), BF16), S((shard, ff), BF16), S((ff, shard), BF16),
            S((shard, cols), BF16), S((shard, cols), BF16), S((shard, cols), BF16), S((cols, shard), BF16),
            S((2, d // 2, 3 * cols), BF16), S((2, d // 2, cols), BF16),
            S((blocks, 2, d // 2, 3 * fw), BF16), S((blocks, LEN, fw), BF16),
            S((count, line, most, shard), BF16), S((count, line + 1, most, shard), BF16),
            S((LEN, d), BF16), S((LEN, d), BF16), slab, slab, slab, S((cols, LEN), BF16), S((LEN, 128), F32),
            S((LEN, 128), F32), S((LEN, 128), F32), S((LEN, 128), jnp.int32), S((4, 8, LEN // 4), jnp.int32),
        ],
        scratch_shapes=[
            V((local, d), BF16), V((shard, 3 * cols), BF16), V((shard, cols), BF16),
            V((blocks, shard, 3 * fw), BF16), V((2, line * 16, shard), BF16),
            V((LEN, d), BF16), V((LEN, d), BF16), V((LEN, d), BF16),
            piece, piece, piece, V((9, most, shard), BF16), V((most, shard), F32), V((3, shard, 256), BF16),
            V((3, local, d), BF16), V((3, local, d), BF16), V((local, d), F32), V((local, d), F32),
            V((local, d), F32), V((8, d), F32), V((dp + 1, 8, d), F32),
            dma((4 * line + 3 + 2 * blocks,)), dma((2, dp)), dma((6, line)), dma((6, line)),
            dma((blocks, 6, line)), dma((8,)), dma((8,)), dma((8,)), dma((8,)), dma((12,)),
            dma((count, 2 * line + 1)), dma((12,)), dma((3,)), dma((dp + 1, 2)), dma((3 * blocks,)), dma((2, 2)),
            regular, regular, regular,
        ],
        compiler_params=pltpu.CompilerParams(
            vmem_limit_bytes=VMEM_BYTES, collective_id=0, has_side_effects=True
        ),
        name="layer",
    )(x, g, gains, wq, wk, wv, wo, gate, up, down, docs)


def widen_kernel(*refs):
    count = (len(refs) - 2) // 4
    ins, outs = refs[:count], refs[count : 2 * count]
    here, wide = refs[2 * count : 3 * count], refs[3 * count : 4 * count]
    sem_in, sem_out = refs[-2:]
    loads = [pltpu.make_async_copy(a, b, sem_in.at[n]) for n, (a, b) in enumerate(zip(ins, here))]
    stores = [pltpu.make_async_copy(a, b, sem_out.at[n]) for n, (a, b) in enumerate(zip(wide, outs))]
    for copy in loads:
        copy.start()
    for n, (load, store) in enumerate(zip(loads, stores)):
        load.wait()
        rows = here[n].shape[0]
        step = min(rows, 64)

        @pl.loop(0, rows // step)
        def _(i, n=n, step=step):
            at = pl.ds(pl.multiple_of(i * step, step), step)
            wide[n][at, :] = here[n][at, :].astype(wide[n].dtype)

        store.start()
    for store in stores:
        store.wait()


def widen(arrays, dtypes):
    hbm = pl.BlockSpec(memory_space=pl.ANY)
    return pl.pallas_call(
        widen_kernel,
        in_specs=[hbm] * len(arrays),
        out_specs=[hbm] * len(arrays),
        out_shape=[jax.ShapeDtypeStruct(a.shape, t) for a, t in zip(arrays, dtypes)],
        scratch_shapes=[pltpu.VMEM(a.shape, a.dtype) for a in arrays]
        + [pltpu.VMEM(a.shape, t) for a, t in zip(arrays, dtypes)]
        + [pltpu.SemaphoreType.DMA((len(arrays),))] * 2,
        compiler_params=pltpu.CompilerParams(vmem_limit_bytes=VMEM_BYTES),
        name="widen",
    )(*arrays)


def on_device(
    dp, tensor, hidden_in, doc_lengths, gain_attn, w_query, w_key, w_value, w_out, gain_mlp,
    w_gate, w_up, w_down, cotangent,
):
    line = dp // 2
    core = lax.axis_index("dp") % 2
    place = lax.axis_index("tensor")
    square = tensor == 4 and dp == 8
    same_core = [[c + 2 * z for z in range(line)] for c in range(2)]
    sibling = [(i, i ^ 1) for i in range(dp)]
    d = hidden_in.shape[1]
    local = hidden_in.shape[0]

    def own_first(a):
        s = a.reshape(a.shape[:-1] + (line, 2, d // dp))
        even, odd = s[..., 0, :], s[..., 1, :]
        out = jnp.concatenate(
            [jnp.where(core == 0, even, odd), jnp.where(core == 0, odd, even)], axis=-2
        )
        return out.reshape(a.shape)

    def true_order(a):
        s = a.reshape(a.shape[:-1] + (2, line, d // dp))
        first, second = s[..., 0, :, :], s[..., 1, :, :]
        out = jnp.stack(
            [jnp.where(core == 0, first, second), jnp.where(core == 0, second, first)], axis=-2
        )
        return out.reshape(a.shape)

    def hop(a, step):
        return lax.ppermute(a, "tensor", [(i, i ^ step) for i in range(tensor)])

    def gather_rows(a):
        if not square:
            return lax.all_gather(a, "tensor", axis=0, tiled=True)
        half = a.shape[0] // 2
        from_x, from_y = hop(a, 1), hop(a, 2)
        top, bottom = hop(from_x[:half], 2), hop(from_y[half:], 1)
        return jnp.concatenate([a, from_x, from_y, top, bottom], axis=0)

    def scatter_rows(a):
        if not square:
            return lax.psum_scatter(a, "tensor", scatter_dimension=0, tiled=True).astype(F32)
        n = a.shape[0] // 4
        half = n // 2
        top = hop(a[3 * n : 3 * n + half], 2)
        bottom = hop(a[3 * n + half :], 1)
        for_x = jnp.concatenate([a[n : n + half] + top, a[n + half : 2 * n]], axis=0)
        for_y = jnp.concatenate([a[2 * n : 2 * n + half], a[2 * n + half : 3 * n] + bottom], axis=0)
        return (a[:n].astype(F32) + hop(for_x, 1).astype(F32)) + hop(for_y, 2).astype(F32)

    def line_gather(a):
        own = lax.all_gather(a, "dp", axis=0, axis_index_groups=same_core, tiled=True)
        return own, lax.ppermute(own, "dp", sibling)

    def line_scatter(own, sib):
        mine = own + lax.ppermute(sib, "dp", sibling)
        return lax.psum_scatter(
            mine, "dp", scatter_dimension=0, axis_index_groups=same_core, tiled=True
        ).astype(F32)

    blocks = 4
    rows = LEN // blocks
    key = place if square else jnp.zeros((), jnp.int32)
    tokens = (
        (jnp.arange(blocks, dtype=jnp.int32) ^ key)[:, None] * rows
        + jnp.arange(rows, dtype=jnp.int32)[None, :]
    ).reshape(LEN)
    segment, position = doc_tables(doc_lengths, tokens)
    cosine, sine = rotary_tables(position)
    segc = jnp.broadcast_to(segment[:, None], (LEN, 128))
    segr = jnp.broadcast_to(segment.reshape(blocks, 1, rows), (blocks, 8, rows))
    key = key.reshape(1)
    cols = w_query.shape[1]
    if square:
        gain_rows = jnp.pad(
            jnp.concatenate([gain_attn, gain_mlp]), (0, 14 * gain_attn.shape[0])
        ).reshape(16, -1)
        (
            output, input_grad, gain_sum, grad_gate, grad_up, grad_down, grad_query, grad_key,
            grad_value, grad_out, *_,
        ) = layer(
            dp, hidden_in, cotangent, gain_rows, w_query, w_key, w_value, w_out, w_gate, w_up,
            w_down, doc_lengths,
        )
        share = d // (dp * tensor)
        first = (lax.axis_index("dp") // 2) * (d // dp) + place * share
        gain_sum = lax.dynamic_slice_in_dim(gain_sum, first, share, 1)
        grads = (grad_gate, grad_up, grad_down, grad_query, grad_key, grad_value, grad_out)
        (
            output, input_grad, grad_gate, grad_up, grad_down, grad_query, grad_key, grad_value, grad_out
        ) = widen((output, input_grad) + grads, (BF16,) + (F32,) * 8)
        return (
            output, input_grad, gain_sum[0], grad_query, grad_key, grad_value, grad_out, gain_sum[1],
            grad_gate, grad_up, grad_down,
        )

    cosine, sine = (jnp.tile(a, (1, GROUP // 128)) for a in (cosine, sine))
    ff = w_gate.shape[1]
    fb = ff // FF_BLOCKS
    down_t = w_down.T
    shards = [
        jnp.concatenate([w[:, b * fb : (b + 1) * fb] for w in (w_gate, w_up, down_t)], axis=1)
        for b in range(FF_BLOCKS)
    ]
    qkv_shard = jnp.concatenate([w_query, w_key, w_value], axis=1)
    g_local = own_first(cotangent)
    inputs = own_first(hidden_in).astype(F32)
    factor_one = norm_factor(inputs)
    gains = lax.all_gather(jnp.stack([gain_attn, gain_mlp]), "dp", axis=0)
    gains = own_first(jnp.moveaxis(gains, 0, 1).reshape(2, d)).astype(F32)
    gain_one, gain_two = gains[0], gains[1]
    qkv_own, qkv_sib = line_gather(qkv_shard)
    out_own, out_sib = line_gather(w_out.T)
    normed = gather_rows((inputs * factor_one * gain_one).astype(BF16))
    g_all = gather_rows(g_local)
    query, keys, values, mixed, lse = attn_forward(
        blocks, key, normed, qkv_own, qkv_sib, cosine, sine, segc, segr
    )
    attended = jnp.concatenate(
        [dot_nt(mixed, out_own).astype(BF16), dot_nt(mixed, out_sib).astype(BF16)], axis=1
    )
    middle = inputs + scatter_rows(attended)
    factor_two = norm_factor(middle)
    normed_mlp = gather_rows((middle * factor_two * gain_two).astype(BF16))
    ff_sets = [jnp.concatenate(line_gather(shard), axis=0) for shard in shards]

    down_sum = jnp.zeros((LEN, d), F32)
    back_sum = jnp.zeros((LEN, d), F32)
    ff_grads = []
    for b in range(FF_BLOCKS):
        gate_w, up_w, down_w = jnp.split(ff_sets[b], 3, axis=1)
        gate_pre = dot_nn(normed_mlp, gate_w)
        upward = dot_nn(normed_mlp, up_w)
        grad_hidden = dot_nn(g_all, down_w)
        sig = jax.nn.sigmoid(gate_pre)
        activated = gate_pre * sig
        hidden = (activated * upward).astype(BF16)
        grad_gate_pre = (grad_hidden * upward * sig * (1.0 + gate_pre * (1.0 - sig))).astype(BF16)
        grad_upward = (grad_hidden * activated).astype(BF16)
        down_sum = down_sum + dot_nt(hidden, down_w)
        back_sum = back_sum + dot_nt(grad_gate_pre, gate_w) + dot_nt(grad_upward, up_w)
        grad = jnp.concatenate(
            [
                dot_tn(normed_mlp, grad_gate_pre).astype(BF16),
                dot_tn(normed_mlp, grad_upward).astype(BF16),
                dot_tn(g_all, hidden).astype(BF16),
            ],
            axis=1,
        )
        ff_grads.append(line_scatter(grad[: d // 2], grad[d // 2 :]))
    grad_norm_two = scatter_rows(back_sum.astype(BF16))
    output = true_order((middle + scatter_rows(down_sum.astype(BF16))).astype(BF16))
    grad_mid_norm, gain_two_part = norm_back(middle, factor_two, gain_two, grad_norm_two)
    grad_middle = g_local.astype(F32) + grad_mid_norm
    grad_mid_all = gather_rows(grad_middle.astype(BF16))

    dq, dk, dv = attn_backward(
        blocks, key, grad_mid_all, out_own, out_sib, query, keys, values, lse, cosine, sine,
        segc, segr,
    )
    grad = jnp.concatenate(
        [dot_tn(normed, dq), dot_tn(normed, dk), dot_tn(normed, dv), dot_tn(grad_mid_all, mixed)],
        axis=1,
    ).astype(BF16)
    attn_grads = line_scatter(grad[: d // 2], grad[d // 2 :])
    rows_grad = jnp.concatenate([dq, dk, dv], axis=1)
    back = jnp.concatenate(
        [
            dot_nt(rows_grad, qkv_own).astype(BF16),
            dot_nt(rows_grad, qkv_sib).astype(BF16),
        ],
        axis=1,
    )
    grad_in_norm, gain_one_part = norm_back(inputs, factor_one, gain_one, scatter_rows(back))
    input_grad = true_order(grad_middle + grad_in_norm)

    parts = true_order(jnp.stack([gain_one_part, gain_two_part])).reshape(2 * d)
    shares = lax.all_gather(parts, ("dp", "tensor"), axis=0)
    gain_sum = jnp.sum(shares, axis=0).reshape(2, d)
    share = d // (dp * tensor)
    first = (lax.axis_index("dp") * tensor + place) * share
    gain_sum = lax.dynamic_slice_in_dim(gain_sum, first, share, 1)

    return (
        output,
        input_grad,
        gain_sum[0],
        attn_grads[:, :cols],
        attn_grads[:, cols : 2 * cols],
        attn_grads[:, 2 * cols : 3 * cols],
        attn_grads[:, 3 * cols :].T,
        gain_sum[1],
        jnp.concatenate([g[:, :fb] for g in ff_grads], axis=1),
        jnp.concatenate([g[:, fb : 2 * fb] for g in ff_grads], axis=1),
        jnp.concatenate([g[:, 2 * fb :] for g in ff_grads], axis=1).T,
    )


def solution(mesh):
    shape = dict(mesh.shape)
    return jax.shard_map(
        functools.partial(on_device, shape["dp"], shape["tensor"]),
        mesh=mesh,
        in_specs=(
            P(("dp", "tensor"), None),
            P("dp", None),
            P("dp"),
            P("dp", "tensor"),
            P("dp", "tensor"),
            P("dp", "tensor"),
            P("tensor", "dp"),
            P("dp"),
            P("dp", "tensor"),
            P("dp", "tensor"),
            P("tensor", "dp"),
            P(("dp", "tensor"), None),
        ),
        out_specs=(
            P(("dp", "tensor"), None),
            P(("dp", "tensor"), None),
            P(("dp", "tensor")),
            P("dp", "tensor"),
            P("dp", "tensor"),
            P("dp", "tensor"),
            P("tensor", "dp"),
            P(("dp", "tensor")),
            P("dp", "tensor"),
            P("dp", "tensor"),
            P("tensor", "dp"),
        ),
        check_vma=False,
    )
```
